32 devices in a mesh: section: 2 (over core), dp: 8 (over z, x), tensor: 2 (over y).
Axes of the slice: x: 2, y: 2, z: 4, core: 2. Of those that a mesh axis runs over, the one named last changes fastest.
Arguments:
- boundary: bfloat16 [2, 2, 1024, 2048], P('section', None, ('dp', 'tensor')), may hold values from -6 to 6
- doc_lengths: int32 [2, 1, 8], replicated, may hold values from 1 to 960, as said below
- qkv_weight: bfloat16 [2, 2048, 3, 2048], P('section', 'dp', None, 'tensor'), may hold values from -0.125 to 0.125
- qv_bias: bfloat16 [2, 2, 16, 128], P('section', None, 'tensor', 'dp'), may hold values from -3 to 3
- out_weight: bfloat16 [2, 2048, 2048], P('section', 'tensor', 'dp'), may hold values from -1.5 to 1.5
- up_weight: bfloat16 [2, 2048, 8192], P('section', 'dp', 'tensor'), may hold values from -0.125 to 0.125
- up_bias: bfloat16 [2, 64, 128], P('section', 'tensor', 'dp'), may hold values from -3 to 3
- down_weight: bfloat16 [2, 8192, 2048], P('section', 'tensor', 'dp'), may hold values from -0.0625 to 0.0625
- norm_gains: bfloat16 [2, 2, 2048], P('section', None, ('dp', 'tensor')), may hold values from 0.5 to 1.5
- norm_biases: bfloat16 [2, 4, 2048], P('section', None, ('dp', 'tensor')), may hold values from -2 to 2
Outputs:
- acts: bfloat16 [2, 2, 1024, 2048], P('section', None, ('dp', 'tensor'))
- input_grads: float32 [2, 2, 1024, 2048], P('section', None, ('dp', 'tensor'))
- qkv_weight_grad: float32 [2, 2048, 3, 2048], P('section', 'dp', None, 'tensor')
- qv_bias_grad: float32 [2, 2, 16, 128], P('section', None, 'tensor', 'dp')
- out_weight_grad: float32 [2, 2048, 2048], P('section', 'tensor', 'dp')
- up_weight_grad: float32 [2, 2048, 8192], P('section', 'dp', 'tensor')
- up_bias_grad: float32 [2, 64, 128], P('section', 'tensor', 'dp')
- down_weight_grad: float32 [2, 8192, 2048], P('section', 'tensor', 'dp')
- norm_gains_grad: float32 [2, 2, 2048], P('section', None, ('dp', 'tensor'))
- norm_biases_grad: float32 [2, 4, 2048], P('section', None, ('dp', 'tensor'))
The draws below stay inside these ranges and needn't reach their ends.
Inputs may be any that keep to these rules, and one draw needn't show every extreme that they name: `doc_lengths`: each row lists the 8 documents of a packed sequence in order; one has exactly 960 tokens, the others together 32 to 63 tokens; the tokens after the last document are padding.
All inputs are finite; a program needn't handle non-finite values.
Results may differ from the reference program's by a relative error of at most 0.025.
Values may be sent and summed in bfloat16 or wider, within the bound.
A program may use at most 384 MiB of HBM per device.

```python
import math
import jax
import jax.numpy as jnp
from jax import lax

D = 2048
H = 16
HD = 128
FF = 8192
ROWS = 128
MICRO = 2
DOCS = 8
SEQ = 1024
SEQLEN = 1024
NSEQ = 1
N_SECTION = 2


def draw_doc_lengths(key, part):
    key = jax.random.fold_in(key, 11)
    short_total = ROWS // 2
    candidates = short_total - 1
    longest = SEQLEN - short_total

    def one_row(row_key):
        pad_key, cut_key, slot_key = jax.random.split(row_key, 3)
        padding = jax.random.randint(pad_key, (), 1, ROWS // 4 + 1).astype(jnp.int32)
        available = short_total - padding
        cut_values = jnp.arange(1, short_total, dtype=jnp.int32)
        rank_values = jax.random.permutation(cut_key, candidates).astype(jnp.int32)
        scores = jnp.where(cut_values < available, rank_values, -cut_values)
        chosen = lax.top_k(scores, DOCS - 2)[1]
        cut_points = jnp.sort(cut_values[chosen])
        bounds = jnp.concatenate([jnp.zeros((1,), jnp.int32), cut_points, available[None]])
        shorts = bounds[1:] - bounds[:-1]
        long_slot = jax.random.randint(slot_key, (), 0, DOCS).astype(jnp.int32)
        places = jnp.arange(DOCS, dtype=jnp.int32)
        source = jnp.clip(jnp.where(places < long_slot, places, places - 1), 0, DOCS - 2)
        return jnp.where(places == long_slot, longest, shorts[source]).astype(jnp.int32)
    rows = jax.vmap(one_row)(jax.random.split(key, MICRO * NSEQ))
    return rows.reshape(MICRO, NSEQ, DOCS)


def block_scale(stream_key, shape, cuts, least, top_value):
    level = 1.0
    for axis_at, parts in cuts:
        heights = jax.random.uniform(jax.random.fold_in(jax.random.fold_in(stream_key, 6), axis_at), (parts,), jnp.float32, least / len(cuts), top_value / len(cuts))
        level = level * jnp.repeat(jnp.exp(heights), shape[axis_at] // parts).reshape((-1,) + (1,) * (len(shape) - 1 - axis_at))
    return level


def bell_draw(own_key, dims, width, most, cuts=(), held_as=jnp.bfloat16):
    level = block_scale(own_key, dims, cuts, -0.22, 0.18) if cuts else 1.0
    entries = jax.random.normal(own_key, dims, jnp.float32) * width * level
    return jnp.minimum(jnp.maximum(entries, -most), most).astype(held_as)


def setup_inputs(seed: int = 0) -> dict:
    arg_keys = jax.random.split(jax.random.key(seed), 11)
    return {
        "boundary": bell_draw(arg_keys[0], (N_SECTION, MICRO, SEQ, D), 1.0, 6.0, ((0, 2), (2, 16))),
        "doc_lengths": draw_doc_lengths(jax.random.fold_in(arg_keys[10], 71), 0),
        "qkv_weight": bell_draw(arg_keys[2], (N_SECTION, D, 3, D), D ** -0.5, 0.125, ((0, 2), (1, 8), (3, 2))),
        "qv_bias": bell_draw(arg_keys[3], (N_SECTION, 2, H, HD), 0.5, 3.0, ((0, 2), (2, 2), (3, 8))),
        "out_weight": bell_draw(arg_keys[4], (N_SECTION, D, D), (max(1, 8 * D // SEQLEN)) ** -0.5, 1.5, ((0, 2), (1, 2), (2, 8))),
        "up_weight": bell_draw(arg_keys[5], (N_SECTION, D, FF), D ** -0.5, 0.125, ((0, 2), (1, 8), (2, 2))),
        "up_bias": bell_draw(arg_keys[6], (N_SECTION, FF // HD, HD), 0.5, 3.0, ((0, 2), (1, 2), (2, 8))),
        "down_weight": bell_draw(arg_keys[7], (N_SECTION, FF, D), FF ** -0.5, 0.0625, ((0, 2), (1, 2), (2, 8))),
        "norm_gains": jnp.clip(1.0 + 0.1 * jax.random.normal(arg_keys[8], (N_SECTION, 2, D), jnp.float32), 0.5, 1.5).astype(jnp.bfloat16),
        "norm_biases": bell_draw(arg_keys[9], (N_SECTION, 4, D), 0.3, 2.0, ((0, 2), (2, 16))),
    }


@jax.custom_vjp
def low(v):
    return lax.optimization_barrier(v.astype(jnp.bfloat16)).astype(jnp.float32)

@jax.custom_vjp
def low_back(v):
    return v

def low_keep(v):
    return (low(v), None)

def low_pass(kept, grad):
    return (grad,)

def back_keep(v):
    return (v, None)

def back_low(kept, grad):
    return (low(grad),)
low.defvjp(low_keep, low_pass)
low_back.defvjp(back_keep, back_low)
HIGH = lax.Precision.HIGHEST
EPSILON = 1e-05
NEG_FILL = -1e+30

def layer_norm(hidden, gain, shift):
    average = lax.optimization_barrier(jnp.mean(hidden, axis=-1, keepdims=True))
    centred = hidden - average
    variance = lax.optimization_barrier(jnp.mean(centred * centred, axis=-1, keepdims=True))
    return centred * lax.rsqrt(variance + EPSILON) * gain + shift

def visibility(lengths):
    positions = jnp.arange(SEQ, dtype=jnp.int32)
    seq_of = (positions // SEQLEN).astype(jnp.int32)
    local = (positions - seq_of * SEQLEN).astype(jnp.int32)
    doc_ends = jnp.cumsum(lengths.astype(jnp.int32), axis=1).astype(jnp.int32)
    ends_row = jnp.take(doc_ends, seq_of, axis=0)
    counted = lax.optimization_barrier(jnp.sum((local[:, None] >= ends_row).astype(jnp.int32), axis=1)).astype(jnp.int32)
    segment = (seq_of * (DOCS + 1) + counted).astype(jnp.int32)
    live_rows = local < ends_row[:, DOCS - 1]
    return (positions, segment, live_rows)

def attention(queries, keys, values, positions, segment, live_rows):
    block_rows = math.gcd(SEQ, 512)
    blocks = SEQ // block_rows
    query_blocks = queries.reshape(blocks, block_rows, H, HD)
    key_heads = keys.reshape(SEQ, H, HD)
    value_heads = values.reshape(SEQ, H, HD)
    scaling = HD ** (-0.5)

    def one_block(pieces):
        query_block, pos_block, seg_block, live_block = pieces
        scores = jnp.einsum('qhd,khd->hqk', query_block, key_heads, precision=HIGH) * scaling
        scores = low_back(scores)
        allowed = (seg_block[:, None] == segment[None, :]) & (positions[None, :] <= pos_block[:, None]) & live_block[:, None]
        scores = jnp.where(allowed[None], scores, NEG_FILL)
        probs = low(jax.nn.softmax(scores, axis=-1))
        return jnp.einsum('hqk,khd->qhd', probs, value_heads, precision=HIGH)
    result = lax.map(jax.checkpoint(one_block), (query_blocks, positions.reshape(blocks, block_rows), segment.reshape(blocks, block_rows), live_rows.reshape(blocks, block_rows)))
    return result.reshape(SEQ, D)

def layer(hidden, params, section_index, positions, segment, live_rows):
    qkv_w, qv_b, out_w, up_w, up_b, down_w, gain_rows, bias_rows = params
    normed = low(layer_norm(hidden, gain_rows[section_index, 0], bias_rows[section_index, 0]))
    projected = jnp.einsum('td,djh->tjh', normed, qkv_w[section_index], precision=HIGH)
    bias_qv = qv_b[section_index].reshape(2, D)
    queries = low_back(low(projected[:, 0] + bias_qv[0]))
    keys = low_back(low(projected[:, 1]))
    values = low_back(low(projected[:, 2] + bias_qv[1]))
    heads_out = attention(queries, keys, values, positions, segment, live_rows)
    heads_out = low_back(low(heads_out * live_rows.astype(jnp.float32)[:, None]))
    attn = low_back(jnp.dot(heads_out, out_w[section_index], precision=HIGH) + bias_rows[section_index, 1])
    middle = hidden + attn
    second = low(layer_norm(middle, gain_rows[section_index, 1], bias_rows[section_index, 2]))
    preact = low_back(jnp.dot(second, up_w[section_index], precision=HIGH) + up_b[section_index].reshape(FF))
    activated = low(jax.nn.gelu(preact, approximate=False))
    branch = low_back(jnp.dot(activated, down_w[section_index], precision=HIGH) + bias_rows[section_index, 3])
    return middle + branch

def reference(boundary, doc_lengths, qkv_weight, qv_bias, out_weight, up_weight, up_bias, down_weight, norm_gains, norm_biases):
    params = tuple((weight.astype(jnp.float32) for weight in (qkv_weight, qv_bias, out_weight, up_weight, up_bias, down_weight, norm_gains, norm_biases)))
    totals = tuple((jnp.zeros_like(weight) for weight in params))
    first_acts, last_acts, first_grads, last_grads = ([], [], [], [])
    for batch_index in range(MICRO):
        positions, segment, live_rows = visibility(doc_lengths[batch_index])

        def chain(entering, offset, weights):
            first_out = low(layer(entering, weights, 0, positions, segment, live_rows))
            carried = low_back(first_out) + offset
            return (layer(carried, weights, 1, positions, segment, live_rows), first_out)
        start = boundary[0, batch_index].astype(jnp.float32)
        offset = jnp.zeros((SEQ, D), jnp.float32)
        final_out, pullback, first_out = jax.vjp(chain, start, offset, params, has_aux=True)
        grad_start, grad_offset, grad_params = pullback(boundary[1, batch_index].astype(jnp.float32))
        totals = tuple((former + latter for former, latter in zip(totals, grad_params)))
        first_acts.append(first_out.astype(jnp.bfloat16))
        last_acts.append(final_out.astype(jnp.bfloat16))
        first_grads.append(grad_start)
        last_grads.append(grad_offset)
    acts = jnp.stack([jnp.stack(first_acts), jnp.stack(last_acts)])
    input_grads = jnp.stack([jnp.stack(first_grads), jnp.stack(last_grads)])
    return (acts, input_grads, totals[0], totals[1], totals[2], totals[3], totals[4], totals[5], totals[6], totals[7])
```

```python
from functools import partial
import math

import jax
import jax.numpy as jnp
from jax import lax
from jax.experimental import pallas as pl
from jax.experimental.pallas import tpu as pltpu
from jax.sharding import PartitionSpec as P

HD = 128


EPSILON = 1e-05
NEG_FILL = -1e30
MESH = pl.DeviceIdType.MESH


def from_behind(value, axis, steps):
    count = lax.axis_size(axis)
    first, last = (max(0, -steps), min(count, count - steps))
    return lax.ppermute(value, axis, [(source, source + steps) for source in range(first, last)])


def layer_norm(hidden, gain, shift):
    average = jnp.mean(hidden, axis=-1, keepdims=True)
    centred = hidden - average
    variance = jnp.mean(centred * centred, axis=-1, keepdims=True)
    inverse = lax.rsqrt(variance + EPSILON)
    normed = centred * inverse
    return (normed * gain + shift, normed, inverse)


def norm_back(grad_out, normed, inverse, gain):
    scaled = grad_out * gain
    return inverse * (
        scaled
        - jnp.mean(scaled, axis=-1, keepdims=True)
        - normed * jnp.mean(scaled * normed, axis=-1, keepdims=True)
    )


def visibility(lengths, dp_index, rows_dp, seq_len):
    per_seq = seq_len // lengths.shape[0]
    docs = lengths.shape[1]
    key_pos = jnp.arange(seq_len, dtype=jnp.int32)
    seq_of = key_pos // per_seq
    local = key_pos - seq_of * per_seq
    doc_ends = jnp.cumsum(lengths, axis=1)
    ends_row = jnp.take(doc_ends, seq_of, axis=0)
    key_seg = seq_of * (docs + 1) + jnp.sum((local[:, None] >= ends_row).astype(jnp.int32), axis=1)
    key_live = local < ends_row[:, docs - 1]
    start_row = dp_index * rows_dp
    query_pos = start_row + jnp.arange(rows_dp, dtype=jnp.int32)
    query_seg = lax.dynamic_slice_in_dim(key_seg, start_row, rows_dp)
    query_live = lax.dynamic_slice_in_dim(key_live, start_row, rows_dp)
    return (query_pos, query_seg, query_live, key_pos, key_seg, key_live)


def widen(rows_low):
    return lax.all_gather(rows_low, "tensor", axis=0, tiled=True)


def narrow(partial_rows):
    return lax.psum_scatter(
        partial_rows.astype(jnp.bfloat16), "tensor", scatter_dimension=0, tiled=True
    ).astype(jnp.float32)


def fetch_weights(
    qkv_weight, qv_bias, out_weight, up_weight, up_bias, down_weight, norm_gains, norm_biases
):
    w_qkv, b_qv, w_out, w_up, b_up, w_down = (
        lax.all_gather(qkv_weight[0], "dp", axis=0, tiled=True),
        lax.all_gather(qv_bias[0], "dp", axis=2, tiled=True),
        lax.all_gather(out_weight[0], "dp", axis=1, tiled=True),
        lax.all_gather(up_weight[0], "dp", axis=0, tiled=True),
        lax.all_gather(up_bias[0], "dp", axis=1, tiled=True),
        lax.all_gather(down_weight[0], "dp", axis=1, tiled=True),
    )
    gain_rows, bias_rows = (
        lax.all_gather(norm_gains[0], ("dp", "tensor"), axis=1, tiled=True),
        lax.all_gather(norm_biases[0], ("dp", "tensor"), axis=1, tiled=True),
    )
    return (
        w_qkv,
        b_qv.reshape(2, -1).astype(jnp.float32),
        w_out,
        w_up,
        b_up.reshape(-1).astype(jnp.float32),
        w_down,
        gain_rows.astype(jnp.float32),
        bias_rows.astype(jnp.float32),
    )


def block_scores(q_heads, key_block, kpos_block, kseg_block, sight):
    scores = jnp.einsum(
        "qhd,khd->hqk", q_heads, key_block, preferred_element_type=jnp.float32
    ) * HD ** (-0.5)
    allowed = (
        (sight[1][:, None] == kseg_block[None, :])
        & (kpos_block[None, :] <= sight[0][:, None])
        & sight[2][:, None]
    )
    return (jnp.where(allowed[None], scores, NEG_FILL), allowed)


def key_blocks(keys, values, sight):
    seq_len = keys.shape[0]
    block_rows = math.gcd(seq_len, 512)
    blocks = seq_len // block_rows
    heads = keys.shape[1] // HD
    return (
        keys.reshape(blocks, block_rows, heads, HD),
        values.reshape(blocks, block_rows, heads, HD),
        sight[3].reshape(blocks, block_rows),
        sight[4].reshape(blocks, block_rows),
    )


def attend(queries, keys, values, sight):
    rows = queries.shape[0]
    heads = queries.shape[1] // HD
    q_heads = queries.reshape(rows, heads, HD)
    stacked = key_blocks(keys, values, sight)

    def find_scale(carry, pieces):
        top, total = carry
        scores, allowed = block_scores(q_heads, pieces[0], pieces[2], pieces[3], sight)
        new_top = jnp.maximum(top, jnp.max(scores, axis=-1))
        total = total * jnp.exp(top - new_top) + jnp.sum(
            jnp.exp(scores - new_top[..., None]), axis=-1
        )
        return ((new_top, total), None)

    start = (jnp.full((heads, rows), -jnp.inf, jnp.float32), jnp.zeros((heads, rows), jnp.float32))
    (top, total), ignored = lax.scan(find_scale, start, stacked)
    log_total = top + jnp.log(total)

    def weigh(carry, pieces):
        scores, allowed = block_scores(q_heads, pieces[0], pieces[2], pieces[3], sight)
        probs = jnp.exp(scores - log_total[..., None]).astype(jnp.bfloat16)
        return (
            carry
            + jnp.einsum("hqk,khd->qhd", probs, pieces[1], preferred_element_type=jnp.float32),
            None,
        )

    heads_out, ignored = lax.scan(weigh, jnp.zeros((rows, heads, HD), jnp.float32), stacked)
    return (heads_out, log_total, q_heads)


def attend_back(q_heads, keys, values, sight, log_total, grad_heads, delta):
    seq_len = keys.shape[0]
    stacked = key_blocks(keys, values, sight)
    scaling = HD ** (-0.5)

    def one_step(grad_q, pieces):
        scores, allowed = block_scores(q_heads, pieces[0], pieces[2], pieces[3], sight)
        probs = jnp.exp(scores - log_total[..., None])
        grad_p = jnp.einsum(
            "qhd,khd->hqk", grad_heads, pieces[1], preferred_element_type=jnp.float32
        )
        grad_s = jnp.where(allowed[None], probs * (grad_p - delta[..., None]), 0.0).astype(
            jnp.bfloat16
        )
        grad_q = (
            grad_q
            + jnp.einsum("hqk,khd->qhd", grad_s, pieces[0], preferred_element_type=jnp.float32)
            * scaling
        )
        grad_v = jnp.einsum(
            "hqk,qhd->khd",
            probs.astype(jnp.bfloat16),
            grad_heads,
            preferred_element_type=jnp.float32,
        )
        grad_k = (
            jnp.einsum("hqk,qhd->khd", grad_s, q_heads, preferred_element_type=jnp.float32)
            * scaling
        )
        return (grad_q, (grad_k, grad_v))

    grad_q, outputs = lax.scan(one_step, jnp.zeros(q_heads.shape, jnp.float32), stacked)
    return (grad_q, outputs[0].reshape(seq_len, -1), outputs[1].reshape(seq_len, -1))


def forward(entering, weights, sight):
    w_qkv, b_qv, w_out, w_up, b_up, w_down, gain_rows, bias_rows = weights
    hidden = entering.astype(jnp.float32)
    normed_a, unit_a, inverse_a = layer_norm(hidden, gain_rows[0], bias_rows[0])
    rows_a = widen(normed_a.astype(jnp.bfloat16))
    projected = jnp.einsum("rd,djh->rjh", rows_a, w_qkv, preferred_element_type=jnp.float32)
    queries = (projected[:, 0] + b_qv[0]).astype(jnp.bfloat16)
    keys_own = projected[:, 1].astype(jnp.bfloat16)
    values_own = (projected[:, 2] + b_qv[1]).astype(jnp.bfloat16)
    keys, values = (
        lax.all_gather(keys_own, "dp", axis=0, tiled=True),
        lax.all_gather(values_own, "dp", axis=0, tiled=True),
    )
    heads_out, log_total, q_heads = attend(queries, keys, values, sight)
    live_rows = sight[2].astype(jnp.float32)
    mixed_low = (heads_out.reshape(heads_out.shape[0], -1) * live_rows[:, None]).astype(
        jnp.bfloat16
    )
    middle = (
        hidden
        + narrow(jnp.dot(mixed_low, w_out, preferred_element_type=jnp.float32))
        + bias_rows[1]
    )
    normed_b, unit_b, inverse_b = layer_norm(middle, gain_rows[1], bias_rows[2])
    rows_b = widen(normed_b.astype(jnp.bfloat16))
    preact = jnp.dot(rows_b, w_up, preferred_element_type=jnp.float32) + b_up
    activated = jax.nn.gelu(preact, approximate=False).astype(jnp.bfloat16)
    result = (
        middle
        + narrow(jnp.dot(activated, w_down, preferred_element_type=jnp.float32))
        + bias_rows[3]
    )
    saved = (
        unit_a,
        inverse_a,
        rows_a,
        q_heads,
        keys,
        values,
        heads_out,
        log_total,
        mixed_low,
        unit_b,
        inverse_b,
        rows_b,
        preact,
        activated,
    )
    return (result, saved)


def backward(saved, grad_out, weights, sight):
    w_qkv, b_qv, w_out, w_up, b_up, w_down, gain_rows, bias_rows = weights
    (
        unit_a,
        inverse_a,
        rows_a,
        q_heads,
        keys,
        values,
        heads_out,
        log_total,
        mixed_low,
        unit_b,
        inverse_b,
        rows_b,
        preact,
        activated,
    ) = saved
    rows = rows_a.shape[0]
    grad_branch = grad_out.astype(jnp.bfloat16)
    down_bias_grad = jnp.sum(grad_branch.astype(jnp.float32), axis=0)
    wide_branch = widen(grad_branch)
    grad_act = jnp.einsum("rd,fd->rf", wide_branch, w_down, preferred_element_type=jnp.float32)
    ignored, gelu_pull = jax.vjp(partial(jax.nn.gelu, approximate=False), preact)
    grad_pre = gelu_pull(grad_act)[0].astype(jnp.bfloat16)
    up_bias_grad = jnp.sum(grad_pre.astype(jnp.float32), axis=0)
    grad_normed_b = narrow(
        jnp.einsum("rf,df->rd", grad_pre, w_up, preferred_element_type=jnp.float32)
    )
    gain_b_grad = jnp.sum(grad_normed_b * unit_b, axis=0)
    shift_b_grad = jnp.sum(grad_normed_b, axis=0)
    grad_middle = grad_out + norm_back(grad_normed_b, unit_b, inverse_b, gain_rows[1])
    grad_attn = grad_middle.astype(jnp.bfloat16)
    out_bias_grad = jnp.sum(grad_attn.astype(jnp.float32), axis=0)
    wide_attn = widen(grad_attn)
    live_rows = sight[2].astype(jnp.bfloat16)
    grad_flat = (
        jnp.einsum("rd,ed->re", wide_attn, w_out, preferred_element_type=jnp.float32).astype(
            jnp.bfloat16
        )
        * live_rows[:, None]
    )
    grad_heads = grad_flat.reshape(heads_out.shape)
    delta = jnp.einsum("qhd,qhd->hq", grad_heads.astype(jnp.float32), heads_out)
    grad_q, grad_k_all, grad_v_all = attend_back(
        q_heads, keys, values, sight, log_total, grad_heads, delta
    )
    grad_k, grad_v = (
        lax.psum_scatter(
            grad_k_all.astype(jnp.bfloat16), "dp", scatter_dimension=0, tiled=True
        ).astype(jnp.float32),
        lax.psum_scatter(
            grad_v_all.astype(jnp.bfloat16), "dp", scatter_dimension=0, tiled=True
        ).astype(jnp.float32),
    )
    grad_proj = jnp.stack((grad_q.reshape(rows, -1), grad_k, grad_v), axis=1).astype(jnp.bfloat16)
    proj_sums = jnp.sum(grad_proj.astype(jnp.float32), axis=0)
    qv_grad = jnp.stack((proj_sums[0], proj_sums[2]))
    grad_normed_a = narrow(
        jnp.einsum("rjh,djh->rd", grad_proj, w_qkv, preferred_element_type=jnp.float32)
    )
    gain_a_grad = jnp.sum(grad_normed_a * unit_a, axis=0)
    shift_a_grad = jnp.sum(grad_normed_a, axis=0)
    grad_in = grad_middle + norm_back(grad_normed_a, unit_a, inverse_a, gain_rows[0])
    gains_grad = jnp.stack((gain_a_grad, gain_b_grad))
    biases_grad = jnp.stack((shift_a_grad, out_bias_grad, shift_b_grad, down_bias_grad))
    factors = (rows_b, grad_pre, activated, wide_branch, mixed_low, wide_attn, rows_a, grad_proj)
    vectors = (qv_grad, up_bias_grad, gains_grad, biases_grad)
    return (grad_in, factors, vectors)


def weight_products(factors):
    rows_b, grad_pre, activated, wide_branch, mixed_low, wide_attn, rows_a, grad_proj = factors
    down_grad = jnp.einsum("rf,rd->fd", activated, wide_branch, preferred_element_type=jnp.float32)
    up_grad = jnp.einsum("rd,rf->df", rows_b, grad_pre, preferred_element_type=jnp.float32)
    out_grad = jnp.einsum("re,rd->ed", mixed_low, wide_attn, preferred_element_type=jnp.float32)
    qkv_grad = jnp.einsum("rd,rjh->djh", rows_a, grad_proj, preferred_element_type=jnp.float32)
    return (qkv_grad, out_grad, up_grad, down_grad)


def assemble(products, vectors):
    qkv_grad, out_grad, up_grad, down_grad = products
    qv_grad, up_bias_grad, gains_grad, biases_grad = vectors
    return (qkv_grad, qv_grad, out_grad, up_grad, up_bias_grad, down_grad, gains_grad, biases_grad)


def reduce_grads(local_grads):
    qkv_grad, qv_grad, out_grad, up_grad, up_bias_grad, down_grad, gains_grad, biases_grad = (
        local_grads
    )
    heads = qv_grad.shape[1] // HD
    shards = (
        lax.psum_scatter(
            qkv_grad[None].astype(jnp.bfloat16), "dp", scatter_dimension=1, tiled=True
        ).astype(jnp.float32),
        lax.psum_scatter(
            qv_grad.reshape(1, 2, heads, HD).astype(jnp.bfloat16),
            "dp",
            scatter_dimension=3,
            tiled=True,
        ).astype(jnp.float32),
        lax.psum_scatter(
            out_grad[None].astype(jnp.bfloat16), "dp", scatter_dimension=2, tiled=True
        ).astype(jnp.float32),
        lax.psum_scatter(
            up_grad[None].astype(jnp.bfloat16), "dp", scatter_dimension=1, tiled=True
        ).astype(jnp.float32),
        lax.psum_scatter(
            up_bias_grad.reshape(1, -1, HD).astype(jnp.bfloat16),
            "dp",
            scatter_dimension=2,
            tiled=True,
        ).astype(jnp.float32),
        lax.psum_scatter(
            down_grad[None].astype(jnp.bfloat16), "dp", scatter_dimension=2, tiled=True
        ).astype(jnp.float32),
    )
    vectors = (
        lax.psum_scatter(gains_grad[None], ("dp", "tensor"), scatter_dimension=2, tiled=True),
        lax.psum_scatter(biases_grad[None], ("dp", "tensor"), scatter_dimension=2, tiled=True),
    )
    return tuple(shards) + tuple(vectors)


def body(
    boundary,
    doc_lengths,
    qkv_weight,
    qv_bias,
    out_weight,
    up_weight,
    up_bias,
    down_weight,
    norm_gains,
    norm_biases,
):
    section_index = lax.axis_index("section")
    on_first = section_index == 0
    own_part = boundary[0]
    batches = own_part.shape[0]
    rows_dp = own_part.shape[1] * lax.axis_size("tensor")
    seq_len = rows_dp * lax.axis_size("dp")
    dp_index = lax.axis_index("dp")
    sources = (
        qkv_weight,
        qv_bias,
        out_weight,
        up_weight,
        up_bias,
        down_weight,
        norm_gains,
        norm_biases,
    )
    fixed_weights = fetch_weights(*sources)

    def current():
        return fixed_weights

    def sight_for(batch_at):
        lengths = lax.dynamic_index_in_dim(doc_lengths, batch_at, 0, keepdims=False)
        return visibility(lengths, dp_index, rows_dp, seq_len)

    def pick(first_value, second_value):
        return jnp.where(on_first, first_value, second_value)

    received = jnp.zeros_like(own_part[0])
    kept_ticks, exits = ([], [])
    for tick_index in range(batches + 1):
        entering = jnp.where(on_first, own_part[min(tick_index, batches - 1)], received)
        batch_at = jnp.clip(tick_index - section_index, 0, batches - 1)
        result, saved = forward(entering, current(), sight_for(batch_at))
        leaving = result.astype(jnp.bfloat16)
        kept_ticks.append(saved)
        exits.append(leaving)
        if tick_index < batches:
            received = from_behind(leaving, "section", 1)
    acts = jnp.stack(
        [jnp.where(on_first, exits[number], exits[number + 1]) for number in range(batches)]
    )[None]
    returned = jnp.zeros_like(own_part[0])
    summed = None
    vector_sum = None
    factor_ticks = []
    leaving_grads = []
    for tick_index in range(batches + 1):
        own_grad = own_part[min(tick_index, batches - 1)].astype(jnp.float32)
        if tick_index == batches:
            own_grad = jnp.zeros_like(own_grad)
        grad_out = jnp.where(on_first, returned.astype(jnp.float32), own_grad)
        saved = jax.tree.map(
            pick, kept_ticks[max(tick_index - 1, 0)], kept_ticks[min(tick_index + 1, batches)]
        )
        batch_at = jnp.where(on_first, max(tick_index - 1, 0), min(tick_index, batches - 1))
        grad_in, factors, vectors = backward(saved, grad_out, current(), sight_for(batch_at))
        leaving_grads.append(grad_in)
        if tick_index < batches:
            returned = from_behind(grad_in.astype(jnp.bfloat16), "section", -1)
        factor_ticks.append(factors)
        vector_sum = (
            vectors
            if vector_sum is None
            else tuple((former + latter for former, latter in zip(vector_sum, vectors)))
        )
    joined = tuple(
        (
            jnp.concatenate([entry[number] for entry in factor_ticks], axis=0)
            for number in range(len(factor_ticks[0]))
        )
    )
    summed = reduce_grads(assemble(weight_products(joined), vector_sum))
    input_grads = jnp.stack(
        [
            jnp.where(on_first, leaving_grads[number + 1], leaving_grads[number])
            for number in range(batches)
        ]
    )[None]
    return (acts, input_grads) + tuple(summed)


def place():
    dp = lax.axis_index("dp")
    return (lax.axis_index("section"), dp // 2, lax.rem(dp, 2), lax.axis_index("tensor"))


def device(core, z, x, y):
    return (core, z * 2 + x, y)


def greet(partners):
    barrier = pltpu.get_barrier_semaphore()
    expected = 0
    for present, partner in partners:
        if present is True:
            pl.semaphore_signal(barrier, inc=1, device_id=partner, device_id_type=MESH)
            expected = expected + 1
        else:

            @pl.when(present)
            def _(partner=partner):
                pl.semaphore_signal(barrier, inc=1, device_id=partner, device_id_type=MESH)

            expected = expected + present.astype(jnp.int32)
    pl.semaphore_wait(barrier, expected)


def guarded(present, act):
    if present is True:
        act()
    else:
        pl.when(present)(act)


class Sends:
    def __init__(self, sems):
        self.sems = sems
        self.pending = []

    def start(self, present, source, target, arrived, partner):
        copy = pltpu.make_async_remote_copy(
            src_ref=source,
            dst_ref=target,
            send_sem=self.sems.at[len(self.pending)],
            recv_sem=arrived,
            device_id=partner,
            device_id_type=MESH,
        )
        guarded(present, copy.start)
        self.pending.append((present, copy))

    def finish(self):
        for present, copy in self.pending:
            guarded(present, copy.wait_send)


def await_block(block, arrived, partner):
    pltpu.make_async_remote_copy(
        src_ref=block,
        dst_ref=block,
        send_sem=arrived,
        recv_sem=arrived,
        device_id=partner,
        device_id_type=MESH,
    ).wait_recv()


def plane_neighbours(levels):
    core, z, x, y = place()
    return (
        device(1 - core, z, x, y),
        device(core, z, x, 1 - y),
        device(core, jnp.maximum(z - 1, 0), x, y),
        device(core, jnp.minimum(z + 1, levels - 1), x, y),
    )


def gather_kernel(levels, own_ref, all_ref, send_sems, recv_sems, local_sem):
    core, z, x, y = place()
    sibling, across, left, right = plane_neighbours(levels)
    has_left, has_right = (z > 0, z < levels - 1)
    greet([(True, sibling), (True, across), (has_left, left), (has_right, right)])
    rows = own_ref.shape[0]

    def block(zz, cc, yy):
        number = zz * 4 + cc * 2 + yy
        return (
            all_ref.at[pl.ds(pl.multiple_of(number * rows, rows), rows)],
            recv_sems.at[number],
        )

    sends = Sends(send_sems)
    home, home_sem = block(z, core, y)
    keep = pltpu.make_async_copy(own_ref, home, local_sem)
    for present, partner in (
        (True, across),
        (has_left, left),
        (has_right, right),
        (True, sibling),
    ):
        sends.start(present, own_ref, home, home_sem, partner)
    keep.start()

    def take_across(distance):
        for zz in (z,) if distance == 0 else (z - distance, z + distance):
            present = True if distance == 0 else (zz >= 0) & (zz < levels)
            held, arrived = block(jnp.clip(zz, 0, levels - 1), core, 1 - y)
            guarded(present, partial(await_block, held, arrived, across))
            sends.start(present, held, held, arrived, sibling)

    for distance in range(1, levels):
        for zz, onward, can_go, source in (
            (z - distance, right, has_right, left),
            (z + distance, left, has_left, right),
        ):
            present = (zz >= 0) & (zz < levels)
            held, arrived = block(jnp.clip(zz, 0, levels - 1), core, y)
            guarded(present, partial(await_block, held, arrived, source))
            sends.start(present, held, held, arrived, across)
            sends.start(present & can_go, held, held, arrived, onward)
            sends.start(present, held, held, arrived, sibling)
        take_across(distance - 1)
    take_across(levels - 1)
    for zz in range(levels):
        for yy in (0, 1):
            held, arrived = block(zz, 1 - core, yy)
            await_block(held, arrived, sibling)
    keep.wait()
    sends.finish()


def gather_rows(own):
    levels = lax.axis_size("dp") // 2
    rows, width = own.shape
    blocks = levels * 4
    return pl.pallas_call(
        partial(gather_kernel, levels),
        out_shape=jax.ShapeDtypeStruct((blocks * rows, width), own.dtype),
        in_specs=[pl.BlockSpec(memory_space=pl.ANY)],
        out_specs=pl.BlockSpec(memory_space=pl.ANY),
        scratch_shapes=[
            pltpu.SemaphoreType.DMA((4 + 6 * (levels - 1) + 2 * levels - 1,)),
            pltpu.SemaphoreType.DMA((blocks,)),
            pltpu.SemaphoreType.DMA,
        ],
        compiler_params=pltpu.CompilerParams(collective_id=0, has_side_effects=True),
        name="gather_rows",
    )(own)


def scatter_kernel(
    levels,
    part_ref,
    sum_ref,
    from_sibling,
    from_across,
    from_left,
    from_right,
    to_across,
    to_left,
    to_right,
    send_sems,
    sibling_sems,
    across_sems,
    left_sems,
    right_sems,
):
    core, z, x, y = place()
    sibling, across, left, right = plane_neighbours(levels)
    has_left, has_right = (z > 0, z < levels - 1)
    greet([(True, sibling), (True, across), (has_left, left), (has_right, right)])
    rows = sum_ref.shape[0]

    def part(zz, cc, yy):
        number = zz * 4 + cc * 2 + yy
        return part_ref.at[pl.ds(pl.multiple_of(number * rows, rows), rows)]

    def wide(ref):
        return ref[...].astype(jnp.float32)

    sends = Sends(send_sems)
    order = []
    for distance in range(levels - 1, -1, -1):
        for zz in (z,) if distance == 0 else (z + distance, z - distance):
            present = True if distance == 0 else (zz >= 0) & (zz < levels)
            order.append((distance, present, jnp.clip(zz, 0, levels - 1)))
    for yy in (1 - y, y):
        for distance, present, zz in order:
            slot = zz * 2 + yy
            sends.start(
                present,
                part(zz, 1 - core, yy),
                from_sibling.at[slot],
                sibling_sems.at[slot],
                sibling,
            )

    def pair(zz, yy):
        slot = zz * 2 + yy
        await_block(from_sibling.at[slot], sibling_sems.at[slot], sibling)
        return wide(part(zz, core, yy)) + wide(from_sibling.at[slot])

    for distance, present, zz in order:

        def stage(zz=zz):
            to_across[zz] = pair(zz, 1 - y).astype(to_across.dtype)

        guarded(present, stage)
        sends.start(present, to_across.at[zz], from_across.at[zz], across_sems.at[zz], across)

    def plane_sum(zz):
        total = pair(zz, y)
        await_block(from_across.at[zz], across_sems.at[zz], across)
        return total + wide(from_across.at[zz])

    for distance in range(levels - 1, 0, -1):
        for zz, staging, landing, sems, onward, behind, has_behind, came, came_sems in (
            (z + distance, to_right, from_left, left_sems, right, left, has_left, from_left, left_sems),
            (z - distance, to_left, from_right, right_sems, left, right, has_right, from_right, right_sems),
        ):
            present = (zz >= 0) & (zz < levels)
            zz = jnp.clip(zz, 0, levels - 1)

            def stage(zz=zz, staging=staging, behind=behind, has_behind=has_behind, came=came, came_sems=came_sems):
                total = plane_sum(zz)

                @pl.when(has_behind)
                def _():
                    await_block(came.at[zz], came_sems.at[zz], behind)
                    staging[zz] = (total + wide(came.at[zz])).astype(staging.dtype)

                @pl.when(jnp.logical_not(has_behind))
                def _():
                    staging[zz] = total.astype(staging.dtype)

            guarded(present, stage)
            sends.start(present, staging.at[zz], landing.at[zz], sems.at[zz], onward)
    sum_ref[...] = plane_sum(z)
    for present, came, came_sems, behind in (
        (has_left, from_left, left_sems, left),
        (has_right, from_right, right_sems, right),
    ):

        def take(came=came, came_sems=came_sems, behind=behind):
            await_block(came.at[z], came_sems.at[z], behind)
            sum_ref[...] += wide(came.at[z])

        guarded(present, take)
    sends.finish()


def scatter_sum(part):
    levels = lax.axis_size("dp") // 2
    blocks = levels * 4
    rows, width = (part.shape[0] // blocks, part.shape[1])

    def held(count):
        return pltpu.VMEM((count, rows, width), part.dtype)

    return pl.pallas_call(
        partial(scatter_kernel, levels),
        out_shape=jax.ShapeDtypeStruct((rows, width), jnp.float32),
        in_specs=[pl.BlockSpec(memory_space=pltpu.VMEM)],
        out_specs=pl.BlockSpec(memory_space=pltpu.VMEM),
        scratch_shapes=[
            held(2 * levels),
            held(levels),
            held(levels),
            held(levels),
            held(levels),
            held(levels),
            held(levels),
            pltpu.SemaphoreType.DMA((3 * (2 * levels - 1) + 2 * (levels - 1),)),
            pltpu.SemaphoreType.DMA((2 * levels,)),
            pltpu.SemaphoreType.DMA((levels,)),
            pltpu.SemaphoreType.DMA((levels,)),
            pltpu.SemaphoreType.DMA((levels,)),
        ],
        compiler_params=pltpu.CompilerParams(
            collective_id=1, has_side_effects=True, vmem_limit_bytes=32 << 20
        ),
        name="scatter_sum",
    )(part)


def piece_of_shard(which, ref, member, depth):
    if which in (1, 3):
        return ref.at[pl.ds(pl.multiple_of(member * depth, depth), depth)]
    return ref.at[:, pl.ds(pl.multiple_of(member * depth, depth), depth)]


def piece_of_slice(which, ref, layer, shard, depth):
    if which in (1, 3):
        return ref.at[layer, :, pl.ds(pl.multiple_of(shard * depth, depth), depth)]
    return ref.at[layer, pl.ds(pl.multiple_of(shard * depth, depth), depth)]


def everyone_in_column(levels):
    core, z, x, y = place()
    partners = []
    for step in range(levels):
        zz = lax.rem(z + step, levels)
        for other in (0, 1):
            if step or other:
                partners.append((True, device(1 - core if other else core, zz, x, y)))
    return partners


def fetch_kernel(levels, *refs):
    shards, slices = (refs[:4], refs[4:8])
    send_sems, column_sems, cross_sems, local_sems = refs[8:]
    core, z, x, y = place()
    over = device(core, z, 1 - x, y)
    greet(everyone_in_column(levels) + [(True, over)])
    own_shard = z * 2 + x
    members = 2 * levels
    sends = Sends(send_sems)
    keeps = []

    def spread(which):
        shard_ref, slice_ref = (shards[which], slices[which])
        member_depth = shard_ref.shape[0 if which in (1, 3) else 1] // members
        slice_depth = slice_ref.shape[2 if which in (1, 3) else 1] // members
        target = piece_of_slice(which, slice_ref, core, own_shard, slice_depth)
        for step in range(levels):
            zz = lax.rem(z + step, levels)
            for other in (0, 1):
                cc = 1 - core if other else core
                source = piece_of_shard(which, shard_ref, zz * 2 + cc, member_depth)
                if step or other:
                    sends.start(
                        True, source, target, column_sems.at[which, core, z], device(cc, zz, x, y)
                    )
                else:
                    keep = pltpu.make_async_copy(source, target, local_sems.at[which])
                    keep.start()
                    keeps.append(keep)
                    sends.start(True, source, target, cross_sems.at[which, core, z], over)

    def hand_over(which):
        slice_ref = slices[which]
        slice_depth = slice_ref.shape[2 if which in (1, 3) else 1] // members
        for step in range(levels):
            zz = lax.rem(z - step + levels, levels)
            for other in (0, 1):
                if step or other:
                    layer = 1 - core if other else core
                    held = piece_of_slice(which, slice_ref, layer, zz * 2 + x, slice_depth)
                    await_block(held, column_sems.at[which, layer, zz], over)
                    sends.start(True, held, held, cross_sems.at[which, layer, zz], over)

    for which in range(4):
        spread(which)
    for which in range(4):
        hand_over(which)
    for which in range(4):
        slice_ref = slices[which]
        slice_depth = slice_ref.shape[2 if which in (1, 3) else 1] // members
        for zz in range(levels):
            for layer in (0, 1):
                held = piece_of_slice(which, slice_ref, layer, zz * 2 + 1 - x, slice_depth)
                await_block(held, cross_sems.at[which, layer, zz], over)
    for keep in keeps:
        keep.wait()
    sends.finish()


def fetch_slices(shards):
    levels = lax.axis_size("dp") // 2
    members = 2 * levels
    shapes = [
        (2, shard.shape[0] // members, shard.shape[1] * members)
        if which in (1, 3)
        else (2, shard.shape[0] * members, shard.shape[1] // members)
        for which, shard in enumerate(shards)
    ]
    anywhere = pl.BlockSpec(memory_space=pl.ANY)
    return pl.pallas_call(
        partial(fetch_kernel, levels),
        out_shape=[jax.ShapeDtypeStruct(shape, jnp.bfloat16) for shape in shapes],
        in_specs=[anywhere] * 4,
        out_specs=[anywhere] * 4,
        scratch_shapes=[
            pltpu.SemaphoreType.DMA((4 * 4 * levels,)),
            pltpu.SemaphoreType.DMA((4, 2, levels)),
            pltpu.SemaphoreType.DMA((4, 2, levels)),
            pltpu.SemaphoreType.DMA((4,)),
        ],
        compiler_params=pltpu.CompilerParams(collective_id=2, has_side_effects=True),
        name="fetch_slices",
    )(*shards)


def return_kernel(levels, *refs):
    slices, shards, landed = (refs[:4], refs[4:8], refs[8:12])
    send_sems, column_sems, cross_sems, local_sems = refs[12:]
    core, z, x, y = place()
    over = device(core, z, 1 - x, y)
    greet(everyone_in_column(levels) + [(True, over)])
    members = 2 * levels
    sends = Sends(send_sems)
    keeps = []
    order = [
        (lax.rem(z + step, levels), 1 - core if other else core, bool(step or other))
        for step in range(levels - 1, -1, -1)
        for other in (1, 0)
    ]

    def depth_of(which):
        return slices[which].shape[2 if which in (1, 3) else 1] // members

    for which in (3, 2, 1, 0):
        for zz, layer, away in order:
            sends.start(
                True,
                piece_of_slice(which, slices[which], layer, zz * 2 + 1 - x, depth_of(which)),
                landed[which].at[layer, zz],
                cross_sems.at[which, layer, zz],
                over,
            )
    for which in (3, 2, 1, 0):
        member_depth = shards[which].shape[0 if which in (1, 3) else 1] // members
        target = piece_of_shard(which, shards[which], z * 2 + core, member_depth)
        for zz, layer, away in order:
            held = landed[which].at[layer, zz]
            await_block(held, cross_sems.at[which, layer, zz], over)
            own = piece_of_slice(which, slices[which], layer, zz * 2 + x, depth_of(which))
            held[...] = (held[...].astype(jnp.float32) + own[...].astype(jnp.float32)).astype(
                held.dtype
            )
            if away:
                sends.start(
                    True, held, target, column_sems.at[which, core, z], device(layer, zz, x, y)
                )
            else:
                keep = pltpu.make_async_copy(held, target, local_sems.at[which])
                keep.start()
                keeps.append(keep)
    for which in (3, 2, 1, 0):
        member_depth = shards[which].shape[0 if which in (1, 3) else 1] // members
        for step in range(levels):
            zz = lax.rem(z + step, levels)
            for other in (0, 1):
                if step or other:
                    cc = 1 - core if other else core
                    held = piece_of_shard(which, shards[which], zz * 2 + cc, member_depth)
                    await_block(held, column_sems.at[which, cc, zz], over)
    for keep in keeps:
        keep.wait()
    sends.finish()


def return_slices(slices):
    levels = lax.axis_size("dp") // 2
    members = 2 * levels
    shapes, landing = ([], [])
    for which, held in enumerate(slices):
        if which in (1, 3):
            shapes.append((held.shape[1] * members, held.shape[2] // members))
            landing.append((2, levels, held.shape[1], held.shape[2] // members))
        else:
            shapes.append((held.shape[1] // members, held.shape[2] * members))
            landing.append((2, levels, held.shape[1] // members, held.shape[2]))
    return pl.pallas_call(
        partial(return_kernel, levels),
        out_shape=[jax.ShapeDtypeStruct(shape, jnp.bfloat16) for shape in shapes],
        in_specs=[pl.BlockSpec(memory_space=pltpu.VMEM)] * 4,
        out_specs=[pl.BlockSpec(memory_space=pl.ANY)] * 4,
        scratch_shapes=[pltpu.VMEM(shape, jnp.bfloat16) for shape in landing]
        + [
            pltpu.SemaphoreType.DMA((4 * 4 * levels,)),
            pltpu.SemaphoreType.DMA((4, 2, levels)),
            pltpu.SemaphoreType.DMA((4, 2, levels)),
            pltpu.SemaphoreType.DMA((4,)),
        ],
        compiler_params=pltpu.CompilerParams(
            collective_id=3, has_side_effects=True, vmem_limit_bytes=48 << 20
        ),
        name="return_slices",
    )(*slices)


def regroup_kernel(levels, inward, *refs):
    count = len(refs) // 2 - 1
    sources, targets = (refs[:count], refs[count : 2 * count])
    send_sems, recv_sems = refs[2 * count :]
    core, z, x, y = place()
    sibling, over, corner = (
        device(1 - core, z, x, y),
        device(core, z, 1 - x, y),
        device(1 - core, z, 1 - x, y),
    )
    greet([(True, sibling), (True, over), (True, corner)])
    waits = []
    for number, (source, target) in enumerate(zip(sources, targets)):
        for slot in (0, 1):
            to_core, to_x, to_slot = (x, slot, core) if inward else (slot, core, x)
            arrived = recv_sems.at[number, to_slot]
            sent = send_sems.at[number, slot]
            for is_here, is_over, partner in (
                (True, False, over),
                (False, True, corner),
                (True, True, sibling),
            ):
                chosen = (to_core == core) if not (is_here and is_over) else (to_core != core)
                same_x = to_x == x
                if partner is over:
                    chosen = (to_core == core) & jnp.logical_not(same_x)
                elif partner is corner:
                    chosen = (to_core != core) & jnp.logical_not(same_x)
                else:
                    chosen = (to_core != core) & same_x
                copy = pltpu.make_async_remote_copy(
                    src_ref=source.at[slot],
                    dst_ref=target.at[to_slot],
                    send_sem=sent,
                    recv_sem=arrived,
                    device_id=partner,
                    device_id_type=MESH,
                )
                pl.when(chosen)(copy.start)
                waits.append((chosen, copy.wait_send))
            here = (to_core == core) & (to_x == x)
            keep = pltpu.make_async_copy(source.at[slot], target.at[to_slot], sent)
            pl.when(here)(keep.start)
            waits.append((here, keep.wait))
    for number, target in enumerate(targets):
        for slot in (0, 1):
            from_core, from_x = (slot, core) if inward else (x, slot)
            away = jnp.logical_not((from_core == core) & (from_x == x))
            pl.when(away)(
                partial(await_block, target.at[slot], recv_sems.at[number, slot], over)
            )
    for present, wait in waits:
        pl.when(present)(wait)


def regroup(inward, arrays):
    levels = lax.axis_size("dp") // 2
    anywhere = pl.BlockSpec(memory_space=pl.ANY)
    return pl.pallas_call(
        partial(regroup_kernel, levels, inward),
        out_shape=[jax.ShapeDtypeStruct(array.shape, array.dtype) for array in arrays],
        in_specs=[anywhere] * len(arrays),
        out_specs=[anywhere] * len(arrays),
        scratch_shapes=[
            pltpu.SemaphoreType.DMA((len(arrays), 2)),
            pltpu.SemaphoreType.DMA((len(arrays), 2)),
        ],
        compiler_params=pltpu.CompilerParams(
            collective_id=4 if inward else 5, has_side_effects=True
        ),
        name="regroup_in" if inward else "regroup_out",
    )(*arrays)


def attention_weights(queries, keys, allowed):
    scores = lax.dot_general(
        queries, keys, (((1,), (1,)), ((), ())), preferred_element_type=jnp.float32
    ) * HD ** (-0.5)
    scores = jnp.where(allowed, scores, NEG_FILL)
    top = jnp.max(scores, axis=-1, keepdims=True)
    raised = jnp.exp(scores - top)
    return raised / jnp.sum(raised, axis=-1, keepdims=True)


def plane_body(
    boundary,
    doc_lengths,
    qkv_weight,
    qv_bias,
    out_weight,
    up_weight,
    up_bias,
    down_weight,
    norm_gains,
    norm_biases,
):
    core, z, x, y = place()
    levels = lax.axis_size("dp") // 2
    members = 2 * levels
    member = z * 2 + core
    width = boundary.shape[3]
    heads_shard = qv_bias.shape[2]
    head_cut = qv_bias.shape[3]
    block_shard = up_bias.shape[1]
    own_blocks = block_shard // members
    f32, bf16 = (jnp.float32, jnp.bfloat16)

    pieces = (qv_bias[0], up_bias[0], norm_gains[0], norm_biases[0])
    packed = jnp.concatenate([piece.reshape(-1) for piece in pieces])
    shared = lax.all_gather(packed, ("section", "dp", "tensor"), axis=0, tiled=False)
    shared = shared.reshape(2, members, 2, -1)
    cuts = [0]
    for piece in pieces:
        cuts.append(cuts[-1] + piece.size)
    plane_part = lax.dynamic_index_in_dim(shared, y, 2, keepdims=False)
    qv = plane_part[:, :, cuts[0] : cuts[1]].reshape(2, members, 2, heads_shard, head_cut)
    qv = lax.dynamic_index_in_dim(qv, member, 3, keepdims=False)
    b_qv = qv.transpose(0, 2, 1, 3).reshape(2, 2, HD).astype(f32)
    ub = plane_part[:, :, cuts[1] : cuts[2]].reshape(2, members, block_shard, head_cut)
    ub = lax.dynamic_slice_in_dim(ub, member * own_blocks, own_blocks, axis=2)
    b_up = ub.transpose(0, 2, 1, 3).reshape(2, own_blocks * HD).astype(f32)
    gain_rows = (
        shared[..., cuts[2] : cuts[3]].reshape(2, members * 2, 2, -1).transpose(0, 2, 1, 3)
    ).reshape(2, 2, width).astype(f32)
    bias_rows = (
        shared[..., cuts[3] : cuts[4]].reshape(2, members * 2, 4, -1).transpose(0, 2, 1, 3)
    ).reshape(2, 4, width).astype(f32)

    (planes,) = regroup(True, (boundary[0],))
    depth = qkv_weight.shape[1]
    by_head = (
        qkv_weight[0]
        .reshape(depth, 3, members, HD)
        .transpose(0, 2, 1, 3)
        .reshape(depth, members * 3 * HD)
    )
    w_qkv, w_out, w_up, w_down = fetch_slices(
        (by_head, out_weight[0], up_weight[0], down_weight[0])
    )

    lengths = lax.dynamic_index_in_dim(doc_lengths, x, 0, keepdims=False)
    tokens = boundary.shape[2] * 4 * levels
    position, segment, live, _, _, _ = visibility(lengths, 0, tokens, tokens)
    allowed = (
        (segment[:, None] == segment[None, :])
        & (position[None, :] <= position[:, None])
        & live[:, None]
    )
    live_column = live.astype(f32)[:, None]
    scaling = HD ** (-0.5)

    def dot(left, right):
        return jnp.dot(left, right, preferred_element_type=f32)

    def dot_back(left, right):
        return lax.dot_general(left, right, (((1,), (1,)), ((), ())), preferred_element_type=f32)

    def dot_rows(left, right):
        return lax.dot_general(left, right, (((0,), (0,)), ((), ())), preferred_element_type=f32)

    entering = planes[0]
    saved, acts = ([], [])
    for layer in (0, 1):
        gains, biases = (gain_rows[layer], bias_rows[layer])
        hidden = entering.astype(f32)
        normed, unit_a, inverse_a = layer_norm(hidden, gains[0], biases[0])
        rows_a = gather_rows(normed.astype(bf16))
        projected = dot(rows_a, w_qkv[layer])
        queries = (projected[:, :HD] + b_qv[layer, 0]).astype(bf16)
        keys = projected[:, HD : 2 * HD].astype(bf16)
        values = (projected[:, 2 * HD :] + b_qv[layer, 1]).astype(bf16)
        probs = attention_weights(queries, keys, allowed)
        mixed = (dot(probs.astype(bf16), values) * live_column).astype(bf16)
        middle = hidden + scatter_sum(dot(mixed, w_out[layer]).astype(bf16)) + biases[1]
        normed, unit_b, inverse_b = layer_norm(middle, gains[1], biases[2])
        rows_b = gather_rows(normed.astype(bf16))
        preact = dot(rows_b, w_up[layer]) + b_up[layer]
        activated = jax.nn.gelu(preact, approximate=False).astype(bf16)
        result = middle + scatter_sum(dot(activated, w_down[layer]).astype(bf16)) + biases[3]
        entering = result.astype(bf16)
        acts.append(entering)
        saved.append(
            (unit_a, inverse_a, rows_a, queries, keys, values, probs, mixed)
            + (unit_b, inverse_b, rows_b, preact, activated)
        )

    grad_out = planes[1].astype(f32)
    slices, vectors, input_grads = ([None, None], [None, None], [None, None])
    for layer in (1, 0):
        gains = gain_rows[layer]
        unit_a, inverse_a, rows_a, queries, keys, values, probs, mixed = saved[layer][:8]
        unit_b, inverse_b, rows_b, preact, activated = saved[layer][8:]
        low_branch = grad_out.astype(bf16)
        down_bias_grad = jnp.sum(low_branch.astype(f32), axis=0)
        wide_branch = gather_rows(low_branch)
        grad_act = dot_back(wide_branch, w_down[layer])
        _, pull = jax.vjp(partial(jax.nn.gelu, approximate=False), preact)
        grad_pre = pull(grad_act)[0].astype(bf16)
        up_bias_grad = jnp.sum(grad_pre.astype(f32), axis=0)
        grad_b = scatter_sum(dot_back(grad_pre, w_up[layer]).astype(bf16))
        down_grad = dot_rows(activated, wide_branch).astype(bf16)
        up_grad = dot_rows(rows_b, grad_pre).astype(bf16)
        grad_middle = grad_out + norm_back(grad_b, unit_b, inverse_b, gains[1])
        low_middle = grad_middle.astype(bf16)
        wide_middle = gather_rows(low_middle)
        out_grad = dot_rows(mixed, wide_middle).astype(bf16)
        grad_mixed = dot_back(wide_middle, w_out[layer]).astype(bf16) * live_column.astype(bf16)
        grad_probs = dot_back(grad_mixed, values)
        delta = jnp.sum(probs * grad_probs, axis=-1, keepdims=True)
        grad_scores = jnp.where(allowed, probs * (grad_probs - delta), 0.0).astype(bf16)
        grad_q = dot(grad_scores, keys) * scaling
        grad_k = dot_rows(grad_scores, queries) * scaling
        grad_v = dot_rows(probs.astype(bf16), grad_mixed)
        grad_proj = jnp.concatenate((grad_q, grad_k, grad_v), axis=1).astype(bf16)
        proj_sums = jnp.sum(grad_proj.astype(f32), axis=0)
        grad_a = scatter_sum(dot_back(grad_proj, w_qkv[layer]).astype(bf16))
        qkv_grad = dot_rows(rows_a, grad_proj).astype(bf16)
        grad_in = grad_middle + norm_back(grad_a, unit_a, inverse_a, gains[0])
        input_grads[layer] = grad_in
        grad_out = grad_in.astype(bf16).astype(f32)
        slices[layer] = (qkv_grad, out_grad, up_grad, down_grad)
        vectors[layer] = (
            jnp.stack((proj_sums[:HD], proj_sums[2 * HD :])),
            up_bias_grad,
            jnp.stack((jnp.sum(grad_a * unit_a, axis=0), jnp.sum(grad_b * unit_b, axis=0))),
            jnp.stack(
                (
                    jnp.sum(grad_a, axis=0),
                    jnp.sum(low_middle.astype(f32), axis=0),
                    jnp.sum(grad_b, axis=0),
                    down_bias_grad,
                )
            ),
        )

    shards = return_slices([jnp.stack(pair) for pair in zip(*slices)])
    qkv_shard = (
        shards[0]
        .reshape(depth, members, 3, HD)
        .transpose(0, 2, 1, 3)
        .reshape(depth, 3, members * HD)
        .astype(f32)
    )
    outward = []
    for layer in (0, 1):
        qv_grad, up_bias_grad, gains_grad, biases_grad = vectors[layer]
        qv_all = jnp.zeros((2, 2, heads_shard, HD), f32)
        qv_all = lax.dynamic_update_slice(qv_all, qv_grad[None, :, None], (y, 0, member, 0))
        up_all = jnp.zeros((2, block_shard, HD), f32)
        up_all = lax.dynamic_update_slice(
            up_all, up_bias_grad.reshape(1, own_blocks, HD), (y, member * own_blocks, 0)
        )
        outward.append(
            jnp.concatenate(
                (
                    qv_all.reshape(2, 2, heads_shard, members, head_cut)
                    .transpose(3, 0, 1, 2, 4)
                    .reshape(members * 2, -1),
                    up_all.reshape(2, block_shard, members, head_cut)
                    .transpose(2, 0, 1, 3)
                    .reshape(members * 2, -1),
                    gains_grad.reshape(2, members * 2, -1).transpose(1, 0, 2).reshape(members * 2, -1),
                    biases_grad.reshape(4, members * 2, -1).transpose(1, 0, 2).reshape(members * 2, -1),
                ),
                axis=1,
            )
        )
    own_vector = lax.psum_scatter(
        jnp.stack(outward).reshape(4 * members, -1),
        ("section", "dp", "tensor"),
        scatter_dimension=0,
        tiled=True,
    ).reshape(-1)
    small = [
        own_vector[cuts[at] : cuts[at + 1]].reshape((1,) + pieces[at].shape) for at in range(4)
    ]
    acts_out, grads_out = regroup(False, (jnp.stack(acts), jnp.stack(input_grads)))
    return (
        acts_out[None],
        grads_out[None],
        qkv_shard[None],
        small[0],
        shards[1].astype(f32)[None],
        shards[2].astype(f32)[None],
        small[1],
        shards[3].astype(f32)[None],
        small[2],
        small[3],
    )


def fits_plane(mesh):
    return mesh.shape["dp"] == 8 and mesh.shape["tensor"] == 2 and mesh.shape["section"] == 2


def solution(mesh):
    placed = (
        P("section", None, ("dp", "tensor"), None),
        P(),
        P("section", "dp", None, "tensor"),
        P("section", None, "tensor", "dp"),
        P("section", "tensor", "dp"),
        P("section", "dp", "tensor"),
        P("section", "tensor", "dp"),
        P("section", "tensor", "dp"),
        P("section", None, ("dp", "tensor")),
        P("section", None, ("dp", "tensor")),
    )
    return jax.shard_map(
        plane_body if fits_plane(mesh) else body,
        mesh=mesh,
        in_specs=placed,
        out_specs=(
            P("section", None, ("dp", "tensor"), None),
            P("section", None, ("dp", "tensor"), None),
            P("section", "dp", None, "tensor"),
            P("section", None, "tensor", "dp"),
            P("section", "tensor", "dp"),
            P("section", "dp", "tensor"),
            P("section", "tensor", "dp"),
            P("section", "tensor", "dp"),
            P("section", None, ("dp", "tensor")),
            P("section", None, ("dp", "tensor")),
        ),
        check_vma=False,
    )
```

```python
from functools import partial
import math
from types import SimpleNamespace

import jax
import jax.numpy as jnp
from jax import lax
from jax.experimental import pallas as pl
from jax.experimental.pallas import tpu as pltpu
from jax.sharding import PartitionSpec as P

HD = 128


EPSILON = 1e-05
NEG_FILL = -1e30
MESH = pl.DeviceIdType.MESH


def from_behind(value, axis, steps):
    count = lax.axis_size(axis)
    first, last = (max(0, -steps), min(count, count - steps))
    return lax.ppermute(value, axis, [(source, source + steps) for source in range(first, last)])


def layer_norm(hidden, gain, shift):
    average = jnp.mean(hidden, axis=-1, keepdims=True)
    centred = hidden - average
    variance = jnp.mean(centred * centred, axis=-1, keepdims=True)
    inverse = lax.rsqrt(variance + EPSILON)
    normed = centred * inverse
    return (normed * gain + shift, normed, inverse)


def norm_back(grad_out, normed, inverse, gain):
    scaled = grad_out * gain
    return inverse * (
        scaled
        - jnp.mean(scaled, axis=-1, keepdims=True)
        - normed * jnp.mean(scaled * normed, axis=-1, keepdims=True)
    )


def visibility(lengths, dp_index, rows_dp, seq_len):
    per_seq = seq_len // lengths.shape[0]
    docs = lengths.shape[1]
    key_pos = jnp.arange(seq_len, dtype=jnp.int32)
    seq_of = key_pos // per_seq
    local = key_pos - seq_of * per_seq
    doc_ends = jnp.cumsum(lengths, axis=1)
    ends_row = jnp.take(doc_ends, seq_of, axis=0)
    key_seg = seq_of * (docs + 1) + jnp.sum((local[:, None] >= ends_row).astype(jnp.int32), axis=1)
    key_live = local < ends_row[:, docs - 1]
    start_row = dp_index * rows_dp
    query_pos = start_row + jnp.arange(rows_dp, dtype=jnp.int32)
    query_seg = lax.dynamic_slice_in_dim(key_seg, start_row, rows_dp)
    query_live = lax.dynamic_slice_in_dim(key_live, start_row, rows_dp)
    return (query_pos, query_seg, query_live, key_pos, key_seg, key_live)


def widen(rows_low):
    return lax.all_gather(rows_low, "tensor", axis=0, tiled=True)


def narrow(partial_rows):
    return lax.psum_scatter(
        partial_rows.astype(jnp.bfloat16), "tensor", scatter_dimension=0, tiled=True
    ).astype(jnp.float32)


def fetch_weights(
    qkv_weight, qv_bias, out_weight, up_weight, up_bias, down_weight, norm_gains, norm_biases
):
    w_qkv, b_qv, w_out, w_up, b_up, w_down = (
        lax.all_gather(qkv_weight[0], "dp", axis=0, tiled=True),
        lax.all_gather(qv_bias[0], "dp", axis=2, tiled=True),
        lax.all_gather(out_weight[0], "dp", axis=1, tiled=True),
        lax.all_gather(up_weight[0], "dp", axis=0, tiled=True),
        lax.all_gather(up_bias[0], "dp", axis=1, tiled=True),
        lax.all_gather(down_weight[0], "dp", axis=1, tiled=True),
    )
    gain_rows, bias_rows = (
        lax.all_gather(norm_gains[0], ("dp", "tensor"), axis=1, tiled=True),
        lax.all_gather(norm_biases[0], ("dp", "tensor"), axis=1, tiled=True),
    )
    return (
        w_qkv,
        b_qv.reshape(2, -1).astype(jnp.float32),
        w_out,
        w_up,
        b_up.reshape(-1).astype(jnp.float32),
        w_down,
        gain_rows.astype(jnp.float32),
        bias_rows.astype(jnp.float32),
    )


def block_scores(q_heads, key_block, kpos_block, kseg_block, sight):
    scores = jnp.einsum(
        "qhd,khd->hqk", q_heads, key_block, preferred_element_type=jnp.float32
    ) * HD ** (-0.5)
    allowed = (
        (sight[1][:, None] == kseg_block[None, :])
        & (kpos_block[None, :] <= sight[0][:, None])
        & sight[2][:, None]
    )
    return (jnp.where(allowed[None], scores, NEG_FILL), allowed)


def key_blocks(keys, values, sight):
    seq_len = keys.shape[0]
    block_rows = math.gcd(seq_len, 512)
    blocks = seq_len // block_rows
    heads = keys.shape[1] // HD
    return (
        keys.reshape(blocks, block_rows, heads, HD),
        values.reshape(blocks, block_rows, heads, HD),
        sight[3].reshape(blocks, block_rows),
        sight[4].reshape(blocks, block_rows),
    )


def attend(queries, keys, values, sight):
    rows = queries.shape[0]
    heads = queries.shape[1] // HD
    q_heads = queries.reshape(rows, heads, HD)
    stacked = key_blocks(keys, values, sight)

    def find_scale(carry, pieces):
        top, total = carry
        scores, allowed = block_scores(q_heads, pieces[0], pieces[2], pieces[3], sight)
        new_top = jnp.maximum(top, jnp.max(scores, axis=-1))
        total = total * jnp.exp(top - new_top) + jnp.sum(
            jnp.exp(scores - new_top[..., None]), axis=-1
        )
        return ((new_top, total), None)

    start = (jnp.full((heads, rows), -jnp.inf, jnp.float32), jnp.zeros((heads, rows), jnp.float32))
    (top, total), ignored = lax.scan(find_scale, start, stacked)
    log_total = top + jnp.log(total)

    def weigh(carry, pieces):
        scores, allowed = block_scores(q_heads, pieces[0], pieces[2], pieces[3], sight)
        probs = jnp.exp(scores - log_total[..., None]).astype(jnp.bfloat16)
        return (
            carry
            + jnp.einsum("hqk,khd->qhd", probs, pieces[1], preferred_element_type=jnp.float32),
            None,
        )

    heads_out, ignored = lax.scan(weigh, jnp.zeros((rows, heads, HD), jnp.float32), stacked)
    return (heads_out, log_total, q_heads)


def attend_back(q_heads, keys, values, sight, log_total, grad_heads, delta):
    seq_len = keys.shape[0]
    stacked = key_blocks(keys, values, sight)
    scaling = HD ** (-0.5)

    def one_step(grad_q, pieces):
        scores, allowed = block_scores(q_heads, pieces[0], pieces[2], pieces[3], sight)
        probs = jnp.exp(scores - log_total[..., None])
        grad_p = jnp.einsum(
            "qhd,khd->hqk", grad_heads, pieces[1], preferred_element_type=jnp.float32
        )
        grad_s = jnp.where(allowed[None], probs * (grad_p - delta[..., None]), 0.0).astype(
            jnp.bfloat16
        )
        grad_q = (
            grad_q
            + jnp.einsum("hqk,khd->qhd", grad_s, pieces[0], preferred_element_type=jnp.float32)
            * scaling
        )
        grad_v = jnp.einsum(
            "hqk,qhd->khd",
            probs.astype(jnp.bfloat16),
            grad_heads,
            preferred_element_type=jnp.float32,
        )
        grad_k = (
            jnp.einsum("hqk,qhd->khd", grad_s, q_heads, preferred_element_type=jnp.float32)
            * scaling
        )
        return (grad_q, (grad_k, grad_v))

    grad_q, outputs = lax.scan(one_step, jnp.zeros(q_heads.shape, jnp.float32), stacked)
    return (grad_q, outputs[0].reshape(seq_len, -1), outputs[1].reshape(seq_len, -1))


def forward(entering, weights, sight):
    w_qkv, b_qv, w_out, w_up, b_up, w_down, gain_rows, bias_rows = weights
    hidden = entering.astype(jnp.float32)
    normed_a, unit_a, inverse_a = layer_norm(hidden, gain_rows[0], bias_rows[0])
    rows_a = widen(normed_a.astype(jnp.bfloat16))
    projected = jnp.einsum("rd,djh->rjh", rows_a, w_qkv, preferred_element_type=jnp.float32)
    queries = (projected[:, 0] + b_qv[0]).astype(jnp.bfloat16)
    keys_own = projected[:, 1].astype(jnp.bfloat16)
    values_own = (projected[:, 2] + b_qv[1]).astype(jnp.bfloat16)
    keys, values = (
        lax.all_gather(keys_own, "dp", axis=0, tiled=True),
        lax.all_gather(values_own, "dp", axis=0, tiled=True),
    )
    heads_out, log_total, q_heads = attend(queries, keys, values, sight)
    live_rows = sight[2].astype(jnp.float32)
    mixed_low = (heads_out.reshape(heads_out.shape[0], -1) * live_rows[:, None]).astype(
        jnp.bfloat16
    )
    middle = (
        hidden
        + narrow(jnp.dot(mixed_low, w_out, preferred_element_type=jnp.float32))
        + bias_rows[1]
    )
    normed_b, unit_b, inverse_b = layer_norm(middle, gain_rows[1], bias_rows[2])
    rows_b = widen(normed_b.astype(jnp.bfloat16))
    preact = jnp.dot(rows_b, w_up, preferred_element_type=jnp.float32) + b_up
    activated = jax.nn.gelu(preact, approximate=False).astype(jnp.bfloat16)
    result = (
        middle
        + narrow(jnp.dot(activated, w_down, preferred_element_type=jnp.float32))
        + bias_rows[3]
    )
    saved = (
        unit_a,
        inverse_a,
        rows_a,
        q_heads,
        keys,
        values,
        heads_out,
        log_total,
        mixed_low,
        unit_b,
        inverse_b,
        rows_b,
        preact,
        activated,
    )
    return (result, saved)


def backward(saved, grad_out, weights, sight):
    w_qkv, b_qv, w_out, w_up, b_up, w_down, gain_rows, bias_rows = weights
    (
        unit_a,
        inverse_a,
        rows_a,
        q_heads,
        keys,
        values,
        heads_out,
        log_total,
        mixed_low,
        unit_b,
        inverse_b,
        rows_b,
        preact,
        activated,
    ) = saved
    rows = rows_a.shape[0]
    grad_branch = grad_out.astype(jnp.bfloat16)
    down_bias_grad = jnp.sum(grad_branch.astype(jnp.float32), axis=0)
    wide_branch = widen(grad_branch)
    grad_act = jnp.einsum("rd,fd->rf", wide_branch, w_down, preferred_element_type=jnp.float32)
    ignored, gelu_pull = jax.vjp(partial(jax.nn.gelu, approximate=False), preact)
    grad_pre = gelu_pull(grad_act)[0].astype(jnp.bfloat16)
    up_bias_grad = jnp.sum(grad_pre.astype(jnp.float32), axis=0)
    grad_normed_b = narrow(
        jnp.einsum("rf,df->rd", grad_pre, w_up, preferred_element_type=jnp.float32)
    )
    gain_b_grad = jnp.sum(grad_normed_b * unit_b, axis=0)
    shift_b_grad = jnp.sum(grad_normed_b, axis=0)
    grad_middle = grad_out + norm_back(grad_normed_b, unit_b, inverse_b, gain_rows[1])
    grad_attn = grad_middle.astype(jnp.bfloat16)
    out_bias_grad = jnp.sum(grad_attn.astype(jnp.float32), axis=0)
    wide_attn = widen(grad_attn)
    live_rows = sight[2].astype(jnp.bfloat16)
    grad_flat = (
        jnp.einsum("rd,ed->re", wide_attn, w_out, preferred_element_type=jnp.float32).astype(
            jnp.bfloat16
        )
        * live_rows[:, None]
    )
    grad_heads = grad_flat.reshape(heads_out.shape)
    delta = jnp.einsum("qhd,qhd->hq", grad_heads.astype(jnp.float32), heads_out)
    grad_q, grad_k_all, grad_v_all = attend_back(
        q_heads, keys, values, sight, log_total, grad_heads, delta
    )
    grad_k, grad_v = (
        lax.psum_scatter(
            grad_k_all.astype(jnp.bfloat16), "dp", scatter_dimension=0, tiled=True
        ).astype(jnp.float32),
        lax.psum_scatter(
            grad_v_all.astype(jnp.bfloat16), "dp", scatter_dimension=0, tiled=True
        ).astype(jnp.float32),
    )
    grad_proj = jnp.stack((grad_q.reshape(rows, -1), grad_k, grad_v), axis=1).astype(jnp.bfloat16)
    proj_sums = jnp.sum(grad_proj.astype(jnp.float32), axis=0)
    qv_grad = jnp.stack((proj_sums[0], proj_sums[2]))
    grad_normed_a = narrow(
        jnp.einsum("rjh,djh->rd", grad_proj, w_qkv, preferred_element_type=jnp.float32)
    )
    gain_a_grad = jnp.sum(grad_normed_a * unit_a, axis=0)
    shift_a_grad = jnp.sum(grad_normed_a, axis=0)
    grad_in = grad_middle + norm_back(grad_normed_a, unit_a, inverse_a, gain_rows[0])
    gains_grad = jnp.stack((gain_a_grad, gain_b_grad))
    biases_grad = jnp.stack((shift_a_grad, out_bias_grad, shift_b_grad, down_bias_grad))
    factors = (rows_b, grad_pre, activated, wide_branch, mixed_low, wide_attn, rows_a, grad_proj)
    vectors = (qv_grad, up_bias_grad, gains_grad, biases_grad)
    return (grad_in, factors, vectors)


def weight_products(factors):
    rows_b, grad_pre, activated, wide_branch, mixed_low, wide_attn, rows_a, grad_proj = factors
    down_grad = jnp.einsum("rf,rd->fd", activated, wide_branch, preferred_element_type=jnp.float32)
    up_grad = jnp.einsum("rd,rf->df", rows_b, grad_pre, preferred_element_type=jnp.float32)
    out_grad = jnp.einsum("re,rd->ed", mixed_low, wide_attn, preferred_element_type=jnp.float32)
    qkv_grad = jnp.einsum("rd,rjh->djh", rows_a, grad_proj, preferred_element_type=jnp.float32)
    return (qkv_grad, out_grad, up_grad, down_grad)


def assemble(products, vectors):
    qkv_grad, out_grad, up_grad, down_grad = products
    qv_grad, up_bias_grad, gains_grad, biases_grad = vectors
    return (qkv_grad, qv_grad, out_grad, up_grad, up_bias_grad, down_grad, gains_grad, biases_grad)


def reduce_grads(local_grads):
    qkv_grad, qv_grad, out_grad, up_grad, up_bias_grad, down_grad, gains_grad, biases_grad = (
        local_grads
    )
    heads = qv_grad.shape[1] // HD
    shards = (
        lax.psum_scatter(
            qkv_grad[None].astype(jnp.bfloat16), "dp", scatter_dimension=1, tiled=True
        ).astype(jnp.float32),
        lax.psum_scatter(
            qv_grad.reshape(1, 2, heads, HD).astype(jnp.bfloat16),
            "dp",
            scatter_dimension=3,
            tiled=True,
        ).astype(jnp.float32),
        lax.psum_scatter(
            out_grad[None].astype(jnp.bfloat16), "dp", scatter_dimension=2, tiled=True
        ).astype(jnp.float32),
        lax.psum_scatter(
            up_grad[None].astype(jnp.bfloat16), "dp", scatter_dimension=1, tiled=True
        ).astype(jnp.float32),
        lax.psum_scatter(
            up_bias_grad.reshape(1, -1, HD).astype(jnp.bfloat16),
            "dp",
            scatter_dimension=2,
            tiled=True,
        ).astype(jnp.float32),
        lax.psum_scatter(
            down_grad[None].astype(jnp.bfloat16), "dp", scatter_dimension=2, tiled=True
        ).astype(jnp.float32),
    )
    vectors = (
        lax.psum_scatter(gains_grad[None], ("dp", "tensor"), scatter_dimension=2, tiled=True),
        lax.psum_scatter(biases_grad[None], ("dp", "tensor"), scatter_dimension=2, tiled=True),
    )
    return tuple(shards) + tuple(vectors)


def body(
    boundary,
    doc_lengths,
    qkv_weight,
    qv_bias,
    out_weight,
    up_weight,
    up_bias,
    down_weight,
    norm_gains,
    norm_biases,
):
    section_index = lax.axis_index("section")
    on_first = section_index == 0
    own_part = boundary[0]
    batches = own_part.shape[0]
    rows_dp = own_part.shape[1] * lax.axis_size("tensor")
    seq_len = rows_dp * lax.axis_size("dp")
    dp_index = lax.axis_index("dp")
    sources = (
        qkv_weight,
        qv_bias,
        out_weight,
        up_weight,
        up_bias,
        down_weight,
        norm_gains,
        norm_biases,
    )
    fixed_weights = fetch_weights(*sources)

    def current():
        return fixed_weights

    def sight_for(batch_at):
        lengths = lax.dynamic_index_in_dim(doc_lengths, batch_at, 0, keepdims=False)
        return visibility(lengths, dp_index, rows_dp, seq_len)

    def pick(first_value, second_value):
        return jnp.where(on_first, first_value, second_value)

    received = jnp.zeros_like(own_part[0])
    kept_ticks, exits = ([], [])
    for tick_index in range(batches + 1):
        entering = jnp.where(on_first, own_part[min(tick_index, batches - 1)], received)
        batch_at = jnp.clip(tick_index - section_index, 0, batches - 1)
        result, saved = forward(entering, current(), sight_for(batch_at))
        leaving = result.astype(jnp.bfloat16)
        kept_ticks.append(saved)
        exits.append(leaving)
        if tick_index < batches:
            received = from_behind(leaving, "section", 1)
    acts = jnp.stack(
        [jnp.where(on_first, exits[number], exits[number + 1]) for number in range(batches)]
    )[None]
    returned = jnp.zeros_like(own_part[0])
    summed = None
    vector_sum = None
    factor_ticks = []
    leaving_grads = []
    for tick_index in range(batches + 1):
        own_grad = own_part[min(tick_index, batches - 1)].astype(jnp.float32)
        if tick_index == batches:
            own_grad = jnp.zeros_like(own_grad)
        grad_out = jnp.where(on_first, returned.astype(jnp.float32), own_grad)
        saved = jax.tree.map(
            pick, kept_ticks[max(tick_index - 1, 0)], kept_ticks[min(tick_index + 1, batches)]
        )
        batch_at = jnp.where(on_first, max(tick_index - 1, 0), min(tick_index, batches - 1))
        grad_in, factors, vectors = backward(saved, grad_out, current(), sight_for(batch_at))
        leaving_grads.append(grad_in)
        if tick_index < batches:
            returned = from_behind(grad_in.astype(jnp.bfloat16), "section", -1)
        factor_ticks.append(factors)
        vector_sum = (
            vectors
            if vector_sum is None
            else tuple((former + latter for former, latter in zip(vector_sum, vectors)))
        )
    joined = tuple(
        (
            jnp.concatenate([entry[number] for entry in factor_ticks], axis=0)
            for number in range(len(factor_ticks[0]))
        )
    )
    summed = reduce_grads(assemble(weight_products(joined), vector_sum))
    input_grads = jnp.stack(
        [
            jnp.where(on_first, leaving_grads[number + 1], leaving_grads[number])
            for number in range(batches)
        ]
    )[None]
    return (acts, input_grads) + tuple(summed)


LOW, WIDE = (jnp.bfloat16, jnp.float32)
HBM, VMEM = (pl.ANY, pltpu.VMEM)


def dot(left, right):
    return jnp.dot(left, right, preferred_element_type=WIDE)


def dot_back(left, right):
    return lax.dot_general(left, right, (((1,), (1,)), ((), ())), preferred_element_type=WIDE)


def dot_rows(left, right):
    return lax.dot_general(left, right, (((0,), (0,)), ((), ())), preferred_element_type=WIDE)


def device(core, z, x, y):
    return (core, z * 2 + x, y)


class Plane:
    def __init__(self):
        dp = lax.axis_index("dp")
        self.levels = lax.axis_size("dp") // 2
        self.core, self.y = (lax.axis_index("section"), lax.axis_index("tensor"))
        self.z, self.x = (dp // 2, lax.rem(dp, 2))
        self.sibling = device(1 - self.core, self.z, self.x, self.y)
        self.across = device(self.core, self.z, self.x, 1 - self.y)
        self.over = device(self.core, self.z, 1 - self.x, self.y)
        self.corner = device(1 - self.core, self.z, 1 - self.x, self.y)
        self.member = self.z * 2 + self.core
        self.block = self.z * 4 + self.core * 2 + self.y

    def along(self, z):
        return device(self.core, jnp.clip(z, 0, self.levels - 1), self.x, self.y)

    def neighbours(self):
        return [
            (True, self.sibling),
            (True, self.across),
            (self.z > 0, self.along(self.z - 1)),
            (self.z < self.levels - 1, self.along(self.z + 1)),
        ]

    def column(self):
        partners = []
        for step in range(self.levels):
            zz = lax.rem(self.z + step, self.levels)
            for other in (0, 1):
                if step or other:
                    core = 1 - self.core if other else self.core
                    partners.append((True, device(core, zz, self.x, self.y)))
        return partners

    def nearest(self):
        tables = []
        for z in range(self.levels):
            tables.append(sorted(range(self.levels), key=lambda zz: (abs(zz - z), zz)))
        found = []
        for place in range(self.levels):
            number = jnp.int32(tables[0][place])
            for z in range(1, self.levels):
                number = jnp.where(self.z == z, tables[z][place], number)
            found.append(number)
        return found


def guarded(present, act):
    if present is True:
        act()
    else:
        pl.when(present)(act)


class Greeting:
    def __init__(self, partners):
        self.barrier = pltpu.get_barrier_semaphore()
        self.expected = 0
        for present, partner in partners:
            guarded(present, partial(self.tell, partner))
            self.expected = self.expected + (1 if present is True else present.astype(jnp.int32))

    def tell(self, partner):
        pl.semaphore_signal(self.barrier, inc=1, device_id=partner, device_id_type=MESH)

    def wait(self):
        pl.semaphore_wait(self.barrier, self.expected)


class Sends:
    def __init__(self, sems):
        self.sems = sems
        self.pending = []

    def start(self, present, source, target, arrived, partner):
        copy = pltpu.make_async_remote_copy(
            src_ref=source,
            dst_ref=target,
            send_sem=self.sems.at[len(self.pending)],
            recv_sem=arrived,
            device_id=partner,
            device_id_type=MESH,
        )
        guarded(present, copy.start)
        self.pending.append((present, copy))

    def finish(self):
        for present, copy in self.pending:
            guarded(present, copy.wait_send)


class Copies:
    def __init__(self, sems):
        self.sems = sems
        self.pending = []

    def start(self, source, target, present=True):
        copy = pltpu.make_async_copy(source, target, self.sems.at[len(self.pending)])
        guarded(present, copy.start)
        self.pending.append([present, copy, False])
        return len(self.pending) - 1

    def wait(self, number):
        present, copy, done = self.pending[number]
        if not done:
            guarded(present, copy.wait)
            self.pending[number][2] = True

    def finish(self):
        for number in range(len(self.pending)):
            self.wait(number)


def await_block(block, arrived, partner):
    pltpu.make_async_remote_copy(
        src_ref=block,
        dst_ref=block,
        send_sem=arrived,
        recv_sem=arrived,
        device_id=partner,
        device_id_type=MESH,
    ).wait_recv()


def span(start, size):
    return pl.ds(pl.multiple_of(start * size, size), size)


class Gather:
    def __init__(self, plane, sends, rows, sems):
        self.plane, self.sends, self.rows, self.sems = (plane, sends, rows, sems)
        self.chunks = sems.shape[1]
        self.size = rows.shape[0] // (sems.shape[0] * self.chunks)

    def spot(self, zz, core, y, chunk):
        number = zz * 4 + core * 2 + y
        return (
            self.rows.at[span(number * self.chunks + chunk, self.size)],
            self.sems.at[number, chunk],
        )

    def open(self):
        plane = self.plane
        for chunk in range(self.chunks):
            held, arrived = self.spot(plane.z, plane.core, plane.y, chunk)
            for present, partner in (
                (True, plane.across),
                (plane.z > 0, plane.along(plane.z - 1)),
                (plane.z < plane.levels - 1, plane.along(plane.z + 1)),
                (True, plane.sibling),
            ):
                self.sends.start(present, held, held, arrived, partner)

    def run(self, on_group, tick):
        plane = self.plane
        order = plane.nearest()

        def complete(step):
            zz = order[step]
            for chunk in range(self.chunks):
                held, arrived = self.spot(zz, plane.core, 1 - plane.y, chunk)
                await_block(held, arrived, plane.across)
                self.sends.start(True, held, held, arrived, plane.sibling)
            for yy in (plane.y, 1 - plane.y):
                for chunk in range(self.chunks):
                    held, arrived = self.spot(zz, 1 - plane.core, yy, chunk)
                    await_block(held, arrived, plane.sibling)
            on_group(step, zz)

        for step in range(1, plane.levels):
            zz = order[step]
            onward = jnp.where(zz < plane.z, plane.z + 1, plane.z - 1)
            can_go = (onward >= 0) & (onward < plane.levels)
            for chunk in range(self.chunks):
                held, arrived = self.spot(zz, plane.core, plane.y, chunk)
                await_block(held, arrived, plane.across)
                self.sends.start(can_go, held, held, arrived, plane.along(onward))
                self.sends.start(True, held, held, arrived, plane.across)
                self.sends.start(True, held, held, arrived, plane.sibling)
            complete(step - 1)
            tick()
        complete(plane.levels - 1)
        tick()

    @staticmethod
    def count(levels, chunks):
        return chunks * (4 + 3 * (levels - 1) + levels)


def gather_scratch(rows, width, levels, chunks, dtype=LOW):
    return {
        "rows": pltpu.VMEM((rows * 4 * levels, width), dtype),
        "gather_sems": pltpu.SemaphoreType.DMA((4 * levels, chunks)),
    }


class Scatter:
    def __init__(self, plane, sends, refs, result):
        self.plane, self.sends, self.refs, self.result = (plane, sends, refs, result)
        self.size = result.shape[0]

    def part(self, zz, core, y):
        return self.refs.part.at[span(zz * 4 + core * 2 + y, self.size)]

    def pair(self, zz, y):
        refs, slot = (self.refs, zz * 2 + y)
        came = refs.from_sibling.at[slot]
        await_block(came, refs.sibling_sems.at[slot], self.plane.sibling)
        return self.part(zz, self.plane.core, y)[...].astype(WIDE) + came[...].astype(WIDE)

    def give_sibling(self, zz):
        plane, refs = (self.plane, self.refs)
        for yy in (1 - plane.y, plane.y):
            slot = zz * 2 + yy
            self.sends.start(
                True,
                self.part(zz, 1 - plane.core, yy),
                refs.from_sibling.at[slot],
                refs.sibling_sems.at[slot],
                plane.sibling,
            )

    def give_across(self, zz):
        plane, refs = (self.plane, self.refs)
        refs.to_across[zz] = self.pair(zz, 1 - plane.y).astype(refs.to_across.dtype)
        self.sends.start(
            True, refs.to_across.at[zz], refs.from_across.at[zz], refs.across_sems.at[zz], plane.across
        )

    def plane_sum(self, zz):
        refs = self.refs
        total = self.pair(zz, self.plane.y)
        came = refs.from_across.at[zz]
        await_block(came, refs.across_sems.at[zz], self.plane.across)
        return total + came[...].astype(WIDE)

    def come(self, slot):
        came = self.refs.from_behind.at[slot]
        await_block(came, self.refs.behind_sems.at[slot], self.plane.across)
        return came[...].astype(WIDE)

    def give_onward(self, zz):
        plane, refs = (self.plane, self.refs)
        onward = jnp.where(zz > plane.z, plane.z + 1, plane.z - 1)
        behind = plane.z * 2 - onward
        refs.total[...] = self.plane_sum(zz)

        @pl.when((behind >= 0) & (behind < plane.levels))
        def _():
            refs.total[...] += self.come(zz)

        refs.to_onward[zz] = refs.total[...].astype(refs.to_onward.dtype)
        slot = jnp.where((onward == zz) & (zz < plane.z), plane.levels, zz)
        self.sends.start(
            True,
            refs.to_onward.at[zz],
            refs.from_behind.at[slot],
            refs.behind_sems.at[slot],
            plane.along(onward),
        )

    def conclude(self):
        plane = self.plane
        self.result[...] = self.plane_sum(plane.z)

        @pl.when(plane.z > 0)
        def _():
            self.result[...] += self.come(plane.z)

        @pl.when(plane.z < plane.levels - 1)
        def _():
            self.result[...] += self.come(plane.levels)

    @staticmethod
    def count(levels):
        return 4 * levels - 1

    def run(self, make, tick, fill=None):
        levels = self.plane.levels
        order = self.plane.nearest()[::-1]
        for step in range(levels + 3):
            if step < levels:
                make(step, order[step])
                self.give_sibling(order[step])
            if 0 < step <= levels:
                self.give_across(order[step - 1])
            if step >= levels - 1:
                tick()
                if fill is not None:
                    fill(step - levels + 1)
            if 3 <= step < levels + 2:
                self.give_onward(order[step - 3])
        self.conclude()


def scatter_scratch(rows, width, levels, dtype=LOW):
    return {
        "part": pltpu.VMEM((rows * 4 * levels, width), dtype),
        "from_sibling": pltpu.VMEM((2 * levels, rows, width), dtype),
        "from_across": pltpu.VMEM((levels, rows, width), dtype),
        "from_behind": pltpu.VMEM((levels + 1, rows, width), dtype),
        "to_across": pltpu.VMEM((levels, rows, width), dtype),
        "to_onward": pltpu.VMEM((levels, rows, width), dtype),
        "total": pltpu.VMEM((rows, width), WIDE),
        "sum": pltpu.VMEM((rows, width), WIDE),
        "sibling_sems": pltpu.SemaphoreType.DMA((2 * levels,)),
        "across_sems": pltpu.SemaphoreType.DMA((levels,)),
        "behind_sems": pltpu.SemaphoreType.DMA((levels + 1,)),
    }


def by_rows(which):
    return which in (1, 3)


def piece_of_shard(which, ref, member, members):
    if by_rows(which):
        return ref.at[span(member, ref.shape[0] // members)]
    return ref.at[:, span(member, ref.shape[1] // members)]


def piece_of_slice(which, ref, shard, shards):
    if by_rows(which):
        return ref.at[:, span(shard, ref.shape[1] // shards)]
    return ref.at[span(shard, ref.shape[0] // shards)]


def slice_shape(which, shape, shards):
    rows, columns = shape
    if by_rows(which):
        return (rows // shards, columns * shards)
    return (rows * shards, columns // shards)


def shard_shape(which, shape, shards):
    rows, columns = shape
    if by_rows(which):
        return (rows * shards, columns // shards)
    return (rows // shards, columns * shards)


class Paced:
    def __init__(self):
        self.steps = []

    def declare(self, inputs, outputs, scratch):
        return (0, 0)

    def partners(self, plane):
        return plane.column() + [(True, plane.over), (True, plane.corner)]

    def begin(self, plane, refs, sends, copies):
        pass

    def tick(self):
        if self.steps:
            self.steps.pop(0)()

    def drain(self):
        while self.steps:
            self.tick()

    def finish(self):
        pass


class Nothing(Paced):
    def partners(self, plane):
        return []


class Fetch(Paced):
    def __init__(self, layer, weights, together=1, lag=2):
        super().__init__()
        self.layer, self.weights, self.together, self.lag = (layer, weights, together, lag)

    def declare(self, inputs, outputs, scratch):
        levels = lax.axis_size("dp") // 2
        for which, shard in self.weights.items():
            inputs[f"shard{which}"] = (shard, HBM)
            outputs[f"slice{which}"] = (slice_shape(which, shard.shape, 2 * levels), LOW, HBM)
        count = len(self.weights)
        scratch["column_sems"] = pltpu.SemaphoreType.DMA((count, levels))
        scratch["cross_sems"] = pltpu.SemaphoreType.DMA((count, levels))
        return (count * 3 * levels, count)

    def begin(self, plane, refs, sends, copies):
        self.plane, self.refs, self.sends, self.copies = (plane, refs, sends, copies)
        spreads, hands = ([], [])
        for number, which in enumerate(self.weights):
            for step in range(plane.levels - 1, -1, -1):
                spreads.append(partial(self.spread, number, which, step))
                hands.append(partial(self.hand_over, number, which, step))
        moments = [[] for _ in range(len(spreads) + self.lag)]
        for at, (spread, hand) in enumerate(zip(spreads, hands)):
            moments[at].append(spread)
            moments[at + self.lag].append(hand)
        for at in range(0, len(moments), self.together):
            acts = [act for moment in moments[at : at + self.together] for act in moment]
            self.steps.append(lambda acts=acts: [act() for act in acts])
        self.tick()

    def ends(self, which):
        return getattr(self.refs, f"shard{which}"), getattr(self.refs, f"slice{which}")

    def spread(self, number, which, step):
        plane, refs = (self.plane, self.refs)
        shard, part = self.ends(which)
        members = 2 * plane.levels
        owner = plane.core == self.layer
        target = piece_of_slice(which, part, plane.z * 2 + plane.x, members)
        zz = lax.rem(plane.z + step, plane.levels)
        for other in (0, 1):
            core = 1 - plane.core if other else plane.core
            source = piece_of_shard(which, shard, zz * 2 + core, members)
            if step or other:
                self.sends.start(
                    owner,
                    source,
                    target,
                    refs.column_sems.at[number, plane.z],
                    device(core, zz, plane.x, plane.y),
                )
            else:
                self.copies.start(source, target, owner)

    def hand_over(self, number, which, step):
        plane, refs = (self.plane, self.refs)
        shard, part = self.ends(which)
        members = 2 * plane.levels
        zz = lax.rem(plane.z - step + plane.levels, plane.levels)
        held = piece_of_slice(which, part, zz * 2 + plane.x, members)
        arrived = refs.column_sems.at[number, zz]
        cross = refs.cross_sems.at[number, zz]
        if step:
            await_block(held, arrived, plane.over)
            self.sends.start(True, held, held, cross, plane.over)
        else:
            owner = plane.core == self.layer
            source = piece_of_shard(which, shard, plane.member, members)
            guarded(jnp.logical_not(owner), partial(await_block, held, arrived, plane.over))
            self.sends.start(jnp.logical_not(owner), held, held, cross, plane.over)
            self.sends.start(owner, source, held, cross, plane.over)

    def finish(self):
        self.drain()
        plane, refs = (self.plane, self.refs)
        members = 2 * plane.levels
        for number, which in enumerate(self.weights):
            part = self.ends(which)[1]
            for zz in range(plane.levels):
                held = piece_of_slice(which, part, zz * 2 + 1 - plane.x, members)
                await_block(held, refs.cross_sems.at[number, zz], plane.over)


class Return(Paced):
    def __init__(self, layer, weights, lag=1):
        super().__init__()
        self.layer, self.weights, self.lag = (layer, weights, lag)

    def declare(self, inputs, outputs, scratch):
        levels = lax.axis_size("dp") // 2
        for which, part in self.weights.items():
            inputs[f"slice{which}"] = (part, VMEM)
            shape = shard_shape(which, part.shape, 2 * levels)
            outputs[f"shard{which}"] = (shape, LOW, HBM)
            piece = (
                (part.shape[0], part.shape[1] // (2 * levels))
                if by_rows(which)
                else (part.shape[0] // (2 * levels), part.shape[1])
            )
            scratch[f"landed{which}"] = pltpu.VMEM((levels,) + piece, LOW)
        count = len(self.weights)
        scratch["column_sems"] = pltpu.SemaphoreType.DMA((count, 2, levels))
        scratch["cross_sems"] = pltpu.SemaphoreType.DMA((count, levels))
        return (count * 2 * levels, count)

    def ends(self, which):
        refs = self.refs
        return (
            getattr(refs, f"slice{which}"),
            getattr(refs, f"landed{which}"),
            getattr(refs, f"shard{which}"),
        )

    def begin(self, plane, refs, sends, copies):
        self.plane, self.refs, self.sends, self.copies = (plane, refs, sends, copies)
        members = 2 * plane.levels
        self.steps.extend([lambda: None] * self.lag)
        for number, which in enumerate(self.weights):
            part, landed, _ = self.ends(which)
            for step in range(plane.levels - 1, -1, -1):
                zz = lax.rem(plane.z + step, plane.levels)
                self.sends.start(
                    True,
                    piece_of_slice(which, part, zz * 2 + 1 - plane.x, members),
                    landed.at[zz],
                    refs.cross_sems.at[number, zz],
                    plane.over,
                )
                self.steps.append(partial(self.add, number, which, step))

    def add(self, number, which, step):
        plane, refs = (self.plane, self.refs)
        part, landed, shard = self.ends(which)
        members = 2 * plane.levels
        here = plane.core == self.layer
        target = piece_of_shard(which, shard, plane.member, members)
        zz = lax.rem(plane.z + step, plane.levels)
        held = landed.at[zz]
        await_block(held, refs.cross_sems.at[number, zz], plane.over)
        own = piece_of_slice(which, part, zz * 2 + plane.x, members)
        held[...] = (held[...].astype(WIDE) + own[...].astype(WIDE)).astype(LOW)
        self.sends.start(
            True if step else jnp.logical_not(here),
            held,
            target,
            refs.column_sems.at[number, plane.core, plane.z],
            device(self.layer, zz, plane.x, plane.y),
        )
        if step == 0:
            self.copies.start(held, target, here)

    def finish(self):
        self.drain()
        plane, refs = (self.plane, self.refs)
        members = 2 * plane.levels
        here = plane.core == self.layer
        for number, which in enumerate(self.weights):
            shard = self.ends(which)[2]
            for core in (0, 1):
                for step in range(plane.levels):
                    zz = lax.rem(plane.z + step, plane.levels)
                    present = here if step else here & (plane.core != core)
                    held = piece_of_shard(which, shard, zz * 2 + core, members)
                    guarded(
                        present,
                        partial(
                            await_block, held, refs.column_sems.at[number, core, zz], plane.over
                        ),
                    )


class Outward(Paced):
    def __init__(self, layers):
        super().__init__()
        self.layers = layers

    def declare(self, inputs, outputs, scratch):
        for layer, rows in self.layers.items():
            inputs[f"leaving_rows{layer}"] = (rows, HBM)
            outputs["owned_rows"] = ((2,) + rows.shape, rows.dtype, HBM)
        scratch["outward_sems"] = pltpu.SemaphoreType.DMA((2,))
        return (3 * len(self.layers), len(self.layers))

    def begin(self, plane, refs, sends, copies):
        self.plane, self.refs = (plane, refs)
        for layer in self.layers:
            source = getattr(refs, f"leaving_rows{layer}")
            target = refs.owned_rows.at[plane.x]
            same_core, same_x = (plane.core == layer, plane.core == plane.x)
            other_core, other_x = (plane.core != layer, plane.core != plane.x)
            for present, partner in (
                (same_core & other_x, plane.over),
                (other_core & same_x, plane.sibling),
                (other_core & other_x, plane.corner),
            ):
                sends.start(present, source, target, refs.outward_sems.at[plane.x], partner)
            copies.start(source, target, same_core & same_x)

    def finish(self):
        plane, refs = (self.plane, self.refs)
        owner = False
        for layer in self.layers:
            owner = owner | (plane.core == layer)
        for slot in (0, 1):
            away = jnp.logical_not((plane.core == plane.x) & (plane.x == slot))
            guarded(
                owner & away,
                partial(await_block, refs.owned_rows.at[slot], refs.outward_sems.at[slot], plane.over),
            )


class Together(Paced):
    def __init__(self, *parts):
        self.parts = parts

    def declare(self, inputs, outputs, scratch):
        counts = [part.declare(inputs, outputs, scratch) for part in self.parts]
        return tuple(map(sum, zip(*counts)))

    def begin(self, plane, refs, sends, copies):
        for part in self.parts:
            part.begin(plane, refs, sends, copies)

    def tick(self):
        for part in self.parts:
            part.tick()

    def drain(self):
        for part in self.parts:
            part.drain()

    def finish(self):
        for part in self.parts:
            part.finish()


def launch(name, ident, kernel, beside, counts, inputs, outputs, scratch):
    inputs, outputs, scratch = (dict(inputs), dict(outputs), dict(scratch))
    more = beside.declare(inputs, outputs, scratch)
    scratch["send_sems"] = pltpu.SemaphoreType.DMA((counts[0] + more[0],))
    scratch["copy_sems"] = pltpu.SemaphoreType.DMA((max(1, counts[1] + more[1]),))
    names = list(inputs) + list(outputs) + list(scratch)

    def body(*refs):
        held = SimpleNamespace(**dict(zip(names, refs)))
        plane = Plane()
        partners = plane.neighbours()
        if not isinstance(beside, Nothing):
            partners = [(True, plane.across)] + beside.partners(plane)
        greeting = Greeting(partners)
        sends, copies = (Sends(held.send_sems), Copies(held.copy_sems))
        kernel(held, plane, greeting, sends, copies)
        beside.finish()
        copies.finish()
        sends.finish()
        assert len(sends.pending) == counts[0] + more[0], len(sends.pending)
        assert len(copies.pending) == counts[1] + more[1], len(copies.pending)

    results = pl.pallas_call(
        body,
        out_shape=[jax.ShapeDtypeStruct(shape, dtype) for shape, dtype, _ in outputs.values()],
        in_specs=[pl.BlockSpec(memory_space=space) for _, space in inputs.values()],
        out_specs=[pl.BlockSpec(memory_space=space) for _, _, space in outputs.values()],
        scratch_shapes=list(scratch.values()),
        compiler_params=pltpu.CompilerParams(
            collective_id=ident, has_side_effects=True, vmem_limit_bytes=56 << 20
        ),
        name=name,
    )(*[array for array, _ in inputs.values()])
    return SimpleNamespace(**dict(zip(outputs, results)))


def sizes():
    levels = lax.axis_size("dp") // 2
    return levels, 4 * levels


CHUNKS = 2


def opening(ident, boundary, packed, beside):
    levels, blocks = sizes()
    rows, width = boundary.shape[1:]
    lines, lanes = packed.shape

    def kernel(refs, plane, greeting, sends, copies):
        core, x = (plane.core, plane.x)
        block = plane.block * 2 + x
        refs.small[span(block, lines)] = refs.packed[...]
        greeting.wait()
        own_small = refs.small.at[span(block, lines)]
        sends.start(True, own_small, own_small, refs.pair_sem.at[0], plane.over)
        for slot in (0, 1):
            source, target = (refs.boundary.at[slot], refs.landed_planes.at[core])
            arrived = refs.inward_sems.at[core]
            for present, partner in (
                ((x == core) & (slot != x), plane.over),
                ((x != core) & (slot == x), plane.sibling),
                ((x != core) & (slot != x), plane.corner),
            ):
                sends.start(present, source, target, arrived, partner)
            copies.start(source, target, (x == core) & (slot == x))
        beside.begin(plane, refs, sends, copies)
        other_small = refs.small.at[span(plane.block * 2 + 1 - x, lines)]
        await_block(other_small, refs.pair_sem.at[0], plane.over)
        small = Gather(plane, sends, refs.small, refs.small_sems)
        small.open()
        small.run(lambda step, zz: None, lambda: None)
        refs.vectors[...] = refs.small[...]
        for slot in (0, 1):
            here = (core == x) & (core == slot)
            guarded(
                jnp.logical_not(here),
                partial(await_block, refs.landed_planes.at[slot], refs.inward_sems.at[slot], plane.over),
            )
        copies.wait(0)
        copies.wait(1)
        refs.planes[...] = refs.landed_planes[...]
        refs.rows[span(plane.block, rows)] = refs.landed_planes[1]
        gather = Gather(plane, sends, refs.rows, refs.gather_sems)
        gather.open()

        def keep(step, zz):
            group = span(zz, 4 * rows)
            copies.start(refs.rows.at[group], refs.gathered.at[group])

        gather.run(keep, beside.tick)

    return launch(
        "opening",
        ident,
        kernel,
        beside,
        (7 + Gather.count(levels, 1) + Gather.count(levels, CHUNKS), 2 + levels),
        {"boundary": (boundary, HBM), "packed": (packed, VMEM)},
        {
            "planes": ((2, rows, width), LOW, VMEM),
            "gathered": ((blocks * rows, width), LOW, HBM),
            "vectors": ((2 * blocks * lines, lanes), LOW, VMEM),
        },
        gather_scratch(rows, width, levels, CHUNKS)
        | {
            "small": pltpu.VMEM((2 * blocks * lines, lanes), LOW),
            "small_sems": pltpu.SemaphoreType.DMA((blocks, 1)),
            "pair_sem": pltpu.SemaphoreType.DMA((1,)),
            "inward_sems": pltpu.SemaphoreType.DMA((2,)),
            "landed_planes": pltpu.VMEM((2, rows, width), LOW),
        },
    )


def visible(refs, group, size, tokens):
    segment = refs.query_segment[group]
    place = group.start + lax.broadcasted_iota(jnp.int32, (size, tokens), 0)
    keys = lax.broadcasted_iota(jnp.int32, (size, tokens), 1)
    return (segment == refs.key_segment[...]) & (keys <= place)


def attention_forward(ident, beside, entering, gains, biases, b_qv, segments, w_qkv, w_out):
    levels, blocks = sizes()
    rows, width = entering.shape
    tokens, size = (blocks * rows, 4 * rows)
    scaling = HD ** (-0.5)

    def kernel(refs, plane, greeting, sends, copies):
        first = copies.start(refs.w_qkv, refs.own_qkv)
        second = copies.start(refs.w_out, refs.own_out)
        hidden = refs.entering[...].astype(WIDE)
        normed, _, _ = layer_norm(hidden, refs.gains[0:1], refs.biases[0:1])
        refs.rows[span(plane.block, rows)] = normed.astype(LOW)
        greeting.wait()
        gather = Gather(plane, sends, refs.rows, refs.gather_sems)
        gather.open()
        beside.begin(plane, refs, sends, copies)
        copies.wait(first)

        def project(step, zz):
            group = span(zz, size)
            projected = dot(refs.rows[group], refs.own_qkv[...])
            refs.queries[group] = (projected[:, :HD] + refs.b_qv[0:1]).astype(LOW)
            refs.keys[group] = projected[:, HD : 2 * HD].astype(LOW)
            refs.values[group] = (projected[:, 2 * HD :] + refs.b_qv[1:2]).astype(LOW)
            copies.start(refs.rows.at[group], refs.rows_a.at[group])

        gather.run(project, beside.tick)
        copies.wait(second)

        def make(step, zz):
            group = span(zz, size)
            allowed = visible(refs, group, size, tokens)
            scores = dot_back(refs.queries[group], refs.keys[...]) * scaling
            scores = jnp.where(allowed, scores, NEG_FILL)
            top = jnp.max(scores, axis=-1, keepdims=True)
            raised = jnp.exp(scores - top)
            total = jnp.sum(raised, axis=-1, keepdims=True)
            refs.log_total[group] = top + jnp.log(total)
            probs = (raised / total).astype(LOW)
            live = (refs.query_segment[group] >= 0).astype(WIDE)
            mixed = (dot(probs, refs.values[...]) * live).astype(LOW)
            refs.mixed[group] = mixed
            for cut in range(0, width, 512):
                refs.part[group, cut : cut + 512] = dot(
                    mixed, refs.own_out[:, cut : cut + 512]
                ).astype(LOW)

        Scatter(plane, sends, refs, refs.sum).run(make, beside.tick)
        refs.middle[...] = refs.entering[...].astype(WIDE) + refs.sum[...] + refs.biases[1:2]

    head = ((tokens, HD), LOW, VMEM)
    return launch(
        f"attention_forward{ident}",
        ident,
        kernel,
        beside,
        (Gather.count(levels, CHUNKS) + Scatter.count(levels), 2 + levels),
        {
            "entering": (entering, VMEM),
            "gains": (gains, VMEM),
            "biases": (biases, VMEM),
            "b_qv": (b_qv, VMEM),
            "query_segment": (segments[0], VMEM),
            "key_segment": (segments[1], VMEM),
            "w_qkv": (w_qkv, HBM),
            "w_out": (w_out, HBM),
        },
        {
            "middle": ((rows, width), WIDE, VMEM),
            "rows_a": ((tokens, width), LOW, HBM),
            "queries": head,
            "keys": head,
            "values": head,
            "mixed": head,
            "log_total": ((tokens, 1), WIDE, VMEM),
        },
        gather_scratch(rows, width, levels, CHUNKS)
        | scatter_scratch(rows, width, levels)
        | {"own_qkv": pltpu.VMEM(w_qkv.shape, LOW), "own_out": pltpu.VMEM(w_out.shape, LOW)},
    )


def feed_forward(ident, beside, middle, gains, biases, b_up, w_up, w_down):
    levels, blocks = sizes()
    rows, width = middle.shape
    tokens, size = (blocks * rows, 4 * rows)
    units = w_up.shape[1]

    def kernel(refs, plane, greeting, sends, copies):
        first = copies.start(refs.w_up, refs.own_up)
        second = copies.start(refs.w_down, refs.own_down)
        normed, _, _ = layer_norm(refs.middle[...], refs.gains[1:2], refs.biases[2:3])
        refs.rows[span(plane.block, rows)] = normed.astype(LOW)
        greeting.wait()
        gather = Gather(plane, sends, refs.rows, refs.gather_sems)
        gather.open()
        beside.begin(plane, refs, sends, copies)
        copies.wait(first)

        def expand(step, zz):
            group = span(zz, size)
            preact = dot(refs.rows[group], refs.own_up[...]) + refs.b_up[...]
            refs.preact[group] = preact
            refs.activated[group] = (
                0.5 * preact * (1.0 + lax.erf(preact * math.sqrt(0.5)))
            ).astype(LOW)
            copies.start(refs.rows.at[group], refs.rows_b.at[group])

        gather.run(expand, beside.tick)
        copies.wait(second)

        def make(step, zz):
            group = span(zz, size)
            for cut in range(0, width, 512):
                refs.part[group, cut : cut + 512] = dot(
                    refs.activated[group], refs.own_down[:, cut : cut + 512]
                ).astype(LOW)

        Scatter(plane, sends, refs, refs.sum).run(make, beside.tick)
        result = refs.middle[...] + refs.sum[...] + refs.biases[3:4]
        refs.leaving[...] = result.astype(LOW)

    return launch(
        f"feed_forward{ident}",
        ident,
        kernel,
        beside,
        (Gather.count(levels, CHUNKS) + Scatter.count(levels), 2 + levels),
        {
            "middle": (middle, VMEM),
            "gains": (gains, VMEM),
            "biases": (biases, VMEM),
            "b_up": (b_up, VMEM),
            "w_up": (w_up, HBM),
            "w_down": (w_down, HBM),
        },
        {
            "leaving": ((rows, width), LOW, VMEM),
            "rows_b": ((tokens, width), LOW, HBM),
            "preact": ((tokens, units), WIDE, VMEM),
            "activated": ((tokens, units), LOW, VMEM),
        },
        gather_scratch(rows, width, levels, CHUNKS)
        | scatter_scratch(rows, width, levels)
        | {"own_up": pltpu.VMEM(w_up.shape, LOW), "own_down": pltpu.VMEM(w_down.shape, LOW)},
    )


def feed_backward(ident, beside, grad, gathered, middle, gains, w_up, w_down, rows_b, preact, activated):
    levels, blocks = sizes()
    rows, width = middle.shape
    tokens, size = (blocks * rows, 4 * rows)
    units = w_up.shape[1]

    def kernel(refs, plane, greeting, sends, copies):
        loads = [copies.start(refs.w_down, refs.own_down), copies.start(refs.preact, refs.own_preact)]
        if gathered is not None:
            loads.append(copies.start(refs.gathered, refs.rows))
        late = [copies.start(refs.w_up, refs.own_up)]
        last = [
            copies.start(refs.activated, refs.own_activated),
            copies.start(refs.rows_b, refs.own_rows_b),
        ]
        low = refs.grad[...].astype(LOW)
        if gathered is None:
            refs.rows[span(plane.block, rows)] = low
        refs.down_bias[...] = jnp.sum(low.astype(WIDE), axis=0, keepdims=True)
        refs.up_bias[...] = jnp.zeros_like(refs.up_bias)
        greeting.wait()
        if gathered is None:
            gather = Gather(plane, sends, refs.rows, refs.gather_sems)
            gather.open()
        beside.begin(plane, refs, sends, copies)
        for number in loads:
            copies.wait(number)

        def shrink(step, zz):
            group = span(zz, size)
            grad_act = dot_back(refs.rows[group], refs.own_down[...])
            value = refs.own_preact[group]
            slope = 0.5 * (1.0 + lax.erf(value * math.sqrt(0.5))) + value * jnp.exp(
                -0.5 * value * value
            ) * (1.0 / math.sqrt(2.0 * math.pi))
            grad_pre = (grad_act * slope).astype(LOW)
            refs.grad_pre[group] = grad_pre
            refs.up_bias[...] += jnp.sum(grad_pre.astype(WIDE), axis=0, keepdims=True)

        if gathered is None:
            gather.run(shrink, beside.tick)
        for number in late:
            copies.wait(number)

        def make(step, zz):
            group = span(zz, size)
            if gathered is not None:
                shrink(step, zz)
            for cut in range(0, width, 512):
                refs.part[group, cut : cut + 512] = dot_back(
                    refs.grad_pre[group], refs.own_up[cut : cut + 512]
                ).astype(LOW)

        def down_product(at, carry):
            cut = span(at, 128)
            refs.down_grad[cut] = dot_rows(refs.own_activated[:, cut], refs.rows[...]).astype(LOW)
            return carry

        def up_product(at, carry):
            cut = span(at, 256)
            refs.up_grad[cut] = dot_rows(refs.own_rows_b[:, cut], refs.grad_pre[...]).astype(LOW)
            return carry

        def fill(at):
            if at == 0:
                for number in last:
                    copies.wait(number)
            if at == 1:
                lax.fori_loop(0, units // 128, down_product, 0)
            if at == 2:
                lax.fori_loop(0, width // 512, up_product, 0)
            if at == 3:
                lax.fori_loop(width // 512, width // 256, up_product, 0)

        Scatter(plane, sends, refs, refs.sum).run(make, beside.tick, fill)
        _, unit, inverse = layer_norm(refs.middle[...], refs.gains[1:2], refs.gains[1:2])
        refs.gain_grad[...] = jnp.sum(refs.sum[...] * unit, axis=0, keepdims=True)
        refs.shift_grad[...] = jnp.sum(refs.sum[...], axis=0, keepdims=True)
        refs.grad_middle[...] = refs.grad[...].astype(WIDE) + norm_back(
            refs.sum[...], unit, inverse, refs.gains[1:2]
        )

    line = ((1, width), WIDE, VMEM)
    inputs = {
        "grad": (grad, VMEM),
        "middle": (middle, VMEM),
        "gains": (gains, VMEM),
        "w_up": (w_up, HBM),
        "w_down": (w_down, HBM),
        "rows_b": (rows_b, HBM),
        "preact": (preact, HBM),
        "activated": (activated, HBM),
    }
    if gathered is not None:
        inputs["gathered"] = (gathered, HBM)
    return launch(
        f"feed_backward{ident}",
        ident,
        kernel,
        beside,
        ((0 if gathered is not None else Gather.count(levels, CHUNKS)) + Scatter.count(levels), 5 + (gathered is not None)),
        inputs,
        {
            "grad_middle": ((rows, width), WIDE, VMEM),
            "up_grad": (w_up.shape, LOW, VMEM),
            "down_grad": (w_down.shape, LOW, VMEM),
            "up_bias": ((1, units), WIDE, VMEM),
            "gain_grad": line,
            "shift_grad": line,
            "down_bias": line,
        },
        gather_scratch(rows, width, levels, CHUNKS)
        | scatter_scratch(rows, width, levels)
        | {
            "own_up": pltpu.VMEM(w_up.shape, LOW),
            "own_down": pltpu.VMEM(w_down.shape, LOW),
            "own_preact": pltpu.VMEM((tokens, units), WIDE),
            "own_activated": pltpu.VMEM((tokens, units), LOW),
            "own_rows_b": pltpu.VMEM((tokens, width), LOW),
            "grad_pre": pltpu.VMEM((tokens, units), LOW),
        },
    )


def attention_backward(ident, beside, grad_middle, entering, gains, segments, w_qkv, w_out, kept):
    levels, blocks = sizes()
    rows, width = entering.shape
    tokens, size = (blocks * rows, 4 * rows)
    scaling = HD ** (-0.5)

    def kernel(refs, plane, greeting, sends, copies):
        loads = [copies.start(refs.w_out, refs.own_out)]
        late = [copies.start(refs.w_qkv, refs.own_qkv), copies.start(refs.rows_a, refs.own_rows_a)]
        low = refs.grad_middle[...].astype(LOW)
        refs.rows[span(plane.block, rows)] = low
        refs.out_bias[...] = jnp.sum(low.astype(WIDE), axis=0, keepdims=True)
        refs.grad_keys[...] = jnp.zeros_like(refs.grad_keys)
        refs.grad_values[...] = jnp.zeros_like(refs.grad_values)
        greeting.wait()
        gather = Gather(plane, sends, refs.rows, refs.gather_sems)
        gather.open()
        beside.begin(plane, refs, sends, copies)
        for number in loads:
            copies.wait(number)

        def attend_group(step, zz):
            group = span(zz, size)
            live = (refs.query_segment[group] >= 0).astype(WIDE)
            grad_mixed = (dot_back(refs.rows[group], refs.own_out[...]).astype(LOW) * live).astype(LOW)
            allowed = visible(refs, group, size, tokens)
            queries = refs.queries[group]
            scores = dot_back(queries, refs.keys[...]) * scaling
            scores = jnp.where(allowed, scores, NEG_FILL)
            probs = jnp.exp(scores - refs.log_total[group])
            grad_probs = dot_back(grad_mixed, refs.values[...])
            delta = jnp.sum(probs * grad_probs, axis=-1, keepdims=True)
            grad_scores = jnp.where(allowed, probs * (grad_probs - delta), 0.0).astype(LOW)
            refs.grad_proj[group, :HD] = (dot(grad_scores, refs.keys[...]) * scaling).astype(LOW)
            refs.grad_keys[...] += dot_rows(grad_scores, queries)
            refs.grad_values[...] += dot_rows(probs.astype(LOW), grad_mixed)

        gather.run(attend_group, beside.tick)
        refs.grad_proj[:, HD : 2 * HD] = (refs.grad_keys[...] * scaling).astype(LOW)
        refs.grad_proj[:, 2 * HD :] = refs.grad_values[...].astype(LOW)
        for number in late:
            copies.wait(number)

        def make(step, zz):
            group = span(zz, size)
            for cut in range(0, width, 512):
                refs.part[group, cut : cut + 512] = dot_back(
                    refs.grad_proj[group], refs.own_qkv[cut : cut + 512]
                ).astype(LOW)

        def qkv_product(at, carry):
            cut = span(at, 256)
            refs.qkv_grad[cut] = dot_rows(refs.own_rows_a[:, cut], refs.grad_proj[...]).astype(LOW)
            return carry

        def fill(at):
            if at == 0:
                proj_sums = jnp.sum(refs.grad_proj[...].astype(WIDE), axis=0, keepdims=True)
                refs.qv_grad[0:1] = proj_sums[:, :HD]
                refs.qv_grad[1:2] = proj_sums[:, 2 * HD :]
            if at == 1:
                refs.out_grad[...] = dot_rows(refs.mixed[...], refs.rows[...]).astype(LOW)
            if at == 2:
                lax.fori_loop(0, width // 512, qkv_product, 0)
            if at == 3:
                lax.fori_loop(width // 512, width // 256, qkv_product, 0)

        Scatter(plane, sends, refs, refs.sum).run(make, beside.tick, fill)
        hidden = refs.entering[...].astype(WIDE)
        _, unit, inverse = layer_norm(hidden, refs.gains[0:1], refs.gains[0:1])
        refs.gain_grad[...] = jnp.sum(refs.sum[...] * unit, axis=0, keepdims=True)
        refs.shift_grad[...] = jnp.sum(refs.sum[...], axis=0, keepdims=True)
        refs.grad_in[...] = refs.grad_middle[...] + norm_back(
            refs.sum[...], unit, inverse, refs.gains[0:1]
        )

    line = ((1, width), WIDE, VMEM)
    return launch(
        f"attention_backward{ident}",
        ident,
        kernel,
        beside,
        (Gather.count(levels, CHUNKS) + Scatter.count(levels), 3),
        {
            "grad_middle": (grad_middle, VMEM),
            "entering": (entering, VMEM),
            "gains": (gains, VMEM),
            "query_segment": (segments[0], VMEM),
            "key_segment": (segments[1], VMEM),
            "w_qkv": (w_qkv, HBM),
            "w_out": (w_out, HBM),
            "rows_a": (kept.rows_a, HBM),
            "queries": (kept.queries, VMEM),
            "keys": (kept.keys, VMEM),
            "values": (kept.values, VMEM),
            "mixed": (kept.mixed, VMEM),
            "log_total": (kept.log_total, VMEM),
        },
        {
            "grad_in": ((rows, width), WIDE, VMEM),
            "qkv_grad": (w_qkv.shape, LOW, VMEM),
            "out_grad": (w_out.shape, LOW, VMEM),
            "qv_grad": ((2, HD), WIDE, VMEM),
            "gain_grad": line,
            "shift_grad": line,
            "out_bias": line,
        },
        gather_scratch(rows, width, levels, CHUNKS)
        | scatter_scratch(rows, width, levels)
        | {
            "own_qkv": pltpu.VMEM(w_qkv.shape, LOW),
            "own_out": pltpu.VMEM(w_out.shape, LOW),
            "own_rows_a": pltpu.VMEM((tokens, width), LOW),
            "grad_proj": pltpu.VMEM((tokens, 3 * HD), LOW),
            "grad_keys": pltpu.VMEM((tokens, HD), WIDE),
            "grad_values": pltpu.VMEM((tokens, HD), WIDE),
        },
    )


VECTOR_LINES = 8


def closing(ident, beside, vectors):
    levels, blocks = sizes()
    members = 2 * levels
    lines = (2 + members) * VECTOR_LINES
    inputs = {}
    for layer, (norms, heads, units) in enumerate(vectors):
        for at, line in enumerate(norms):
            inputs[f"norm{layer}{at}"] = (line, VMEM)
        inputs[f"heads{layer}"] = (heads, VMEM)
        inputs[f"units{layer}"] = (units, VMEM)
    count, unit_lines = (len(vectors[0][0]), vectors[0][2].shape[1] // HD)

    def kernel(refs, plane, greeting, sends, copies):
        refs.part[...] = jnp.zeros_like(refs.part)
        for layer in (0, 1):
            for z in range(levels):
                for y in (0, 1):
                    base = (z * 4 + layer * 2 + y) * lines
                    for x in (0, 1):
                        cut = (z * 4 + x * 2 + y) * HD
                        for at in range(count):
                            line = base + x * VECTOR_LINES + at
                            refs.part[line : line + 1] = getattr(refs, f"norm{layer}{at}")[
                                :, cut : cut + HD
                            ]
            own = [getattr(refs, f"heads{layer}")[...]]
            for at in range(unit_lines):
                own.append(getattr(refs, f"units{layer}")[:, at * HD : (at + 1) * HD])
            own.append(jnp.zeros((VECTOR_LINES - 2 - unit_lines, HD), WIDE))
            refs.own[layer] = jnp.concatenate(own, axis=0)
            for z in range(levels):
                start = (z * 4 + layer * 2 + plane.y) * lines + (2 + plane.member) * VECTOR_LINES
                refs.part[pl.ds(pl.multiple_of(start, VECTOR_LINES), VECTOR_LINES)] = refs.own[layer]
        greeting.wait()
        beside.begin(plane, refs, sends, copies)
        Scatter(plane, sends, refs, refs.sum).run(lambda step, zz: None, beside.tick)
        beside.drain()
        sends.start(True, refs.sum, refs.other, refs.pair_sem.at[0], plane.over)
        await_block(refs.other, refs.pair_sem.at[0], plane.over)
        refs.vectors[...] = refs.sum[...] + refs.other[...]

    return launch(
        "closing",
        ident,
        kernel,
        beside,
        (Scatter.count(levels) + 1, 0),
        inputs,
        {"vectors": ((lines, HD), WIDE, VMEM)},
        scatter_scratch(lines, HD, levels, WIDE)
        | {
            "own": pltpu.VMEM((2, VECTOR_LINES, HD), WIDE),
            "other": pltpu.VMEM((lines, HD), WIDE),
            "pair_sem": pltpu.SemaphoreType.DMA((1,)),
        },
    )


def plane_body(
    boundary,
    doc_lengths,
    qkv_weight,
    qv_bias,
    out_weight,
    up_weight,
    up_bias,
    down_weight,
    norm_gains,
    norm_biases,
):
    plane = Plane()
    levels, y, member = (plane.levels, plane.y, plane.member)
    members = 2 * levels
    width = boundary.shape[3]
    heads_shard = qv_bias.shape[2]
    head_cut = qv_bias.shape[3]
    block_shard = up_bias.shape[1]
    own_blocks = block_shard // members

    pieces = (qv_bias[0], up_bias[0], norm_gains[0], norm_biases[0])
    packed = jnp.concatenate([piece.reshape(-1) for piece in pieces])
    lines = 16 * -(-packed.size // (16 * HD))
    packed = jnp.pad(packed, (0, lines * HD - packed.size)).reshape(lines, HD)
    depth = qkv_weight.shape[1]
    by_head = (
        qkv_weight[0]
        .reshape(depth, 3, members, HD)
        .transpose(0, 2, 1, 3)
        .reshape(depth, members * 3 * HD)
    )
    attention_shards = {0: by_head, 1: out_weight[0]}
    feed_shards = {2: up_weight[0], 3: down_weight[0]}
    start = opening(1, boundary[0], packed, Fetch(0, attention_shards, together=2, lag=3))
    planes = start.planes
    shared = start.vectors.reshape(levels, 2, 2, 2, -1).transpose(1, 0, 3, 2, 4)
    shared = shared.reshape(2, members, 2, -1)
    cuts = [0]
    for piece in pieces:
        cuts.append(cuts[-1] + piece.size)
    plane_part = lax.dynamic_index_in_dim(shared, y, 2, keepdims=False)
    qv = plane_part[:, :, cuts[0] : cuts[1]].reshape(2, members, 2, heads_shard, head_cut)
    qv = lax.dynamic_index_in_dim(qv, member, 3, keepdims=False)
    b_qv = qv.transpose(0, 2, 1, 3).reshape(2, 2, HD).astype(WIDE)
    ub = plane_part[:, :, cuts[1] : cuts[2]].reshape(2, members, block_shard, head_cut)
    ub = lax.dynamic_slice_in_dim(ub, member * own_blocks, own_blocks, axis=2)
    b_up = ub.transpose(0, 2, 1, 3).reshape(2, 1, own_blocks * HD).astype(WIDE)
    gains = (
        shared[..., cuts[2] : cuts[3]].reshape(2, members * 2, 2, -1).transpose(0, 2, 1, 3)
    ).reshape(2, 2, width).astype(WIDE)
    biases = (
        shared[..., cuts[3] : cuts[4]].reshape(2, members * 2, 4, -1).transpose(0, 2, 1, 3)
    ).reshape(2, 4, width).astype(WIDE)

    lengths = lax.dynamic_index_in_dim(doc_lengths, plane.x, 0, keepdims=False)
    tokens = boundary.shape[2] * 4 * levels
    _, segment, live, _, _, _ = visibility(lengths, 0, tokens, tokens)
    segments = (jnp.where(live, segment, -1)[:, None], segment[None, :])

    entering = planes[0]
    att0 = attention_forward(
        2, Fetch(0, feed_shards), entering, gains[0], biases[0], b_qv[0], segments, start.slice0, start.slice1
    )
    ffn0 = feed_forward(
        3, Fetch(1, attention_shards), att0.middle, gains[0], biases[0], b_up[0], att0.slice2, att0.slice3
    )
    att1 = attention_forward(
        4, Fetch(1, feed_shards), ffn0.leaving, gains[1], biases[1], b_qv[1], segments, ffn0.slice0, ffn0.slice1
    )
    ffn1 = feed_forward(
        5, Nothing(), att1.middle, gains[1], biases[1], b_up[1], att1.slice2, att1.slice3
    )
    back1 = feed_backward(
        6, Outward({0: ffn0.leaving, 1: ffn1.leaving}), planes[1], start.gathered, att1.middle, gains[1],
        att1.slice2, att1.slice3, ffn1.rows_b, ffn1.preact, ffn1.activated,
    )
    wards1 = attention_backward(
        7, Return(1, {2: back1.up_grad, 3: back1.down_grad}), back1.grad_middle, ffn0.leaving, gains[1],
        segments, ffn0.slice0, ffn0.slice1, att1,
    )
    back0 = feed_backward(
        8,
        Together(
            Outward({1: wards1.grad_in}),
            Return(1, {0: wards1.qkv_grad, 1: wards1.out_grad}),
        ),
        wards1.grad_in.astype(LOW), None, att0.middle,
        gains[0], att0.slice2, att0.slice3, ffn0.rows_b, ffn0.preact, ffn0.activated,
    )
    wards0 = attention_backward(
        9, Return(0, {2: back0.up_grad, 3: back0.down_grad}), back0.grad_middle, entering, gains[0],
        segments, start.slice0, start.slice1, att0,
    )
    vectors = [
        (
            (
                attend.gain_grad,
                feed.gain_grad,
                attend.shift_grad,
                attend.out_bias,
                feed.shift_grad,
                feed.down_bias,
            ),
            attend.qv_grad,
            feed.up_bias,
        )
        for attend, feed in ((wards0, back0), (wards1, back1))
    ]
    end = closing(
        10,
        Together(
            Return(0, {0: wards0.qkv_grad, 1: wards0.out_grad}, lag=0), Outward({0: wards0.grad_in})
        ),
        vectors,
    )
    summed = end.vectors.reshape(2 + members, VECTOR_LINES, HD)
    norms = lax.dynamic_index_in_dim(summed, plane.x, 0, keepdims=False)
    by_member = lax.dynamic_slice_in_dim(
        summed[2:], (plane.z * 2 + plane.x) * head_cut, head_cut, axis=2
    )
    own_lines = 2 + own_blocks

    def owned(first, second):
        return jnp.where(plane.core == 0, first, second).astype(WIDE)

    qkv_shard = (
        owned(end.shard0, back0.shard0)
        .reshape(depth, members, 3, HD)
        .transpose(0, 2, 1, 3)
        .reshape(depth, 3, members * HD)
    )
    return (
        back1.owned_rows[None],
        owned(end.owned_rows, back0.owned_rows)[None],
        qkv_shard[None],
        by_member[:, :2].transpose(1, 0, 2)[None],
        owned(end.shard1, back0.shard1)[None],
        owned(wards0.shard2, wards1.shard2)[None],
        by_member[:, 2:own_lines].reshape(1, block_shard, head_cut),
        owned(wards0.shard3, wards1.shard3)[None],
        norms[None, :2],
        norms[None, 2:6],
    )


def fits_plane(mesh):
    return mesh.shape["dp"] == 8 and mesh.shape["tensor"] == 2 and mesh.shape["section"] == 2


def solution(mesh):
    placed = (
        P("section", None, ("dp", "tensor"), None),
        P(),
        P("section", "dp", None, "tensor"),
        P("section", None, "tensor", "dp"),
        P("section", "tensor", "dp"),
        P("section", "dp", "tensor"),
        P("section", "tensor", "dp"),
        P("section", "tensor", "dp"),
        P("section", None, ("dp", "tensor")),
        P("section", None, ("dp", "tensor")),
    )
    return jax.shard_map(
        plane_body if fits_plane(mesh) else body,
        mesh=mesh,
        in_specs=placed,
        out_specs=(
            P("section", None, ("dp", "tensor"), None),
            P("section", None, ("dp", "tensor"), None),
            P("section", "dp", None, "tensor"),
            P("section", None, "tensor", "dp"),
            P("section", "tensor", "dp"),
            P("section", "dp", "tensor"),
            P("section", "tensor", "dp"),
            P("section", "tensor", "dp"),
            P("section", None, ("dp", "tensor")),
            P("section", None, ("dp", "tensor")),
        ),
        check_vma=False,
    )
```

```python
from functools import partial
import math
from types import SimpleNamespace

import jax
import jax.numpy as jnp
from jax import lax
from jax.experimental import pallas as pl
from jax.experimental.pallas import tpu as pltpu
from jax.sharding import PartitionSpec as P

HD = 128


EPSILON = 1e-05
NEG_FILL = -1e30
MESH = pl.DeviceIdType.MESH


def from_behind(value, axis, steps):
    count = lax.axis_size(axis)
    first, last = (max(0, -steps), min(count, count - steps))
    return lax.ppermute(value, axis, [(source, source + steps) for source in range(first, last)])


def layer_norm(hidden, gain, shift):
    average = jnp.mean(hidden, axis=-1, keepdims=True)
    centred = hidden - average
    variance = jnp.mean(centred * centred, axis=-1, keepdims=True)
    inverse = lax.rsqrt(variance + EPSILON)
    normed = centred * inverse
    return (normed * gain + shift, normed, inverse)


def norm_back(grad_out, normed, inverse, gain):
    scaled = grad_out * gain
    return inverse * (
        scaled
        - jnp.mean(scaled, axis=-1, keepdims=True)
        - normed * jnp.mean(scaled * normed, axis=-1, keepdims=True)
    )


def visibility(lengths, dp_index, rows_dp, seq_len):
    per_seq = seq_len // lengths.shape[0]
    docs = lengths.shape[1]
    key_pos = jnp.arange(seq_len, dtype=jnp.int32)
    seq_of = key_pos // per_seq
    local = key_pos - seq_of * per_seq
    doc_ends = jnp.cumsum(lengths, axis=1)
    ends_row = jnp.take(doc_ends, seq_of, axis=0)
    key_seg = seq_of * (docs + 1) + jnp.sum((local[:, None] >= ends_row).astype(jnp.int32), axis=1)
    key_live = local < ends_row[:, docs - 1]
    start_row = dp_index * rows_dp
    query_pos = start_row + jnp.arange(rows_dp, dtype=jnp.int32)
    query_seg = lax.dynamic_slice_in_dim(key_seg, start_row, rows_dp)
    query_live = lax.dynamic_slice_in_dim(key_live, start_row, rows_dp)
    return (query_pos, query_seg, query_live, key_pos, key_seg, key_live)


def widen(rows_low):
    return lax.all_gather(rows_low, "tensor", axis=0, tiled=True)


def narrow(partial_rows):
    return lax.psum_scatter(
        partial_rows.astype(jnp.bfloat16), "tensor", scatter_dimension=0, tiled=True
    ).astype(jnp.float32)


def fetch_weights(
    qkv_weight, qv_bias, out_weight, up_weight, up_bias, down_weight, norm_gains, norm_biases
):
    w_qkv, b_qv, w_out, w_up, b_up, w_down = (
        lax.all_gather(qkv_weight[0], "dp", axis=0, tiled=True),
        lax.all_gather(qv_bias[0], "dp", axis=2, tiled=True),
        lax.all_gather(out_weight[0], "dp", axis=1, tiled=True),
        lax.all_gather(up_weight[0], "dp", axis=0, tiled=True),
        lax.all_gather(up_bias[0], "dp", axis=1, tiled=True),
        lax.all_gather(down_weight[0], "dp", axis=1, tiled=True),
    )
    gain_rows, bias_rows = (
        lax.all_gather(norm_gains[0], ("dp", "tensor"), axis=1, tiled=True),
        lax.all_gather(norm_biases[0], ("dp", "tensor"), axis=1, tiled=True),
    )
    return (
        w_qkv,
        b_qv.reshape(2, -1).astype(jnp.float32),
        w_out,
        w_up,
        b_up.reshape(-1).astype(jnp.float32),
        w_down,
        gain_rows.astype(jnp.float32),
        bias_rows.astype(jnp.float32),
    )


def block_scores(q_heads, key_block, kpos_block, kseg_block, sight):
    scores = jnp.einsum(
        "qhd,khd->hqk", q_heads, key_block, preferred_element_type=jnp.float32
    ) * HD ** (-0.5)
    allowed = (
        (sight[1][:, None] == kseg_block[None, :])
        & (kpos_block[None, :] <= sight[0][:, None])
        & sight[2][:, None]
    )
    return (jnp.where(allowed[None], scores, NEG_FILL), allowed)


def key_blocks(keys, values, sight):
    seq_len = keys.shape[0]
    block_rows = math.gcd(seq_len, 512)
    blocks = seq_len // block_rows
    heads = keys.shape[1] // HD
    return (
        keys.reshape(blocks, block_rows, heads, HD),
        values.reshape(blocks, block_rows, heads, HD),
        sight[3].reshape(blocks, block_rows),
        sight[4].reshape(blocks, block_rows),
    )


def attend(queries, keys, values, sight):
    rows = queries.shape[0]
    heads = queries.shape[1] // HD
    q_heads = queries.reshape(rows, heads, HD)
    stacked = key_blocks(keys, values, sight)

    def find_scale(carry, pieces):
        top, total = carry
        scores, allowed = block_scores(q_heads, pieces[0], pieces[2], pieces[3], sight)
        new_top = jnp.maximum(top, jnp.max(scores, axis=-1))
        total = total * jnp.exp(top - new_top) + jnp.sum(
            jnp.exp(scores - new_top[..., None]), axis=-1
        )
        return ((new_top, total), None)

    start = (jnp.full((heads, rows), -jnp.inf, jnp.float32), jnp.zeros((heads, rows), jnp.float32))
    (top, total), ignored = lax.scan(find_scale, start, stacked)
    log_total = top + jnp.log(total)

    def weigh(carry, pieces):
        scores, allowed = block_scores(q_heads, pieces[0], pieces[2], pieces[3], sight)
        probs = jnp.exp(scores - log_total[..., None]).astype(jnp.bfloat16)
        return (
            carry
            + jnp.einsum("hqk,khd->qhd", probs, pieces[1], preferred_element_type=jnp.float32),
            None,
        )

    heads_out, ignored = lax.scan(weigh, jnp.zeros((rows, heads, HD), jnp.float32), stacked)
    return (heads_out, log_total, q_heads)


def attend_back(q_heads, keys, values, sight, log_total, grad_heads, delta):
    seq_len = keys.shape[0]
    stacked = key_blocks(keys, values, sight)
    scaling = HD ** (-0.5)

    def one_step(grad_q, pieces):
        scores, allowed = block_scores(q_heads, pieces[0], pieces[2], pieces[3], sight)
        probs = jnp.exp(scores - log_total[..., None])
        grad_p = jnp.einsum(
            "qhd,khd->hqk", grad_heads, pieces[1], preferred_element_type=jnp.float32
        )
        grad_s = jnp.where(allowed[None], probs * (grad_p - delta[..., None]), 0.0).astype(
            jnp.bfloat16
        )
        grad_q = (
            grad_q
            + jnp.einsum("hqk,khd->qhd", grad_s, pieces[0], preferred_element_type=jnp.float32)
            * scaling
        )
        grad_v = jnp.einsum(
            "hqk,qhd->khd",
            probs.astype(jnp.bfloat16),
            grad_heads,
            preferred_element_type=jnp.float32,
        )
        grad_k = (
            jnp.einsum("hqk,qhd->khd", grad_s, q_heads, preferred_element_type=jnp.float32)
            * scaling
        )
        return (grad_q, (grad_k, grad_v))

    grad_q, outputs = lax.scan(one_step, jnp.zeros(q_heads.shape, jnp.float32), stacked)
    return (grad_q, outputs[0].reshape(seq_len, -1), outputs[1].reshape(seq_len, -1))


def forward(entering, weights, sight):
    w_qkv, b_qv, w_out, w_up, b_up, w_down, gain_rows, bias_rows = weights
    hidden = entering.astype(jnp.float32)
    normed_a, unit_a, inverse_a = layer_norm(hidden, gain_rows[0], bias_rows[0])
    rows_a = widen(normed_a.astype(jnp.bfloat16))
    projected = jnp.einsum("rd,djh->rjh", rows_a, w_qkv, preferred_element_type=jnp.float32)
    queries = (projected[:, 0] + b_qv[0]).astype(jnp.bfloat16)
    keys_own = projected[:, 1].astype(jnp.bfloat16)
    values_own = (projected[:, 2] + b_qv[1]).astype(jnp.bfloat16)
    keys, values = (
        lax.all_gather(keys_own, "dp", axis=0, tiled=True),
        lax.all_gather(values_own, "dp", axis=0, tiled=True),
    )
    heads_out, log_total, q_heads = attend(queries, keys, values, sight)
    live_rows = sight[2].astype(jnp.float32)
    mixed_low = (heads_out.reshape(heads_out.shape[0], -1) * live_rows[:, None]).astype(
        jnp.bfloat16
    )
    middle = (
        hidden
        + narrow(jnp.dot(mixed_low, w_out, preferred_element_type=jnp.float32))
        + bias_rows[1]
    )
    normed_b, unit_b, inverse_b = layer_norm(middle, gain_rows[1], bias_rows[2])
    rows_b = widen(normed_b.astype(jnp.bfloat16))
    preact = jnp.dot(rows_b, w_up, preferred_element_type=jnp.float32) + b_up
    activated = jax.nn.gelu(preact, approximate=False).astype(jnp.bfloat16)
    result = (
        middle
        + narrow(jnp.dot(activated, w_down, preferred_element_type=jnp.float32))
        + bias_rows[3]
    )
    saved = (
        unit_a,
        inverse_a,
        rows_a,
        q_heads,
        keys,
        values,
        heads_out,
        log_total,
        mixed_low,
        unit_b,
        inverse_b,
        rows_b,
        preact,
        activated,
    )
    return (result, saved)


def backward(saved, grad_out, weights, sight):
    w_qkv, b_qv, w_out, w_up, b_up, w_down, gain_rows, bias_rows = weights
    (
        unit_a,
        inverse_a,
        rows_a,
        q_heads,
        keys,
        values,
        heads_out,
        log_total,
        mixed_low,
        unit_b,
        inverse_b,
        rows_b,
        preact,
        activated,
    ) = saved
    rows = rows_a.shape[0]
    grad_branch = grad_out.astype(jnp.bfloat16)
    down_bias_grad = jnp.sum(grad_branch.astype(jnp.float32), axis=0)
    wide_branch = widen(grad_branch)
    grad_act = jnp.einsum("rd,fd->rf", wide_branch, w_down, preferred_element_type=jnp.float32)
    ignored, gelu_pull = jax.vjp(partial(jax.nn.gelu, approximate=False), preact)
    grad_pre = gelu_pull(grad_act)[0].astype(jnp.bfloat16)
    up_bias_grad = jnp.sum(grad_pre.astype(jnp.float32), axis=0)
    grad_normed_b = narrow(
        jnp.einsum("rf,df->rd", grad_pre, w_up, preferred_element_type=jnp.float32)
    )
    gain_b_grad = jnp.sum(grad_normed_b * unit_b, axis=0)
    shift_b_grad = jnp.sum(grad_normed_b, axis=0)
    grad_middle = grad_out + norm_back(grad_normed_b, unit_b, inverse_b, gain_rows[1])
    grad_attn = grad_middle.astype(jnp.bfloat16)
    out_bias_grad = jnp.sum(grad_attn.astype(jnp.float32), axis=0)
    wide_attn = widen(grad_attn)
    live_rows = sight[2].astype(jnp.bfloat16)
    grad_flat = (
        jnp.einsum("rd,ed->re", wide_attn, w_out, preferred_element_type=jnp.float32).astype(
            jnp.bfloat16
        )
        * live_rows[:, None]
    )
    grad_heads = grad_flat.reshape(heads_out.shape)
    delta = jnp.einsum("qhd,qhd->hq", grad_heads.astype(jnp.float32), heads_out)
    grad_q, grad_k_all, grad_v_all = attend_back(
        q_heads, keys, values, sight, log_total, grad_heads, delta
    )
    grad_k, grad_v = (
        lax.psum_scatter(
            grad_k_all.astype(jnp.bfloat16), "dp", scatter_dimension=0, tiled=True
        ).astype(jnp.float32),
        lax.psum_scatter(
            grad_v_all.astype(jnp.bfloat16), "dp", scatter_dimension=0, tiled=True
        ).astype(jnp.float32),
    )
    grad_proj = jnp.stack((grad_q.reshape(rows, -1), grad_k, grad_v), axis=1).astype(jnp.bfloat16)
    proj_sums = jnp.sum(grad_proj.astype(jnp.float32), axis=0)
    qv_grad = jnp.stack((proj_sums[0], proj_sums[2]))
    grad_normed_a = narrow(
        jnp.einsum("rjh,djh->rd", grad_proj, w_qkv, preferred_element_type=jnp.float32)
    )
    gain_a_grad = jnp.sum(grad_normed_a * unit_a, axis=0)
    shift_a_grad = jnp.sum(grad_normed_a, axis=0)
    grad_in = grad_middle + norm_back(grad_normed_a, unit_a, inverse_a, gain_rows[0])
    gains_grad = jnp.stack((gain_a_grad, gain_b_grad))
    biases_grad = jnp.stack((shift_a_grad, out_bias_grad, shift_b_grad, down_bias_grad))
    factors = (rows_b, grad_pre, activated, wide_branch, mixed_low, wide_attn, rows_a, grad_proj)
    vectors = (qv_grad, up_bias_grad, gains_grad, biases_grad)
    return (grad_in, factors, vectors)


def weight_products(factors):
    rows_b, grad_pre, activated, wide_branch, mixed_low, wide_attn, rows_a, grad_proj = factors
    down_grad = jnp.einsum("rf,rd->fd", activated, wide_branch, preferred_element_type=jnp.float32)
    up_grad = jnp.einsum("rd,rf->df", rows_b, grad_pre, preferred_element_type=jnp.float32)
    out_grad = jnp.einsum("re,rd->ed", mixed_low, wide_attn, preferred_element_type=jnp.float32)
    qkv_grad = jnp.einsum("rd,rjh->djh", rows_a, grad_proj, preferred_element_type=jnp.float32)
    return (qkv_grad, out_grad, up_grad, down_grad)


def assemble(products, vectors):
    qkv_grad, out_grad, up_grad, down_grad = products
    qv_grad, up_bias_grad, gains_grad, biases_grad = vectors
    return (qkv_grad, qv_grad, out_grad, up_grad, up_bias_grad, down_grad, gains_grad, biases_grad)


def reduce_grads(local_grads):
    qkv_grad, qv_grad, out_grad, up_grad, up_bias_grad, down_grad, gains_grad, biases_grad = (
        local_grads
    )
    heads = qv_grad.shape[1] // HD
    shards = (
        lax.psum_scatter(
            qkv_grad[None].astype(jnp.bfloat16), "dp", scatter_dimension=1, tiled=True
        ).astype(jnp.float32),
        lax.psum_scatter(
            qv_grad.reshape(1, 2, heads, HD).astype(jnp.bfloat16),
            "dp",
            scatter_dimension=3,
            tiled=True,
        ).astype(jnp.float32),
        lax.psum_scatter(
            out_grad[None].astype(jnp.bfloat16), "dp", scatter_dimension=2, tiled=True
        ).astype(jnp.float32),
        lax.psum_scatter(
            up_grad[None].astype(jnp.bfloat16), "dp", scatter_dimension=1, tiled=True
        ).astype(jnp.float32),
        lax.psum_scatter(
            up_bias_grad.reshape(1, -1, HD).astype(jnp.bfloat16),
            "dp",
            scatter_dimension=2,
            tiled=True,
        ).astype(jnp.float32),
        lax.psum_scatter(
            down_grad[None].astype(jnp.bfloat16), "dp", scatter_dimension=2, tiled=True
        ).astype(jnp.float32),
    )
    vectors = (
        lax.psum_scatter(gains_grad[None], ("dp", "tensor"), scatter_dimension=2, tiled=True),
        lax.psum_scatter(biases_grad[None], ("dp", "tensor"), scatter_dimension=2, tiled=True),
    )
    return tuple(shards) + tuple(vectors)


def body(
    boundary,
    doc_lengths,
    qkv_weight,
    qv_bias,
    out_weight,
    up_weight,
    up_bias,
    down_weight,
    norm_gains,
    norm_biases,
):
    section_index = lax.axis_index("section")
    on_first = section_index == 0
    own_part = boundary[0]
    batches = own_part.shape[0]
    rows_dp = own_part.shape[1] * lax.axis_size("tensor")
    seq_len = rows_dp * lax.axis_size("dp")
    dp_index = lax.axis_index("dp")
    sources = (
        qkv_weight,
        qv_bias,
        out_weight,
        up_weight,
        up_bias,
        down_weight,
        norm_gains,
        norm_biases,
    )
    fixed_weights = fetch_weights(*sources)

    def current():
        return fixed_weights

    def sight_for(batch_at):
        lengths = lax.dynamic_index_in_dim(doc_lengths, batch_at, 0, keepdims=False)
        return visibility(lengths, dp_index, rows_dp, seq_len)

    def pick(first_value, second_value):
        return jnp.where(on_first, first_value, second_value)

    received = jnp.zeros_like(own_part[0])
    kept_ticks, exits = ([], [])
    for tick_index in range(batches + 1):
        entering = jnp.where(on_first, own_part[min(tick_index, batches - 1)], received)
        batch_at = jnp.clip(tick_index - section_index, 0, batches - 1)
        result, saved = forward(entering, current(), sight_for(batch_at))
        leaving = result.astype(jnp.bfloat16)
        kept_ticks.append(saved)
        exits.append(leaving)
        if tick_index < batches:
            received = from_behind(leaving, "section", 1)
    acts = jnp.stack(
        [jnp.where(on_first, exits[number], exits[number + 1]) for number in range(batches)]
    )[None]
    returned = jnp.zeros_like(own_part[0])
    summed = None
    vector_sum = None
    factor_ticks = []
    leaving_grads = []
    for tick_index in range(batches + 1):
        own_grad = own_part[min(tick_index, batches - 1)].astype(jnp.float32)
        if tick_index == batches:
            own_grad = jnp.zeros_like(own_grad)
        grad_out = jnp.where(on_first, returned.astype(jnp.float32), own_grad)
        saved = jax.tree.map(
            pick, kept_ticks[max(tick_index - 1, 0)], kept_ticks[min(tick_index + 1, batches)]
        )
        batch_at = jnp.where(on_first, max(tick_index - 1, 0), min(tick_index, batches - 1))
        grad_in, factors, vectors = backward(saved, grad_out, current(), sight_for(batch_at))
        leaving_grads.append(grad_in)
        if tick_index < batches:
            returned = from_behind(grad_in.astype(jnp.bfloat16), "section", -1)
        factor_ticks.append(factors)
        vector_sum = (
            vectors
            if vector_sum is None
            else tuple((former + latter for former, latter in zip(vector_sum, vectors)))
        )
    joined = tuple(
        (
            jnp.concatenate([entry[number] for entry in factor_ticks], axis=0)
            for number in range(len(factor_ticks[0]))
        )
    )
    summed = reduce_grads(assemble(weight_products(joined), vector_sum))
    input_grads = jnp.stack(
        [
            jnp.where(on_first, leaving_grads[number + 1], leaving_grads[number])
            for number in range(batches)
        ]
    )[None]
    return (acts, input_grads) + tuple(summed)


LOW, WIDE = (jnp.bfloat16, jnp.float32)
HBM, VMEM, DMAS = (pl.ANY, pltpu.VMEM, pltpu.SemaphoreType.DMA)


def dot(left, right):
    return jnp.dot(left, right, preferred_element_type=WIDE)


def dot_back(left, right):
    return lax.dot_general(left, right, (((1,), (1,)), ((), ())), preferred_element_type=WIDE)


def dot_rows(left, right):
    return lax.dot_general(left, right, (((0,), (0,)), ((), ())), preferred_element_type=WIDE)


def device(core, z, x, y):
    return (core, z * 2 + x, y)


class Plane:
    def __init__(self):
        dp = lax.axis_index("dp")
        self.levels = lax.axis_size("dp") // 2
        self.core, self.y = (lax.axis_index("section"), lax.axis_index("tensor"))
        self.z, self.x = (dp // 2, lax.rem(dp, 2))
        self.sibling = device(1 - self.core, self.z, self.x, self.y)
        self.across = device(self.core, self.z, self.x, 1 - self.y)
        self.over = device(self.core, self.z, 1 - self.x, self.y)
        self.corner = device(1 - self.core, self.z, 1 - self.x, self.y)
        self.member = self.z * 2 + self.core
        self.block = self.z * 4 + self.core * 2 + self.y

    def along(self, z):
        return device(self.core, jnp.clip(z, 0, self.levels - 1), self.x, self.y)

    def partners(self):
        partners = [self.across, self.over, self.corner]
        for step in range(self.levels):
            zz = lax.rem(self.z + step, self.levels)
            for other in (0, 1):
                if step or other:
                    core = 1 - self.core if other else self.core
                    partners.append(device(core, zz, self.x, self.y))
        return partners

    def nearest(self):
        tables = []
        for z in range(self.levels):
            tables.append(sorted(range(self.levels), key=lambda zz: (abs(zz - z), zz)))
        found = []
        for place in range(self.levels):
            number = jnp.int32(tables[0][place])
            for z in range(1, self.levels):
                number = jnp.where(self.z == z, tables[z][place], number)
            found.append(number)
        return found


def guarded(present, act):
    if present is True:
        act()
    else:
        pl.when(present)(act)


class Sends:
    def __init__(self, sems):
        self.sems = sems
        self.pending = []

    def start(self, present, source, target, arrived, partner):
        copy = pltpu.make_async_remote_copy(
            src_ref=source,
            dst_ref=target,
            send_sem=self.sems.at[len(self.pending)],
            recv_sem=arrived,
            device_id=partner,
            device_id_type=MESH,
        )
        guarded(present, copy.start)
        self.pending.append([present, copy, False])
        return len(self.pending) - 1

    def wait(self, *numbers):
        for number in numbers:
            present, copy, done = self.pending[number]
            if not done:
                guarded(present, copy.wait_send)
                self.pending[number][2] = True

    def finish(self):
        self.wait(*range(len(self.pending)))


class Copies:
    def __init__(self, sems):
        self.sems = sems
        self.pending = []

    def start(self, source, target, present=True):
        copy = pltpu.make_async_copy(source, target, self.sems.at[len(self.pending)])
        guarded(present, copy.start)
        self.pending.append([present, copy, False])
        return len(self.pending) - 1

    def wait(self, *numbers):
        for number in numbers:
            present, copy, done = self.pending[number]
            if not done:
                guarded(present, copy.wait)
                self.pending[number][2] = True

    def finish(self):
        for number in range(len(self.pending)):
            self.wait(number)


def await_block(block, arrived, partner):
    pltpu.make_async_remote_copy(
        src_ref=block,
        dst_ref=block,
        send_sem=arrived,
        recv_sem=arrived,
        device_id=partner,
        device_id_type=MESH,
    ).wait_recv()


def span(start, size):
    return pl.ds(pl.multiple_of(start * size, size), size)


class Gather:
    def __init__(self, plane, sends, rows, sems):
        self.plane, self.sends, self.rows, self.sems = (plane, sends, rows, sems)
        self.chunks = sems.shape[1]
        self.size = rows.shape[0] // (sems.shape[0] * self.chunks)

    def spot(self, zz, core, y, chunk):
        number = zz * 4 + core * 2 + y
        return (
            self.rows.at[span(number * self.chunks + chunk, self.size)],
            self.sems.at[number, chunk],
        )

    def open(self):
        plane = self.plane
        for chunk in range(self.chunks):
            held, arrived = self.spot(plane.z, plane.core, plane.y, chunk)
            for present, partner in (
                (True, plane.across),
                (plane.z > 0, plane.along(plane.z - 1)),
                (plane.z < plane.levels - 1, plane.along(plane.z + 1)),
                (True, plane.sibling),
            ):
                self.sends.start(present, held, held, arrived, partner)

    def run(self, on_group, tick):
        plane = self.plane
        order = plane.nearest()

        def complete(step):
            zz = order[step]
            for chunk in range(self.chunks):
                held, arrived = self.spot(zz, plane.core, 1 - plane.y, chunk)
                await_block(held, arrived, plane.across)
                self.sends.start(True, held, held, arrived, plane.sibling)
            for yy in (plane.y, 1 - plane.y):
                for chunk in range(self.chunks):
                    held, arrived = self.spot(zz, 1 - plane.core, yy, chunk)
                    await_block(held, arrived, plane.sibling)
            on_group(step, zz)

        for step in range(1, plane.levels):
            zz = order[step]
            onward = jnp.where(zz < plane.z, plane.z + 1, plane.z - 1)
            can_go = (onward >= 0) & (onward < plane.levels)
            for chunk in range(self.chunks):
                held, arrived = self.spot(zz, plane.core, plane.y, chunk)
                await_block(held, arrived, plane.across)
                self.sends.start(can_go, held, held, arrived, plane.along(onward))
                self.sends.start(True, held, held, arrived, plane.across)
                self.sends.start(True, held, held, arrived, plane.sibling)
            complete(step - 1)
            tick()
        complete(plane.levels - 1)
        tick()

    @staticmethod
    def count(levels, chunks):
        return chunks * (4 + 3 * (levels - 1) + levels)


class Scatter:
    def __init__(self, plane, sends, refs, result):
        self.plane, self.sends, self.refs, self.result = (plane, sends, refs, result)
        self.chunks = refs.across_sems.shape[1]
        self.size = result.shape[0] // self.chunks

    @staticmethod
    def count(levels, chunks):
        return chunks * (4 * levels - 1)

    def part(self, zz, core, y, chunk):
        number = (zz * 4 + core * 2 + y) * self.chunks + chunk
        return self.refs.part.at[span(number, self.size)]

    def spot(self, buffer, sems, slot, chunk):
        return buffer.at[slot, span(chunk, self.size)], sems.at[slot, chunk]

    def take(self, buffer, sems, slot, chunk):
        came, arrived = self.spot(buffer, sems, slot, chunk)
        await_block(came, arrived, self.plane.across)
        return came[...].astype(WIDE)

    def pair(self, zz, y, chunk):
        refs = self.refs
        own = self.part(zz, self.plane.core, y, chunk)[...].astype(WIDE)
        return own + self.take(refs.from_sibling, refs.sibling_sems, zz * 2 + y, chunk)

    def give_sibling(self, zz):
        plane, refs = (self.plane, self.refs)
        for yy in (1 - plane.y, plane.y):
            for chunk in range(self.chunks):
                landing, arrived = self.spot(
                    refs.from_sibling, refs.sibling_sems, zz * 2 + yy, chunk
                )
                self.sends.start(
                    True, self.part(zz, 1 - plane.core, yy, chunk), landing, arrived, plane.sibling
                )

    def give_across(self, zz):
        plane, refs = (self.plane, self.refs)
        for chunk in range(self.chunks):
            staged = refs.from_sibling.at[zz * 2 + 1 - plane.y, span(chunk, self.size)]
            staged[...] = self.pair(zz, 1 - plane.y, chunk).astype(staged.dtype)
            landing, arrived = self.spot(refs.from_across, refs.across_sems, zz, chunk)
            self.sends.start(True, staged, landing, arrived, plane.across)

    def plane_sum(self, zz, chunk):
        refs = self.refs
        total = self.pair(zz, self.plane.y, chunk)
        return total + self.take(refs.from_across, refs.across_sems, zz, chunk)

    def come(self, slot, chunk):
        return self.take(self.refs.from_behind, self.refs.behind_sems, slot, chunk)

    def give_onward(self, zz):
        plane, refs = (self.plane, self.refs)
        onward = jnp.where(zz > plane.z, plane.z + 1, plane.z - 1)
        behind = plane.z * 2 - onward
        slot = jnp.where((onward == zz) & (zz < plane.z), plane.levels, zz)
        for chunk in range(self.chunks):
            refs.total[...] = self.plane_sum(zz, chunk)

            @pl.when((behind >= 0) & (behind < plane.levels))
            def _(chunk=chunk):
                refs.total[...] += self.come(zz, chunk)

            staged = refs.from_sibling.at[zz * 2 + plane.y, span(chunk, self.size)]
            staged[...] = refs.total[...].astype(staged.dtype)
            landing, arrived = self.spot(refs.from_behind, refs.behind_sems, slot, chunk)
            self.sends.start(True, staged, landing, arrived, plane.along(onward))

    def conclude(self):
        plane = self.plane
        for chunk in range(self.chunks):
            own = self.result.at[span(chunk, self.size)]
            own[...] = self.plane_sum(plane.z, chunk)

            @pl.when(plane.z > 0)
            def _(own=own, chunk=chunk):
                own[...] += self.come(plane.z, chunk)

            @pl.when(plane.z < plane.levels - 1)
            def _(own=own, chunk=chunk):
                own[...] += self.come(plane.levels, chunk)

    def run(self, make, tick, fill=None):
        levels = self.plane.levels
        order = self.plane.nearest()[::-1]
        for step in range(levels + 3):
            if step < levels:
                make(step, order[step])
                self.give_sibling(order[step])
            if 0 < step <= levels:
                self.give_across(order[step - 1])
            if step >= levels - 1:
                tick()
                if fill is not None:
                    fill(step - levels + 1)
            if 3 <= step < levels + 2:
                self.give_onward(order[step - 3])
        self.conclude()


def scatter_scratch(rows, width, levels, chunks, dtype=LOW):
    def held(count):
        return VMEM((count, rows, width), dtype)

    return dict(
        part=VMEM((rows * 4 * levels, width), dtype),
        from_sibling=held(2 * levels),
        from_across=held(levels),
        from_behind=held(levels + 1),
        total=VMEM((rows // chunks, width), WIDE),
        sum=VMEM((rows, width), WIDE),
        sibling_sems=DMAS((2 * levels, chunks)),
        across_sems=DMAS((levels, chunks)),
        behind_sems=DMAS((levels + 1, chunks)),
    )


def by_rows(which):
    return which in (1, 3)


def piece_of_shard(which, ref, member, members):
    if by_rows(which):
        return ref.at[span(member, ref.shape[0] // members)]
    return ref.at[:, span(member, ref.shape[1] // members)]


def piece_of_slice(which, ref, shard, shards):
    if by_rows(which):
        return ref.at[:, span(shard, ref.shape[1] // shards)]
    return ref.at[span(shard, ref.shape[0] // shards)]


def slice_shape(which, shape, shards):
    rows, columns = shape
    if by_rows(which):
        return (rows // shards, columns * shards)
    return (rows * shards, columns // shards)


def shard_shape(which, shape, shards):
    rows, columns = shape
    if by_rows(which):
        return (rows * shards, columns // shards)
    return (rows // shards, columns * shards)


class Fetch:
    UNITS = ((0, (0, 1)), (0, (2,)), (0, (3,)), (1, (0, 1)), (1, (2,)), (1, (3,)))
    LAG = 4

    def __init__(self, plane, shards, slices, refs, sends, copies):
        self.plane, self.shards, self.slices = (plane, shards, slices)
        self.refs, self.sends, self.copies = (refs, sends, copies)
        acts = []
        for unit in range(len(self.UNITS)):
            for step in range(plane.levels - 1, -1, -1):
                acts.append((unit, step))
        self.moments = []
        for at in range(len(acts) + self.LAG):
            moment = []
            if at < len(acts):
                moment.append((self.spread,) + acts[at])
            if at >= self.LAG:
                moment.append((self.hand_over,) + acts[at - self.LAG])
            self.moments.append(moment)
        self.left = [plane.levels] * len(self.UNITS)
        self.kept = [[] for _ in self.UNITS]

    @staticmethod
    def count(levels):
        return 4 * 2 * (3 * levels), 4 * 2 + 8

    def tick(self, times=1):
        for _ in range(times):
            if self.moments:
                for act, unit, step in self.moments.pop(0):
                    for which in self.UNITS[unit][1]:
                        act(unit, which, step)
                    if act == self.hand_over:
                        self.left[unit] -= 1

    def require(self, unit):
        while self.left[unit]:
            self.tick()
        plane, refs = (self.plane, self.refs)
        layer, weights = self.UNITS[unit]
        for which in weights:
            part = self.slices[which].at[layer]
            for zz in range(plane.levels):
                held = piece_of_slice(which, part, zz * 2 + 1 - plane.x, 2 * plane.levels)
                await_block(held, refs.cross_sems.at[which, layer, zz], plane.over)
        self.copies.wait(*self.kept[unit])
        for which in weights:
            self.copies.start(self.slices[which].at[layer], refs.slices_out[which].at[layer])

    def spread(self, unit, which, step):
        plane, refs, layer = (self.plane, self.refs, self.UNITS[unit][0])
        members = 2 * plane.levels
        shard, part = (self.shards[which], self.slices[which].at[layer])
        owner = plane.core == layer
        target = piece_of_slice(which, part, plane.z * 2 + plane.x, members)
        zz = lax.rem(plane.z + step, plane.levels)
        for other in (0, 1):
            core = 1 - plane.core if other else plane.core
            source = piece_of_shard(which, shard, zz * 2 + core, members)
            if step or other:
                self.sends.start(
                    owner,
                    source,
                    target,
                    refs.column_sems.at[which, layer, plane.z],
                    device(core, zz, plane.x, plane.y),
                )
            else:
                self.kept[unit].append(self.copies.start(source, target, owner))

    def hand_over(self, unit, which, step):
        plane, refs, layer = (self.plane, self.refs, self.UNITS[unit][0])
        members = 2 * plane.levels
        shard, part = (self.shards[which], self.slices[which].at[layer])
        zz = lax.rem(plane.z - step + plane.levels, plane.levels)
        held = piece_of_slice(which, part, zz * 2 + plane.x, members)
        arrived = refs.column_sems.at[which, layer, zz]
        cross = refs.cross_sems.at[which, layer, zz]
        if step:
            await_block(held, arrived, plane.over)
            self.sends.start(True, held, held, cross, plane.over)
        else:
            owner = plane.core == layer
            source = piece_of_shard(which, shard, plane.member, members)
            guarded(jnp.logical_not(owner), partial(await_block, held, arrived, plane.over))
            self.sends.start(jnp.logical_not(owner), held, held, cross, plane.over)
            self.sends.start(owner, source, held, cross, plane.over)


class Return:
    def __init__(self, plane, slices, landed, shards, refs, sends, copies):
        self.plane, self.slices, self.landed, self.shards = (plane, slices, landed, shards)
        self.refs, self.sends, self.copies = (refs, sends, copies)
        self.moments, self.left, self.given = ([], {}, {})

    @staticmethod
    def count(levels):
        return 4 * 2 * (2 * levels), 4 * 2

    def give(self, layer, which, lag=0):
        plane = self.plane
        self.moments.extend([None] * lag)
        self.left[layer, which], self.given[layer, which] = (plane.levels, [])
        for step in range(plane.levels - 1, -1, -1):
            zz = lax.rem(plane.z + step, plane.levels)
            number = self.sends.start(
                True,
                piece_of_slice(which, self.slices[which], zz * 2 + 1 - plane.x, 2 * plane.levels),
                self.landed[which].at[layer, zz],
                self.refs.cross_sems.at[which, layer, zz],
                plane.over,
            )
            self.given[layer, which].append(number)
            self.moments.append((layer, which, step))

    def tick(self, times=1):
        for _ in range(times):
            if self.moments:
                moment = self.moments.pop(0)
                if moment is not None:
                    self.add(*moment)
                    self.left[moment[:2]] -= 1

    def require(self, layer, which):
        while self.left[layer, which]:
            self.tick()
        self.sends.wait(*self.given[layer, which])

    def add(self, layer, which, step):
        plane, refs = (self.plane, self.refs)
        members = 2 * plane.levels
        here = plane.core == layer
        target = piece_of_shard(which, self.shards[which], plane.member, members)
        zz = lax.rem(plane.z + step, plane.levels)
        held = self.landed[which].at[layer, zz]
        await_block(held, refs.cross_sems.at[which, layer, zz], plane.over)
        own = piece_of_slice(which, self.slices[which], zz * 2 + plane.x, members)
        held[...] = (held[...].astype(WIDE) + own[...].astype(WIDE)).astype(LOW)
        self.sends.start(
            True if step else jnp.logical_not(here),
            held,
            target,
            refs.column_sems.at[which, plane.core, plane.z],
            device(layer, zz, plane.x, plane.y),
        )
        if step == 0:
            self.copies.start(held, target, here)

    def finish(self):
        while self.moments:
            self.tick()
        plane, refs = (self.plane, self.refs)
        members = 2 * plane.levels
        for which in range(4):
            for core in (0, 1):
                for step in range(plane.levels):
                    zz = lax.rem(plane.z + step, plane.levels)
                    held = piece_of_shard(which, self.shards[which], zz * 2 + core, members)
                    guarded(
                        True if step else plane.core != core,
                        partial(
                            await_block, held, refs.column_sems.at[which, core, zz], plane.over
                        ),
                    )


class Outward:
    @staticmethod
    def count():
        return 6, 2

    def __init__(self, plane, target, sems):
        self.plane, self.target, self.sems = (plane, target, sems)

    def give(self, layer, source, sends, copies):
        plane, target = (self.plane, self.target.at[self.plane.x])
        same_core, same_x = (plane.core == layer, plane.core == plane.x)
        other_core, other_x = (plane.core != layer, plane.core != plane.x)
        for present, partner in (
            (same_core & other_x, plane.over),
            (other_core & same_x, plane.sibling),
            (other_core & other_x, plane.corner),
        ):
            sends.start(present, source, target, self.sems.at[plane.x], partner)
        copies.start(source, target, same_core & same_x)

    def finish(self):
        plane = self.plane
        for slot in (0, 1):
            away = jnp.logical_not((plane.core == plane.x) & (plane.x == slot))
            guarded(away, partial(await_block, self.target.at[slot], self.sems.at[slot], plane.over))


def launch(name, ident, kernel, counts, inputs, outputs, scratch):
    scratch = dict(
        scratch,
        send_sems=DMAS((counts[0],)),
        phase_sems=DMAS((counts[1],)),
        copy_sems=DMAS((counts[2],)),
    )
    names = list(inputs) + list(outputs) + list(scratch)

    def body(*refs):
        held = SimpleNamespace(**dict(zip(names, refs)))
        plane = Plane()
        barrier = pltpu.get_barrier_semaphore()
        partners = plane.partners()
        for partner in partners:
            pl.semaphore_signal(barrier, inc=1, device_id=partner, device_id_type=MESH)
        sends, copies = (Sends(held.send_sems), Copies(held.copy_sems))
        kernel(held, plane, lambda: pl.semaphore_wait(barrier, len(partners)), sends, copies)
        copies.finish()
        sends.finish()
        assert len(sends.pending) == counts[0], len(sends.pending)
        assert len(copies.pending) == counts[2], len(copies.pending)

    results = pl.pallas_call(
        body,
        out_shape=[jax.ShapeDtypeStruct(shape, dtype) for shape, dtype, _ in outputs.values()],
        in_specs=[pl.BlockSpec(memory_space=space) for _, space in inputs.values()],
        out_specs=[pl.BlockSpec(memory_space=space) for _, _, space in outputs.values()],
        scratch_shapes=list(scratch.values()),
        compiler_params=pltpu.CompilerParams(
            collective_id=ident, has_side_effects=True, vmem_limit_bytes=60 << 20
        ),
        name=name,
    )(*[array for array, _ in inputs.values()])
    return SimpleNamespace(**dict(zip(outputs, results)))


CHUNKS, SUM_CHUNKS, CUT = (2, 2, 512)
NORM_LINES, HEAD_LINES, LINES = (6, 8, 16)


def unpack_vectors(refs, plane, levels):
    members, blocks = (2 * levels, 4 * levels)
    for layer in (0, 1):
        for z in range(levels):
            for x in (0, 1):
                for y in (0, 1):
                    start = ((z * 4 + layer * 2 + y) * 2 + x) * LINES
                    cut = (z * 4 + x * 2 + y) * HD
                    refs.norms[layer, :, cut : cut + HD] = refs.small[
                        start : start + LINES
                    ].astype(WIDE)[:HEAD_LINES]
    lines = []
    for layer in (0, 1):
        pieces = []
        for z in range(levels):
            for x in (0, 1):
                number = (z * 4 + layer * 2 + plane.y) * 2 + x
                pieces.append(refs.small[span(number, LINES)].astype(WIDE)[HEAD_LINES:])
        lines.append(jnp.concatenate(pieces, axis=1))
    lines = jnp.concatenate(lines, axis=0).astype(LOW)
    width = HD // members
    place = lax.broadcasted_iota(jnp.int32, (members * HD, HD), 0)
    lane = lax.broadcasted_iota(jnp.int32, (members * HD, HD), 1)

    def pick(first):
        chosen = (place // HD == lane // width) & (place % HD == lane % width + first)
        return dot(lines, chosen.astype(WIDE).astype(LOW))

    heads = pick(plane.member * width)
    units = refs.b_up.shape[2] // HD
    per_line = HD // (units * width)
    row = lax.broadcasted_iota(jnp.int32, (HEAD_LINES, HD), 0)
    for layer in (0, 1):
        refs.b_qv[layer] = heads[layer * HEAD_LINES : layer * HEAD_LINES + 2]
    for unit in range(units):
        found = pick((lax.rem(plane.member, per_line) * units + unit) * width)
        for layer in (0, 1):
            own = found[layer * HEAD_LINES : (layer + 1) * HEAD_LINES]
            own = jnp.where(row == 2 + plane.member // per_line, own, 0.0)
            refs.b_up[layer, :, unit * HD : (unit + 1) * HD] = jnp.sum(own, axis=0, keepdims=True)


def visible(refs, group, size, tokens):
    segment = refs.query_segment[group]
    place = group.start + lax.broadcasted_iota(jnp.int32, (size, tokens), 0)
    keys = lax.broadcasted_iota(jnp.int32, (size, tokens), 1)
    return (segment == refs.key_segment[...]) & (keys <= place)


def forward_planes(ident, boundary, packed, segments, shards):
    levels = lax.axis_size("dp") // 2
    blocks, members = (4 * levels, 2 * levels)
    rows, width = boundary.shape[1:]
    tokens, size = (blocks * rows, 4 * rows)
    slice_shapes = [
        slice_shape(which, shard.shape, members) for which, shard in enumerate(shards)
    ]
    units = slice_shapes[2][1]
    scaling = HD ** (-0.5)

    def kernel(refs, plane, greet, sends, copies):
        core, x = (plane.core, plane.x)
        own_block = span(plane.block, rows)
        refs.slices_out = [refs.out0, refs.out1, refs.out2, refs.out3]
        slices = [refs.w0, refs.w1, refs.w2, refs.w3]
        fetch = Fetch(
            plane, [refs.shard0, refs.shard1, refs.shard2, refs.shard3], slices, refs, sends, copies
        )
        small_block = span(plane.block * 2 + x, LINES)
        refs.small[small_block] = refs.packed[...]
        greet()
        phase = Sends(refs.phase_sems)
        own_small = refs.small.at[small_block]
        phase.start(True, own_small, own_small, refs.pair_sem.at[0], plane.over)
        inward = []
        for slot in (0, 1):
            source, target = (refs.boundary.at[slot], refs.landed_planes.at[core])
            arrived = refs.inward_sems.at[core]
            for present, partner in (
                ((x == core) & (slot != x), plane.over),
                ((x != core) & (slot == x), plane.sibling),
                ((x != core) & (slot != x), plane.corner),
            ):
                phase.start(present, source, target, arrived, partner)
            inward.append(copies.start(source, target, (x == core) & (slot == x)))
        fetch.tick(levels)
        other_small = refs.small.at[span(plane.block * 2 + 1 - x, LINES)]
        await_block(other_small, refs.pair_sem.at[0], plane.over)
        small = Gather(plane, phase, refs.small, refs.small_sems)
        small.open()
        small.run(lambda step, zz: None, lambda: None)
        for slot in (0, 1):
            here = (core == x) & (core == slot)
            guarded(
                jnp.logical_not(here),
                partial(await_block, refs.landed_planes.at[slot], refs.inward_sems.at[slot], plane.over),
            )
        copies.wait(*inward)
        refs.planes[...] = refs.landed_planes[...]
        refs.rows[0, own_block] = refs.landed_planes[1]
        gather = Gather(plane, phase, refs.rows.at[0], refs.gather_sems.at[0])
        gather.open()
        unpack_vectors(refs, plane, levels)
        kept = []

        def keep(step, zz):
            group = span(zz, size)
            kept.append(copies.start(refs.rows.at[0, group], refs.gathered.at[group]))

        gather.run(keep, fetch.tick)
        copies.wait(*kept)
        phase.finish()

        for layer in (0, 1):
            number = 1 + 2 * layer
            norms = refs.norms.at[layer]
            held, sems = (refs.rows.at[number % 2], refs.gather_sems.at[number % 2])
            entering = refs.planes[0] if layer == 0 else refs.leaving[0]
            hidden = entering.astype(WIDE)
            normed, _, _ = layer_norm(hidden, norms[0:1], norms[2:3])
            held[own_block] = normed.astype(LOW)
            phase = Sends(refs.phase_sems)
            gather = Gather(plane, phase, held, sems)
            gather.open()
            fetch.require(3 * layer)
            kept = []

            def project(step, zz):
                group = span(zz, size)
                projected = dot(held[group], refs.w0[layer])
                refs.queries[layer, group] = (projected[:, :HD] + refs.b_qv[layer, 0:1]).astype(LOW)
                refs.keys[layer, group] = projected[:, HD : 2 * HD].astype(LOW)
                refs.values[layer, group] = (
                    projected[:, 2 * HD :] + refs.b_qv[layer, 1:2]
                ).astype(LOW)
                kept.append(copies.start(held.at[group], refs.rows_a.at[layer, group]))

            gather.run(project, fetch.tick)

            def attend(step, zz):
                group = span(zz, size)
                allowed = visible(refs, group, size, tokens)
                scores = dot_back(refs.queries[layer, group], refs.keys[layer]) * scaling
                scores = jnp.where(allowed, scores, NEG_FILL)
                top = jnp.max(scores, axis=-1, keepdims=True)
                raised = jnp.exp(scores - top)
                total = jnp.sum(raised, axis=-1, keepdims=True)
                refs.log_total[layer, group] = top + jnp.log(total)
                probs = (raised / total).astype(LOW)
                live = (refs.query_segment[group] >= 0).astype(WIDE)
                mixed = (dot(probs, refs.values[layer]) * live).astype(LOW)
                refs.mixed[layer, group] = mixed
                for cut in range(0, width, CUT):
                    refs.part[group, cut : cut + CUT] = dot(
                        mixed, refs.w1[layer, :, cut : cut + CUT]
                    ).astype(LOW)

            Scatter(plane, phase, refs, refs.sum).run(attend, fetch.tick)
            middle = hidden + refs.sum[...] + norms[3:4]
            refs.middle[layer] = middle
            copies.wait(*kept)
            phase.finish()

            number = number + 1
            held, sems = (refs.rows.at[number % 2], refs.gather_sems.at[number % 2])
            normed, _, _ = layer_norm(middle, norms[1:2], norms[4:5])
            held[own_block] = normed.astype(LOW)
            phase = Sends(refs.phase_sems)
            gather = Gather(plane, phase, held, sems)
            gather.open()
            fetch.require(3 * layer + 1)
            kept = []

            def expand(step, zz):
                group = span(zz, size)
                preact = dot(held[group], refs.w2[layer]) + refs.b_up[layer]
                refs.own_preact[layer, group] = preact
                refs.own_activated[layer, group] = (
                    0.5 * preact * (1.0 + lax.erf(preact * math.sqrt(0.5)))
                ).astype(LOW)
                for own, out in (
                    (held.at[group], refs.rows_b),
                    (refs.own_preact.at[layer, group], refs.preact),
                    (refs.own_activated.at[layer, group], refs.activated),
                ):
                    kept.append(copies.start(own, out.at[layer, group]))

            gather.run(expand, fetch.tick)
            fetch.require(3 * layer + 2)

            def shrink(step, zz):
                group = span(zz, size)
                for cut in range(0, width, CUT):
                    refs.part[group, cut : cut + CUT] = dot(
                        refs.own_activated[layer, group], refs.w3[layer, :, cut : cut + CUT]
                    ).astype(LOW)

            Scatter(plane, phase, refs, refs.sum).run(shrink, fetch.tick)
            refs.leaving[layer] = (refs.middle[layer] + refs.sum[...] + norms[5:6]).astype(LOW)
            copies.wait(*kept)
            phase.finish()

    head = ((2, tokens, HD), LOW, VMEM)
    gathers = Gather.count(levels, CHUNKS)
    lasting = Fetch.count(levels)
    return launch(
        "forward_planes",
        ident,
        kernel,
        (
            lasting[0],
            max(gathers + Scatter.count(levels, SUM_CHUNKS), 7 + Gather.count(levels, 1) + gathers),
            lasting[1] + 2 + levels + 2 * 4 * levels,
        ),
        dict(
            boundary=(boundary, HBM),
            packed=(packed, VMEM),
            query_segment=(segments[0], VMEM),
            key_segment=(segments[1], VMEM),
            shard0=(shards[0], HBM),
            shard1=(shards[1], HBM),
            shard2=(shards[2], HBM),
            shard3=(shards[3], HBM),
        ),
        dict(
            planes=((2, rows, width), LOW, VMEM),
            leaving=((2, rows, width), LOW, VMEM),
            middle=((2, rows, width), WIDE, VMEM),
            norms=((2, HEAD_LINES, width), WIDE, VMEM),
            queries=head,
            keys=head,
            values=head,
            mixed=head,
            log_total=((2, tokens, 1), WIDE, VMEM),
            gathered=((tokens, width), LOW, HBM),
            rows_a=((2, tokens, width), LOW, HBM),
            rows_b=((2, tokens, width), LOW, HBM),
            preact=((2, tokens, units), WIDE, HBM),
            activated=((2, tokens, units), LOW, HBM),
            out0=((2,) + slice_shapes[0], LOW, HBM),
            out1=((2,) + slice_shapes[1], LOW, HBM),
            out2=((2,) + slice_shapes[2], LOW, HBM),
            out3=((2,) + slice_shapes[3], LOW, HBM),
        ),
        dict(
            scatter_scratch(rows, width, levels, SUM_CHUNKS),
            rows=VMEM((2, tokens, width), LOW),
            gather_sems=DMAS((2, blocks, CHUNKS)),
            small=VMEM((2 * blocks * LINES, HD), LOW),
            small_sems=DMAS((blocks, 1)),
            pair_sem=DMAS((1,)),
            inward_sems=DMAS((2,)),
            landed_planes=VMEM((2, rows, width), LOW),
            b_qv=VMEM((2, 2, HD), WIDE),
            b_up=VMEM((2, 1, units), WIDE),
            w0=VMEM((2,) + slice_shapes[0], LOW),
            w1=VMEM((2,) + slice_shapes[1], LOW),
            w2=VMEM((2,) + slice_shapes[2], LOW),
            w3=VMEM((2,) + slice_shapes[3], LOW),
            own_preact=VMEM((2, tokens, units), WIDE),
            own_activated=VMEM((2, tokens, units), LOW),
            column_sems=DMAS((4, 2, levels)),
            cross_sems=DMAS((4, 2, levels)),
        ),
    )


def backward_planes(ident, kept, segments):
    levels = lax.axis_size("dp") // 2
    blocks, members = (4 * levels, 2 * levels)
    rows, width = kept.planes.shape[1:]
    tokens, size = (blocks * rows, 4 * rows)
    slice_shapes = [array.shape[1:] for array in (kept.out0, kept.out1, kept.out2, kept.out3)]
    shard_shapes = [shard_shape(which, shape, members) for which, shape in enumerate(slice_shapes)]
    units = slice_shapes[2][1]
    unit_lines = units // HD
    scaling = HD ** (-0.5)
    vector_lines = (2 + members) * HEAD_LINES

    def landing(which):
        shape = slice_shapes[which]
        if by_rows(which):
            return VMEM((2, levels, shape[0], shape[1] // members), LOW)
        return VMEM((2, levels, shape[0] // members, shape[1]), LOW)

    def kernel(refs, plane, greet, sends, copies):
        own_block = span(plane.block, rows)
        back = Return(
            plane,
            [refs.grad0, refs.grad1, refs.grad2, refs.grad3],
            [refs.landed0, refs.landed1, refs.landed2, refs.landed3],
            [refs.shard0, refs.shard1, refs.shard2, refs.shard3],
            refs,
            sends,
            copies,
        )
        acts = Outward(plane, refs.acts, refs.acts_sems)
        ends = Outward(plane, refs.input_grads, refs.ends_sems)

        def load(layer):
            return [
                copies.start(refs.out3.at[layer], refs.w3),
                copies.start(refs.preact.at[layer], refs.own_preact),
                copies.start(refs.out2.at[layer], refs.w2),
                copies.start(refs.activated.at[layer], refs.own_activated),
                copies.start(refs.rows_b.at[layer], refs.own_rows),
                copies.start(refs.out1.at[layer], refs.w1),
                copies.start(refs.out0.at[layer], refs.w0),
                copies.start(refs.all_queries.at[layer], refs.queries),
                copies.start(refs.all_keys.at[layer], refs.keys),
                copies.start(refs.all_values.at[layer], refs.values),
                copies.start(refs.all_mixed.at[layer], refs.mixed),
                copies.start(refs.all_totals.at[layer], refs.log_total),
            ]

        loads = load(1)
        first = copies.start(refs.gathered, refs.rows.at[0])
        greet()
        acts.give(0, refs.leaving.at[0], sends, copies)
        acts.give(1, refs.leaving.at[1], sends, copies)

        for layer in (1, 0):
            number = 2 * (1 - layer)
            norms = refs.norms.at[layer]
            vectors = refs.vectors.at[layer]
            held, sems = (refs.rows.at[number % 2], refs.gather_sems.at[number % 2])
            phase = Sends(refs.phase_sems)
            low = refs.planes[1] if layer == 1 else refs.leaving_grads[1].astype(LOW)
            vectors[5:6] = jnp.sum(low.astype(WIDE), axis=0, keepdims=True)
            refs.unit_sums[layer] = jnp.zeros((1, units), WIDE)
            if layer == 0:
                held[own_block] = low
                gather = Gather(plane, phase, held, sems)
                gather.open()
            else:
                copies.wait(first)
            copies.wait(loads[0], loads[1])

            def slope(step, zz):
                group = span(zz, size)
                grad_act = dot_back(held[group], refs.w3[...])
                value = refs.own_preact[group]
                rise = 0.5 * (1.0 + lax.erf(value * math.sqrt(0.5))) + value * jnp.exp(
                    -0.5 * value * value
                ) * (1.0 / math.sqrt(2.0 * math.pi))
                grad_pre = (grad_act * rise).astype(LOW)
                refs.grad_pre[group] = grad_pre
                refs.unit_sums[layer] += jnp.sum(grad_pre.astype(WIDE), axis=0, keepdims=True)

            if layer == 0:
                gather.run(slope, back.tick)
            copies.wait(loads[2])

            def widen_units(step, zz):
                group = span(zz, size)
                if layer == 1:
                    slope(step, zz)
                for cut in range(0, width, CUT):
                    refs.part[group, cut : cut + CUT] = dot_back(
                        refs.grad_pre[group], refs.w2[cut : cut + CUT]
                    ).astype(LOW)

            def down_product(at, carry):
                cut = span(at, 128)
                refs.grad3[cut] = dot_rows(refs.own_activated[:, cut], held[...]).astype(LOW)
                return carry

            def up_product(at, carry):
                cut = span(at, 256)
                refs.grad2[cut] = dot_rows(refs.own_rows[:, cut], refs.grad_pre[...]).astype(LOW)
                return carry

            def products(at):
                if at == 0:
                    copies.wait(loads[3], loads[4])
                    if layer == 0:
                        back.require(1, 3)
                        back.require(1, 2)
                if at == 1:
                    lax.fori_loop(0, units // 128, down_product, 0)
                    back.give(layer, 3, lag=1)
                if at == 2:
                    lax.fori_loop(0, width // 512, up_product, 0)
                if at == 3:
                    lax.fori_loop(width // 512, width // 256, up_product, 0)
                    back.give(layer, 2)

            Scatter(plane, phase, refs, refs.sum).run(widen_units, back.tick, products)
            loads.append(copies.start(refs.rows_a.at[layer], refs.own_rows))
            _, unit, inverse = layer_norm(refs.middle[layer], norms[1:2], norms[1:2])
            vectors[1:2] = jnp.sum(refs.sum[...] * unit, axis=0, keepdims=True)
            vectors[4:5] = jnp.sum(refs.sum[...], axis=0, keepdims=True)
            grad_out = refs.planes[1].astype(WIDE) if layer == 1 else refs.leaving_grads[1].astype(LOW).astype(WIDE)
            grad_middle = grad_out + norm_back(refs.sum[...], unit, inverse, norms[1:2])
            phase.finish()

            number = number + 1
            held, sems = (refs.rows.at[number % 2], refs.gather_sems.at[number % 2])
            phase = Sends(refs.phase_sems)
            refs.grad_middle[...] = grad_middle
            low = grad_middle.astype(LOW)
            held[own_block] = low
            gather = Gather(plane, phase, held, sems)
            gather.open()
            vectors[3:4] = jnp.sum(low.astype(WIDE), axis=0, keepdims=True)
            refs.grad_keys[...] = jnp.zeros_like(refs.grad_keys)
            refs.grad_values[...] = jnp.zeros_like(refs.grad_values)
            copies.wait(loads[5], *loads[7:12])

            def attend(step, zz):
                group = span(zz, size)
                live = (refs.query_segment[group] >= 0).astype(WIDE)
                grad_mixed = (
                    dot_back(held[group], refs.w1[...]).astype(LOW) * live
                ).astype(LOW)
                allowed = visible(refs, group, size, tokens)
                queries = refs.queries[group]
                scores = dot_back(queries, refs.keys[...]) * scaling
                scores = jnp.where(allowed, scores, NEG_FILL)
                probs = jnp.exp(scores - refs.log_total[group])
                grad_probs = dot_back(grad_mixed, refs.values[...])
                delta = jnp.sum(probs * grad_probs, axis=-1, keepdims=True)
                grad_scores = jnp.where(allowed, probs * (grad_probs - delta), 0.0).astype(LOW)
                refs.grad_proj[group, :HD] = (dot(grad_scores, refs.keys[...]) * scaling).astype(LOW)
                refs.grad_keys[...] += dot_rows(grad_scores, queries)
                refs.grad_values[...] += dot_rows(probs.astype(LOW), grad_mixed)

            gather.run(attend, back.tick)
            refs.grad_proj[:, HD : 2 * HD] = (refs.grad_keys[...] * scaling).astype(LOW)
            refs.grad_proj[:, 2 * HD :] = refs.grad_values[...].astype(LOW)
            copies.wait(loads[6])

            def widen_heads(step, zz):
                group = span(zz, size)
                for cut in range(0, width, CUT):
                    refs.part[group, cut : cut + CUT] = dot_back(
                        refs.grad_proj[group], refs.w0[cut : cut + CUT]
                    ).astype(LOW)

            def qkv_product(at, carry):
                cut = span(at, 256)
                refs.grad0[cut] = dot_rows(refs.own_rows[:, cut], refs.grad_proj[...]).astype(LOW)
                return carry

            def more_products(at):
                if at == 0:
                    sums = jnp.sum(refs.grad_proj[...].astype(WIDE), axis=0, keepdims=True)
                    refs.head_sums[layer, 0:1] = sums[:, :HD]
                    refs.head_sums[layer, 1:2] = sums[:, 2 * HD :]
                    copies.wait(loads[12])
                    if layer == 0:
                        back.require(1, 1)
                        back.require(1, 0)
                if at == 1:
                    refs.grad1[...] = dot_rows(refs.mixed[...], held[...]).astype(LOW)
                    back.give(layer, 1, lag=layer)
                    lax.fori_loop(0, width // 1024, qkv_product, 0)
                if at == 2:
                    lax.fori_loop(width // 1024, width // 512, qkv_product, 0)
                if at == 3:
                    lax.fori_loop(width // 512, width // 256, qkv_product, 0)
                    back.give(layer, 0)

            Scatter(plane, phase, refs, refs.sum).run(widen_heads, back.tick, more_products)
            if layer == 1:
                loads = load(0)
            entering = refs.planes[0] if layer == 0 else refs.leaving[0]
            _, unit, inverse = layer_norm(entering.astype(WIDE), norms[0:1], norms[0:1])
            vectors[0:1] = jnp.sum(refs.sum[...] * unit, axis=0, keepdims=True)
            vectors[2:3] = jnp.sum(refs.sum[...], axis=0, keepdims=True)
            refs.leaving_grads[layer] = refs.grad_middle[...] + norm_back(
                refs.sum[...], unit, inverse, norms[0:1]
            )
            ends.give(layer, refs.leaving_grads.at[layer], sends, copies)
            phase.finish()

        tail = SimpleNamespace(
            part=refs.vector_part,
            from_sibling=refs.vector_from_sibling,
            from_across=refs.vector_from_across,
            from_behind=refs.vector_from_behind,
            total=refs.vector_total,
            sibling_sems=refs.vector_sibling_sems,
            across_sems=refs.vector_across_sems,
            behind_sems=refs.vector_behind_sems,
        )
        tail.part[...] = jnp.zeros_like(tail.part)
        for layer in (0, 1):
            own = [refs.head_sums[layer]]
            for at in range(unit_lines):
                own.append(refs.unit_sums[layer, :, at * HD : (at + 1) * HD])
            own.append(jnp.zeros((HEAD_LINES - 2 - unit_lines, HD), WIDE))
            own = jnp.concatenate(own, axis=0)
            for z in range(levels):
                for y in (0, 1):
                    base = (z * 4 + layer * 2 + y) * vector_lines
                    for x in (0, 1):
                        cut = (z * 4 + x * 2 + y) * HD
                        line = base + x * HEAD_LINES
                        tail.part[line : line + HEAD_LINES] = refs.vectors[layer, :, cut : cut + HD]
                start = (z * 4 + layer * 2 + plane.y) * vector_lines
                start = start + (2 + plane.member) * HEAD_LINES
                tail.part[pl.ds(pl.multiple_of(start, HEAD_LINES), HEAD_LINES)] = own
        phase = Sends(refs.phase_sems)
        Scatter(plane, phase, tail, refs.vector_sum).run(lambda step, zz: None, back.tick)
        phase.start(True, refs.vector_sum, refs.vector_other, refs.pair_sem.at[0], plane.over)
        await_block(refs.vector_other, refs.pair_sem.at[0], plane.over)
        refs.vector_out[...] = refs.vector_sum[...] + refs.vector_other[...]
        acts.finish()
        back.finish()
        ends.finish()
        phase.finish()

    lasting = Return.count(levels)
    outward = Outward.count()
    vector = scatter_scratch(vector_lines, HD, levels, 1, WIDE)
    return launch(
        "backward_planes",
        ident,
        kernel,
        (
            lasting[0] + 2 * outward[0],
            Gather.count(levels, CHUNKS) + Scatter.count(levels, SUM_CHUNKS),
            lasting[1] + 2 * outward[1] + 2 * 13 + 1,
        ),
        dict(
            planes=(kept.planes, VMEM),
            leaving=(kept.leaving, VMEM),
            middle=(kept.middle, VMEM),
            norms=(kept.norms, VMEM),
            query_segment=(segments[0], VMEM),
            key_segment=(segments[1], VMEM),
            all_queries=(kept.queries, HBM),
            all_keys=(kept.keys, HBM),
            all_values=(kept.values, HBM),
            all_mixed=(kept.mixed, HBM),
            all_totals=(kept.log_total, HBM),
            gathered=(kept.gathered, HBM),
            rows_a=(kept.rows_a, HBM),
            rows_b=(kept.rows_b, HBM),
            preact=(kept.preact, HBM),
            activated=(kept.activated, HBM),
            out0=(kept.out0, HBM),
            out1=(kept.out1, HBM),
            out2=(kept.out2, HBM),
            out3=(kept.out3, HBM),
        ),
        dict(
            acts=((2, rows, width), LOW, HBM),
            input_grads=((2, rows, width), WIDE, HBM),
            shard0=(shard_shapes[0], LOW, HBM),
            shard1=(shard_shapes[1], LOW, HBM),
            shard2=(shard_shapes[2], LOW, HBM),
            shard3=(shard_shapes[3], LOW, HBM),
            vector_out=((vector_lines, HD), WIDE, VMEM),
        ),
        dict(
            scatter_scratch(rows, width, levels, SUM_CHUNKS),
            rows=VMEM((2, tokens, width), LOW),
            gather_sems=DMAS((2, blocks, CHUNKS)),
            w0=VMEM(slice_shapes[0], LOW),
            w1=VMEM(slice_shapes[1], LOW),
            w2=VMEM(slice_shapes[2], LOW),
            w3=VMEM(slice_shapes[3], LOW),
            own_preact=VMEM((tokens, units), WIDE),
            own_activated=VMEM((tokens, units), LOW),
            own_rows=VMEM((tokens, width), LOW),
            grad_pre=VMEM((tokens, units), LOW),
            grad_proj=VMEM((tokens, 3 * HD), LOW),
            queries=VMEM((tokens, HD), LOW),
            keys=VMEM((tokens, HD), LOW),
            values=VMEM((tokens, HD), LOW),
            mixed=VMEM((tokens, HD), LOW),
            log_total=VMEM((tokens, 1), WIDE),
            grad_keys=VMEM((tokens, HD), WIDE),
            grad_values=VMEM((tokens, HD), WIDE),
            grad_middle=VMEM((rows, width), WIDE),
            leaving_grads=VMEM((2, rows, width), WIDE),
            grad0=VMEM(slice_shapes[0], LOW),
            grad1=VMEM(slice_shapes[1], LOW),
            grad2=VMEM(slice_shapes[2], LOW),
            grad3=VMEM(slice_shapes[3], LOW),
            landed0=landing(0),
            landed1=landing(1),
            landed2=landing(2),
            landed3=landing(3),
            column_sems=DMAS((4, 2, levels)),
            cross_sems=DMAS((4, 2, levels)),
            acts_sems=DMAS((2,)),
            ends_sems=DMAS((2,)),
            pair_sem=DMAS((1,)),
            vectors=VMEM((2, HEAD_LINES, width), WIDE),
            head_sums=VMEM((2, 2, HD), WIDE),
            unit_sums=VMEM((2, 1, units), WIDE),
            vector_part=vector["part"],
            vector_from_sibling=vector["from_sibling"],
            vector_from_across=vector["from_across"],
            vector_from_behind=vector["from_behind"],
            vector_total=vector["total"],
            vector_sum=vector["sum"],
            vector_other=VMEM((vector_lines, HD), WIDE),
            vector_sibling_sems=vector["sibling_sems"],
            vector_across_sems=vector["across_sems"],
            vector_behind_sems=vector["behind_sems"],
        ),
    )


def plane_body(
    boundary,
    doc_lengths,
    qkv_weight,
    qv_bias,
    out_weight,
    up_weight,
    up_bias,
    down_weight,
    norm_gains,
    norm_biases,
):
    plane = Plane()
    levels = plane.levels
    members = 2 * levels
    head_cut = qv_bias.shape[3]
    block_shard = up_bias.shape[1]
    own_blocks = block_shard // members

    def lines(piece):
        return piece.reshape(-1, HD)

    packed = jnp.concatenate(
        (
            lines(norm_gains[0]),
            lines(norm_biases[0]),
            jnp.zeros((HEAD_LINES - NORM_LINES, HD), LOW),
            lines(qv_bias[0]),
            lines(up_bias[0]),
            jnp.zeros((LINES - HEAD_LINES - 2 - up_bias[0].size // HD, HD), LOW),
        )
    )
    depth = qkv_weight.shape[1]
    by_head = (
        qkv_weight[0]
        .reshape(depth, 3, members, HD)
        .transpose(0, 2, 1, 3)
        .reshape(depth, members * 3 * HD)
    )
    lengths = lax.dynamic_index_in_dim(doc_lengths, plane.x, 0, keepdims=False)
    tokens = boundary.shape[2] * 4 * levels
    _, segment, live, _, _, _ = visibility(lengths, 0, tokens, tokens)
    segments = (jnp.where(live, segment, -1)[:, None], segment[None, :])

    kept = forward_planes(
        0, boundary[0], packed, segments, (by_head, out_weight[0], up_weight[0], down_weight[0])
    )
    end = backward_planes(1, kept, segments)

    summed = end.vector_out.reshape(2 + members, HEAD_LINES, HD)
    norms = lax.dynamic_index_in_dim(summed, plane.x, 0, keepdims=False)
    by_member = lax.dynamic_slice_in_dim(
        summed[2:], (plane.z * 2 + plane.x) * head_cut, head_cut, axis=2
    )
    qkv_shard = (
        end.shard0.reshape(depth, members, 3, HD)
        .transpose(0, 2, 1, 3)
        .reshape(depth, 3, members * HD)
    )
    return (
        end.acts[None],
        end.input_grads[None],
        qkv_shard.astype(WIDE)[None],
        by_member[:, :2].transpose(1, 0, 2)[None],
        end.shard1.astype(WIDE)[None],
        end.shard2.astype(WIDE)[None],
        by_member[:, 2 : 2 + own_blocks].reshape(1, block_shard, head_cut),
        end.shard3.astype(WIDE)[None],
        norms[None, :2],
        norms[None, 2:NORM_LINES],
    )


def fits_plane(mesh):
    return mesh.shape["dp"] == 8 and mesh.shape["tensor"] == 2 and mesh.shape["section"] == 2


def solution(mesh):
    placed = (
        P("section", None, ("dp", "tensor"), None),
        P(),
        P("section", "dp", None, "tensor"),
        P("section", None, "tensor", "dp"),
        P("section", "tensor", "dp"),
        P("section", "dp", "tensor"),
        P("section", "tensor", "dp"),
        P("section", "tensor", "dp"),
        P("section", None, ("dp", "tensor")),
        P("section", None, ("dp", "tensor")),
    )
    return jax.shard_map(
        plane_body if fits_plane(mesh) else body,
        mesh=mesh,
        in_specs=placed,
        out_specs=(
            P("section", None, ("dp", "tensor"), None),
            P("section", None, ("dp", "tensor"), None),
            P("section", "dp", None, "tensor"),
            P("section", None, "tensor", "dp"),
            P("section", "tensor", "dp"),
            P("section", "dp", "tensor"),
            P("section", "tensor", "dp"),
            P("section", "tensor", "dp"),
            P("section", None, ("dp", "tensor")),
            P("section", None, ("dp", "tensor")),
        ),
        check_vma=False,
    )
```

```python
from functools import partial
import math
from types import SimpleNamespace

import jax
import jax.numpy as jnp
from jax import lax
from jax.experimental import pallas as pl
from jax.experimental.pallas import tpu as pltpu
from jax.sharding import PartitionSpec as P

HD = 128


EPSILON = 1e-05
NEG_FILL = -1e30
MESH = pl.DeviceIdType.MESH


def from_behind(value, axis, steps):
    count = lax.axis_size(axis)
    first, last = (max(0, -steps), min(count, count - steps))
    return lax.ppermute(value, axis, [(source, source + steps) for source in range(first, last)])


def layer_norm(hidden, gain, shift):
    average = jnp.mean(hidden, axis=-1, keepdims=True)
    centred = hidden - average
    variance = jnp.mean(centred * centred, axis=-1, keepdims=True)
    inverse = lax.rsqrt(variance + EPSILON)
    normed = centred * inverse
    return (normed * gain + shift, normed, inverse)


def norm_back(grad_out, normed, inverse, gain):
    scaled = grad_out * gain
    return inverse * (
        scaled
        - jnp.mean(scaled, axis=-1, keepdims=True)
        - normed * jnp.mean(scaled * normed, axis=-1, keepdims=True)
    )


def visibility(lengths, dp_index, rows_dp, seq_len):
    per_seq = seq_len // lengths.shape[0]
    docs = lengths.shape[1]
    key_pos = jnp.arange(seq_len, dtype=jnp.int32)
    seq_of = key_pos // per_seq
    local = key_pos - seq_of * per_seq
    doc_ends = jnp.cumsum(lengths, axis=1)
    ends_row = jnp.take(doc_ends, seq_of, axis=0)
    key_seg = seq_of * (docs + 1) + jnp.sum((local[:, None] >= ends_row).astype(jnp.int32), axis=1)
    key_live = local < ends_row[:, docs - 1]
    start_row = dp_index * rows_dp
    query_pos = start_row + jnp.arange(rows_dp, dtype=jnp.int32)
    query_seg = lax.dynamic_slice_in_dim(key_seg, start_row, rows_dp)
    query_live = lax.dynamic_slice_in_dim(key_live, start_row, rows_dp)
    return (query_pos, query_seg, query_live, key_pos, key_seg, key_live)


def widen(rows_low):
    return lax.all_gather(rows_low, "tensor", axis=0, tiled=True)


def narrow(partial_rows):
    return lax.psum_scatter(
        partial_rows.astype(jnp.bfloat16), "tensor", scatter_dimension=0, tiled=True
    ).astype(jnp.float32)


def fetch_weights(
    qkv_weight, qv_bias, out_weight, up_weight, up_bias, down_weight, norm_gains, norm_biases
):
    w_qkv, b_qv, w_out, w_up, b_up, w_down = (
        lax.all_gather(qkv_weight[0], "dp", axis=0, tiled=True),
        lax.all_gather(qv_bias[0], "dp", axis=2, tiled=True),
        lax.all_gather(out_weight[0], "dp", axis=1, tiled=True),
        lax.all_gather(up_weight[0], "dp", axis=0, tiled=True),
        lax.all_gather(up_bias[0], "dp", axis=1, tiled=True),
        lax.all_gather(down_weight[0], "dp", axis=1, tiled=True),
    )
    gain_rows, bias_rows = (
        lax.all_gather(norm_gains[0], ("dp", "tensor"), axis=1, tiled=True),
        lax.all_gather(norm_biases[0], ("dp", "tensor"), axis=1, tiled=True),
    )
    return (
        w_qkv,
        b_qv.reshape(2, -1).astype(jnp.float32),
        w_out,
        w_up,
        b_up.reshape(-1).astype(jnp.float32),
        w_down,
        gain_rows.astype(jnp.float32),
        bias_rows.astype(jnp.float32),
    )


def block_scores(q_heads, key_block, kpos_block, kseg_block, sight):
    scores = jnp.einsum(
        "qhd,khd->hqk", q_heads, key_block, preferred_element_type=jnp.float32
    ) * HD ** (-0.5)
    allowed = (
        (sight[1][:, None] == kseg_block[None, :])
        & (kpos_block[None, :] <= sight[0][:, None])
        & sight[2][:, None]
    )
    return (jnp.where(allowed[None], scores, NEG_FILL), allowed)


def key_blocks(keys, values, sight):
    seq_len = keys.shape[0]
    block_rows = math.gcd(seq_len, 512)
    blocks = seq_len // block_rows
    heads = keys.shape[1] // HD
    return (
        keys.reshape(blocks, block_rows, heads, HD),
        values.reshape(blocks, block_rows, heads, HD),
        sight[3].reshape(blocks, block_rows),
        sight[4].reshape(blocks, block_rows),
    )


def attend(queries, keys, values, sight):
    rows = queries.shape[0]
    heads = queries.shape[1] // HD
    q_heads = queries.reshape(rows, heads, HD)
    stacked = key_blocks(keys, values, sight)

    def find_scale(carry, pieces):
        top, total = carry
        scores, allowed = block_scores(q_heads, pieces[0], pieces[2], pieces[3], sight)
        new_top = jnp.maximum(top, jnp.max(scores, axis=-1))
        total = total * jnp.exp(top - new_top) + jnp.sum(
            jnp.exp(scores - new_top[..., None]), axis=-1
        )
        return ((new_top, total), None)

    start = (jnp.full((heads, rows), -jnp.inf, jnp.float32), jnp.zeros((heads, rows), jnp.float32))
    (top, total), ignored = lax.scan(find_scale, start, stacked)
    log_total = top + jnp.log(total)

    def weigh(carry, pieces):
        scores, allowed = block_scores(q_heads, pieces[0], pieces[2], pieces[3], sight)
        probs = jnp.exp(scores - log_total[..., None]).astype(jnp.bfloat16)
        return (
            carry
            + jnp.einsum("hqk,khd->qhd", probs, pieces[1], preferred_element_type=jnp.float32),
            None,
        )

    heads_out, ignored = lax.scan(weigh, jnp.zeros((rows, heads, HD), jnp.float32), stacked)
    return (heads_out, log_total, q_heads)


def attend_back(q_heads, keys, values, sight, log_total, grad_heads, delta):
    seq_len = keys.shape[0]
    stacked = key_blocks(keys, values, sight)
    scaling = HD ** (-0.5)

    def one_step(grad_q, pieces):
        scores, allowed = block_scores(q_heads, pieces[0], pieces[2], pieces[3], sight)
        probs = jnp.exp(scores - log_total[..., None])
        grad_p = jnp.einsum(
            "qhd,khd->hqk", grad_heads, pieces[1], preferred_element_type=jnp.float32
        )
        grad_s = jnp.where(allowed[None], probs * (grad_p - delta[..., None]), 0.0).astype(
            jnp.bfloat16
        )
        grad_q = (
            grad_q
            + jnp.einsum("hqk,khd->qhd", grad_s, pieces[0], preferred_element_type=jnp.float32)
            * scaling
        )
        grad_v = jnp.einsum(
            "hqk,qhd->khd",
            probs.astype(jnp.bfloat16),
            grad_heads,
            preferred_element_type=jnp.float32,
        )
        grad_k = (
            jnp.einsum("hqk,qhd->khd", grad_s, q_heads, preferred_element_type=jnp.float32)
            * scaling
        )
        return (grad_q, (grad_k, grad_v))

    grad_q, outputs = lax.scan(one_step, jnp.zeros(q_heads.shape, jnp.float32), stacked)
    return (grad_q, outputs[0].reshape(seq_len, -1), outputs[1].reshape(seq_len, -1))


def forward(entering, weights, sight):
    w_qkv, b_qv, w_out, w_up, b_up, w_down, gain_rows, bias_rows = weights
    hidden = entering.astype(jnp.float32)
    normed_a, unit_a, inverse_a = layer_norm(hidden, gain_rows[0], bias_rows[0])
    rows_a = widen(normed_a.astype(jnp.bfloat16))
    projected = jnp.einsum("rd,djh->rjh", rows_a, w_qkv, preferred_element_type=jnp.float32)
    queries = (projected[:, 0] + b_qv[0]).astype(jnp.bfloat16)
    keys_own = projected[:, 1].astype(jnp.bfloat16)
    values_own = (projected[:, 2] + b_qv[1]).astype(jnp.bfloat16)
    keys, values = (
        lax.all_gather(keys_own, "dp", axis=0, tiled=True),
        lax.all_gather(values_own, "dp", axis=0, tiled=True),
    )
    heads_out, log_total, q_heads = attend(queries, keys, values, sight)
    live_rows = sight[2].astype(jnp.float32)
    mixed_low = (heads_out.reshape(heads_out.shape[0], -1) * live_rows[:, None]).astype(
        jnp.bfloat16
    )
    middle = (
        hidden
        + narrow(jnp.dot(mixed_low, w_out, preferred_element_type=jnp.float32))
        + bias_rows[1]
    )
    normed_b, unit_b, inverse_b = layer_norm(middle, gain_rows[1], bias_rows[2])
    rows_b = widen(normed_b.astype(jnp.bfloat16))
    preact = jnp.dot(rows_b, w_up, preferred_element_type=jnp.float32) + b_up
    activated = jax.nn.gelu(preact, approximate=False).astype(jnp.bfloat16)
    result = (
        middle
        + narrow(jnp.dot(activated, w_down, preferred_element_type=jnp.float32))
        + bias_rows[3]
    )
    saved = (
        unit_a,
        inverse_a,
        rows_a,
        q_heads,
        keys,
        values,
        heads_out,
        log_total,
        mixed_low,
        unit_b,
        inverse_b,
        rows_b,
        preact,
        activated,
    )
    return (result, saved)


def backward(saved, grad_out, weights, sight):
    w_qkv, b_qv, w_out, w_up, b_up, w_down, gain_rows, bias_rows = weights
    (
        unit_a,
        inverse_a,
        rows_a,
        q_heads,
        keys,
        values,
        heads_out,
        log_total,
        mixed_low,
        unit_b,
        inverse_b,
        rows_b,
        preact,
        activated,
    ) = saved
    rows = rows_a.shape[0]
    grad_branch = grad_out.astype(jnp.bfloat16)
    down_bias_grad = jnp.sum(grad_branch.astype(jnp.float32), axis=0)
    wide_branch = widen(grad_branch)
    grad_act = jnp.einsum("rd,fd->rf", wide_branch, w_down, preferred_element_type=jnp.float32)
    ignored, gelu_pull = jax.vjp(partial(jax.nn.gelu, approximate=False), preact)
    grad_pre = gelu_pull(grad_act)[0].astype(jnp.bfloat16)
    up_bias_grad = jnp.sum(grad_pre.astype(jnp.float32), axis=0)
    grad_normed_b = narrow(
        jnp.einsum("rf,df->rd", grad_pre, w_up, preferred_element_type=jnp.float32)
    )
    gain_b_grad = jnp.sum(grad_normed_b * unit_b, axis=0)
    shift_b_grad = jnp.sum(grad_normed_b, axis=0)
    grad_middle = grad_out + norm_back(grad_normed_b, unit_b, inverse_b, gain_rows[1])
    grad_attn = grad_middle.astype(jnp.bfloat16)
    out_bias_grad = jnp.sum(grad_attn.astype(jnp.float32), axis=0)
    wide_attn = widen(grad_attn)
    live_rows = sight[2].astype(jnp.bfloat16)
    grad_flat = (
        jnp.einsum("rd,ed->re", wide_attn, w_out, preferred_element_type=jnp.float32).astype(
            jnp.bfloat16
        )
        * live_rows[:, None]
    )
    grad_heads = grad_flat.reshape(heads_out.shape)
    delta = jnp.einsum("qhd,qhd->hq", grad_heads.astype(jnp.float32), heads_out)
    grad_q, grad_k_all, grad_v_all = attend_back(
        q_heads, keys, values, sight, log_total, grad_heads, delta
    )
    grad_k, grad_v = (
        lax.psum_scatter(
            grad_k_all.astype(jnp.bfloat16), "dp", scatter_dimension=0, tiled=True
        ).astype(jnp.float32),
        lax.psum_scatter(
            grad_v_all.astype(jnp.bfloat16), "dp", scatter_dimension=0, tiled=True
        ).astype(jnp.float32),
    )
    grad_proj = jnp.stack((grad_q.reshape(rows, -1), grad_k, grad_v), axis=1).astype(jnp.bfloat16)
    proj_sums = jnp.sum(grad_proj.astype(jnp.float32), axis=0)
    qv_grad = jnp.stack((proj_sums[0], proj_sums[2]))
    grad_normed_a = narrow(
        jnp.einsum("rjh,djh->rd", grad_proj, w_qkv, preferred_element_type=jnp.float32)
    )
    gain_a_grad = jnp.sum(grad_normed_a * unit_a, axis=0)
    shift_a_grad = jnp.sum(grad_normed_a, axis=0)
    grad_in = grad_middle + norm_back(grad_normed_a, unit_a, inverse_a, gain_rows[0])
    gains_grad = jnp.stack((gain_a_grad, gain_b_grad))
    biases_grad = jnp.stack((shift_a_grad, out_bias_grad, shift_b_grad, down_bias_grad))
    factors = (rows_b, grad_pre, activated, wide_branch, mixed_low, wide_attn, rows_a, grad_proj)
    vectors = (qv_grad, up_bias_grad, gains_grad, biases_grad)
    return (grad_in, factors, vectors)


def weight_products(factors):
    rows_b, grad_pre, activated, wide_branch, mixed_low, wide_attn, rows_a, grad_proj = factors
    down_grad = jnp.einsum("rf,rd->fd", activated, wide_branch, preferred_element_type=jnp.float32)
    up_grad = jnp.einsum("rd,rf->df", rows_b, grad_pre, preferred_element_type=jnp.float32)
    out_grad = jnp.einsum("re,rd->ed", mixed_low, wide_attn, preferred_element_type=jnp.float32)
    qkv_grad = jnp.einsum("rd,rjh->djh", rows_a, grad_proj, preferred_element_type=jnp.float32)
    return (qkv_grad, out_grad, up_grad, down_grad)


def assemble(products, vectors):
    qkv_grad, out_grad, up_grad, down_grad = products
    qv_grad, up_bias_grad, gains_grad, biases_grad = vectors
    return (qkv_grad, qv_grad, out_grad, up_grad, up_bias_grad, down_grad, gains_grad, biases_grad)


def reduce_grads(local_grads):
    qkv_grad, qv_grad, out_grad, up_grad, up_bias_grad, down_grad, gains_grad, biases_grad = (
        local_grads
    )
    heads = qv_grad.shape[1] // HD
    shards = (
        lax.psum_scatter(
            qkv_grad[None].astype(jnp.bfloat16), "dp", scatter_dimension=1, tiled=True
        ).astype(jnp.float32),
        lax.psum_scatter(
            qv_grad.reshape(1, 2, heads, HD).astype(jnp.bfloat16),
            "dp",
            scatter_dimension=3,
            tiled=True,
        ).astype(jnp.float32),
        lax.psum_scatter(
            out_grad[None].astype(jnp.bfloat16), "dp", scatter_dimension=2, tiled=True
        ).astype(jnp.float32),
        lax.psum_scatter(
            up_grad[None].astype(jnp.bfloat16), "dp", scatter_dimension=1, tiled=True
        ).astype(jnp.float32),
        lax.psum_scatter(
            up_bias_grad.reshape(1, -1, HD).astype(jnp.bfloat16),
            "dp",
            scatter_dimension=2,
            tiled=True,
        ).astype(jnp.float32),
        lax.psum_scatter(
            down_grad[None].astype(jnp.bfloat16), "dp", scatter_dimension=2, tiled=True
        ).astype(jnp.float32),
    )
    vectors = (
        lax.psum_scatter(gains_grad[None], ("dp", "tensor"), scatter_dimension=2, tiled=True),
        lax.psum_scatter(biases_grad[None], ("dp", "tensor"), scatter_dimension=2, tiled=True),
    )
    return tuple(shards) + tuple(vectors)


def body(
    boundary,
    doc_lengths,
    qkv_weight,
    qv_bias,
    out_weight,
    up_weight,
    up_bias,
    down_weight,
    norm_gains,
    norm_biases,
):
    section_index = lax.axis_index("section")
    on_first = section_index == 0
    own_part = boundary[0]
    batches = own_part.shape[0]
    rows_dp = own_part.shape[1] * lax.axis_size("tensor")
    seq_len = rows_dp * lax.axis_size("dp")
    dp_index = lax.axis_index("dp")
    sources = (
        qkv_weight,
        qv_bias,
        out_weight,
        up_weight,
        up_bias,
        down_weight,
        norm_gains,
        norm_biases,
    )
    fixed_weights = fetch_weights(*sources)

    def current():
        return fixed_weights

    def sight_for(batch_at):
        lengths = lax.dynamic_index_in_dim(doc_lengths, batch_at, 0, keepdims=False)
        return visibility(lengths, dp_index, rows_dp, seq_len)

    def pick(first_value, second_value):
        return jnp.where(on_first, first_value, second_value)

    received = jnp.zeros_like(own_part[0])
    kept_ticks, exits = ([], [])
    for tick_index in range(batches + 1):
        entering = jnp.where(on_first, own_part[min(tick_index, batches - 1)], received)
        batch_at = jnp.clip(tick_index - section_index, 0, batches - 1)
        result, saved = forward(entering, current(), sight_for(batch_at))
        leaving = result.astype(jnp.bfloat16)
        kept_ticks.append(saved)
        exits.append(leaving)
        if tick_index < batches:
            received = from_behind(leaving, "section", 1)
    acts = jnp.stack(
        [jnp.where(on_first, exits[number], exits[number + 1]) for number in range(batches)]
    )[None]
    returned = jnp.zeros_like(own_part[0])
    summed = None
    vector_sum = None
    factor_ticks = []
    leaving_grads = []
    for tick_index in range(batches + 1):
        own_grad = own_part[min(tick_index, batches - 1)].astype(jnp.float32)
        if tick_index == batches:
            own_grad = jnp.zeros_like(own_grad)
        grad_out = jnp.where(on_first, returned.astype(jnp.float32), own_grad)
        saved = jax.tree.map(
            pick, kept_ticks[max(tick_index - 1, 0)], kept_ticks[min(tick_index + 1, batches)]
        )
        batch_at = jnp.where(on_first, max(tick_index - 1, 0), min(tick_index, batches - 1))
        grad_in, factors, vectors = backward(saved, grad_out, current(), sight_for(batch_at))
        leaving_grads.append(grad_in)
        if tick_index < batches:
            returned = from_behind(grad_in.astype(jnp.bfloat16), "section", -1)
        factor_ticks.append(factors)
        vector_sum = (
            vectors
            if vector_sum is None
            else tuple((former + latter for former, latter in zip(vector_sum, vectors)))
        )
    joined = tuple(
        (
            jnp.concatenate([entry[number] for entry in factor_ticks], axis=0)
            for number in range(len(factor_ticks[0]))
        )
    )
    summed = reduce_grads(assemble(weight_products(joined), vector_sum))
    input_grads = jnp.stack(
        [
            jnp.where(on_first, leaving_grads[number + 1], leaving_grads[number])
            for number in range(batches)
        ]
    )[None]
    return (acts, input_grads) + tuple(summed)


LOW, WIDE = (jnp.bfloat16, jnp.float32)
HBM, VMEM, DMAS = (pl.ANY, pltpu.VMEM, pltpu.SemaphoreType.DMA)


def dot(left, right):
    return jnp.dot(left, right, preferred_element_type=WIDE)


def dot_back(left, right):
    return lax.dot_general(left, right, (((1,), (1,)), ((), ())), preferred_element_type=WIDE)


def dot_rows(left, right):
    return lax.dot_general(left, right, (((0,), (0,)), ((), ())), preferred_element_type=WIDE)


def device(core, z, x, y):
    return (core, z * 2 + x, y)


class Plane:
    def __init__(self):
        dp = lax.axis_index("dp")
        self.levels = lax.axis_size("dp") // 2
        self.core, self.y = (lax.axis_index("section"), lax.axis_index("tensor"))
        self.z, self.x = (dp // 2, lax.rem(dp, 2))
        self.sibling = device(1 - self.core, self.z, self.x, self.y)
        self.across = device(self.core, self.z, self.x, 1 - self.y)
        self.over = device(self.core, self.z, 1 - self.x, self.y)
        self.corner = device(1 - self.core, self.z, 1 - self.x, self.y)
        self.member = self.z * 2 + self.core
        self.block = self.z * 4 + self.core * 2 + self.y

    def along(self, z):
        return device(self.core, jnp.clip(z, 0, self.levels - 1), self.x, self.y)

    def partners(self):
        partners = [self.across, self.over, self.corner]
        for step in range(self.levels):
            zz = lax.rem(self.z + step, self.levels)
            for other in (0, 1):
                if step or other:
                    core = 1 - self.core if other else self.core
                    partners.append(device(core, zz, self.x, self.y))
        return partners

    def nearest(self):
        tables = []
        for z in range(self.levels):
            tables.append(sorted(range(self.levels), key=lambda zz: (abs(zz - z), zz)))
        found = []
        for place in range(self.levels):
            number = jnp.int32(tables[0][place])
            for z in range(1, self.levels):
                number = jnp.where(self.z == z, tables[z][place], number)
            found.append(number)
        return found


def guarded(present, act):
    if present is True:
        act()
    else:
        pl.when(present)(act)


class Sends:
    def __init__(self, sems):
        self.sems = sems
        self.pending = []

    def start(self, present, source, target, arrived, partner):
        copy = pltpu.make_async_remote_copy(
            src_ref=source,
            dst_ref=target,
            send_sem=self.sems.at[len(self.pending)],
            recv_sem=arrived,
            device_id=partner,
            device_id_type=MESH,
        )
        guarded(present, copy.start)
        self.pending.append([present, copy, False])
        return len(self.pending) - 1

    def wait(self, *numbers):
        for number in numbers:
            present, copy, done = self.pending[number]
            if not done:
                guarded(present, copy.wait_send)
                self.pending[number][2] = True

    def finish(self):
        self.wait(*range(len(self.pending)))


class Copies:
    def __init__(self, sems):
        self.sems = sems
        self.pending = []

    def start(self, source, target, present=True):
        copy = pltpu.make_async_copy(source, target, self.sems.at[len(self.pending)])
        guarded(present, copy.start)
        self.pending.append([present, copy, False])
        return len(self.pending) - 1

    def wait(self, *numbers):
        for number in numbers:
            present, copy, done = self.pending[number]
            if not done:
                guarded(present, copy.wait)
                self.pending[number][2] = True

    def finish(self):
        for number in range(len(self.pending)):
            self.wait(number)


def await_block(block, arrived, partner):
    pltpu.make_async_remote_copy(
        src_ref=block,
        dst_ref=block,
        send_sem=arrived,
        recv_sem=arrived,
        device_id=partner,
        device_id_type=MESH,
    ).wait_recv()


def span(start, size):
    return pl.ds(pl.multiple_of(start * size, size), size)


class Gather:
    def __init__(self, plane, sends, rows, sems):
        self.plane, self.sends, self.rows, self.sems = (plane, sends, rows, sems)
        self.chunks = sems.shape[1]
        self.size = rows.shape[0] // (sems.shape[0] * self.chunks)

    def spot(self, zz, core, y, chunk):
        number = zz * 4 + core * 2 + y
        return (
            self.rows.at[span(number * self.chunks + chunk, self.size)],
            self.sems.at[number, chunk],
        )

    def open(self):
        plane = self.plane
        for chunk in range(self.chunks):
            held, arrived = self.spot(plane.z, plane.core, plane.y, chunk)
            for present, partner in (
                (True, plane.across),
                (plane.z > 0, plane.along(plane.z - 1)),
                (plane.z < plane.levels - 1, plane.along(plane.z + 1)),
                (True, plane.sibling),
            ):
                self.sends.start(present, held, held, arrived, partner)

    def run(self, on_group, tick):
        plane = self.plane
        order = plane.nearest()

        def complete(step):
            zz = order[step]
            for chunk in range(self.chunks):
                held, arrived = self.spot(zz, plane.core, 1 - plane.y, chunk)
                await_block(held, arrived, plane.across)
                self.sends.start(True, held, held, arrived, plane.sibling)
            for yy in (plane.y, 1 - plane.y):
                for chunk in range(self.chunks):
                    held, arrived = self.spot(zz, 1 - plane.core, yy, chunk)
                    await_block(held, arrived, plane.sibling)
            on_group(step, zz)

        for step in range(1, plane.levels):
            zz = order[step]
            onward = jnp.where(zz < plane.z, plane.z + 1, plane.z - 1)
            can_go = (onward >= 0) & (onward < plane.levels)
            for chunk in range(self.chunks):
                held, arrived = self.spot(zz, plane.core, plane.y, chunk)
                await_block(held, arrived, plane.across)
                self.sends.start(can_go, held, held, arrived, plane.along(onward))
                self.sends.start(True, held, held, arrived, plane.across)
                self.sends.start(True, held, held, arrived, plane.sibling)
            tick()
            complete(step - 1)
        complete(plane.levels - 1)
        tick()

    @staticmethod
    def count(levels, chunks):
        return chunks * (4 + 3 * (levels - 1) + levels)


class Scatter:
    def __init__(self, plane, sends, refs, result):
        self.plane, self.sends, self.refs, self.result = (plane, sends, refs, result)
        self.chunks = refs.across_sems.shape[1]
        self.size = result.shape[0] // self.chunks

    @staticmethod
    def count(levels, chunks):
        return chunks * (4 * levels - 1)

    def part(self, zz, core, y, chunk):
        number = (zz * 4 + core * 2 + y) * self.chunks + chunk
        return self.refs.part.at[span(number, self.size)]

    def spot(self, buffer, sems, slot, chunk):
        return buffer.at[slot, span(chunk, self.size)], sems.at[slot, chunk]

    def take(self, buffer, sems, slot, chunk):
        came, arrived = self.spot(buffer, sems, slot, chunk)
        await_block(came, arrived, self.plane.across)
        return came[...].astype(WIDE)

    def pair(self, zz, y, chunk):
        refs = self.refs
        own = self.part(zz, self.plane.core, y, chunk)[...].astype(WIDE)
        return own + self.take(refs.from_sibling, refs.sibling_sems, zz * 2 + y, chunk)

    def give_sibling(self, zz):
        plane, refs = (self.plane, self.refs)
        for yy in (1 - plane.y, plane.y):
            for chunk in range(self.chunks):
                landing, arrived = self.spot(
                    refs.from_sibling, refs.sibling_sems, zz * 2 + yy, chunk
                )
                self.sends.start(
                    True, self.part(zz, 1 - plane.core, yy, chunk), landing, arrived, plane.sibling
                )

    def give_across(self, zz):
        plane, refs = (self.plane, self.refs)
        for chunk in range(self.chunks):
            staged = refs.from_sibling.at[zz * 2 + 1 - plane.y, span(chunk, self.size)]
            staged[...] = self.pair(zz, 1 - plane.y, chunk).astype(staged.dtype)
            landing, arrived = self.spot(refs.from_across, refs.across_sems, zz, chunk)
            self.sends.start(True, staged, landing, arrived, plane.across)

    def plane_sum(self, zz, chunk):
        refs = self.refs
        total = self.pair(zz, self.plane.y, chunk)
        return total + self.take(refs.from_across, refs.across_sems, zz, chunk)

    def come(self, slot, chunk):
        return self.take(self.refs.from_behind, self.refs.behind_sems, slot, chunk)

    def give_onward(self, zz):
        plane, refs = (self.plane, self.refs)
        onward = jnp.where(zz > plane.z, plane.z + 1, plane.z - 1)
        behind = plane.z * 2 - onward
        slot = jnp.where((onward == zz) & (zz < plane.z), plane.levels, zz)
        for chunk in range(self.chunks):
            refs.total[...] = self.plane_sum(zz, chunk)

            @pl.when((behind >= 0) & (behind < plane.levels))
            def _(chunk=chunk):
                refs.total[...] += self.come(zz, chunk)

            staged = refs.from_sibling.at[zz * 2 + plane.y, span(chunk, self.size)]
            staged[...] = refs.total[...].astype(staged.dtype)
            landing, arrived = self.spot(refs.from_behind, refs.behind_sems, slot, chunk)
            self.sends.start(True, staged, landing, arrived, plane.along(onward))

    def conclude(self):
        plane = self.plane
        for chunk in range(self.chunks):
            own = self.result.at[span(chunk, self.size)]
            own[...] = self.plane_sum(plane.z, chunk)

            @pl.when(plane.z > 0)
            def _(own=own, chunk=chunk):
                own[...] += self.come(plane.z, chunk)

            @pl.when(plane.z < plane.levels - 1)
            def _(own=own, chunk=chunk):
                own[...] += self.come(plane.levels, chunk)

    def run(self, make, tick, fill=None):
        levels = self.plane.levels
        order = self.plane.nearest()[::-1]
        for step in range(levels + 3):
            if step < levels:
                make(step, order[step])
                self.give_sibling(order[step])
            if 0 < step <= levels:
                self.give_across(order[step - 1])
            if step >= levels - 1:
                tick()
                if fill is not None:
                    fill(step - levels + 1)
            if 3 <= step < levels + 2:
                self.give_onward(order[step - 3])
        self.conclude()


def scatter_scratch(rows, width, levels, chunks, dtype=LOW):
    def held(count):
        return VMEM((count, rows, width), dtype)

    return dict(
        part=VMEM((rows * 4 * levels, width), dtype),
        from_sibling=held(2 * levels),
        from_across=held(levels),
        from_behind=held(levels + 1),
        total=VMEM((rows // chunks, width), WIDE),
        sum=VMEM((rows, width), WIDE),
        sibling_sems=DMAS((2 * levels, chunks)),
        across_sems=DMAS((levels, chunks)),
        behind_sems=DMAS((levels + 1, chunks)),
    )


def by_rows(which):
    return which in (1, 3)


def piece_of_shard(which, ref, member, members):
    if by_rows(which):
        return ref.at[span(member, ref.shape[0] // members)]
    return ref.at[:, span(member, ref.shape[1] // members)]


def piece_of_slice(which, ref, shard, shards):
    if by_rows(which):
        return ref.at[:, span(shard, ref.shape[1] // shards)]
    return ref.at[span(shard, ref.shape[0] // shards)]


def slice_shape(which, shape, shards):
    rows, columns = shape
    if by_rows(which):
        return (rows // shards, columns * shards)
    return (rows * shards, columns // shards)


def shard_shape(which, shape, shards):
    rows, columns = shape
    if by_rows(which):
        return (rows * shards, columns // shards)
    return (rows // shards, columns * shards)


FETCHES = (
    ((0, 0), (0, 2), (0, 2), (0, 0)),
    ((0, 1), (0, 1), (2, 1), (2, 1), (0, 0), (0, 0), (0, 1), (0, 1)),
    ((0, 1), (0, 1), (2, 0), (2, 0), (0, 0), (0, 1), (2, 1), (2, 2)),
    ((0, 1), (0, 1), (2, 1), (2, 1), (0, 0), (0, 0), (0, 2), (0, 1)),
    ((0, 1), (0, 0), (0, 0), (0, 0), (0, 0), (0, 0), (0, 0), (0, 0)),
)
ADDS = (
    (0, 0, 1, 2),
    (0, 0, 2, 3, 0, 0, 0, 0),
    (2, 2, 2, 2, 0, 0, 1, 1),
    (0, 1, 2, 3, 0, 0, 0, 2),
    (2, 1, 1, 1),
)


class Fetch:
    UNITS = ((0, (0, 1)), (0, (2,)), (0, (3,)), (1, (0, 1)), (1, (2,)), (1, (3,)))

    def __init__(self, plane, shards, slices, refs, sends, copies):
        self.plane, self.shards, self.slices = (plane, shards, slices)
        self.refs, self.sends, self.copies = (refs, sends, copies)
        self.spreads = []
        for unit in range(len(self.UNITS)):
            for step in range(plane.levels - 1, -1, -1):
                self.spreads.append((unit, step))
        self.hands = list(self.spreads)
        self.left = [plane.levels] * len(self.UNITS)
        self.kept = [[] for _ in self.UNITS]
        self.plan = [moment for stage in FETCHES for moment in stage]

    @staticmethod
    def count(levels):
        return 4 * 2 * (3 * levels), 4 * 2 + 8

    def tick(self):
        self.start(*self.plan.pop(0))

    def start(self, spreads, hands):
        for _ in range(spreads):
            if self.spreads:
                unit, step = self.spreads.pop(0)
                for which in self.UNITS[unit][1]:
                    self.spread(unit, which, step)
        for _ in range(hands):
            if len(self.hands) > len(self.spreads):
                unit, step = self.hands.pop(0)
                for which in self.UNITS[unit][1]:
                    self.hand_over(unit, which, step)
                self.left[unit] -= 1

    def require(self, unit):
        while self.left[unit]:
            self.start(0, 1) if len(self.hands) > len(self.spreads) else self.start(1, 0)
        plane, refs = (self.plane, self.refs)
        layer, weights = self.UNITS[unit]
        for which in weights:
            part = self.slices[which].at[layer]
            for zz in range(plane.levels):
                held = piece_of_slice(which, part, zz * 2 + 1 - plane.x, 2 * plane.levels)
                await_block(held, refs.cross_sems.at[which, layer, zz], plane.over)
        self.copies.wait(*self.kept[unit])
        for which in weights:
            self.copies.start(self.slices[which].at[layer], refs.slices_out[which].at[layer])

    def spread(self, unit, which, step):
        plane, refs, layer = (self.plane, self.refs, self.UNITS[unit][0])
        members = 2 * plane.levels
        shard, part = (self.shards[which], self.slices[which].at[layer])
        owner = plane.core == layer
        target = piece_of_slice(which, part, plane.z * 2 + plane.x, members)
        zz = lax.rem(plane.z + step, plane.levels)
        for other in (0, 1):
            core = 1 - plane.core if other else plane.core
            source = piece_of_shard(which, shard, zz * 2 + core, members)
            if step or other:
                self.sends.start(
                    owner,
                    source,
                    target,
                    refs.column_sems.at[which, layer, plane.z],
                    device(core, zz, plane.x, plane.y),
                )
            else:
                self.kept[unit].append(self.copies.start(source, target, owner))

    def hand_over(self, unit, which, step):
        plane, refs, layer = (self.plane, self.refs, self.UNITS[unit][0])
        members = 2 * plane.levels
        shard, part = (self.shards[which], self.slices[which].at[layer])
        zz = lax.rem(plane.z - step + plane.levels, plane.levels)
        held = piece_of_slice(which, part, zz * 2 + plane.x, members)
        arrived = refs.column_sems.at[which, layer, zz]
        cross = refs.cross_sems.at[which, layer, zz]
        if step:
            await_block(held, arrived, plane.over)
            self.sends.start(True, held, held, cross, plane.over)
        else:
            owner = plane.core == layer
            source = piece_of_shard(which, shard, plane.member, members)
            guarded(jnp.logical_not(owner), partial(await_block, held, arrived, plane.over))
            self.sends.start(jnp.logical_not(owner), held, held, cross, plane.over)
            self.sends.start(owner, source, held, cross, plane.over)


class Return:
    def __init__(self, plane, slices, landed, shards, refs, sends, copies):
        self.plane, self.slices, self.landed, self.shards = (plane, slices, landed, shards)
        self.refs, self.sends, self.copies = (refs, sends, copies)
        self.moments, self.left, self.given = ([], {}, {})
        self.plan = [count for stage in ADDS for count in stage]

    @staticmethod
    def count(levels):
        return 4 * 2 * (2 * levels), 4 * 2

    def give(self, layer, which):
        plane = self.plane
        self.left[layer, which], self.given[layer, which] = (plane.levels, [])
        for step in range(plane.levels - 1, -1, -1):
            zz = lax.rem(plane.z + step, plane.levels)
            number = self.sends.start(
                True,
                piece_of_slice(which, self.slices[which], zz * 2 + 1 - plane.x, 2 * plane.levels),
                self.landed[which].at[layer, zz],
                self.refs.cross_sems.at[which, layer, zz],
                plane.over,
            )
            self.given[layer, which].append(number)
            self.moments.append((layer, which, step))

    def tick(self):
        self.start(self.plan.pop(0))

    def start(self, adds):
        for _ in range(adds):
            if self.moments:
                moment = self.moments.pop(0)
                self.add(*moment)
                self.left[moment[:2]] -= 1

    def require(self, layer, which):
        while self.left[layer, which]:
            self.start(1)
        self.sends.wait(*self.given[layer, which])

    def add(self, layer, which, step):
        plane, refs = (self.plane, self.refs)
        members = 2 * plane.levels
        here = plane.core == layer
        target = piece_of_shard(which, self.shards[which], plane.member, members)
        zz = lax.rem(plane.z + step, plane.levels)
        held = self.landed[which].at[layer, zz]
        await_block(held, refs.cross_sems.at[which, layer, zz], plane.over)
        own = piece_of_slice(which, self.slices[which], zz * 2 + plane.x, members)
        held[...] = (held[...].astype(WIDE) + own[...].astype(WIDE)).astype(LOW)
        self.sends.start(
            True if step else jnp.logical_not(here),
            held,
            target,
            refs.column_sems.at[which, plane.core, plane.z],
            device(layer, zz, plane.x, plane.y),
        )
        if step == 0:
            self.copies.start(held, target, here)

    def finish(self):
        self.start(len(self.moments))
        plane, refs = (self.plane, self.refs)
        members = 2 * plane.levels
        for which in range(4):
            for core in (0, 1):
                for step in range(plane.levels):
                    zz = lax.rem(plane.z + step, plane.levels)
                    held = piece_of_shard(which, self.shards[which], zz * 2 + core, members)
                    guarded(
                        True if step else plane.core != core,
                        partial(
                            await_block, held, refs.column_sems.at[which, core, zz], plane.over
                        ),
                    )


class Outward:
    @staticmethod
    def count():
        return 6, 2

    def __init__(self, plane, target, sems):
        self.plane, self.target, self.sems = (plane, target, sems)

    def give(self, layer, source, sends, copies):
        plane, target = (self.plane, self.target.at[self.plane.x])
        same_core, same_x = (plane.core == layer, plane.core == plane.x)
        other_core, other_x = (plane.core != layer, plane.core != plane.x)
        for present, partner in (
            (same_core & other_x, plane.over),
            (other_core & same_x, plane.sibling),
            (other_core & other_x, plane.corner),
        ):
            sends.start(present, source, target, self.sems.at[plane.x], partner)
        copies.start(source, target, same_core & same_x)

    def finish(self):
        plane = self.plane
        for slot in (0, 1):
            away = jnp.logical_not((plane.core == plane.x) & (plane.x == slot))
            guarded(away, partial(await_block, self.target.at[slot], self.sems.at[slot], plane.over))


def launch(name, ident, kernel, counts, inputs, outputs, scratch):
    scratch = dict(
        scratch,
        send_sems=DMAS((counts[0],)),
        phase_sems=DMAS((counts[1],)),
        copy_sems=DMAS((counts[2],)),
    )
    names = list(inputs) + list(outputs) + list(scratch)

    def body(*refs):
        held = SimpleNamespace(**dict(zip(names, refs)))
        plane = Plane()
        barrier = pltpu.get_barrier_semaphore()
        partners = plane.partners()
        for partner in partners:
            pl.semaphore_signal(barrier, inc=1, device_id=partner, device_id_type=MESH)
        sends, copies = (Sends(held.send_sems), Copies(held.copy_sems))
        kernel(held, plane, lambda: pl.semaphore_wait(barrier, len(partners)), sends, copies)
        copies.finish()
        sends.finish()
        assert len(sends.pending) == counts[0], len(sends.pending)
        assert len(copies.pending) == counts[2], len(copies.pending)

    results = pl.pallas_call(
        body,
        out_shape=[jax.ShapeDtypeStruct(shape, dtype) for shape, dtype, _ in outputs.values()],
        in_specs=[pl.BlockSpec(memory_space=space) for _, space in inputs.values()],
        out_specs=[pl.BlockSpec(memory_space=space) for _, _, space in outputs.values()],
        scratch_shapes=list(scratch.values()),
        compiler_params=pltpu.CompilerParams(
            collective_id=ident, has_side_effects=True, vmem_limit_bytes=60 << 20
        ),
        name=name,
    )(*[array for array, _ in inputs.values()])
    return SimpleNamespace(**dict(zip(outputs, results)))


CHUNKS, SUM_CHUNKS, CUT = (2, 2, 512)
NORM_LINES, HEAD_LINES, LINES = (6, 8, 16)


def unpack_vectors(refs, plane, levels):
    members, blocks = (2 * levels, 4 * levels)
    for layer in (0, 1):
        for z in range(levels):
            for x in (0, 1):
                for y in (0, 1):
                    start = ((z * 4 + layer * 2 + y) * 2 + x) * LINES
                    cut = (z * 4 + x * 2 + y) * HD
                    refs.norms[layer, :, cut : cut + HD] = refs.small[
                        start : start + LINES
                    ].astype(WIDE)[:HEAD_LINES]
    lines = []
    for layer in (0, 1):
        pieces = []
        for z in range(levels):
            for x in (0, 1):
                number = (z * 4 + layer * 2 + plane.y) * 2 + x
                pieces.append(refs.small[span(number, LINES)].astype(WIDE)[HEAD_LINES:])
        lines.append(jnp.concatenate(pieces, axis=1))
    lines = jnp.concatenate(lines, axis=0).astype(LOW)
    width = HD // members
    place = lax.broadcasted_iota(jnp.int32, (members * HD, HD), 0)
    lane = lax.broadcasted_iota(jnp.int32, (members * HD, HD), 1)

    def pick(first):
        chosen = (place // HD == lane // width) & (place % HD == lane % width + first)
        return dot(lines, chosen.astype(WIDE).astype(LOW))

    heads = pick(plane.member * width)
    units = refs.b_up.shape[2] // HD
    per_line = HD // (units * width)
    row = lax.broadcasted_iota(jnp.int32, (HEAD_LINES, HD), 0)
    for layer in (0, 1):
        refs.b_qv[layer] = heads[layer * HEAD_LINES : layer * HEAD_LINES + 2]
    for unit in range(units):
        found = pick((lax.rem(plane.member, per_line) * units + unit) * width)
        for layer in (0, 1):
            own = found[layer * HEAD_LINES : (layer + 1) * HEAD_LINES]
            own = jnp.where(row == 2 + plane.member // per_line, own, 0.0)
            refs.b_up[layer, :, unit * HD : (unit + 1) * HD] = jnp.sum(own, axis=0, keepdims=True)


def visible(refs, group, size, tokens):
    segment = refs.query_segment[group]
    place = group.start + lax.broadcasted_iota(jnp.int32, (size, tokens), 0)
    keys = lax.broadcasted_iota(jnp.int32, (size, tokens), 1)
    return (segment == refs.key_segment[...]) & (keys <= place)


def forward_planes(ident, boundary, packed, segments, shards):
    levels = lax.axis_size("dp") // 2
    blocks, members = (4 * levels, 2 * levels)
    rows, width = boundary.shape[1:]
    tokens, size = (blocks * rows, 4 * rows)
    slice_shapes = [
        slice_shape(which, shard.shape, members) for which, shard in enumerate(shards)
    ]
    units = slice_shapes[2][1]
    scaling = HD ** (-0.5)

    def kernel(refs, plane, greet, sends, copies):
        core, x = (plane.core, plane.x)
        own_block = span(plane.block, rows)
        refs.slices_out = [refs.out0, refs.out1, refs.out2, refs.out3]
        slices = [refs.w0, refs.w1, refs.w2, refs.w3]
        fetch = Fetch(
            plane, [refs.shard0, refs.shard1, refs.shard2, refs.shard3], slices, refs, sends, copies
        )
        small_block = span(plane.block * 2 + x, LINES)
        refs.small[small_block] = refs.packed[...]
        greet()
        phase = Sends(refs.phase_sems)
        own_small = refs.small.at[small_block]
        phase.start(True, own_small, own_small, refs.pair_sem.at[0], plane.over)
        inward = []
        for slot in (0, 1):
            source, target = (refs.boundary.at[slot], refs.landed_planes.at[core])
            arrived = refs.inward_sems.at[core]
            for present, partner in (
                ((x == core) & (slot != x), plane.over),
                ((x != core) & (slot == x), plane.sibling),
                ((x != core) & (slot != x), plane.corner),
            ):
                phase.start(present, source, target, arrived, partner)
            inward.append(copies.start(source, target, (x == core) & (slot == x)))
        fetch.start(levels, 0)
        other_small = refs.small.at[span(plane.block * 2 + 1 - x, LINES)]
        await_block(other_small, refs.pair_sem.at[0], plane.over)
        small = Gather(plane, phase, refs.small, refs.small_sems)
        small.open()
        small.run(lambda step, zz: None, lambda: None)
        fetch.start(levels, 0)
        for slot in (0, 1):
            here = (core == x) & (core == slot)
            guarded(
                jnp.logical_not(here),
                partial(await_block, refs.landed_planes.at[slot], refs.inward_sems.at[slot], plane.over),
            )
        copies.wait(*inward)
        refs.planes[...] = refs.landed_planes[...]
        refs.rows[0, own_block] = refs.landed_planes[1]
        gather = Gather(plane, phase, refs.rows.at[0], refs.gather_sems.at[0])
        gather.open()
        unpack_vectors(refs, plane, levels)
        kept = []

        def keep(step, zz):
            group = span(zz, size)
            kept.append(copies.start(refs.rows.at[0, group], refs.gathered.at[group]))

        gather.run(keep, fetch.tick)
        copies.wait(*kept)
        phase.finish()

        for layer in (0, 1):
            number = 1 + 2 * layer
            norms = refs.norms.at[layer]
            held, sems = (refs.rows.at[number % 2], refs.gather_sems.at[number % 2])
            entering = refs.planes[0] if layer == 0 else refs.leaving[0]
            hidden = entering.astype(WIDE)
            normed, _, _ = layer_norm(hidden, norms[0:1], norms[2:3])
            held[own_block] = normed.astype(LOW)
            phase = Sends(refs.phase_sems)
            gather = Gather(plane, phase, held, sems)
            gather.open()
            fetch.require(3 * layer)
            kept = []

            def project(step, zz):
                group = span(zz, size)
                projected = dot(held[group], refs.w0[layer])
                refs.queries[layer, group] = (projected[:, :HD] + refs.b_qv[layer, 0:1]).astype(LOW)
                refs.keys[layer, group] = projected[:, HD : 2 * HD].astype(LOW)
                refs.values[layer, group] = (
                    projected[:, 2 * HD :] + refs.b_qv[layer, 1:2]
                ).astype(LOW)
                kept.append(copies.start(held.at[group], refs.rows_a.at[layer, group]))

            gather.run(project, fetch.tick)

            def attend(step, zz):
                group = span(zz, size)
                allowed = visible(refs, group, size, tokens)
                scores = dot_back(refs.queries[layer, group], refs.keys[layer]) * scaling
                scores = jnp.where(allowed, scores, NEG_FILL)
                top = jnp.max(scores, axis=-1, keepdims=True)
                raised = jnp.exp(scores - top)
                total = jnp.sum(raised, axis=-1, keepdims=True)
                refs.log_total[layer, group] = top + jnp.log(total)
                probs = (raised / total).astype(LOW)
                live = (refs.query_segment[group] >= 0).astype(WIDE)
                mixed = (dot(probs, refs.values[layer]) * live).astype(LOW)
                refs.mixed[layer, group] = mixed
                for cut in range(0, width, CUT):
                    refs.part[group, cut : cut + CUT] = dot(
                        mixed, refs.w1[layer, :, cut : cut + CUT]
                    ).astype(LOW)

            Scatter(plane, phase, refs, refs.sum).run(attend, fetch.tick)
            middle = hidden + refs.sum[...] + norms[3:4]
            refs.middle[layer] = middle
            copies.wait(*kept)
            phase.finish()

            number = number + 1
            held, sems = (refs.rows.at[number % 2], refs.gather_sems.at[number % 2])
            normed, _, _ = layer_norm(middle, norms[1:2], norms[4:5])
            held[own_block] = normed.astype(LOW)
            phase = Sends(refs.phase_sems)
            gather = Gather(plane, phase, held, sems)
            gather.open()
            fetch.require(3 * layer + 1)
            kept = []

            def expand(step, zz):
                group = span(zz, size)
                preact = dot(held[group], refs.w2[layer]) + refs.b_up[layer]
                refs.own_preact[layer, group] = preact
                refs.own_activated[layer, group] = (
                    0.5 * preact * (1.0 + lax.erf(preact * math.sqrt(0.5)))
                ).astype(LOW)
                for own, out in (
                    (held.at[group], refs.rows_b),
                    (refs.own_preact.at[layer, group], refs.preact),
                    (refs.own_activated.at[layer, group], refs.activated),
                ):
                    kept.append(copies.start(own, out.at[layer, group]))

            gather.run(expand, fetch.tick)
            fetch.require(3 * layer + 2)

            def shrink(step, zz):
                group = span(zz, size)
                for cut in range(0, width, CUT):
                    refs.part[group, cut : cut + CUT] = dot(
                        refs.own_activated[layer, group], refs.w3[layer, :, cut : cut + CUT]
                    ).astype(LOW)

            Scatter(plane, phase, refs, refs.sum).run(shrink, fetch.tick)
            refs.leaving[layer] = (refs.middle[layer] + refs.sum[...] + norms[5:6]).astype(LOW)
            copies.wait(*kept)
            phase.finish()

    head = ((2, tokens, HD), LOW, VMEM)
    gathers = Gather.count(levels, CHUNKS)
    lasting = Fetch.count(levels)
    return launch(
        "forward_planes",
        ident,
        kernel,
        (
            lasting[0],
            max(gathers + Scatter.count(levels, SUM_CHUNKS), 7 + Gather.count(levels, 1) + gathers),
            lasting[1] + 2 + levels + 2 * 4 * levels,
        ),
        dict(
            boundary=(boundary, HBM),
            packed=(packed, VMEM),
            query_segment=(segments[0], VMEM),
            key_segment=(segments[1], VMEM),
            shard0=(shards[0], HBM),
            shard1=(shards[1], HBM),
            shard2=(shards[2], HBM),
            shard3=(shards[3], HBM),
        ),
        dict(
            planes=((2, rows, width), LOW, VMEM),
            leaving=((2, rows, width), LOW, VMEM),
            middle=((2, rows, width), WIDE, VMEM),
            norms=((2, HEAD_LINES, width), WIDE, VMEM),
            queries=head,
            keys=head,
            values=head,
            mixed=head,
            log_total=((2, tokens, 1), WIDE, VMEM),
            gathered=((tokens, width), LOW, HBM),
            rows_a=((2, tokens, width), LOW, HBM),
            rows_b=((2, tokens, width), LOW, HBM),
            preact=((2, tokens, units), WIDE, HBM),
            activated=((2, tokens, units), LOW, HBM),
            out0=((2,) + slice_shapes[0], LOW, HBM),
            out1=((2,) + slice_shapes[1], LOW, HBM),
            out2=((2,) + slice_shapes[2], LOW, HBM),
            out3=((2,) + slice_shapes[3], LOW, HBM),
        ),
        dict(
            scatter_scratch(rows, width, levels, SUM_CHUNKS),
            rows=VMEM((2, tokens, width), LOW),
            gather_sems=DMAS((2, blocks, CHUNKS)),
            small=VMEM((2 * blocks * LINES, HD), LOW),
            small_sems=DMAS((blocks, 1)),
            pair_sem=DMAS((1,)),
            inward_sems=DMAS((2,)),
            landed_planes=VMEM((2, rows, width), LOW),
            b_qv=VMEM((2, 2, HD), WIDE),
            b_up=VMEM((2, 1, units), WIDE),
            w0=VMEM((2,) + slice_shapes[0], LOW),
            w1=VMEM((2,) + slice_shapes[1], LOW),
            w2=VMEM((2,) + slice_shapes[2], LOW),
            w3=VMEM((2,) + slice_shapes[3], LOW),
            own_preact=VMEM((2, tokens, units), WIDE),
            own_activated=VMEM((2, tokens, units), LOW),
            column_sems=DMAS((4, 2, levels)),
            cross_sems=DMAS((4, 2, levels)),
        ),
    )


def backward_planes(ident, kept, segments):
    levels = lax.axis_size("dp") // 2
    blocks, members = (4 * levels, 2 * levels)
    rows, width = kept.planes.shape[1:]
    tokens, size = (blocks * rows, 4 * rows)
    slice_shapes = [array.shape[1:] for array in (kept.out0, kept.out1, kept.out2, kept.out3)]
    shard_shapes = [shard_shape(which, shape, members) for which, shape in enumerate(slice_shapes)]
    units = slice_shapes[2][1]
    unit_lines = units // HD
    scaling = HD ** (-0.5)
    vector_lines = (2 + members) * HEAD_LINES

    def landing(which):
        shape = slice_shapes[which]
        if by_rows(which):
            return VMEM((2, levels, shape[0], shape[1] // members), LOW)
        return VMEM((2, levels, shape[0] // members, shape[1]), LOW)

    def kernel(refs, plane, greet, sends, copies):
        own_block = span(plane.block, rows)
        back = Return(
            plane,
            [refs.grad0, refs.grad1, refs.grad2, refs.grad3],
            [refs.landed0, refs.landed1, refs.landed2, refs.landed3],
            [refs.shard0, refs.shard1, refs.shard2, refs.shard3],
            refs,
            sends,
            copies,
        )
        acts = Outward(plane, refs.acts, refs.acts_sems)
        ends = Outward(plane, refs.input_grads, refs.ends_sems)

        def load(layer):
            return [
                copies.start(refs.out3.at[layer], refs.w3),
                copies.start(refs.preact.at[layer], refs.own_preact),
                copies.start(refs.out2.at[layer], refs.w2),
                copies.start(refs.activated.at[layer], refs.own_activated),
                copies.start(refs.rows_b.at[layer], refs.own_rows),
                copies.start(refs.out1.at[layer], refs.w1),
                copies.start(refs.out0.at[layer], refs.w0),
                copies.start(refs.all_queries.at[layer], refs.queries),
                copies.start(refs.all_keys.at[layer], refs.keys),
                copies.start(refs.all_values.at[layer], refs.values),
                copies.start(refs.all_mixed.at[layer], refs.mixed),
                copies.start(refs.all_totals.at[layer], refs.log_total),
            ]

        loads = load(1)
        first = copies.start(refs.gathered, refs.rows.at[0])
        greet()
        acts.give(0, refs.leaving.at[0], sends, copies)
        acts.give(1, refs.leaving.at[1], sends, copies)

        for layer in (1, 0):
            number = 2 * (1 - layer)
            norms = refs.norms.at[layer]
            vectors = refs.vectors.at[layer]
            held, sems = (refs.rows.at[number % 2], refs.gather_sems.at[number % 2])
            phase = Sends(refs.phase_sems)
            low = refs.planes[1] if layer == 1 else refs.leaving_grads[1].astype(LOW)
            vectors[5:6] = jnp.sum(low.astype(WIDE), axis=0, keepdims=True)
            refs.unit_sums[layer] = jnp.zeros((1, units), WIDE)
            if layer == 0:
                held[own_block] = low
                gather = Gather(plane, phase, held, sems)
                gather.open()
            else:
                copies.wait(first)
            copies.wait(loads[0], loads[1])

            def slope(step, zz):
                group = span(zz, size)
                grad_act = dot_back(held[group], refs.w3[...])
                value = refs.own_preact[group]
                rise = 0.5 * (1.0 + lax.erf(value * math.sqrt(0.5))) + value * jnp.exp(
                    -0.5 * value * value
                ) * (1.0 / math.sqrt(2.0 * math.pi))
                grad_pre = (grad_act * rise).astype(LOW)
                refs.grad_pre[group] = grad_pre
                refs.unit_sums[layer] += jnp.sum(grad_pre.astype(WIDE), axis=0, keepdims=True)

            if layer == 0:
                gather.run(slope, back.tick)
            copies.wait(loads[2])

            def widen_units(step, zz):
                group = span(zz, size)
                if layer == 1:
                    slope(step, zz)
                for cut in range(0, width, CUT):
                    refs.part[group, cut : cut + CUT] = dot_back(
                        refs.grad_pre[group], refs.w2[cut : cut + CUT]
                    ).astype(LOW)

            def down_product(at, carry):
                cut = span(at, 128)
                refs.grad3[cut] = dot_rows(refs.own_activated[:, cut], held[...]).astype(LOW)
                return carry

            def up_product(at, carry):
                cut = span(at, 256)
                refs.grad2[cut] = dot_rows(refs.own_rows[:, cut], refs.grad_pre[...]).astype(LOW)
                return carry

            def products(at):
                if at == 0:
                    copies.wait(loads[3], loads[4])
                    if layer == 0:
                        back.require(1, 3)
                        back.require(1, 2)
                    lax.fori_loop(0, units // 128, down_product, 0)
                    back.give(layer, 3)
                if at == 1:
                    lax.fori_loop(0, width // 512, up_product, 0)
                if at == 2:
                    lax.fori_loop(width // 512, width // 256, up_product, 0)
                    back.give(layer, 2)

            Scatter(plane, phase, refs, refs.sum).run(widen_units, back.tick, products)
            loads.append(copies.start(refs.rows_a.at[layer], refs.own_rows))
            _, unit, inverse = layer_norm(refs.middle[layer], norms[1:2], norms[1:2])
            vectors[1:2] = jnp.sum(refs.sum[...] * unit, axis=0, keepdims=True)
            vectors[4:5] = jnp.sum(refs.sum[...], axis=0, keepdims=True)
            grad_out = refs.planes[1].astype(WIDE) if layer == 1 else refs.leaving_grads[1].astype(LOW).astype(WIDE)
            grad_middle = grad_out + norm_back(refs.sum[...], unit, inverse, norms[1:2])
            phase.finish()

            number = number + 1
            held, sems = (refs.rows.at[number % 2], refs.gather_sems.at[number % 2])
            phase = Sends(refs.phase_sems)
            refs.grad_middle[...] = grad_middle
            low = grad_middle.astype(LOW)
            held[own_block] = low
            gather = Gather(plane, phase, held, sems)
            gather.open()
            vectors[3:4] = jnp.sum(low.astype(WIDE), axis=0, keepdims=True)
            refs.grad_keys[...] = jnp.zeros_like(refs.grad_keys)
            refs.grad_values[...] = jnp.zeros_like(refs.grad_values)
            copies.wait(loads[5], *loads[7:12])

            def attend(step, zz):
                group = span(zz, size)
                live = (refs.query_segment[group] >= 0).astype(WIDE)
                grad_mixed = (
                    dot_back(held[group], refs.w1[...]).astype(LOW) * live
                ).astype(LOW)
                allowed = visible(refs, group, size, tokens)
                queries = refs.queries[group]
                scores = dot_back(queries, refs.keys[...]) * scaling
                scores = jnp.where(allowed, scores, NEG_FILL)
                probs = jnp.exp(scores - refs.log_total[group])
                grad_probs = dot_back(grad_mixed, refs.values[...])
                delta = jnp.sum(probs * grad_probs, axis=-1, keepdims=True)
                grad_scores = jnp.where(allowed, probs * (grad_probs - delta), 0.0).astype(LOW)
                refs.grad_proj[group, :HD] = (dot(grad_scores, refs.keys[...]) * scaling).astype(LOW)
                refs.grad_keys[...] += dot_rows(grad_scores, queries)
                refs.grad_values[...] += dot_rows(probs.astype(LOW), grad_mixed)

            gather.run(attend, back.tick)
            refs.grad_proj[:, HD : 2 * HD] = (refs.grad_keys[...] * scaling).astype(LOW)
            refs.grad_proj[:, 2 * HD :] = refs.grad_values[...].astype(LOW)
            copies.wait(loads[6])

            def widen_heads(step, zz):
                group = span(zz, size)
                for cut in range(0, width, CUT):
                    refs.part[group, cut : cut + CUT] = dot_back(
                        refs.grad_proj[group], refs.w0[cut : cut + CUT]
                    ).astype(LOW)

            def qkv_product(at, carry):
                cut = span(at, 256)
                refs.grad0[cut] = dot_rows(refs.own_rows[:, cut], refs.grad_proj[...]).astype(LOW)
                return carry

            def more_products(at):
                if at == 0:
                    sums = jnp.sum(refs.grad_proj[...].astype(WIDE), axis=0, keepdims=True)
                    refs.head_sums[layer, 0:1] = sums[:, :HD]
                    refs.head_sums[layer, 1:2] = sums[:, 2 * HD :]
                    copies.wait(loads[12])
                    if layer == 0:
                        back.require(1, 1)
                        back.require(1, 0)
                if at == 1:
                    refs.grad1[...] = dot_rows(refs.mixed[...], held[...]).astype(LOW)
                    back.give(layer, 1)
                    lax.fori_loop(0, width // 1024, qkv_product, 0)
                if at == 2:
                    lax.fori_loop(width // 1024, width // 512, qkv_product, 0)
                if at == 3:
                    lax.fori_loop(width // 512, width // 256, qkv_product, 0)
                    back.give(layer, 0)

            Scatter(plane, phase, refs, refs.sum).run(widen_heads, back.tick, more_products)
            if layer == 1:
                loads = load(0)
            entering = refs.planes[0] if layer == 0 else refs.leaving[0]
            _, unit, inverse = layer_norm(entering.astype(WIDE), norms[0:1], norms[0:1])
            vectors[0:1] = jnp.sum(refs.sum[...] * unit, axis=0, keepdims=True)
            vectors[2:3] = jnp.sum(refs.sum[...], axis=0, keepdims=True)
            refs.leaving_grads[layer] = refs.grad_middle[...] + norm_back(
                refs.sum[...], unit, inverse, norms[0:1]
            )
            ends.give(layer, refs.leaving_grads.at[layer], sends, copies)
            phase.finish()

        tail = SimpleNamespace(
            part=refs.vector_part,
            from_sibling=refs.vector_from_sibling,
            from_across=refs.vector_from_across,
            from_behind=refs.vector_from_behind,
            total=refs.vector_total,
            sibling_sems=refs.vector_sibling_sems,
            across_sems=refs.vector_across_sems,
            behind_sems=refs.vector_behind_sems,
        )
        tail.part[...] = jnp.zeros_like(tail.part)
        for layer in (0, 1):
            own = [refs.head_sums[layer]]
            for at in range(unit_lines):
                own.append(refs.unit_sums[layer, :, at * HD : (at + 1) * HD])
            own.append(jnp.zeros((HEAD_LINES - 2 - unit_lines, HD), WIDE))
            own = jnp.concatenate(own, axis=0)
            for z in range(levels):
                for y in (0, 1):
                    base = (z * 4 + layer * 2 + y) * vector_lines
                    for x in (0, 1):
                        cut = (z * 4 + x * 2 + y) * HD
                        line = base + x * HEAD_LINES
                        tail.part[line : line + HEAD_LINES] = refs.vectors[layer, :, cut : cut + HD]
                start = (z * 4 + layer * 2 + plane.y) * vector_lines
                start = start + (2 + plane.member) * HEAD_LINES
                tail.part[pl.ds(pl.multiple_of(start, HEAD_LINES), HEAD_LINES)] = own
        phase = Sends(refs.phase_sems)
        Scatter(plane, phase, tail, refs.vector_sum).run(lambda step, zz: None, back.tick)
        phase.start(True, refs.vector_sum, refs.vector_other, refs.pair_sem.at[0], plane.over)
        await_block(refs.vector_other, refs.pair_sem.at[0], plane.over)
        refs.vector_out[...] = refs.vector_sum[...] + refs.vector_other[...]
        acts.finish()
        back.finish()
        ends.finish()
        phase.finish()

    lasting = Return.count(levels)
    outward = Outward.count()
    vector = scatter_scratch(vector_lines, HD, levels, 1, WIDE)
    return launch(
        "backward_planes",
        ident,
        kernel,
        (
            lasting[0] + 2 * outward[0],
            Gather.count(levels, CHUNKS) + Scatter.count(levels, SUM_CHUNKS),
            lasting[1] + 2 * outward[1] + 2 * 13 + 1,
        ),
        dict(
            planes=(kept.planes, VMEM),
            leaving=(kept.leaving, VMEM),
            middle=(kept.middle, VMEM),
            norms=(kept.norms, VMEM),
            query_segment=(segments[0], VMEM),
            key_segment=(segments[1], VMEM),
            all_queries=(kept.queries, HBM),
            all_keys=(kept.keys, HBM),
            all_values=(kept.values, HBM),
            all_mixed=(kept.mixed, HBM),
            all_totals=(kept.log_total, HBM),
            gathered=(kept.gathered, HBM),
            rows_a=(kept.rows_a, HBM),
            rows_b=(kept.rows_b, HBM),
            preact=(kept.preact, HBM),
            activated=(kept.activated, HBM),
            out0=(kept.out0, HBM),
            out1=(kept.out1, HBM),
            out2=(kept.out2, HBM),
            out3=(kept.out3, HBM),
        ),
        dict(
            acts=((2, rows, width), LOW, HBM),
            input_grads=((2, rows, width), WIDE, HBM),
            shard0=(shard_shapes[0], LOW, HBM),
            shard1=(shard_shapes[1], LOW, HBM),
            shard2=(shard_shapes[2], LOW, HBM),
            shard3=(shard_shapes[3], LOW, HBM),
            vector_out=((vector_lines, HD), WIDE, VMEM),
        ),
        dict(
            scatter_scratch(rows, width, levels, SUM_CHUNKS),
            rows=VMEM((2, tokens, width), LOW),
            gather_sems=DMAS((2, blocks, CHUNKS)),
            w0=VMEM(slice_shapes[0], LOW),
            w1=VMEM(slice_shapes[1], LOW),
            w2=VMEM(slice_shapes[2], LOW),
            w3=VMEM(slice_shapes[3], LOW),
            own_preact=VMEM((tokens, units), WIDE),
            own_activated=VMEM((tokens, units), LOW),
            own_rows=VMEM((tokens, width), LOW),
            grad_pre=VMEM((tokens, units), LOW),
            grad_proj=VMEM((tokens, 3 * HD), LOW),
            queries=VMEM((tokens, HD), LOW),
            keys=VMEM((tokens, HD), LOW),
            values=VMEM((tokens, HD), LOW),
            mixed=VMEM((tokens, HD), LOW),
            log_total=VMEM((tokens, 1), WIDE),
            grad_keys=VMEM((tokens, HD), WIDE),
            grad_values=VMEM((tokens, HD), WIDE),
            grad_middle=VMEM((rows, width), WIDE),
            leaving_grads=VMEM((2, rows, width), WIDE),
            grad0=VMEM(slice_shapes[0], LOW),
            grad1=VMEM(slice_shapes[1], LOW),
            grad2=VMEM(slice_shapes[2], LOW),
            grad3=VMEM(slice_shapes[3], LOW),
            landed0=landing(0),
            landed1=landing(1),
            landed2=landing(2),
            landed3=landing(3),
            column_sems=DMAS((4, 2, levels)),
            cross_sems=DMAS((4, 2, levels)),
            acts_sems=DMAS((2,)),
            ends_sems=DMAS((2,)),
            pair_sem=DMAS((1,)),
            vectors=VMEM((2, HEAD_LINES, width), WIDE),
            head_sums=VMEM((2, 2, HD), WIDE),
            unit_sums=VMEM((2, 1, units), WIDE),
            vector_part=vector["part"],
            vector_from_sibling=vector["from_sibling"],
            vector_from_across=vector["from_across"],
            vector_from_behind=vector["from_behind"],
            vector_total=vector["total"],
            vector_sum=vector["sum"],
            vector_other=VMEM((vector_lines, HD), WIDE),
            vector_sibling_sems=vector["sibling_sems"],
            vector_across_sems=vector["across_sems"],
            vector_behind_sems=vector["behind_sems"],
        ),
    )


def plane_body(
    boundary,
    doc_lengths,
    qkv_weight,
    qv_bias,
    out_weight,
    up_weight,
    up_bias,
    down_weight,
    norm_gains,
    norm_biases,
):
    plane = Plane()
    levels = plane.levels
    members = 2 * levels
    head_cut = qv_bias.shape[3]
    block_shard = up_bias.shape[1]
    own_blocks = block_shard // members

    def lines(piece):
        return piece.reshape(-1, HD)

    packed = jnp.concatenate(
        (
            lines(norm_gains[0]),
            lines(norm_biases[0]),
            jnp.zeros((HEAD_LINES - NORM_LINES, HD), LOW),
            lines(qv_bias[0]),
            lines(up_bias[0]),
            jnp.zeros((LINES - HEAD_LINES - 2 - up_bias[0].size // HD, HD), LOW),
        )
    )
    depth = qkv_weight.shape[1]
    by_head = (
        qkv_weight[0]
        .reshape(depth, 3, members, HD)
        .transpose(0, 2, 1, 3)
        .reshape(depth, members * 3 * HD)
    )
    lengths = lax.dynamic_index_in_dim(doc_lengths, plane.x, 0, keepdims=False)
    tokens = boundary.shape[2] * 4 * levels
    _, segment, live, _, _, _ = visibility(lengths, 0, tokens, tokens)
    segments = (jnp.where(live, segment, -1)[:, None], segment[None, :])

    kept = forward_planes(
        0, boundary[0], packed, segments, (by_head, out_weight[0], up_weight[0], down_weight[0])
    )
    end = backward_planes(1, kept, segments)

    summed = end.vector_out.reshape(2 + members, HEAD_LINES, HD)
    norms = lax.dynamic_index_in_dim(summed, plane.x, 0, keepdims=False)
    by_member = lax.dynamic_slice_in_dim(
        summed[2:], (plane.z * 2 + plane.x) * head_cut, head_cut, axis=2
    )
    qkv_shard = (
        end.shard0.reshape(depth, members, 3, HD)
        .transpose(0, 2, 1, 3)
        .reshape(depth, 3, members * HD)
    )
    return (
        end.acts[None],
        end.input_grads[None],
        qkv_shard.astype(WIDE)[None],
        by_member[:, :2].transpose(1, 0, 2)[None],
        end.shard1.astype(WIDE)[None],
        end.shard2.astype(WIDE)[None],
        by_member[:, 2 : 2 + own_blocks].reshape(1, block_shard, head_cut),
        end.shard3.astype(WIDE)[None],
        norms[None, :2],
        norms[None, 2:NORM_LINES],
    )


def fits_plane(mesh):
    return mesh.shape["dp"] == 8 and mesh.shape["tensor"] == 2 and mesh.shape["section"] == 2


def solution(mesh):
    placed = (
        P("section", None, ("dp", "tensor"), None),
        P(),
        P("section", "dp", None, "tensor"),
        P("section", None, "tensor", "dp"),
        P("section", "tensor", "dp"),
        P("section", "dp", "tensor"),
        P("section", "tensor", "dp"),
        P("section", "tensor", "dp"),
        P("section", None, ("dp", "tensor")),
        P("section", None, ("dp", "tensor")),
    )
    return jax.shard_map(
        plane_body if fits_plane(mesh) else body,
        mesh=mesh,
        in_specs=placed,
        out_specs=(
            P("section", None, ("dp", "tensor"), None),
            P("section", None, ("dp", "tensor"), None),
            P("section", "dp", None, "tensor"),
            P("section", None, "tensor", "dp"),
            P("section", "tensor", "dp"),
            P("section", "dp", "tensor"),
            P("section", "tensor", "dp"),
            P("section", "tensor", "dp"),
            P("section", None, ("dp", "tensor")),
            P("section", None, ("dp", "tensor")),
        ),
        check_vma=False,
    )
```

```python
from functools import partial
import math
from types import SimpleNamespace

import jax
import jax.numpy as jnp
from jax import lax
from jax.experimental import pallas as pl
from jax.experimental.pallas import tpu as pltpu
from jax.sharding import PartitionSpec as P

HD = 128


EPSILON = 1e-05
NEG_FILL = -1e30
MESH = pl.DeviceIdType.MESH


def from_behind(value, axis, steps):
    count = lax.axis_size(axis)
    first, last = (max(0, -steps), min(count, count - steps))
    return lax.ppermute(value, axis, [(source, source + steps) for source in range(first, last)])


def layer_norm(hidden, gain, shift):
    average = jnp.mean(hidden, axis=-1, keepdims=True)
    centred = hidden - average
    variance = jnp.mean(centred * centred, axis=-1, keepdims=True)
    inverse = lax.rsqrt(variance + EPSILON)
    normed = centred * inverse
    return (normed * gain + shift, normed, inverse)


def norm_back(grad_out, normed, inverse, gain):
    scaled = grad_out * gain
    return inverse * (
        scaled
        - jnp.mean(scaled, axis=-1, keepdims=True)
        - normed * jnp.mean(scaled * normed, axis=-1, keepdims=True)
    )


def visibility(lengths, dp_index, rows_dp, seq_len):
    per_seq = seq_len // lengths.shape[0]
    docs = lengths.shape[1]
    key_pos = jnp.arange(seq_len, dtype=jnp.int32)
    seq_of = key_pos // per_seq
    local = key_pos - seq_of * per_seq
    doc_ends = jnp.cumsum(lengths, axis=1)
    ends_row = jnp.take(doc_ends, seq_of, axis=0)
    key_seg = seq_of * (docs + 1) + jnp.sum((local[:, None] >= ends_row).astype(jnp.int32), axis=1)
    key_live = local < ends_row[:, docs - 1]
    start_row = dp_index * rows_dp
    query_pos = start_row + jnp.arange(rows_dp, dtype=jnp.int32)
    query_seg = lax.dynamic_slice_in_dim(key_seg, start_row, rows_dp)
    query_live = lax.dynamic_slice_in_dim(key_live, start_row, rows_dp)
    return (query_pos, query_seg, query_live, key_pos, key_seg, key_live)


def widen(rows_low):
    return lax.all_gather(rows_low, "tensor", axis=0, tiled=True)


def narrow(partial_rows):
    return lax.psum_scatter(
        partial_rows.astype(jnp.bfloat16), "tensor", scatter_dimension=0, tiled=True
    ).astype(jnp.float32)


def fetch_weights(
    qkv_weight, qv_bias, out_weight, up_weight, up_bias, down_weight, norm_gains, norm_biases
):
    w_qkv, b_qv, w_out, w_up, b_up, w_down = (
        lax.all_gather(qkv_weight[0], "dp", axis=0, tiled=True),
        lax.all_gather(qv_bias[0], "dp", axis=2, tiled=True),
        lax.all_gather(out_weight[0], "dp", axis=1, tiled=True),
        lax.all_gather(up_weight[0], "dp", axis=0, tiled=True),
        lax.all_gather(up_bias[0], "dp", axis=1, tiled=True),
        lax.all_gather(down_weight[0], "dp", axis=1, tiled=True),
    )
    gain_rows, bias_rows = (
        lax.all_gather(norm_gains[0], ("dp", "tensor"), axis=1, tiled=True),
        lax.all_gather(norm_biases[0], ("dp", "tensor"), axis=1, tiled=True),
    )
    return (
        w_qkv,
        b_qv.reshape(2, -1).astype(jnp.float32),
        w_out,
        w_up,
        b_up.reshape(-1).astype(jnp.float32),
        w_down,
        gain_rows.astype(jnp.float32),
        bias_rows.astype(jnp.float32),
    )


def block_scores(q_heads, key_block, kpos_block, kseg_block, sight):
    scores = jnp.einsum(
        "qhd,khd->hqk", q_heads, key_block, preferred_element_type=jnp.float32
    ) * HD ** (-0.5)
    allowed = (
        (sight[1][:, None] == kseg_block[None, :])
        & (kpos_block[None, :] <= sight[0][:, None])
        & sight[2][:, None]
    )
    return (jnp.where(allowed[None], scores, NEG_FILL), allowed)


def key_blocks(keys, values, sight):
    seq_len = keys.shape[0]
    block_rows = math.gcd(seq_len, 512)
    blocks = seq_len // block_rows
    heads = keys.shape[1] // HD
    return (
        keys.reshape(blocks, block_rows, heads, HD),
        values.reshape(blocks, block_rows, heads, HD),
        sight[3].reshape(blocks, block_rows),
        sight[4].reshape(blocks, block_rows),
    )


def attend(queries, keys, values, sight):
    rows = queries.shape[0]
    heads = queries.shape[1] // HD
    q_heads = queries.reshape(rows, heads, HD)
    stacked = key_blocks(keys, values, sight)

    def find_scale(carry, pieces):
        top, total = carry
        scores, allowed = block_scores(q_heads, pieces[0], pieces[2], pieces[3], sight)
        new_top = jnp.maximum(top, jnp.max(scores, axis=-1))
        total = total * jnp.exp(top - new_top) + jnp.sum(
            jnp.exp(scores - new_top[..., None]), axis=-1
        )
        return ((new_top, total), None)

    start = (jnp.full((heads, rows), -jnp.inf, jnp.float32), jnp.zeros((heads, rows), jnp.float32))
    (top, total), ignored = lax.scan(find_scale, start, stacked)
    log_total = top + jnp.log(total)

    def weigh(carry, pieces):
        scores, allowed = block_scores(q_heads, pieces[0], pieces[2], pieces[3], sight)
        probs = jnp.exp(scores - log_total[..., None]).astype(jnp.bfloat16)
        return (
            carry
            + jnp.einsum("hqk,khd->qhd", probs, pieces[1], preferred_element_type=jnp.float32),
            None,
        )

    heads_out, ignored = lax.scan(weigh, jnp.zeros((rows, heads, HD), jnp.float32), stacked)
    return (heads_out, log_total, q_heads)


def attend_back(q_heads, keys, values, sight, log_total, grad_heads, delta):
    seq_len = keys.shape[0]
    stacked = key_blocks(keys, values, sight)
    scaling = HD ** (-0.5)

    def one_step(grad_q, pieces):
        scores, allowed = block_scores(q_heads, pieces[0], pieces[2], pieces[3], sight)
        probs = jnp.exp(scores - log_total[..., None])
        grad_p = jnp.einsum(
            "qhd,khd->hqk", grad_heads, pieces[1], preferred_element_type=jnp.float32
        )
        grad_s = jnp.where(allowed[None], probs * (grad_p - delta[..., None]), 0.0).astype(
            jnp.bfloat16
        )
        grad_q = (
            grad_q
            + jnp.einsum("hqk,khd->qhd", grad_s, pieces[0], preferred_element_type=jnp.float32)
            * scaling
        )
        grad_v = jnp.einsum(
            "hqk,qhd->khd",
            probs.astype(jnp.bfloat16),
            grad_heads,
            preferred_element_type=jnp.float32,
        )
        grad_k = (
            jnp.einsum("hqk,qhd->khd", grad_s, q_heads, preferred_element_type=jnp.float32)
            * scaling
        )
        return (grad_q, (grad_k, grad_v))

    grad_q, outputs = lax.scan(one_step, jnp.zeros(q_heads.shape, jnp.float32), stacked)
    return (grad_q, outputs[0].reshape(seq_len, -1), outputs[1].reshape(seq_len, -1))


def forward(entering, weights, sight):
    w_qkv, b_qv, w_out, w_up, b_up, w_down, gain_rows, bias_rows = weights
    hidden = entering.astype(jnp.float32)
    normed_a, unit_a, inverse_a = layer_norm(hidden, gain_rows[0], bias_rows[0])
    rows_a = widen(normed_a.astype(jnp.bfloat16))
    projected = jnp.einsum("rd,djh->rjh", rows_a, w_qkv, preferred_element_type=jnp.float32)
    queries = (projected[:, 0] + b_qv[0]).astype(jnp.bfloat16)
    keys_own = projected[:, 1].astype(jnp.bfloat16)
    values_own = (projected[:, 2] + b_qv[1]).astype(jnp.bfloat16)
    keys, values = (
        lax.all_gather(keys_own, "dp", axis=0, tiled=True),
        lax.all_gather(values_own, "dp", axis=0, tiled=True),
    )
    heads_out, log_total, q_heads = attend(queries, keys, values, sight)
    live_rows = sight[2].astype(jnp.float32)
    mixed_low = (heads_out.reshape(heads_out.shape[0], -1) * live_rows[:, None]).astype(
        jnp.bfloat16
    )
    middle = (
        hidden
        + narrow(jnp.dot(mixed_low, w_out, preferred_element_type=jnp.float32))
        + bias_rows[1]
    )
    normed_b, unit_b, inverse_b = layer_norm(middle, gain_rows[1], bias_rows[2])
    rows_b = widen(normed_b.astype(jnp.bfloat16))
    preact = jnp.dot(rows_b, w_up, preferred_element_type=jnp.float32) + b_up
    activated = jax.nn.gelu(preact, approximate=False).astype(jnp.bfloat16)
    result = (
        middle
        + narrow(jnp.dot(activated, w_down, preferred_element_type=jnp.float32))
        + bias_rows[3]
    )
    saved = (
        unit_a,
        inverse_a,
        rows_a,
        q_heads,
        keys,
        values,
        heads_out,
        log_total,
        mixed_low,
        unit_b,
        inverse_b,
        rows_b,
        preact,
        activated,
    )
    return (result, saved)


def backward(saved, grad_out, weights, sight):
    w_qkv, b_qv, w_out, w_up, b_up, w_down, gain_rows, bias_rows = weights
    (
        unit_a,
        inverse_a,
        rows_a,
        q_heads,
        keys,
        values,
        heads_out,
        log_total,
        mixed_low,
        unit_b,
        inverse_b,
        rows_b,
        preact,
        activated,
    ) = saved
    rows = rows_a.shape[0]
    grad_branch = grad_out.astype(jnp.bfloat16)
    down_bias_grad = jnp.sum(grad_branch.astype(jnp.float32), axis=0)
    wide_branch = widen(grad_branch)
    grad_act = jnp.einsum("rd,fd->rf", wide_branch, w_down, preferred_element_type=jnp.float32)
    ignored, gelu_pull = jax.vjp(partial(jax.nn.gelu, approximate=False), preact)
    grad_pre = gelu_pull(grad_act)[0].astype(jnp.bfloat16)
    up_bias_grad = jnp.sum(grad_pre.astype(jnp.float32), axis=0)
    grad_normed_b = narrow(
        jnp.einsum("rf,df->rd", grad_pre, w_up, preferred_element_type=jnp.float32)
    )
    gain_b_grad = jnp.sum(grad_normed_b * unit_b, axis=0)
    shift_b_grad = jnp.sum(grad_normed_b, axis=0)
    grad_middle = grad_out + norm_back(grad_normed_b, unit_b, inverse_b, gain_rows[1])
    grad_attn = grad_middle.astype(jnp.bfloat16)
    out_bias_grad = jnp.sum(grad_attn.astype(jnp.float32), axis=0)
    wide_attn = widen(grad_attn)
    live_rows = sight[2].astype(jnp.bfloat16)
    grad_flat = (
        jnp.einsum("rd,ed->re", wide_attn, w_out, preferred_element_type=jnp.float32).astype(
            jnp.bfloat16
        )
        * live_rows[:, None]
    )
    grad_heads = grad_flat.reshape(heads_out.shape)
    delta = jnp.einsum("qhd,qhd->hq", grad_heads.astype(jnp.float32), heads_out)
    grad_q, grad_k_all, grad_v_all = attend_back(
        q_heads, keys, values, sight, log_total, grad_heads, delta
    )
    grad_k, grad_v = (
        lax.psum_scatter(
            grad_k_all.astype(jnp.bfloat16), "dp", scatter_dimension=0, tiled=True
        ).astype(jnp.float32),
        lax.psum_scatter(
            grad_v_all.astype(jnp.bfloat16), "dp", scatter_dimension=0, tiled=True
        ).astype(jnp.float32),
    )
    grad_proj = jnp.stack((grad_q.reshape(rows, -1), grad_k, grad_v), axis=1).astype(jnp.bfloat16)
    proj_sums = jnp.sum(grad_proj.astype(jnp.float32), axis=0)
    qv_grad = jnp.stack((proj_sums[0], proj_sums[2]))
    grad_normed_a = narrow(
        jnp.einsum("rjh,djh->rd", grad_proj, w_qkv, preferred_element_type=jnp.float32)
    )
    gain_a_grad = jnp.sum(grad_normed_a * unit_a, axis=0)
    shift_a_grad = jnp.sum(grad_normed_a, axis=0)
    grad_in = grad_middle + norm_back(grad_normed_a, unit_a, inverse_a, gain_rows[0])
    gains_grad = jnp.stack((gain_a_grad, gain_b_grad))
    biases_grad = jnp.stack((shift_a_grad, out_bias_grad, shift_b_grad, down_bias_grad))
    factors = (rows_b, grad_pre, activated, wide_branch, mixed_low, wide_attn, rows_a, grad_proj)
    vectors = (qv_grad, up_bias_grad, gains_grad, biases_grad)
    return (grad_in, factors, vectors)


def weight_products(factors):
    rows_b, grad_pre, activated, wide_branch, mixed_low, wide_attn, rows_a, grad_proj = factors
    down_grad = jnp.einsum("rf,rd->fd", activated, wide_branch, preferred_element_type=jnp.float32)
    up_grad = jnp.einsum("rd,rf->df", rows_b, grad_pre, preferred_element_type=jnp.float32)
    out_grad = jnp.einsum("re,rd->ed", mixed_low, wide_attn, preferred_element_type=jnp.float32)
    qkv_grad = jnp.einsum("rd,rjh->djh", rows_a, grad_proj, preferred_element_type=jnp.float32)
    return (qkv_grad, out_grad, up_grad, down_grad)


def assemble(products, vectors):
    qkv_grad, out_grad, up_grad, down_grad = products
    qv_grad, up_bias_grad, gains_grad, biases_grad = vectors
    return (qkv_grad, qv_grad, out_grad, up_grad, up_bias_grad, down_grad, gains_grad, biases_grad)


def reduce_grads(local_grads):
    qkv_grad, qv_grad, out_grad, up_grad, up_bias_grad, down_grad, gains_grad, biases_grad = (
        local_grads
    )
    heads = qv_grad.shape[1] // HD
    shards = (
        lax.psum_scatter(
            qkv_grad[None].astype(jnp.bfloat16), "dp", scatter_dimension=1, tiled=True
        ).astype(jnp.float32),
        lax.psum_scatter(
            qv_grad.reshape(1, 2, heads, HD).astype(jnp.bfloat16),
            "dp",
            scatter_dimension=3,
            tiled=True,
        ).astype(jnp.float32),
        lax.psum_scatter(
            out_grad[None].astype(jnp.bfloat16), "dp", scatter_dimension=2, tiled=True
        ).astype(jnp.float32),
        lax.psum_scatter(
            up_grad[None].astype(jnp.bfloat16), "dp", scatter_dimension=1, tiled=True
        ).astype(jnp.float32),
        lax.psum_scatter(
            up_bias_grad.reshape(1, -1, HD).astype(jnp.bfloat16),
            "dp",
            scatter_dimension=2,
            tiled=True,
        ).astype(jnp.float32),
        lax.psum_scatter(
            down_grad[None].astype(jnp.bfloat16), "dp", scatter_dimension=2, tiled=True
        ).astype(jnp.float32),
    )
    vectors = (
        lax.psum_scatter(gains_grad[None], ("dp", "tensor"), scatter_dimension=2, tiled=True),
        lax.psum_scatter(biases_grad[None], ("dp", "tensor"), scatter_dimension=2, tiled=True),
    )
    return tuple(shards) + tuple(vectors)


def body(
    boundary,
    doc_lengths,
    qkv_weight,
    qv_bias,
    out_weight,
    up_weight,
    up_bias,
    down_weight,
    norm_gains,
    norm_biases,
):
    section_index = lax.axis_index("section")
    on_first = section_index == 0
    own_part = boundary[0]
    batches = own_part.shape[0]
    rows_dp = own_part.shape[1] * lax.axis_size("tensor")
    seq_len = rows_dp * lax.axis_size("dp")
    dp_index = lax.axis_index("dp")
    sources = (
        qkv_weight,
        qv_bias,
        out_weight,
        up_weight,
        up_bias,
        down_weight,
        norm_gains,
        norm_biases,
    )
    fixed_weights = fetch_weights(*sources)

    def current():
        return fixed_weights

    def sight_for(batch_at):
        lengths = lax.dynamic_index_in_dim(doc_lengths, batch_at, 0, keepdims=False)
        return visibility(lengths, dp_index, rows_dp, seq_len)

    def pick(first_value, second_value):
        return jnp.where(on_first, first_value, second_value)

    received = jnp.zeros_like(own_part[0])
    kept_ticks, exits = ([], [])
    for tick_index in range(batches + 1):
        entering = jnp.where(on_first, own_part[min(tick_index, batches - 1)], received)
        batch_at = jnp.clip(tick_index - section_index, 0, batches - 1)
        result, saved = forward(entering, current(), sight_for(batch_at))
        leaving = result.astype(jnp.bfloat16)
        kept_ticks.append(saved)
        exits.append(leaving)
        if tick_index < batches:
            received = from_behind(leaving, "section", 1)
    acts = jnp.stack(
        [jnp.where(on_first, exits[number], exits[number + 1]) for number in range(batches)]
    )[None]
    returned = jnp.zeros_like(own_part[0])
    summed = None
    vector_sum = None
    factor_ticks = []
    leaving_grads = []
    for tick_index in range(batches + 1):
        own_grad = own_part[min(tick_index, batches - 1)].astype(jnp.float32)
        if tick_index == batches:
            own_grad = jnp.zeros_like(own_grad)
        grad_out = jnp.where(on_first, returned.astype(jnp.float32), own_grad)
        saved = jax.tree.map(
            pick, kept_ticks[max(tick_index - 1, 0)], kept_ticks[min(tick_index + 1, batches)]
        )
        batch_at = jnp.where(on_first, max(tick_index - 1, 0), min(tick_index, batches - 1))
        grad_in, factors, vectors = backward(saved, grad_out, current(), sight_for(batch_at))
        leaving_grads.append(grad_in)
        if tick_index < batches:
            returned = from_behind(grad_in.astype(jnp.bfloat16), "section", -1)
        factor_ticks.append(factors)
        vector_sum = (
            vectors
            if vector_sum is None
            else tuple((former + latter for former, latter in zip(vector_sum, vectors)))
        )
    joined = tuple(
        (
            jnp.concatenate([entry[number] for entry in factor_ticks], axis=0)
            for number in range(len(factor_ticks[0]))
        )
    )
    summed = reduce_grads(assemble(weight_products(joined), vector_sum))
    input_grads = jnp.stack(
        [
            jnp.where(on_first, leaving_grads[number + 1], leaving_grads[number])
            for number in range(batches)
        ]
    )[None]
    return (acts, input_grads) + tuple(summed)


LOW, WIDE = (jnp.bfloat16, jnp.float32)
HBM, VMEM, DMAS = (pl.ANY, pltpu.VMEM, pltpu.SemaphoreType.DMA)


def dot(left, right):
    return jnp.dot(left, right, preferred_element_type=WIDE)


def dot_back(left, right):
    return lax.dot_general(left, right, (((1,), (1,)), ((), ())), preferred_element_type=WIDE)


def dot_rows(left, right):
    return lax.dot_general(left, right, (((0,), (0,)), ((), ())), preferred_element_type=WIDE)


def device(core, z, x, y):
    return (core, z * 2 + x, y)


class Plane:
    def __init__(self):
        dp = lax.axis_index("dp")
        self.levels = lax.axis_size("dp") // 2
        self.core, self.y = (lax.axis_index("section"), lax.axis_index("tensor"))
        self.z, self.x = (dp // 2, lax.rem(dp, 2))
        self.sibling = device(1 - self.core, self.z, self.x, self.y)
        self.across = device(self.core, self.z, self.x, 1 - self.y)
        self.over = device(self.core, self.z, 1 - self.x, self.y)
        self.corner = device(1 - self.core, self.z, 1 - self.x, self.y)
        self.member = self.z * 2 + self.core
        self.block = self.z * 4 + self.core * 2 + self.y

    def along(self, z):
        return device(self.core, jnp.clip(z, 0, self.levels - 1), self.x, self.y)

    def partners(self):
        partners = [self.across, self.over, self.corner]
        for step in range(self.levels):
            zz = lax.rem(self.z + step, self.levels)
            for other in (0, 1):
                if step or other:
                    core = 1 - self.core if other else self.core
                    partners.append(device(core, zz, self.x, self.y))
        return partners

    def nearest(self):
        tables = []
        for z in range(self.levels):
            tables.append(sorted(range(self.levels), key=lambda zz: (abs(zz - z), zz)))
        found = []
        for place in range(self.levels):
            number = jnp.int32(tables[0][place])
            for z in range(1, self.levels):
                number = jnp.where(self.z == z, tables[z][place], number)
            found.append(number)
        return found


def guarded(present, act):
    if present is True:
        act()
    else:
        pl.when(present)(act)


class Sends:
    def __init__(self, sems):
        self.sems = sems
        self.pending = []

    def start(self, present, source, target, arrived, partner):
        copy = pltpu.make_async_remote_copy(
            src_ref=source,
            dst_ref=target,
            send_sem=self.sems.at[len(self.pending)],
            recv_sem=arrived,
            device_id=partner,
            device_id_type=MESH,
        )
        guarded(present, copy.start)
        self.pending.append([present, copy, False])
        return len(self.pending) - 1

    def wait(self, *numbers):
        for number in numbers:
            present, copy, done = self.pending[number]
            if not done:
                guarded(present, copy.wait_send)
                self.pending[number][2] = True

    def finish(self):
        self.wait(*range(len(self.pending)))


class Copies:
    def __init__(self, sems):
        self.sems = sems
        self.pending = []

    def start(self, source, target, present=True):
        copy = pltpu.make_async_copy(source, target, self.sems.at[len(self.pending)])
        guarded(present, copy.start)
        self.pending.append([present, copy, False])
        return len(self.pending) - 1

    def wait(self, *numbers):
        for number in numbers:
            present, copy, done = self.pending[number]
            if not done:
                guarded(present, copy.wait)
                self.pending[number][2] = True

    def finish(self):
        for number in range(len(self.pending)):
            self.wait(number)


def await_block(block, arrived, partner):
    pltpu.make_async_remote_copy(
        src_ref=block,
        dst_ref=block,
        send_sem=arrived,
        recv_sem=arrived,
        device_id=partner,
        device_id_type=MESH,
    ).wait_recv()


def span(start, size):
    return pl.ds(pl.multiple_of(start * size, size), size)


class Gather:
    def __init__(self, plane, sends, rows, sems):
        self.plane, self.sends, self.rows, self.sems = (plane, sends, rows, sems)
        self.chunks = sems.shape[1]
        self.size = rows.shape[0] // (sems.shape[0] * self.chunks)

    def spot(self, zz, core, y, chunk):
        number = zz * 4 + core * 2 + y
        return (
            self.rows.at[span(number * self.chunks + chunk, self.size)],
            self.sems.at[number, chunk],
        )

    def open(self):
        plane = self.plane
        for chunk in range(self.chunks):
            held, arrived = self.spot(plane.z, plane.core, plane.y, chunk)
            for present, partner in (
                (True, plane.across),
                (plane.z > 0, plane.along(plane.z - 1)),
                (plane.z < plane.levels - 1, plane.along(plane.z + 1)),
                (True, plane.sibling),
            ):
                self.sends.start(present, held, held, arrived, partner)

    def run(self, on_group, tick):
        plane = self.plane
        order = plane.nearest()

        def complete(step):
            zz = order[step]
            for chunk in range(self.chunks):
                held, arrived = self.spot(zz, plane.core, 1 - plane.y, chunk)
                await_block(held, arrived, plane.across)
                self.sends.start(True, held, held, arrived, plane.sibling)
            for yy in (plane.y, 1 - plane.y):
                for chunk in range(self.chunks):
                    held, arrived = self.spot(zz, 1 - plane.core, yy, chunk)
                    await_block(held, arrived, plane.sibling)
            on_group(step, zz)

        for step in range(1, plane.levels):
            zz = order[step]
            onward = jnp.where(zz < plane.z, plane.z + 1, plane.z - 1)
            can_go = (onward >= 0) & (onward < plane.levels)
            for chunk in range(self.chunks):
                held, arrived = self.spot(zz, plane.core, plane.y, chunk)
                await_block(held, arrived, plane.across)
                self.sends.start(can_go, held, held, arrived, plane.along(onward))
                self.sends.start(True, held, held, arrived, plane.across)
                self.sends.start(True, held, held, arrived, plane.sibling)
            tick()
            complete(step - 1)
        complete(plane.levels - 1)
        tick()

    @staticmethod
    def count(levels, chunks):
        return chunks * (4 + 3 * (levels - 1) + levels)


class Scatter:
    def __init__(self, plane, sends, refs, result):
        self.plane, self.sends, self.refs, self.result = (plane, sends, refs, result)
        self.chunks = refs.across_sems.shape[1]
        self.size = result.shape[0] // self.chunks

    @staticmethod
    def count(levels, chunks):
        return chunks * (4 * levels - 1)

    def part(self, zz, core, y, chunk):
        number = (zz * 4 + core * 2 + y) * self.chunks + chunk
        return self.refs.part.at[span(number, self.size)]

    def spot(self, buffer, sems, slot, chunk):
        return buffer.at[slot, span(chunk, self.size)], sems.at[slot, chunk]

    def take(self, buffer, sems, slot, chunk):
        came, arrived = self.spot(buffer, sems, slot, chunk)
        await_block(came, arrived, self.plane.across)
        return came[...].astype(WIDE)

    def pair(self, zz, y, chunk):
        refs = self.refs
        own = self.part(zz, self.plane.core, y, chunk)[...].astype(WIDE)
        return own + self.take(refs.from_sibling, refs.sibling_sems, zz * 2 + y, chunk)

    def give_sibling(self, zz):
        plane, refs = (self.plane, self.refs)
        for yy in (1 - plane.y, plane.y):
            for chunk in range(self.chunks):
                landing, arrived = self.spot(
                    refs.from_sibling, refs.sibling_sems, zz * 2 + yy, chunk
                )
                self.sends.start(
                    True, self.part(zz, 1 - plane.core, yy, chunk), landing, arrived, plane.sibling
                )

    def give_across(self, zz):
        plane, refs = (self.plane, self.refs)
        for chunk in range(self.chunks):
            staged = refs.from_sibling.at[zz * 2 + 1 - plane.y, span(chunk, self.size)]
            staged[...] = self.pair(zz, 1 - plane.y, chunk).astype(staged.dtype)
            landing, arrived = self.spot(refs.from_across, refs.across_sems, zz, chunk)
            self.sends.start(True, staged, landing, arrived, plane.across)

    def plane_sum(self, zz, chunk):
        refs = self.refs
        total = self.pair(zz, self.plane.y, chunk)
        return total + self.take(refs.from_across, refs.across_sems, zz, chunk)

    def come(self, slot, chunk):
        return self.take(self.refs.from_behind, self.refs.behind_sems, slot, chunk)

    def give_onward(self, zz):
        plane, refs = (self.plane, self.refs)
        onward = jnp.where(zz > plane.z, plane.z + 1, plane.z - 1)
        behind = plane.z * 2 - onward
        slot = jnp.where((onward == zz) & (zz < plane.z), plane.levels, zz)
        for chunk in range(self.chunks):
            refs.total[...] = self.plane_sum(zz, chunk)

            @pl.when((behind >= 0) & (behind < plane.levels))
            def _(chunk=chunk):
                refs.total[...] += self.come(zz, chunk)

            staged = refs.from_sibling.at[zz * 2 + plane.y, span(chunk, self.size)]
            staged[...] = refs.total[...].astype(staged.dtype)
            landing, arrived = self.spot(refs.from_behind, refs.behind_sems, slot, chunk)
            self.sends.start(True, staged, landing, arrived, plane.along(onward))

    def conclude(self):
        plane = self.plane
        for chunk in range(self.chunks):
            own = self.result.at[span(chunk, self.size)]
            own[...] = self.plane_sum(plane.z, chunk)

            @pl.when(plane.z > 0)
            def _(own=own, chunk=chunk):
                own[...] += self.come(plane.z, chunk)

            @pl.when(plane.z < plane.levels - 1)
            def _(own=own, chunk=chunk):
                own[...] += self.come(plane.levels, chunk)

    def run(self, make, tick, fill=None):
        levels = self.plane.levels
        order = self.plane.nearest()[::-1]
        for step in range(levels + 3):
            if step < levels:
                make(step, order[step])
                self.give_sibling(order[step])
            if 0 < step <= levels:
                self.give_across(order[step - 1])
            if step >= levels - 1:
                tick()
                if fill is not None:
                    fill(step - levels + 1)
            if 3 <= step < levels + 2:
                self.give_onward(order[step - 3])
        self.conclude()


def scatter_scratch(rows, width, levels, chunks, dtype=LOW):
    def held(count):
        return VMEM((count, rows, width), dtype)

    return dict(
        part=VMEM((rows * 4 * levels, width), dtype),
        from_sibling=held(2 * levels),
        from_across=held(levels),
        from_behind=held(levels + 1),
        total=VMEM((rows // chunks, width), WIDE),
        sum=VMEM((rows, width), WIDE),
        sibling_sems=DMAS((2 * levels, chunks)),
        across_sems=DMAS((levels, chunks)),
        behind_sems=DMAS((levels + 1, chunks)),
    )


def by_rows(which):
    return which in (1, 3)


def piece_of_shard(which, ref, member, members):
    if by_rows(which):
        return ref.at[span(member, ref.shape[0] // members)]
    return ref.at[:, span(member, ref.shape[1] // members)]


def piece_of_slice(which, ref, shard, shards):
    if by_rows(which):
        return ref.at[:, span(shard, ref.shape[1] // shards)]
    return ref.at[span(shard, ref.shape[0] // shards)]


def slice_shape(which, shape, shards):
    rows, columns = shape
    if by_rows(which):
        return (rows // shards, columns * shards)
    return (rows * shards, columns // shards)


def shard_shape(which, shape, shards):
    rows, columns = shape
    if by_rows(which):
        return (rows * shards, columns // shards)
    return (rows // shards, columns * shards)


FETCHES = (
    ((0, 0), (2, 0), (2, 2), (0, 2)),
    ((0, 0), (0, 1), (2, 1), (2, 1), (0, 0), (0, 1), (0, 1), (0, 1)),
    ((0, 1), (0, 1), (2, 0), (2, 0), (0, 0), (0, 1), (2, 1), (2, 2)),
    ((0, 1), (0, 1), (2, 1), (2, 1), (0, 0), (0, 0), (0, 2), (0, 1)),
    ((0, 1), (0, 0), (0, 0), (0, 0), (0, 0), (0, 0), (0, 0), (0, 0)),
)
ADDS = (
    (0, 0, 1, 2),
    (0, 0, 2, 3, 0, 0, 0, 0),
    (2, 2, 2, 2, 0, 0, 1, 1),
    (0, 1, 2, 3, 0, 2, 2, 2),
    (1, 1, 0, 0),
)


class Fetch:
    UNITS = ((0, (0, 1)), (0, (2,)), (0, (3,)), (1, (0, 1)), (1, (2,)), (1, (3,)))

    def __init__(self, plane, shards, slices, refs, sends, copies):
        self.plane, self.shards, self.slices = (plane, shards, slices)
        self.refs, self.sends, self.copies = (refs, sends, copies)
        self.spreads = []
        for unit in range(len(self.UNITS)):
            for step in range(plane.levels - 1, -1, -1):
                self.spreads.append((unit, step))
        self.hands = list(self.spreads)
        self.left = [plane.levels] * len(self.UNITS)
        self.kept = [[] for _ in self.UNITS]
        self.plan = [moment for stage in FETCHES for moment in stage]

    @staticmethod
    def count(levels):
        return 4 * 2 * (3 * levels), 4 * 2 + 8

    def tick(self):
        self.start(*self.plan.pop(0))

    def start(self, spreads, hands):
        for _ in range(spreads):
            if self.spreads:
                unit, step = self.spreads.pop(0)
                for which in self.UNITS[unit][1]:
                    self.spread(unit, which, step)
        for _ in range(hands):
            if len(self.hands) > len(self.spreads):
                unit, step = self.hands.pop(0)
                for which in self.UNITS[unit][1]:
                    self.hand_over(unit, which, step)
                self.left[unit] -= 1

    def require(self, unit):
        while self.left[unit]:
            self.start(0, 1) if len(self.hands) > len(self.spreads) else self.start(1, 0)
        plane, refs = (self.plane, self.refs)
        layer, weights = self.UNITS[unit]
        for which in weights:
            part = self.slices[which].at[layer]
            for zz in range(plane.levels):
                held = piece_of_slice(which, part, zz * 2 + 1 - plane.x, 2 * plane.levels)
                await_block(held, refs.cross_sems.at[which, layer, zz], plane.over)
        self.copies.wait(*self.kept[unit])
        for which in weights:
            self.copies.start(self.slices[which].at[layer], refs.slices_out[which].at[layer])

    def spread(self, unit, which, step):
        plane, refs, layer = (self.plane, self.refs, self.UNITS[unit][0])
        members = 2 * plane.levels
        shard, part = (self.shards[which], self.slices[which].at[layer])
        owner = plane.core == layer
        target = piece_of_slice(which, part, plane.z * 2 + plane.x, members)
        zz = lax.rem(plane.z + step, plane.levels)
        for other in (0, 1):
            core = 1 - plane.core if other else plane.core
            source = piece_of_shard(which, shard, zz * 2 + core, members)
            if step or other:
                self.sends.start(
                    owner,
                    source,
                    target,
                    refs.column_sems.at[which, layer, plane.z],
                    device(core, zz, plane.x, plane.y),
                )
            else:
                self.kept[unit].append(self.copies.start(source, target, owner))

    def hand_over(self, unit, which, step):
        plane, refs, layer = (self.plane, self.refs, self.UNITS[unit][0])
        members = 2 * plane.levels
        shard, part = (self.shards[which], self.slices[which].at[layer])
        zz = lax.rem(plane.z - step + plane.levels, plane.levels)
        held = piece_of_slice(which, part, zz * 2 + plane.x, members)
        arrived = refs.column_sems.at[which, layer, zz]
        cross = refs.cross_sems.at[which, layer, zz]
        if step:
            await_block(held, arrived, plane.over)
            self.sends.start(True, held, held, cross, plane.over)
        else:
            owner = plane.core == layer
            source = piece_of_shard(which, shard, plane.member, members)
            guarded(jnp.logical_not(owner), partial(await_block, held, arrived, plane.over))
            self.sends.start(jnp.logical_not(owner), held, held, cross, plane.over)
            self.sends.start(owner, source, held, cross, plane.over)


class Return:
    def __init__(self, plane, slices, landed, shards, refs, sends, copies):
        self.plane, self.slices, self.landed, self.shards = (plane, slices, landed, shards)
        self.refs, self.sends, self.copies = (refs, sends, copies)
        self.moments, self.left, self.given = ([], {}, {})
        self.plan = [count for stage in ADDS for count in stage]

    @staticmethod
    def count(levels):
        return 4 * 2 * (2 * levels), 4 * 2

    def give(self, layer, which):
        plane = self.plane
        self.left[layer, which], self.given[layer, which] = (plane.levels, [])
        for step in range(plane.levels - 1, -1, -1):
            zz = lax.rem(plane.z + step, plane.levels)
            number = self.sends.start(
                True,
                piece_of_slice(which, self.slices[which], zz * 2 + 1 - plane.x, 2 * plane.levels),
                self.landed[which].at[layer, zz],
                self.refs.cross_sems.at[which, layer, zz],
                plane.over,
            )
            self.given[layer, which].append(number)
            self.moments.append((layer, which, step))

    def tick(self):
        self.start(self.plan.pop(0))

    def start(self, adds):
        for _ in range(adds):
            if self.moments:
                moment = self.moments.pop(0)
                self.add(*moment)
                self.left[moment[:2]] -= 1

    def require(self, layer, which):
        while self.left[layer, which]:
            self.start(1)
        self.sends.wait(*self.given[layer, which])

    def add(self, layer, which, step):
        plane, refs = (self.plane, self.refs)
        members = 2 * plane.levels
        here = plane.core == layer
        target = piece_of_shard(which, self.shards[which], plane.member, members)
        zz = lax.rem(plane.z + step, plane.levels)
        held = self.landed[which].at[layer, zz]
        await_block(held, refs.cross_sems.at[which, layer, zz], plane.over)
        own = piece_of_slice(which, self.slices[which], zz * 2 + plane.x, members)
        held[...] = (held[...].astype(WIDE) + own[...].astype(WIDE)).astype(LOW)
        self.sends.start(
            True if step else jnp.logical_not(here),
            held,
            target,
            refs.column_sems.at[which, plane.core, plane.z],
            device(layer, zz, plane.x, plane.y),
        )
        if step == 0:
            self.copies.start(held, target, here)

    def finish(self):
        self.start(len(self.moments))
        plane, refs = (self.plane, self.refs)
        members = 2 * plane.levels
        for which in range(4):
            for core in (0, 1):
                for step in range(plane.levels):
                    zz = lax.rem(plane.z + step, plane.levels)
                    held = piece_of_shard(which, self.shards[which], zz * 2 + core, members)
                    guarded(
                        True if step else plane.core != core,
                        partial(
                            await_block, held, refs.column_sems.at[which, core, zz], plane.over
                        ),
                    )


class Outward:
    @staticmethod
    def count():
        return 6, 2

    def __init__(self, plane, target, sems):
        self.plane, self.target, self.sems = (plane, target, sems)

    def give(self, layer, source, sends, copies):
        plane, target = (self.plane, self.target.at[self.plane.x])
        same_core, same_x = (plane.core == layer, plane.core == plane.x)
        other_core, other_x = (plane.core != layer, plane.core != plane.x)
        for present, partner in (
            (same_core & other_x, plane.over),
            (other_core & same_x, plane.sibling),
            (other_core & other_x, plane.corner),
        ):
            sends.start(present, source, target, self.sems.at[plane.x], partner)
        copies.start(source, target, same_core & same_x)

    def finish(self):
        plane = self.plane
        for slot in (0, 1):
            away = jnp.logical_not((plane.core == plane.x) & (plane.x == slot))
            guarded(away, partial(await_block, self.target.at[slot], self.sems.at[slot], plane.over))


def launch(name, ident, kernel, counts, inputs, outputs, scratch):
    scratch = dict(
        scratch,
        send_sems=DMAS((counts[0],)),
        phase_sems=DMAS((counts[1],)),
        copy_sems=DMAS((counts[2],)),
    )
    names = list(inputs) + list(outputs) + list(scratch)

    def body(*refs):
        held = SimpleNamespace(**dict(zip(names, refs)))
        plane = Plane()
        barrier = pltpu.get_barrier_semaphore()
        partners = plane.partners()
        for partner in partners:
            pl.semaphore_signal(barrier, inc=1, device_id=partner, device_id_type=MESH)
        sends, copies = (Sends(held.send_sems), Copies(held.copy_sems))
        kernel(held, plane, lambda: pl.semaphore_wait(barrier, len(partners)), sends, copies)
        copies.finish()
        sends.finish()
        assert len(sends.pending) == counts[0], len(sends.pending)
        assert len(copies.pending) == counts[2], len(copies.pending)

    results = pl.pallas_call(
        body,
        out_shape=[jax.ShapeDtypeStruct(shape, dtype) for shape, dtype, _ in outputs.values()],
        in_specs=[pl.BlockSpec(memory_space=space) for _, space in inputs.values()],
        out_specs=[pl.BlockSpec(memory_space=space) for _, _, space in outputs.values()],
        scratch_shapes=list(scratch.values()),
        compiler_params=pltpu.CompilerParams(
            collective_id=ident, has_side_effects=True, vmem_limit_bytes=60 << 20
        ),
        name=name,
    )(*[array for array, _ in inputs.values()])
    return SimpleNamespace(**dict(zip(outputs, results)))


CHUNKS, SUM_CHUNKS, CUT = (2, 2, 512)
NORM_LINES, HEAD_LINES, LINES = (6, 8, 16)


def unpack_vectors(refs, plane, levels):
    members, blocks = (2 * levels, 4 * levels)
    for layer in (0, 1):
        for z in range(levels):
            for x in (0, 1):
                for y in (0, 1):
                    start = ((z * 4 + layer * 2 + y) * 2 + x) * LINES
                    cut = (z * 4 + x * 2 + y) * HD
                    refs.norms[layer, :, cut : cut + HD] = refs.small[
                        start : start + LINES
                    ].astype(WIDE)[:HEAD_LINES]
    lines = []
    for layer in (0, 1):
        pieces = []
        for z in range(levels):
            for x in (0, 1):
                number = (z * 4 + layer * 2 + plane.y) * 2 + x
                pieces.append(refs.small[span(number, LINES)].astype(WIDE)[HEAD_LINES:])
        lines.append(jnp.concatenate(pieces, axis=1))
    lines = jnp.concatenate(lines, axis=0).astype(LOW)
    width = HD // members
    place = lax.broadcasted_iota(jnp.int32, (members * HD, HD), 0)
    lane = lax.broadcasted_iota(jnp.int32, (members * HD, HD), 1)

    def pick(first):
        chosen = (place // HD == lane // width) & (place % HD == lane % width + first)
        return dot(lines, chosen.astype(WIDE).astype(LOW))

    heads = pick(plane.member * width)
    units = refs.b_up.shape[2] // HD
    per_line = HD // (units * width)
    row = lax.broadcasted_iota(jnp.int32, (HEAD_LINES, HD), 0)
    for layer in (0, 1):
        refs.b_qv[layer] = heads[layer * HEAD_LINES : layer * HEAD_LINES + 2]
    for unit in range(units):
        found = pick((lax.rem(plane.member, per_line) * units + unit) * width)
        for layer in (0, 1):
            own = found[layer * HEAD_LINES : (layer + 1) * HEAD_LINES]
            own = jnp.where(row == 2 + plane.member // per_line, own, 0.0)
            refs.b_up[layer, :, unit * HD : (unit + 1) * HD] = jnp.sum(own, axis=0, keepdims=True)


def visible(refs, group, size, tokens):
    segment = refs.query_segment[group]
    place = group.start + lax.broadcasted_iota(jnp.int32, (size, tokens), 0)
    keys = lax.broadcasted_iota(jnp.int32, (size, tokens), 1)
    return (segment == refs.key_segment[...]) & (keys <= place)


def forward_planes(ident, boundary, packed, segments, shards):
    levels = lax.axis_size("dp") // 2
    blocks, members = (4 * levels, 2 * levels)
    rows, width = boundary.shape[1:]
    tokens, size = (blocks * rows, 4 * rows)
    slice_shapes = [
        slice_shape(which, shard.shape, members) for which, shard in enumerate(shards)
    ]
    units = slice_shapes[2][1]
    scaling = HD ** (-0.5)

    def kernel(refs, plane, greet, sends, copies):
        core, x = (plane.core, plane.x)
        own_block = span(plane.block, rows)
        refs.slices_out = [refs.out0, refs.out1, refs.out2, refs.out3]
        slices = [refs.w0, refs.w1, refs.w2, refs.w3]
        fetch = Fetch(
            plane, [refs.shard0, refs.shard1, refs.shard2, refs.shard3], slices, refs, sends, copies
        )
        small_block = span(plane.block * 2 + x, LINES)
        refs.small[small_block] = refs.packed[...]
        greet()
        phase = Sends(refs.phase_sems)
        own_small = refs.small.at[small_block]
        phase.start(True, own_small, own_small, refs.pair_sem.at[0], plane.over)
        inward = []
        for slot in (0, 1):
            source, target = (refs.boundary.at[slot], refs.landed_planes.at[core])
            arrived = refs.inward_sems.at[core]
            for present, partner in (
                ((x == core) & (slot != x), plane.over),
                ((x != core) & (slot == x), plane.sibling),
                ((x != core) & (slot != x), plane.corner),
            ):
                phase.start(present, source, target, arrived, partner)
            inward.append(copies.start(source, target, (x == core) & (slot == x)))
        other_small = refs.small.at[span(plane.block * 2 + 1 - x, LINES)]
        await_block(other_small, refs.pair_sem.at[0], plane.over)
        small = Gather(plane, phase, refs.small, refs.small_sems)
        small.open()
        small.run(lambda step, zz: None, lambda: None)
        fetch.start(levels, 0)
        for slot in (0, 1):
            here = (core == x) & (core == slot)
            guarded(
                jnp.logical_not(here),
                partial(await_block, refs.landed_planes.at[slot], refs.inward_sems.at[slot], plane.over),
            )
        copies.wait(*inward)
        refs.planes[...] = refs.landed_planes[...]
        refs.rows[0, own_block] = refs.landed_planes[1]
        gather = Gather(plane, phase, refs.rows.at[0], refs.gather_sems.at[0])
        gather.open()
        unpack_vectors(refs, plane, levels)
        kept = []

        def keep(step, zz):
            group = span(zz, size)
            kept.append(copies.start(refs.rows.at[0, group], refs.gathered.at[group]))

        gather.run(keep, fetch.tick)
        copies.wait(*kept)
        phase.finish()

        for layer in (0, 1):
            number = 1 + 2 * layer
            norms = refs.norms.at[layer]
            held, sems = (refs.rows.at[number % 2], refs.gather_sems.at[number % 2])
            entering = refs.planes[0] if layer == 0 else refs.leaving[0]
            hidden = entering.astype(WIDE)
            normed, _, _ = layer_norm(hidden, norms[0:1], norms[2:3])
            held[own_block] = normed.astype(LOW)
            phase = Sends(refs.phase_sems)
            gather = Gather(plane, phase, held, sems)
            gather.open()
            fetch.require(3 * layer)
            kept = []

            def project(step, zz):
                group = span(zz, size)
                projected = dot(held[group], refs.w0[layer])
                refs.queries[layer, group] = (projected[:, :HD] + refs.b_qv[layer, 0:1]).astype(LOW)
                refs.keys[layer, group] = projected[:, HD : 2 * HD].astype(LOW)
                refs.values[layer, group] = (
                    projected[:, 2 * HD :] + refs.b_qv[layer, 1:2]
                ).astype(LOW)
                kept.append(copies.start(held.at[group], refs.rows_a.at[layer, group]))

            gather.run(project, fetch.tick)

            def attend(step, zz):
                group = span(zz, size)
                allowed = visible(refs, group, size, tokens)
                scores = dot_back(refs.queries[layer, group], refs.keys[layer]) * scaling
                scores = jnp.where(allowed, scores, NEG_FILL)
                top = jnp.max(scores, axis=-1, keepdims=True)
                raised = jnp.exp(scores - top)
                total = jnp.sum(raised, axis=-1, keepdims=True)
                refs.log_total[layer, group] = top + jnp.log(total)
                probs = (raised / total).astype(LOW)
                live = (refs.query_segment[group] >= 0).astype(WIDE)
                mixed = (dot(probs, refs.values[layer]) * live).astype(LOW)
                refs.mixed[layer, group] = mixed
                for cut in range(0, width, CUT):
                    refs.part[group, cut : cut + CUT] = dot(
                        mixed, refs.w1[layer, :, cut : cut + CUT]
                    ).astype(LOW)

            Scatter(plane, phase, refs, refs.sum).run(attend, fetch.tick)
            middle = hidden + refs.sum[...] + norms[3:4]
            refs.middle[layer] = middle
            copies.wait(*kept)
            phase.finish()

            number = number + 1
            held, sems = (refs.rows.at[number % 2], refs.gather_sems.at[number % 2])
            normed, _, _ = layer_norm(middle, norms[1:2], norms[4:5])
            held[own_block] = normed.astype(LOW)
            phase = Sends(refs.phase_sems)
            gather = Gather(plane, phase, held, sems)
            gather.open()
            fetch.require(3 * layer + 1)
            kept = []

            def expand(step, zz):
                group = span(zz, size)
                preact = dot(held[group], refs.w2[layer]) + refs.b_up[layer]
                refs.own_preact[layer, group] = preact
                refs.own_activated[layer, group] = (
                    0.5 * preact * (1.0 + lax.erf(preact * math.sqrt(0.5)))
                ).astype(LOW)
                for own, out in (
                    (held.at[group], refs.rows_b),
                    (refs.own_preact.at[layer, group], refs.preact),
                    (refs.own_activated.at[layer, group], refs.activated),
                ):
                    kept.append(copies.start(own, out.at[layer, group]))

            gather.run(expand, fetch.tick)
            fetch.require(3 * layer + 2)

            def shrink(step, zz):
                group = span(zz, size)
                for cut in range(0, width, CUT):
                    refs.part[group, cut : cut + CUT] = dot(
                        refs.own_activated[layer, group], refs.w3[layer, :, cut : cut + CUT]
                    ).astype(LOW)

            Scatter(plane, phase, refs, refs.sum).run(shrink, fetch.tick)
            refs.leaving[layer] = (refs.middle[layer] + refs.sum[...] + norms[5:6]).astype(LOW)
            copies.wait(*kept)
            phase.finish()

    head = ((2, tokens, HD), LOW, VMEM)
    gathers = Gather.count(levels, CHUNKS)
    lasting = Fetch.count(levels)
    return launch(
        "forward_planes",
        ident,
        kernel,
        (
            lasting[0],
            max(gathers + Scatter.count(levels, SUM_CHUNKS), 7 + Gather.count(levels, 1) + gathers),
            lasting[1] + 2 + levels + 2 * 4 * levels,
        ),
        dict(
            boundary=(boundary, HBM),
            packed=(packed, VMEM),
            query_segment=(segments[0], VMEM),
            key_segment=(segments[1], VMEM),
            shard0=(shards[0], HBM),
            shard1=(shards[1], HBM),
            shard2=(shards[2], HBM),
            shard3=(shards[3], HBM),
        ),
        dict(
            planes=((2, rows, width), LOW, VMEM),
            leaving=((2, rows, width), LOW, VMEM),
            middle=((2, rows, width), WIDE, VMEM),
            norms=((2, HEAD_LINES, width), WIDE, VMEM),
            queries=head,
            keys=head,
            values=head,
            mixed=head,
            log_total=((2, tokens, 1), WIDE, VMEM),
            gathered=((tokens, width), LOW, HBM),
            rows_a=((2, tokens, width), LOW, HBM),
            rows_b=((2, tokens, width), LOW, HBM),
            preact=((2, tokens, units), WIDE, HBM),
            activated=((2, tokens, units), LOW, HBM),
            out0=((2,) + slice_shapes[0], LOW, HBM),
            out1=((2,) + slice_shapes[1], LOW, HBM),
            out2=((2,) + slice_shapes[2], LOW, HBM),
            out3=((2,) + slice_shapes[3], LOW, HBM),
        ),
        dict(
            scatter_scratch(rows, width, levels, SUM_CHUNKS),
            rows=VMEM((2, tokens, width), LOW),
            gather_sems=DMAS((2, blocks, CHUNKS)),
            small=VMEM((2 * blocks * LINES, HD), LOW),
            small_sems=DMAS((blocks, 1)),
            pair_sem=DMAS((1,)),
            inward_sems=DMAS((2,)),
            landed_planes=VMEM((2, rows, width), LOW),
            b_qv=VMEM((2, 2, HD), WIDE),
            b_up=VMEM((2, 1, units), WIDE),
            w0=VMEM((2,) + slice_shapes[0], LOW),
            w1=VMEM((2,) + slice_shapes[1], LOW),
            w2=VMEM((2,) + slice_shapes[2], LOW),
            w3=VMEM((2,) + slice_shapes[3], LOW),
            own_preact=VMEM((2, tokens, units), WIDE),
            own_activated=VMEM((2, tokens, units), LOW),
            column_sems=DMAS((4, 2, levels)),
            cross_sems=DMAS((4, 2, levels)),
        ),
    )


def backward_planes(ident, kept, segments):
    levels = lax.axis_size("dp") // 2
    blocks, members = (4 * levels, 2 * levels)
    rows, width = kept.planes.shape[1:]
    tokens, size = (blocks * rows, 4 * rows)
    slice_shapes = [array.shape[1:] for array in (kept.out0, kept.out1, kept.out2, kept.out3)]
    shard_shapes = [shard_shape(which, shape, members) for which, shape in enumerate(slice_shapes)]
    units = slice_shapes[2][1]
    unit_lines = units // HD
    scaling = HD ** (-0.5)
    vector_lines = (2 + members) * HEAD_LINES

    def landing(which):
        shape = slice_shapes[which]
        if by_rows(which):
            return VMEM((2, levels, shape[0], shape[1] // members), LOW)
        return VMEM((2, levels, shape[0] // members, shape[1]), LOW)

    def kernel(refs, plane, greet, sends, copies):
        own_block = span(plane.block, rows)
        back = Return(
            plane,
            [refs.grad0, refs.grad1, refs.grad2, refs.grad3],
            [refs.landed0, refs.landed1, refs.landed2, refs.landed3],
            [refs.shard0, refs.shard1, refs.shard2, refs.shard3],
            refs,
            sends,
            copies,
        )
        acts = Outward(plane, refs.acts, refs.acts_sems)
        ends = Outward(plane, refs.input_grads, refs.ends_sems)

        def load(layer):
            return [
                copies.start(refs.out3.at[layer], refs.w3),
                copies.start(refs.preact.at[layer], refs.own_preact),
                copies.start(refs.out2.at[layer], refs.w2),
                copies.start(refs.activated.at[layer], refs.own_activated),
                copies.start(refs.rows_b.at[layer], refs.own_rows),
                copies.start(refs.out1.at[layer], refs.w1),
                copies.start(refs.out0.at[layer], refs.w0),
                copies.start(refs.all_queries.at[layer], refs.queries),
                copies.start(refs.all_keys.at[layer], refs.keys),
                copies.start(refs.all_values.at[layer], refs.values),
                copies.start(refs.all_mixed.at[layer], refs.mixed),
                copies.start(refs.all_totals.at[layer], refs.log_total),
            ]

        loads = load(1)
        first = copies.start(refs.gathered, refs.rows.at[0])
        greet()
        acts.give(0, refs.leaving.at[0], sends, copies)
        acts.give(1, refs.leaving.at[1], sends, copies)

        for layer in (1, 0):
            number = 2 * (1 - layer)
            norms = refs.norms.at[layer]
            vectors = refs.vectors.at[layer]
            held, sems = (refs.rows.at[number % 2], refs.gather_sems.at[number % 2])
            phase = Sends(refs.phase_sems)
            low = refs.planes[1] if layer == 1 else refs.leaving_grads[1].astype(LOW)
            vectors[5:6] = jnp.sum(low.astype(WIDE), axis=0, keepdims=True)
            refs.unit_sums[layer] = jnp.zeros((1, units), WIDE)
            if layer == 0:
                held[own_block] = low
                gather = Gather(plane, phase, held, sems)
                gather.open()
            else:
                copies.wait(first)
            copies.wait(loads[0], loads[1])

            def slope(step, zz):
                group = span(zz, size)
                grad_act = dot_back(held[group], refs.w3[...])
                value = refs.own_preact[group]
                rise = 0.5 * (1.0 + lax.erf(value * math.sqrt(0.5))) + value * jnp.exp(
                    -0.5 * value * value
                ) * (1.0 / math.sqrt(2.0 * math.pi))
                grad_pre = (grad_act * rise).astype(LOW)
                refs.grad_pre[group] = grad_pre
                refs.unit_sums[layer] += jnp.sum(grad_pre.astype(WIDE), axis=0, keepdims=True)

            if layer == 0:
                gather.run(slope, back.tick)
            copies.wait(loads[2])

            def widen_units(step, zz):
                group = span(zz, size)
                if layer == 1:
                    slope(step, zz)
                for cut in range(0, width, CUT):
                    refs.part[group, cut : cut + CUT] = dot_back(
                        refs.grad_pre[group], refs.w2[cut : cut + CUT]
                    ).astype(LOW)

            def down_product(at, carry):
                cut = span(at, 128)
                refs.grad3[cut] = dot_rows(refs.own_activated[:, cut], held[...]).astype(LOW)
                return carry

            def up_product(at, carry):
                cut = span(at, 256)
                refs.grad2[cut] = dot_rows(refs.own_rows[:, cut], refs.grad_pre[...]).astype(LOW)
                return carry

            def products(at):
                if at == 0:
                    copies.wait(loads[3], loads[4])
                    if layer == 0:
                        back.require(1, 3)
                        back.require(1, 2)
                    lax.fori_loop(0, units // 128, down_product, 0)
                    back.give(layer, 3)
                if at == 1:
                    lax.fori_loop(0, width // 512, up_product, 0)
                if at == 2:
                    lax.fori_loop(width // 512, width // 256, up_product, 0)
                    back.give(layer, 2)

            Scatter(plane, phase, refs, refs.sum).run(widen_units, back.tick, products)
            loads.append(copies.start(refs.rows_a.at[layer], refs.own_rows))
            _, unit, inverse = layer_norm(refs.middle[layer], norms[1:2], norms[1:2])
            vectors[1:2] = jnp.sum(refs.sum[...] * unit, axis=0, keepdims=True)
            vectors[4:5] = jnp.sum(refs.sum[...], axis=0, keepdims=True)
            grad_out = refs.planes[1].astype(WIDE) if layer == 1 else refs.leaving_grads[1].astype(LOW).astype(WIDE)
            grad_middle = grad_out + norm_back(refs.sum[...], unit, inverse, norms[1:2])
            phase.finish()

            number = number + 1
            held, sems = (refs.rows.at[number % 2], refs.gather_sems.at[number % 2])
            phase = Sends(refs.phase_sems)
            refs.grad_middle[...] = grad_middle
            low = grad_middle.astype(LOW)
            held[own_block] = low
            gather = Gather(plane, phase, held, sems)
            gather.open()
            vectors[3:4] = jnp.sum(low.astype(WIDE), axis=0, keepdims=True)
            refs.grad_keys[...] = jnp.zeros_like(refs.grad_keys)
            refs.grad_values[...] = jnp.zeros_like(refs.grad_values)
            copies.wait(loads[5], *loads[7:12])

            def attend(step, zz):
                group = span(zz, size)
                live = (refs.query_segment[group] >= 0).astype(WIDE)
                grad_mixed = (
                    dot_back(held[group], refs.w1[...]).astype(LOW) * live
                ).astype(LOW)
                allowed = visible(refs, group, size, tokens)
                queries = refs.queries[group]
                scores = dot_back(queries, refs.keys[...]) * scaling
                scores = jnp.where(allowed, scores, NEG_FILL)
                probs = jnp.exp(scores - refs.log_total[group])
                grad_probs = dot_back(grad_mixed, refs.values[...])
                delta = jnp.sum(probs * grad_probs, axis=-1, keepdims=True)
                grad_scores = jnp.where(allowed, probs * (grad_probs - delta), 0.0).astype(LOW)
                refs.grad_proj[group, :HD] = (dot(grad_scores, refs.keys[...]) * scaling).astype(LOW)
                refs.grad_keys[...] += dot_rows(grad_scores, queries)
                refs.grad_values[...] += dot_rows(probs.astype(LOW), grad_mixed)

            gather.run(attend, back.tick)
            refs.grad_proj[:, HD : 2 * HD] = (refs.grad_keys[...] * scaling).astype(LOW)
            refs.grad_proj[:, 2 * HD :] = refs.grad_values[...].astype(LOW)
            copies.wait(loads[6])

            def widen_heads(step, zz):
                group = span(zz, size)
                for cut in range(0, width, CUT):
                    refs.part[group, cut : cut + CUT] = dot_back(
                        refs.grad_proj[group], refs.w0[cut : cut + CUT]
                    ).astype(LOW)

            def qkv_product(at, carry):
                cut = span(at, 256)
                refs.grad0[cut] = dot_rows(refs.own_rows[:, cut], refs.grad_proj[...]).astype(LOW)
                return carry

            def more_products(at):
                if at == 0:
                    sums = jnp.sum(refs.grad_proj[...].astype(WIDE), axis=0, keepdims=True)
                    refs.head_sums[layer, 0:1] = sums[:, :HD]
                    refs.head_sums[layer, 1:2] = sums[:, 2 * HD :]
                    copies.wait(loads[12])
                    if layer == 0:
                        back.require(1, 1)
                        back.require(1, 0)
                if at == (1 if layer else 0):
                    refs.grad1[...] = dot_rows(refs.mixed[...], held[...]).astype(LOW)
                    back.give(layer, 1)
                if at == (2 if layer else 0):
                    lax.fori_loop(0, width // 512, qkv_product, 0)
                if at == (3 if layer else 0):
                    lax.fori_loop(width // 512, width // 256, qkv_product, 0)
                    back.give(layer, 0)

            Scatter(plane, phase, refs, refs.sum).run(widen_heads, back.tick, more_products)
            if layer == 1:
                loads = load(0)
            entering = refs.planes[0] if layer == 0 else refs.leaving[0]
            _, unit, inverse = layer_norm(entering.astype(WIDE), norms[0:1], norms[0:1])
            vectors[0:1] = jnp.sum(refs.sum[...] * unit, axis=0, keepdims=True)
            vectors[2:3] = jnp.sum(refs.sum[...], axis=0, keepdims=True)
            refs.leaving_grads[layer] = refs.grad_middle[...] + norm_back(
                refs.sum[...], unit, inverse, norms[0:1]
            )
            ends.give(layer, refs.leaving_grads.at[layer], sends, copies)
            phase.finish()

        tail = SimpleNamespace(
            part=refs.vector_part,
            from_sibling=refs.vector_from_sibling,
            from_across=refs.vector_from_across,
            from_behind=refs.vector_from_behind,
            total=refs.vector_total,
            sibling_sems=refs.vector_sibling_sems,
            across_sems=refs.vector_across_sems,
            behind_sems=refs.vector_behind_sems,
        )
        tail.part[...] = jnp.zeros_like(tail.part)
        for layer in (0, 1):
            own = [refs.head_sums[layer]]
            for at in range(unit_lines):
                own.append(refs.unit_sums[layer, :, at * HD : (at + 1) * HD])
            own.append(jnp.zeros((HEAD_LINES - 2 - unit_lines, HD), WIDE))
            own = jnp.concatenate(own, axis=0)
            for z in range(levels):
                for y in (0, 1):
                    base = (z * 4 + layer * 2 + y) * vector_lines
                    for x in (0, 1):
                        cut = (z * 4 + x * 2 + y) * HD
                        line = base + x * HEAD_LINES
                        tail.part[line : line + HEAD_LINES] = refs.vectors[layer, :, cut : cut + HD]
                start = (z * 4 + layer * 2 + plane.y) * vector_lines
                start = start + (2 + plane.member) * HEAD_LINES
                tail.part[pl.ds(pl.multiple_of(start, HEAD_LINES), HEAD_LINES)] = own
        phase = Sends(refs.phase_sems)
        Scatter(plane, phase, tail, refs.vector_sum).run(lambda step, zz: None, back.tick)
        phase.start(True, refs.vector_sum, refs.vector_other, refs.pair_sem.at[0], plane.over)
        await_block(refs.vector_other, refs.pair_sem.at[0], plane.over)
        refs.vector_out[...] = refs.vector_sum[...] + refs.vector_other[...]
        acts.finish()
        back.finish()
        ends.finish()
        phase.finish()

    lasting = Return.count(levels)
    outward = Outward.count()
    vector = scatter_scratch(vector_lines, HD, levels, 1, WIDE)
    return launch(
        "backward_planes",
        ident,
        kernel,
        (
            lasting[0] + 2 * outward[0],
            Gather.count(levels, CHUNKS) + Scatter.count(levels, SUM_CHUNKS),
            lasting[1] + 2 * outward[1] + 2 * 13 + 1,
        ),
        dict(
            planes=(kept.planes, VMEM),
            leaving=(kept.leaving, VMEM),
            middle=(kept.middle, VMEM),
            norms=(kept.norms, VMEM),
            query_segment=(segments[0], VMEM),
            key_segment=(segments[1], VMEM),
            all_queries=(kept.queries, HBM),
            all_keys=(kept.keys, HBM),
            all_values=(kept.values, HBM),
            all_mixed=(kept.mixed, HBM),
            all_totals=(kept.log_total, HBM),
            gathered=(kept.gathered, HBM),
            rows_a=(kept.rows_a, HBM),
            rows_b=(kept.rows_b, HBM),
            preact=(kept.preact, HBM),
            activated=(kept.activated, HBM),
            out0=(kept.out0, HBM),
            out1=(kept.out1, HBM),
            out2=(kept.out2, HBM),
            out3=(kept.out3, HBM),
        ),
        dict(
            acts=((2, rows, width), LOW, HBM),
            input_grads=((2, rows, width), WIDE, HBM),
            shard0=(shard_shapes[0], LOW, HBM),
            shard1=(shard_shapes[1], LOW, HBM),
            shard2=(shard_shapes[2], LOW, HBM),
            shard3=(shard_shapes[3], LOW, HBM),
            vector_out=((vector_lines, HD), WIDE, VMEM),
        ),
        dict(
            scatter_scratch(rows, width, levels, SUM_CHUNKS),
            rows=VMEM((2, tokens, width), LOW),
            gather_sems=DMAS((2, blocks, CHUNKS)),
            w0=VMEM(slice_shapes[0], LOW),
            w1=VMEM(slice_shapes[1], LOW),
            w2=VMEM(slice_shapes[2], LOW),
            w3=VMEM(slice_shapes[3], LOW),
            own_preact=VMEM((tokens, units), WIDE),
            own_activated=VMEM((tokens, units), LOW),
            own_rows=VMEM((tokens, width), LOW),
            grad_pre=VMEM((tokens, units), LOW),
            grad_proj=VMEM((tokens, 3 * HD), LOW),
            queries=VMEM((tokens, HD), LOW),
            keys=VMEM((tokens, HD), LOW),
            values=VMEM((tokens, HD), LOW),
            mixed=VMEM((tokens, HD), LOW),
            log_total=VMEM((tokens, 1), WIDE),
            grad_keys=VMEM((tokens, HD), WIDE),
            grad_values=VMEM((tokens, HD), WIDE),
            grad_middle=VMEM((rows, width), WIDE),
            leaving_grads=VMEM((2, rows, width), WIDE),
            grad0=VMEM(slice_shapes[0], LOW),
            grad1=VMEM(slice_shapes[1], LOW),
            grad2=VMEM(slice_shapes[2], LOW),
            grad3=VMEM(slice_shapes[3], LOW),
            landed0=landing(0),
            landed1=landing(1),
            landed2=landing(2),
            landed3=landing(3),
            column_sems=DMAS((4, 2, levels)),
            cross_sems=DMAS((4, 2, levels)),
            acts_sems=DMAS((2,)),
            ends_sems=DMAS((2,)),
            pair_sem=DMAS((1,)),
            vectors=VMEM((2, HEAD_LINES, width), WIDE),
            head_sums=VMEM((2, 2, HD), WIDE),
            unit_sums=VMEM((2, 1, units), WIDE),
            vector_part=vector["part"],
            vector_from_sibling=vector["from_sibling"],
            vector_from_across=vector["from_across"],
            vector_from_behind=vector["from_behind"],
            vector_total=vector["total"],
            vector_sum=vector["sum"],
            vector_other=VMEM((vector_lines, HD), WIDE),
            vector_sibling_sems=vector["sibling_sems"],
            vector_across_sems=vector["across_sems"],
            vector_behind_sems=vector["behind_sems"],
        ),
    )


def plane_body(
    boundary,
    doc_lengths,
    qkv_weight,
    qv_bias,
    out_weight,
    up_weight,
    up_bias,
    down_weight,
    norm_gains,
    norm_biases,
):
    plane = Plane()
    levels = plane.levels
    members = 2 * levels
    head_cut = qv_bias.shape[3]
    block_shard = up_bias.shape[1]
    own_blocks = block_shard // members

    def lines(piece):
        return piece.reshape(-1, HD)

    packed = jnp.concatenate(
        (
            lines(norm_gains[0]),
            lines(norm_biases[0]),
            jnp.zeros((HEAD_LINES - NORM_LINES, HD), LOW),
            lines(qv_bias[0]),
            lines(up_bias[0]),
            jnp.zeros((LINES - HEAD_LINES - 2 - up_bias[0].size // HD, HD), LOW),
        )
    )
    depth = qkv_weight.shape[1]
    by_head = (
        qkv_weight[0]
        .reshape(depth, 3, members, HD)
        .transpose(0, 2, 1, 3)
        .reshape(depth, members * 3 * HD)
    )
    lengths = lax.dynamic_index_in_dim(doc_lengths, plane.x, 0, keepdims=False)
    tokens = boundary.shape[2] * 4 * levels
    _, segment, live, _, _, _ = visibility(lengths, 0, tokens, tokens)
    segments = (jnp.where(live, segment, -1)[:, None], segment[None, :])

    kept = forward_planes(
        0, boundary[0], packed, segments, (by_head, out_weight[0], up_weight[0], down_weight[0])
    )
    end = backward_planes(1, kept, segments)

    summed = end.vector_out.reshape(2 + members, HEAD_LINES, HD)
    norms = lax.dynamic_index_in_dim(summed, plane.x, 0, keepdims=False)
    by_member = lax.dynamic_slice_in_dim(
        summed[2:], (plane.z * 2 + plane.x) * head_cut, head_cut, axis=2
    )
    qkv_shard = (
        end.shard0.reshape(depth, members, 3, HD)
        .transpose(0, 2, 1, 3)
        .reshape(depth, 3, members * HD)
    )
    return (
        end.acts[None],
        end.input_grads[None],
        qkv_shard.astype(WIDE)[None],
        by_member[:, :2].transpose(1, 0, 2)[None],
        end.shard1.astype(WIDE)[None],
        end.shard2.astype(WIDE)[None],
        by_member[:, 2 : 2 + own_blocks].reshape(1, block_shard, head_cut),
        end.shard3.astype(WIDE)[None],
        norms[None, :2],
        norms[None, 2:NORM_LINES],
    )


def fits_plane(mesh):
    return mesh.shape["dp"] == 8 and mesh.shape["tensor"] == 2 and mesh.shape["section"] == 2


def solution(mesh):
    placed = (
        P("section", None, ("dp", "tensor"), None),
        P(),
        P("section", "dp", None, "tensor"),
        P("section", None, "tensor", "dp"),
        P("section", "tensor", "dp"),
        P("section", "dp", "tensor"),
        P("section", "tensor", "dp"),
        P("section", "tensor", "dp"),
        P("section", None, ("dp", "tensor")),
        P("section", None, ("dp", "tensor")),
    )
    return jax.shard_map(
        plane_body if fits_plane(mesh) else body,
        mesh=mesh,
        in_specs=placed,
        out_specs=(
            P("section", None, ("dp", "tensor"), None),
            P("section", None, ("dp", "tensor"), None),
            P("section", "dp", None, "tensor"),
            P("section", None, "tensor", "dp"),
            P("section", "tensor", "dp"),
            P("section", "dp", "tensor"),
            P("section", "tensor", "dp"),
            P("section", "tensor", "dp"),
            P("section", None, ("dp", "tensor")),
            P("section", None, ("dp", "tensor")),
        ),
        check_vma=False,
    )
```

```python
from functools import partial
import math
from types import SimpleNamespace

import jax
import jax.numpy as jnp
from jax import lax
from jax.experimental import pallas as pl
from jax.experimental.pallas import tpu as pltpu
from jax.sharding import PartitionSpec as P

HD = 128


EPSILON = 1e-05
NEG_FILL = -1e30
MESH = pl.DeviceIdType.MESH


def from_behind(value, axis, steps):
    count = lax.axis_size(axis)
    first, last = (max(0, -steps), min(count, count - steps))
    return lax.ppermute(value, axis, [(source, source + steps) for source in range(first, last)])


def layer_norm(hidden, gain, shift):
    average = jnp.mean(hidden, axis=-1, keepdims=True)
    centred = hidden - average
    variance = jnp.mean(centred * centred, axis=-1, keepdims=True)
    inverse = lax.rsqrt(variance + EPSILON)
    normed = centred * inverse
    return (normed * gain + shift, normed, inverse)


def norm_back(grad_out, normed, inverse, gain):
    scaled = grad_out * gain
    return inverse * (
        scaled
        - jnp.mean(scaled, axis=-1, keepdims=True)
        - normed * jnp.mean(scaled * normed, axis=-1, keepdims=True)
    )


def visibility(lengths, dp_index, rows_dp, seq_len):
    per_seq = seq_len // lengths.shape[0]
    docs = lengths.shape[1]
    key_pos = jnp.arange(seq_len, dtype=jnp.int32)
    seq_of = key_pos // per_seq
    local = key_pos - seq_of * per_seq
    doc_ends = jnp.cumsum(lengths, axis=1)
    ends_row = jnp.take(doc_ends, seq_of, axis=0)
    key_seg = seq_of * (docs + 1) + jnp.sum((local[:, None] >= ends_row).astype(jnp.int32), axis=1)
    key_live = local < ends_row[:, docs - 1]
    start_row = dp_index * rows_dp
    query_pos = start_row + jnp.arange(rows_dp, dtype=jnp.int32)
    query_seg = lax.dynamic_slice_in_dim(key_seg, start_row, rows_dp)
    query_live = lax.dynamic_slice_in_dim(key_live, start_row, rows_dp)
    return (query_pos, query_seg, query_live, key_pos, key_seg, key_live)


def widen(rows_low):
    return lax.all_gather(rows_low, "tensor", axis=0, tiled=True)


def narrow(partial_rows):
    return lax.psum_scatter(
        partial_rows.astype(jnp.bfloat16), "tensor", scatter_dimension=0, tiled=True
    ).astype(jnp.float32)


def fetch_weights(
    qkv_weight, qv_bias, out_weight, up_weight, up_bias, down_weight, norm_gains, norm_biases
):
    w_qkv, b_qv, w_out, w_up, b_up, w_down = (
        lax.all_gather(qkv_weight[0], "dp", axis=0, tiled=True),
        lax.all_gather(qv_bias[0], "dp", axis=2, tiled=True),
        lax.all_gather(out_weight[0], "dp", axis=1, tiled=True),
        lax.all_gather(up_weight[0], "dp", axis=0, tiled=True),
        lax.all_gather(up_bias[0], "dp", axis=1, tiled=True),
        lax.all_gather(down_weight[0], "dp", axis=1, tiled=True),
    )
    gain_rows, bias_rows = (
        lax.all_gather(norm_gains[0], ("dp", "tensor"), axis=1, tiled=True),
        lax.all_gather(norm_biases[0], ("dp", "tensor"), axis=1, tiled=True),
    )
    return (
        w_qkv,
        b_qv.reshape(2, -1).astype(jnp.float32),
        w_out,
        w_up,
        b_up.reshape(-1).astype(jnp.float32),
        w_down,
        gain_rows.astype(jnp.float32),
        bias_rows.astype(jnp.float32),
    )


def block_scores(q_heads, key_block, kpos_block, kseg_block, sight):
    scores = jnp.einsum(
        "qhd,khd->hqk", q_heads, key_block, preferred_element_type=jnp.float32
    ) * HD ** (-0.5)
    allowed = (
        (sight[1][:, None] == kseg_block[None, :])
        & (kpos_block[None, :] <= sight[0][:, None])
        & sight[2][:, None]
    )
    return (jnp.where(allowed[None], scores, NEG_FILL), allowed)


def key_blocks(keys, values, sight):
    seq_len = keys.shape[0]
    block_rows = math.gcd(seq_len, 512)
    blocks = seq_len // block_rows
    heads = keys.shape[1] // HD
    return (
        keys.reshape(blocks, block_rows, heads, HD),
        values.reshape(blocks, block_rows, heads, HD),
        sight[3].reshape(blocks, block_rows),
        sight[4].reshape(blocks, block_rows),
    )


def attend(queries, keys, values, sight):
    rows = queries.shape[0]
    heads = queries.shape[1] // HD
    q_heads = queries.reshape(rows, heads, HD)
    stacked = key_blocks(keys, values, sight)

    def find_scale(carry, pieces):
        top, total = carry
        scores, allowed = block_scores(q_heads, pieces[0], pieces[2], pieces[3], sight)
        new_top = jnp.maximum(top, jnp.max(scores, axis=-1))
        total = total * jnp.exp(top - new_top) + jnp.sum(
            jnp.exp(scores - new_top[..., None]), axis=-1
        )
        return ((new_top, total), None)

    start = (jnp.full((heads, rows), -jnp.inf, jnp.float32), jnp.zeros((heads, rows), jnp.float32))
    (top, total), ignored = lax.scan(find_scale, start, stacked)
    log_total = top + jnp.log(total)

    def weigh(carry, pieces):
        scores, allowed = block_scores(q_heads, pieces[0], pieces[2], pieces[3], sight)
        probs = jnp.exp(scores - log_total[..., None]).astype(jnp.bfloat16)
        return (
            carry
            + jnp.einsum("hqk,khd->qhd", probs, pieces[1], preferred_element_type=jnp.float32),
            None,
        )

    heads_out, ignored = lax.scan(weigh, jnp.zeros((rows, heads, HD), jnp.float32), stacked)
    return (heads_out, log_total, q_heads)


def attend_back(q_heads, keys, values, sight, log_total, grad_heads, delta):
    seq_len = keys.shape[0]
    stacked = key_blocks(keys, values, sight)
    scaling = HD ** (-0.5)

    def one_step(grad_q, pieces):
        scores, allowed = block_scores(q_heads, pieces[0], pieces[2], pieces[3], sight)
        probs = jnp.exp(scores - log_total[..., None])
        grad_p = jnp.einsum(
            "qhd,khd->hqk", grad_heads, pieces[1], preferred_element_type=jnp.float32
        )
        grad_s = jnp.where(allowed[None], probs * (grad_p - delta[..., None]), 0.0).astype(
            jnp.bfloat16
        )
        grad_q = (
            grad_q
            + jnp.einsum("hqk,khd->qhd", grad_s, pieces[0], preferred_element_type=jnp.float32)
            * scaling
        )
        grad_v = jnp.einsum(
            "hqk,qhd->khd",
            probs.astype(jnp.bfloat16),
            grad_heads,
            preferred_element_type=jnp.float32,
        )
        grad_k = (
            jnp.einsum("hqk,qhd->khd", grad_s, q_heads, preferred_element_type=jnp.float32)
            * scaling
        )
        return (grad_q, (grad_k, grad_v))

    grad_q, outputs = lax.scan(one_step, jnp.zeros(q_heads.shape, jnp.float32), stacked)
    return (grad_q, outputs[0].reshape(seq_len, -1), outputs[1].reshape(seq_len, -1))


def forward(entering, weights, sight):
    w_qkv, b_qv, w_out, w_up, b_up, w_down, gain_rows, bias_rows = weights
    hidden = entering.astype(jnp.float32)
    normed_a, unit_a, inverse_a = layer_norm(hidden, gain_rows[0], bias_rows[0])
    rows_a = widen(normed_a.astype(jnp.bfloat16))
    projected = jnp.einsum("rd,djh->rjh", rows_a, w_qkv, preferred_element_type=jnp.float32)
    queries = (projected[:, 0] + b_qv[0]).astype(jnp.bfloat16)
    keys_own = projected[:, 1].astype(jnp.bfloat16)
    values_own = (projected[:, 2] + b_qv[1]).astype(jnp.bfloat16)
    keys, values = (
        lax.all_gather(keys_own, "dp", axis=0, tiled=True),
        lax.all_gather(values_own, "dp", axis=0, tiled=True),
    )
    heads_out, log_total, q_heads = attend(queries, keys, values, sight)
    live_rows = sight[2].astype(jnp.float32)
    mixed_low = (heads_out.reshape(heads_out.shape[0], -1) * live_rows[:, None]).astype(
        jnp.bfloat16
    )
    middle = (
        hidden
        + narrow(jnp.dot(mixed_low, w_out, preferred_element_type=jnp.float32))
        + bias_rows[1]
    )
    normed_b, unit_b, inverse_b = layer_norm(middle, gain_rows[1], bias_rows[2])
    rows_b = widen(normed_b.astype(jnp.bfloat16))
    preact = jnp.dot(rows_b, w_up, preferred_element_type=jnp.float32) + b_up
    activated = jax.nn.gelu(preact, approximate=False).astype(jnp.bfloat16)
    result = (
        middle
        + narrow(jnp.dot(activated, w_down, preferred_element_type=jnp.float32))
        + bias_rows[3]
    )
    saved = (
        unit_a,
        inverse_a,
        rows_a,
        q_heads,
        keys,
        values,
        heads_out,
        log_total,
        mixed_low,
        unit_b,
        inverse_b,
        rows_b,
        preact,
        activated,
    )
    return (result, saved)


def backward(saved, grad_out, weights, sight):
    w_qkv, b_qv, w_out, w_up, b_up, w_down, gain_rows, bias_rows = weights
    (
        unit_a,
        inverse_a,
        rows_a,
        q_heads,
        keys,
        values,
        heads_out,
        log_total,
        mixed_low,
        unit_b,
        inverse_b,
        rows_b,
        preact,
        activated,
    ) = saved
    rows = rows_a.shape[0]
    grad_branch = grad_out.astype(jnp.bfloat16)
    down_bias_grad = jnp.sum(grad_branch.astype(jnp.float32), axis=0)
    wide_branch = widen(grad_branch)
    grad_act = jnp.einsum("rd,fd->rf", wide_branch, w_down, preferred_element_type=jnp.float32)
    ignored, gelu_pull = jax.vjp(partial(jax.nn.gelu, approximate=False), preact)
    grad_pre = gelu_pull(grad_act)[0].astype(jnp.bfloat16)
    up_bias_grad = jnp.sum(grad_pre.astype(jnp.float32), axis=0)
    grad_normed_b = narrow(
        jnp.einsum("rf,df->rd", grad_pre, w_up, preferred_element_type=jnp.float32)
    )
    gain_b_grad = jnp.sum(grad_normed_b * unit_b, axis=0)
    shift_b_grad = jnp.sum(grad_normed_b, axis=0)
    grad_middle = grad_out + norm_back(grad_normed_b, unit_b, inverse_b, gain_rows[1])
    grad_attn = grad_middle.astype(jnp.bfloat16)
    out_bias_grad = jnp.sum(grad_attn.astype(jnp.float32), axis=0)
    wide_attn = widen(grad_attn)
    live_rows = sight[2].astype(jnp.bfloat16)
    grad_flat = (
        jnp.einsum("rd,ed->re", wide_attn, w_out, preferred_element_type=jnp.float32).astype(
            jnp.bfloat16
        )
        * live_rows[:, None]
    )
    grad_heads = grad_flat.reshape(heads_out.shape)
    delta = jnp.einsum("qhd,qhd->hq", grad_heads.astype(jnp.float32), heads_out)
    grad_q, grad_k_all, grad_v_all = attend_back(
        q_heads, keys, values, sight, log_total, grad_heads, delta
    )
    grad_k, grad_v = (
        lax.psum_scatter(
            grad_k_all.astype(jnp.bfloat16), "dp", scatter_dimension=0, tiled=True
        ).astype(jnp.float32),
        lax.psum_scatter(
            grad_v_all.astype(jnp.bfloat16), "dp", scatter_dimension=0, tiled=True
        ).astype(jnp.float32),
    )
    grad_proj = jnp.stack((grad_q.reshape(rows, -1), grad_k, grad_v), axis=1).astype(jnp.bfloat16)
    proj_sums = jnp.sum(grad_proj.astype(jnp.float32), axis=0)
    qv_grad = jnp.stack((proj_sums[0], proj_sums[2]))
    grad_normed_a = narrow(
        jnp.einsum("rjh,djh->rd", grad_proj, w_qkv, preferred_element_type=jnp.float32)
    )
    gain_a_grad = jnp.sum(grad_normed_a * unit_a, axis=0)
    shift_a_grad = jnp.sum(grad_normed_a, axis=0)
    grad_in = grad_middle + norm_back(grad_normed_a, unit_a, inverse_a, gain_rows[0])
    gains_grad = jnp.stack((gain_a_grad, gain_b_grad))
    biases_grad = jnp.stack((shift_a_grad, out_bias_grad, shift_b_grad, down_bias_grad))
    factors = (rows_b, grad_pre, activated, wide_branch, mixed_low, wide_attn, rows_a, grad_proj)
    vectors = (qv_grad, up_bias_grad, gains_grad, biases_grad)
    return (grad_in, factors, vectors)


def weight_products(factors):
    rows_b, grad_pre, activated, wide_branch, mixed_low, wide_attn, rows_a, grad_proj = factors
    down_grad = jnp.einsum("rf,rd->fd", activated, wide_branch, preferred_element_type=jnp.float32)
    up_grad = jnp.einsum("rd,rf->df", rows_b, grad_pre, preferred_element_type=jnp.float32)
    out_grad = jnp.einsum("re,rd->ed", mixed_low, wide_attn, preferred_element_type=jnp.float32)
    qkv_grad = jnp.einsum("rd,rjh->djh", rows_a, grad_proj, preferred_element_type=jnp.float32)
    return (qkv_grad, out_grad, up_grad, down_grad)


def assemble(products, vectors):
    qkv_grad, out_grad, up_grad, down_grad = products
    qv_grad, up_bias_grad, gains_grad, biases_grad = vectors
    return (qkv_grad, qv_grad, out_grad, up_grad, up_bias_grad, down_grad, gains_grad, biases_grad)


def reduce_grads(local_grads):
    qkv_grad, qv_grad, out_grad, up_grad, up_bias_grad, down_grad, gains_grad, biases_grad = (
        local_grads
    )
    heads = qv_grad.shape[1] // HD
    shards = (
        lax.psum_scatter(
            qkv_grad[None].astype(jnp.bfloat16), "dp", scatter_dimension=1, tiled=True
        ).astype(jnp.float32),
        lax.psum_scatter(
            qv_grad.reshape(1, 2, heads, HD).astype(jnp.bfloat16),
            "dp",
            scatter_dimension=3,
            tiled=True,
        ).astype(jnp.float32),
        lax.psum_scatter(
            out_grad[None].astype(jnp.bfloat16), "dp", scatter_dimension=2, tiled=True
        ).astype(jnp.float32),
        lax.psum_scatter(
            up_grad[None].astype(jnp.bfloat16), "dp", scatter_dimension=1, tiled=True
        ).astype(jnp.float32),
        lax.psum_scatter(
            up_bias_grad.reshape(1, -1, HD).astype(jnp.bfloat16),
            "dp",
            scatter_dimension=2,
            tiled=True,
        ).astype(jnp.float32),
        lax.psum_scatter(
            down_grad[None].astype(jnp.bfloat16), "dp", scatter_dimension=2, tiled=True
        ).astype(jnp.float32),
    )
    vectors = (
        lax.psum_scatter(gains_grad[None], ("dp", "tensor"), scatter_dimension=2, tiled=True),
        lax.psum_scatter(biases_grad[None], ("dp", "tensor"), scatter_dimension=2, tiled=True),
    )
    return tuple(shards) + tuple(vectors)


def body(
    boundary,
    doc_lengths,
    qkv_weight,
    qv_bias,
    out_weight,
    up_weight,
    up_bias,
    down_weight,
    norm_gains,
    norm_biases,
):
    section_index = lax.axis_index("section")
    on_first = section_index == 0
    own_part = boundary[0]
    batches = own_part.shape[0]
    rows_dp = own_part.shape[1] * lax.axis_size("tensor")
    seq_len = rows_dp * lax.axis_size("dp")
    dp_index = lax.axis_index("dp")
    sources = (
        qkv_weight,
        qv_bias,
        out_weight,
        up_weight,
        up_bias,
        down_weight,
        norm_gains,
        norm_biases,
    )
    fixed_weights = fetch_weights(*sources)

    def current():
        return fixed_weights

    def sight_for(batch_at):
        lengths = lax.dynamic_index_in_dim(doc_lengths, batch_at, 0, keepdims=False)
        return visibility(lengths, dp_index, rows_dp, seq_len)

    def pick(first_value, second_value):
        return jnp.where(on_first, first_value, second_value)

    received = jnp.zeros_like(own_part[0])
    kept_ticks, exits = ([], [])
    for tick_index in range(batches + 1):
        entering = jnp.where(on_first, own_part[min(tick_index, batches - 1)], received)
        batch_at = jnp.clip(tick_index - section_index, 0, batches - 1)
        result, saved = forward(entering, current(), sight_for(batch_at))
        leaving = result.astype(jnp.bfloat16)
        kept_ticks.append(saved)
        exits.append(leaving)
        if tick_index < batches:
            received = from_behind(leaving, "section", 1)
    acts = jnp.stack(
        [jnp.where(on_first, exits[number], exits[number + 1]) for number in range(batches)]
    )[None]
    returned = jnp.zeros_like(own_part[0])
    summed = None
    vector_sum = None
    factor_ticks = []
    leaving_grads = []
    for tick_index in range(batches + 1):
        own_grad = own_part[min(tick_index, batches - 1)].astype(jnp.float32)
        if tick_index == batches:
            own_grad = jnp.zeros_like(own_grad)
        grad_out = jnp.where(on_first, returned.astype(jnp.float32), own_grad)
        saved = jax.tree.map(
            pick, kept_ticks[max(tick_index - 1, 0)], kept_ticks[min(tick_index + 1, batches)]
        )
        batch_at = jnp.where(on_first, max(tick_index - 1, 0), min(tick_index, batches - 1))
        grad_in, factors, vectors = backward(saved, grad_out, current(), sight_for(batch_at))
        leaving_grads.append(grad_in)
        if tick_index < batches:
            returned = from_behind(grad_in.astype(jnp.bfloat16), "section", -1)
        factor_ticks.append(factors)
        vector_sum = (
            vectors
            if vector_sum is None
            else tuple((former + latter for former, latter in zip(vector_sum, vectors)))
        )
    joined = tuple(
        (
            jnp.concatenate([entry[number] for entry in factor_ticks], axis=0)
            for number in range(len(factor_ticks[0]))
        )
    )
    summed = reduce_grads(assemble(weight_products(joined), vector_sum))
    input_grads = jnp.stack(
        [
            jnp.where(on_first, leaving_grads[number + 1], leaving_grads[number])
            for number in range(batches)
        ]
    )[None]
    return (acts, input_grads) + tuple(summed)


LOW, WIDE = (jnp.bfloat16, jnp.float32)
HBM, VMEM, DMAS = (pl.ANY, pltpu.VMEM, pltpu.SemaphoreType.DMA)


def dot(left, right):
    return jnp.dot(left, right, preferred_element_type=WIDE)


def dot_back(left, right):
    return lax.dot_general(left, right, (((1,), (1,)), ((), ())), preferred_element_type=WIDE)


def dot_rows(left, right):
    return lax.dot_general(left, right, (((0,), (0,)), ((), ())), preferred_element_type=WIDE)


def device(core, z, x, y):
    return (core, z * 2 + x, y)


class Plane:
    def __init__(self):
        dp = lax.axis_index("dp")
        self.levels = lax.axis_size("dp") // 2
        self.core, self.y = (lax.axis_index("section"), lax.axis_index("tensor"))
        self.z, self.x = (dp // 2, lax.rem(dp, 2))
        self.sibling = device(1 - self.core, self.z, self.x, self.y)
        self.across = device(self.core, self.z, self.x, 1 - self.y)
        self.over = device(self.core, self.z, 1 - self.x, self.y)
        self.corner = device(1 - self.core, self.z, 1 - self.x, self.y)
        self.member = self.z * 2 + self.core
        self.block = self.z * 4 + self.core * 2 + self.y

    def along(self, z):
        return device(self.core, jnp.clip(z, 0, self.levels - 1), self.x, self.y)

    def partners(self):
        partners = [self.across, self.over, self.corner]
        for step in range(self.levels):
            zz = lax.rem(self.z + step, self.levels)
            for other in (0, 1):
                if step or other:
                    core = 1 - self.core if other else self.core
                    partners.append(device(core, zz, self.x, self.y))
        return partners

    def nearest(self):
        tables = []
        for z in range(self.levels):
            tables.append(sorted(range(self.levels), key=lambda zz: (abs(zz - z), zz)))
        found = []
        for place in range(self.levels):
            number = jnp.int32(tables[0][place])
            for z in range(1, self.levels):
                number = jnp.where(self.z == z, tables[z][place], number)
            found.append(number)
        return found


def guarded(present, act):
    if present is True:
        act()
    else:
        pl.when(present)(act)


class Sends:
    def __init__(self, sems):
        self.sems = sems
        self.pending = []

    def start(self, present, source, target, arrived, partner):
        copy = pltpu.make_async_remote_copy(
            src_ref=source,
            dst_ref=target,
            send_sem=self.sems.at[len(self.pending)],
            recv_sem=arrived,
            device_id=partner,
            device_id_type=MESH,
        )
        guarded(present, copy.start)
        self.pending.append([present, copy, False])
        return len(self.pending) - 1

    def wait(self, *numbers):
        for number in numbers:
            present, copy, done = self.pending[number]
            if not done:
                guarded(present, copy.wait_send)
                self.pending[number][2] = True

    def finish(self):
        self.wait(*range(len(self.pending)))


class Copies:
    def __init__(self, sems):
        self.sems = sems
        self.pending = []

    def start(self, source, target, present=True):
        copy = pltpu.make_async_copy(source, target, self.sems.at[len(self.pending)])
        guarded(present, copy.start)
        self.pending.append([present, copy, False])
        return len(self.pending) - 1

    def wait(self, *numbers):
        for number in numbers:
            present, copy, done = self.pending[number]
            if not done:
                guarded(present, copy.wait)
                self.pending[number][2] = True

    def finish(self):
        for number in range(len(self.pending)):
            self.wait(number)


def await_block(block, arrived, partner):
    pltpu.make_async_remote_copy(
        src_ref=block,
        dst_ref=block,
        send_sem=arrived,
        recv_sem=arrived,
        device_id=partner,
        device_id_type=MESH,
    ).wait_recv()


def span(start, size):
    return pl.ds(pl.multiple_of(start * size, size), size)


class Gather:
    def __init__(self, plane, sends, rows, sems):
        self.plane, self.sends, self.rows, self.sems = (plane, sends, rows, sems)
        self.chunks = sems.shape[1]
        self.size = rows.shape[0] // (sems.shape[0] * self.chunks)

    def spot(self, zz, core, y, chunk):
        number = zz * 4 + core * 2 + y
        return (
            self.rows.at[span(number * self.chunks + chunk, self.size)],
            self.sems.at[number, chunk],
        )

    def open(self):
        plane = self.plane
        for chunk in range(self.chunks):
            held, arrived = self.spot(plane.z, plane.core, plane.y, chunk)
            for present, partner in (
                (True, plane.across),
                (plane.z > 0, plane.along(plane.z - 1)),
                (plane.z < plane.levels - 1, plane.along(plane.z + 1)),
                (True, plane.sibling),
            ):
                self.sends.start(present, held, held, arrived, partner)

    def run(self, on_group, tick):
        plane = self.plane
        order = plane.nearest()

        def complete(step):
            zz = order[step]
            for chunk in range(self.chunks):
                held, arrived = self.spot(zz, plane.core, 1 - plane.y, chunk)
                await_block(held, arrived, plane.across)
                self.sends.start(True, held, held, arrived, plane.sibling)
            for yy in (plane.y, 1 - plane.y):
                for chunk in range(self.chunks):
                    held, arrived = self.spot(zz, 1 - plane.core, yy, chunk)
                    await_block(held, arrived, plane.sibling)
            on_group(step, zz)

        for step in range(1, plane.levels):
            zz = order[step]
            onward = jnp.where(zz < plane.z, plane.z + 1, plane.z - 1)
            can_go = (onward >= 0) & (onward < plane.levels)
            for chunk in range(self.chunks):
                held, arrived = self.spot(zz, plane.core, plane.y, chunk)
                await_block(held, arrived, plane.across)
                self.sends.start(can_go, held, held, arrived, plane.along(onward))
                self.sends.start(True, held, held, arrived, plane.across)
                self.sends.start(True, held, held, arrived, plane.sibling)
            tick()
            complete(step - 1)
        complete(plane.levels - 1)
        tick()

    @staticmethod
    def count(levels, chunks):
        return chunks * (4 + 3 * (levels - 1) + levels)


class Scatter:
    def __init__(self, plane, sends, refs, result):
        self.plane, self.sends, self.refs, self.result = (plane, sends, refs, result)
        self.chunks = refs.across_sems.shape[1]
        self.size = result.shape[0] // self.chunks

    @staticmethod
    def count(levels, chunks):
        return chunks * (4 * levels - 1)

    def part(self, zz, core, y, chunk):
        number = (zz * 4 + core * 2 + y) * self.chunks + chunk
        return self.refs.part.at[span(number, self.size)]

    def spot(self, buffer, sems, slot, chunk):
        return buffer.at[slot, span(chunk, self.size)], sems.at[slot, chunk]

    def take(self, buffer, sems, slot, chunk):
        came, arrived = self.spot(buffer, sems, slot, chunk)
        await_block(came, arrived, self.plane.across)
        return came[...].astype(WIDE)

    def pair(self, zz, y, chunk):
        refs = self.refs
        own = self.part(zz, self.plane.core, y, chunk)[...].astype(WIDE)
        return own + self.take(refs.from_sibling, refs.sibling_sems, zz * 2 + y, chunk)

    def give_sibling(self, zz):
        plane, refs = (self.plane, self.refs)
        for yy in (1 - plane.y, plane.y):
            for chunk in range(self.chunks):
                landing, arrived = self.spot(
                    refs.from_sibling, refs.sibling_sems, zz * 2 + yy, chunk
                )
                self.sends.start(
                    True, self.part(zz, 1 - plane.core, yy, chunk), landing, arrived, plane.sibling
                )

    def give_across(self, zz):
        plane, refs = (self.plane, self.refs)
        for chunk in range(self.chunks):
            staged = refs.from_sibling.at[zz * 2 + 1 - plane.y, span(chunk, self.size)]
            staged[...] = self.pair(zz, 1 - plane.y, chunk).astype(staged.dtype)
            landing, arrived = self.spot(refs.from_across, refs.across_sems, zz, chunk)
            self.sends.start(True, staged, landing, arrived, plane.across)

    def plane_sum(self, zz, chunk):
        refs = self.refs
        total = self.pair(zz, self.plane.y, chunk)
        return total + self.take(refs.from_across, refs.across_sems, zz, chunk)

    def come(self, slot, chunk):
        return self.take(self.refs.from_behind, self.refs.behind_sems, slot, chunk)

    def give_onward(self, zz):
        plane, refs = (self.plane, self.refs)
        onward = jnp.where(zz > plane.z, plane.z + 1, plane.z - 1)
        behind = plane.z * 2 - onward
        slot = jnp.where((onward == zz) & (zz < plane.z), plane.levels, zz)
        for chunk in range(self.chunks):
            refs.total[...] = self.plane_sum(zz, chunk)

            @pl.when((behind >= 0) & (behind < plane.levels))
            def _(chunk=chunk):
                refs.total[...] += self.come(zz, chunk)

            staged = refs.from_sibling.at[zz * 2 + plane.y, span(chunk, self.size)]
            staged[...] = refs.total[...].astype(staged.dtype)
            landing, arrived = self.spot(refs.from_behind, refs.behind_sems, slot, chunk)
            self.sends.start(True, staged, landing, arrived, plane.along(onward))

    def conclude(self):
        plane = self.plane
        for chunk in range(self.chunks):
            own = self.result.at[span(chunk, self.size)]
            own[...] = self.plane_sum(plane.z, chunk)

            @pl.when(plane.z > 0)
            def _(own=own, chunk=chunk):
                own[...] += self.come(plane.z, chunk)

            @pl.when(plane.z < plane.levels - 1)
            def _(own=own, chunk=chunk):
                own[...] += self.come(plane.levels, chunk)

    def run(self, make, tick, fill=None):
        levels = self.plane.levels
        order = self.plane.nearest()[::-1]
        for step in range(levels + 3):
            if step < levels:
                make(step, order[step])
                self.give_sibling(order[step])
            if 0 < step <= levels:
                self.give_across(order[step - 1])
            if step >= levels - 1:
                tick()
                if fill is not None:
                    fill(step - levels + 1)
            if 3 <= step < levels + 2:
                self.give_onward(order[step - 3])
        self.conclude()


def scatter_scratch(rows, width, levels, chunks, dtype=LOW):
    def held(count):
        return VMEM((count, rows, width), dtype)

    return dict(
        part=VMEM((rows * 4 * levels, width), dtype),
        from_sibling=held(2 * levels),
        from_across=held(levels),
        from_behind=held(levels + 1),
        total=VMEM((rows // chunks, width), WIDE),
        sum=VMEM((rows, width), WIDE),
        sibling_sems=DMAS((2 * levels, chunks)),
        across_sems=DMAS((levels, chunks)),
        behind_sems=DMAS((levels + 1, chunks)),
    )


def by_rows(which):
    return which in (1, 3)


def piece_of_shard(which, ref, member, members):
    if which == 0:
        return ref.at[:, :, span(member, ref.shape[2] // members)]
    if by_rows(which):
        return ref.at[span(member, ref.shape[0] // members)]
    return ref.at[:, span(member, ref.shape[1] // members)]


def piece_of_slice(which, ref, shard, shards):
    if by_rows(which):
        return ref.at[:, span(shard, ref.shape[1] // shards)]
    return ref.at[span(shard, ref.shape[0] // shards)]


def matched(which, of_shard, of_slice):
    if which:
        return [(of_shard, of_slice)]
    kinds, _, depth = of_shard.shape
    return [
        (of_shard.at[kind], of_slice.at[:, pl.ds(kind * depth, depth)]) for kind in range(kinds)
    ]


def slice_shape(which, shape, shards):
    if which == 0:
        return (shape[1] * shards, shape[0] * shape[2] // shards)
    rows, columns = shape
    if by_rows(which):
        return (rows // shards, columns * shards)
    return (rows * shards, columns // shards)


def shard_shape(which, shape, shards):
    rows, columns = shape
    if which == 0:
        return (3, rows // shards, columns * shards // 3)
    if by_rows(which):
        return (rows * shards, columns // shards)
    return (rows // shards, columns * shards)


FETCHES = (
    ((0, 0), (2, 0), (2, 2), (0, 2)),
    ((0, 0), (0, 1), (2, 1), (2, 1), (0, 0), (0, 1), (0, 1), (0, 1)),
    ((0, 1), (0, 1), (2, 0), (2, 0), (0, 0), (0, 1), (2, 1), (2, 2)),
    ((0, 1), (0, 1), (2, 1), (2, 1), (0, 0), (0, 0), (0, 2), (0, 1)),
    ((0, 1), (0, 0), (0, 0), (0, 0), (0, 0), (0, 0), (0, 0), (0, 0)),
)
ADDS = (
    (0, 0, 1, 2),
    (0, 0, 2, 3, 0, 0, 0, 0),
    (2, 2, 2, 2, 0, 0, 1, 1),
    (0, 1, 2, 3, 0, 2, 2, 2),
    (1, 1, 0, 0),
)


class Fetch:
    UNITS = ((0, (0, 1)), (0, (2,)), (0, (3,)), (1, (0, 1)), (1, (2,)), (1, (3,)))

    def __init__(self, plane, shards, slices, refs, sends, copies):
        self.plane, self.shards, self.slices = (plane, shards, slices)
        self.refs, self.sends, self.copies = (refs, sends, copies)
        self.spreads = []
        for unit in range(len(self.UNITS)):
            for step in range(plane.levels - 1, -1, -1):
                self.spreads.append((unit, step))
        self.hands = list(self.spreads)
        self.left = [plane.levels] * len(self.UNITS)
        self.kept = [[] for _ in self.UNITS]
        self.plan = [moment for stage in FETCHES for moment in stage]

    @staticmethod
    def count(levels):
        return 4 * 2 * (3 * levels) + 8 * levels, 4 * 2 + 8 + 4

    def tick(self):
        self.start(*self.plan.pop(0))

    def start(self, spreads, hands):
        for _ in range(spreads):
            if self.spreads:
                unit, step = self.spreads.pop(0)
                for which in self.UNITS[unit][1]:
                    self.spread(unit, which, step)
        for _ in range(hands):
            if len(self.hands) > len(self.spreads):
                unit, step = self.hands.pop(0)
                for which in self.UNITS[unit][1]:
                    self.hand_over(unit, which, step)
                self.left[unit] -= 1

    def require(self, unit):
        while self.left[unit]:
            self.start(0, 1) if len(self.hands) > len(self.spreads) else self.start(1, 0)
        plane, refs = (self.plane, self.refs)
        layer, weights = self.UNITS[unit]
        for which in weights:
            part = self.slices[which].at[layer]
            for zz in range(plane.levels):
                held = piece_of_slice(which, part, zz * 2 + 1 - plane.x, 2 * plane.levels)
                await_block(held, refs.cross_sems.at[which, layer, zz], plane.over)
        self.copies.wait(*self.kept[unit])
        for which in weights:
            self.copies.start(self.slices[which].at[layer], refs.slices_out[which].at[layer])

    def spread(self, unit, which, step):
        plane, refs, layer = (self.plane, self.refs, self.UNITS[unit][0])
        members = 2 * plane.levels
        shard, part = (self.shards[which], self.slices[which].at[layer])
        owner = plane.core == layer
        target = piece_of_slice(which, part, plane.z * 2 + plane.x, members)
        zz = lax.rem(plane.z + step, plane.levels)
        for other in (0, 1):
            core = 1 - plane.core if other else plane.core
            piece = piece_of_shard(which, shard, zz * 2 + core, members)
            for source, landing in matched(which, piece, target):
                if step or other:
                    self.sends.start(
                        owner,
                        source,
                        landing,
                        refs.column_sems.at[which, layer, plane.z],
                        device(core, zz, plane.x, plane.y),
                    )
                else:
                    self.kept[unit].append(self.copies.start(source, landing, owner))

    def hand_over(self, unit, which, step):
        plane, refs, layer = (self.plane, self.refs, self.UNITS[unit][0])
        members = 2 * plane.levels
        shard, part = (self.shards[which], self.slices[which].at[layer])
        zz = lax.rem(plane.z - step + plane.levels, plane.levels)
        held = piece_of_slice(which, part, zz * 2 + plane.x, members)
        arrived = refs.column_sems.at[which, layer, zz]
        cross = refs.cross_sems.at[which, layer, zz]
        if step:
            await_block(held, arrived, plane.over)
            self.sends.start(True, held, held, cross, plane.over)
        else:
            owner = plane.core == layer
            source = piece_of_shard(which, shard, plane.member, members)
            guarded(jnp.logical_not(owner), partial(await_block, held, arrived, plane.over))
            self.sends.start(jnp.logical_not(owner), held, held, cross, plane.over)
            for end, landing in matched(which, source, held):
                self.sends.start(owner, end, landing, cross, plane.over)


class Return:
    def __init__(self, plane, slices, landed, shards, refs, sends, copies):
        self.plane, self.slices, self.landed, self.shards = (plane, slices, landed, shards)
        self.refs, self.sends, self.copies = (refs, sends, copies)
        self.moments, self.left, self.given = ([], {}, {})
        self.plan = [count for stage in ADDS for count in stage]

    @staticmethod
    def count(levels):
        return 4 * 2 * (2 * levels) + 4 * levels, 4 * 2 + 4

    def give(self, layer, which):
        plane = self.plane
        self.left[layer, which], self.given[layer, which] = (plane.levels, [])
        for step in range(plane.levels - 1, -1, -1):
            zz = lax.rem(plane.z + step, plane.levels)
            number = self.sends.start(
                True,
                piece_of_slice(which, self.slices[which], zz * 2 + 1 - plane.x, 2 * plane.levels),
                self.landed[which].at[layer, zz],
                self.refs.cross_sems.at[which, layer, zz],
                plane.over,
            )
            self.given[layer, which].append(number)
            self.moments.append((layer, which, step))

    def tick(self):
        self.start(self.plan.pop(0))

    def start(self, adds):
        for _ in range(adds):
            if self.moments:
                moment = self.moments.pop(0)
                self.add(*moment)
                self.left[moment[:2]] -= 1

    def require(self, layer, which):
        while self.left[layer, which]:
            self.start(1)
        self.sends.wait(*self.given[layer, which])

    def add(self, layer, which, step):
        plane, refs = (self.plane, self.refs)
        members = 2 * plane.levels
        here = plane.core == layer
        target = piece_of_shard(which, self.shards[which], plane.member, members)
        zz = lax.rem(plane.z + step, plane.levels)
        held = self.landed[which].at[layer, zz]
        await_block(held, refs.cross_sems.at[which, layer, zz], plane.over)
        own = piece_of_slice(which, self.slices[which], zz * 2 + plane.x, members)
        held[...] = (held[...].astype(WIDE) + own[...].astype(WIDE)).astype(LOW)
        for landing, source in matched(which, target, held):
            self.sends.start(
                True if step else jnp.logical_not(here),
                source,
                landing,
                refs.column_sems.at[which, plane.core, plane.z],
                device(layer, zz, plane.x, plane.y),
            )
            if step == 0:
                self.copies.start(source, landing, here)

    def finish(self):
        self.start(len(self.moments))
        plane, refs = (self.plane, self.refs)
        members = 2 * plane.levels
        for which in range(4):
            for core in (0, 1):
                for step in range(plane.levels):
                    zz = lax.rem(plane.z + step, plane.levels)
                    held = piece_of_shard(which, self.shards[which], zz * 2 + core, members)
                    guarded(
                        True if step else plane.core != core,
                        partial(
                            await_block, held, refs.column_sems.at[which, core, zz], plane.over
                        ),
                    )


class Outward:
    @staticmethod
    def count():
        return 6, 2

    def __init__(self, plane, target, sems):
        self.plane, self.target, self.sems = (plane, target, sems)

    def give(self, layer, source, sends, copies):
        plane, target = (self.plane, self.target.at[self.plane.x])
        same_core, same_x = (plane.core == layer, plane.core == plane.x)
        other_core, other_x = (plane.core != layer, plane.core != plane.x)
        for present, partner in (
            (same_core & other_x, plane.over),
            (other_core & same_x, plane.sibling),
            (other_core & other_x, plane.corner),
        ):
            sends.start(present, source, target, self.sems.at[plane.x], partner)
        copies.start(source, target, same_core & same_x)

    def finish(self):
        plane = self.plane
        for slot in (0, 1):
            away = jnp.logical_not((plane.core == plane.x) & (plane.x == slot))
            guarded(away, partial(await_block, self.target.at[slot], self.sems.at[slot], plane.over))


def launch(name, ident, kernel, counts, inputs, outputs, scratch):
    scratch = dict(
        scratch,
        send_sems=DMAS((counts[0],)),
        phase_sems=DMAS((counts[1],)),
        copy_sems=DMAS((counts[2],)),
    )
    names = list(inputs) + list(outputs) + list(scratch)

    def body(*refs):
        held = SimpleNamespace(**dict(zip(names, refs)))
        plane = Plane()
        barrier = pltpu.get_barrier_semaphore()
        partners = plane.partners()
        for partner in partners:
            pl.semaphore_signal(barrier, inc=1, device_id=partner, device_id_type=MESH)
        sends, copies = (Sends(held.send_sems), Copies(held.copy_sems))
        kernel(held, plane, lambda: pl.semaphore_wait(barrier, len(partners)), sends, copies)
        copies.finish()
        sends.finish()
        assert len(sends.pending) == counts[0], len(sends.pending)
        assert len(copies.pending) == counts[2], len(copies.pending)

    results = pl.pallas_call(
        body,
        out_shape=[jax.ShapeDtypeStruct(shape, dtype) for shape, dtype, _ in outputs.values()],
        in_specs=[pl.BlockSpec(memory_space=space) for _, space in inputs.values()],
        out_specs=[pl.BlockSpec(memory_space=space) for _, _, space in outputs.values()],
        scratch_shapes=list(scratch.values()),
        compiler_params=pltpu.CompilerParams(
            collective_id=ident, has_side_effects=True, vmem_limit_bytes=60 << 20
        ),
        name=name,
    )(*[array for array, _ in inputs.values()])
    return SimpleNamespace(**dict(zip(outputs, results)))


CHUNKS, SUM_CHUNKS, CUT = (2, 2, 512)
NORM_LINES, HEAD_LINES, LINES = (6, 8, 16)


def unpack_vectors(refs, plane, levels):
    members, blocks = (2 * levels, 4 * levels)
    for layer in (0, 1):
        for z in range(levels):
            for x in (0, 1):
                for y in (0, 1):
                    start = ((z * 4 + layer * 2 + y) * 2 + x) * LINES
                    cut = (z * 4 + x * 2 + y) * HD
                    refs.norms[layer, :, cut : cut + HD] = refs.small[
                        start : start + LINES
                    ].astype(WIDE)[:HEAD_LINES]
    lines = []
    for layer in (0, 1):
        pieces = []
        for z in range(levels):
            for x in (0, 1):
                number = (z * 4 + layer * 2 + plane.y) * 2 + x
                pieces.append(refs.small[span(number, LINES)].astype(WIDE)[HEAD_LINES:])
        lines.append(jnp.concatenate(pieces, axis=1))
    lines = jnp.concatenate(lines, axis=0).astype(LOW)
    width = HD // members
    place = lax.broadcasted_iota(jnp.int32, (members * HD, HD), 0)
    lane = lax.broadcasted_iota(jnp.int32, (members * HD, HD), 1)

    def pick(first):
        chosen = (place // HD == lane // width) & (place % HD == lane % width + first)
        return dot(lines, chosen.astype(WIDE).astype(LOW))

    heads = pick(plane.member * width)
    units = refs.b_up.shape[2] // HD
    per_line = HD // (units * width)
    row = lax.broadcasted_iota(jnp.int32, (HEAD_LINES, HD), 0)
    for layer in (0, 1):
        refs.b_qv[layer] = heads[layer * HEAD_LINES : layer * HEAD_LINES + 2]
    for unit in range(units):
        found = pick((lax.rem(plane.member, per_line) * units + unit) * width)
        for layer in (0, 1):
            own = found[layer * HEAD_LINES : (layer + 1) * HEAD_LINES]
            own = jnp.where(row == 2 + plane.member // per_line, own, 0.0)
            refs.b_up[layer, :, unit * HD : (unit + 1) * HD] = jnp.sum(own, axis=0, keepdims=True)


def visible(refs, group, size, tokens):
    segment = refs.query_segment[group]
    place = group.start + lax.broadcasted_iota(jnp.int32, (size, tokens), 0)
    keys = lax.broadcasted_iota(jnp.int32, (size, tokens), 1)
    return (segment == refs.key_segment[...]) & (keys <= place)


def forward_planes(ident, boundary, packed, segments, shards):
    levels = lax.axis_size("dp") // 2
    blocks, members = (4 * levels, 2 * levels)
    rows, width = boundary.shape[1:]
    tokens, size = (blocks * rows, 4 * rows)
    slice_shapes = [
        slice_shape(which, shard.shape, members) for which, shard in enumerate(shards)
    ]
    units = slice_shapes[2][1]
    scaling = HD ** (-0.5)

    def kernel(refs, plane, greet, sends, copies):
        core, x = (plane.core, plane.x)
        own_block = span(plane.block, rows)
        refs.slices_out = [refs.out0, refs.out1, refs.out2, refs.out3]
        slices = [refs.w0, refs.w1, refs.w2, refs.w3]
        fetch = Fetch(
            plane, [refs.shard0, refs.shard1, refs.shard2, refs.shard3], slices, refs, sends, copies
        )
        small_block = span(plane.block * 2 + x, LINES)
        refs.small[small_block] = refs.packed[...]
        greet()
        phase = Sends(refs.phase_sems)
        own_small = refs.small.at[small_block]
        phase.start(True, own_small, own_small, refs.pair_sem.at[0], plane.over)
        inward = []
        for slot in (0, 1):
            source, target = (refs.boundary.at[slot], refs.landed_planes.at[core])
            arrived = refs.inward_sems.at[core]
            for present, partner in (
                ((x == core) & (slot != x), plane.over),
                ((x != core) & (slot == x), plane.sibling),
                ((x != core) & (slot != x), plane.corner),
            ):
                phase.start(present, source, target, arrived, partner)
            inward.append(copies.start(source, target, (x == core) & (slot == x)))
        other_small = refs.small.at[span(plane.block * 2 + 1 - x, LINES)]
        await_block(other_small, refs.pair_sem.at[0], plane.over)
        small = Gather(plane, phase, refs.small, refs.small_sems)
        small.open()
        small.run(lambda step, zz: None, lambda: None)
        fetch.start(levels, 0)
        for slot in (0, 1):
            here = (core == x) & (core == slot)
            guarded(
                jnp.logical_not(here),
                partial(await_block, refs.landed_planes.at[slot], refs.inward_sems.at[slot], plane.over),
            )
        copies.wait(*inward)
        refs.planes[...] = refs.landed_planes[...]
        refs.rows[0, own_block] = refs.landed_planes[1]
        gather = Gather(plane, phase, refs.rows.at[0], refs.gather_sems.at[0])
        gather.open()
        unpack_vectors(refs, plane, levels)
        kept = []

        def keep(step, zz):
            group = span(zz, size)
            kept.append(copies.start(refs.rows.at[0, group], refs.gathered.at[group]))

        gather.run(keep, fetch.tick)
        copies.wait(*kept)
        phase.finish()

        for layer in (0, 1):
            number = 1 + 2 * layer
            norms = refs.norms.at[layer]
            held, sems = (refs.rows.at[number % 2], refs.gather_sems.at[number % 2])
            entering = refs.planes[0] if layer == 0 else refs.leaving[0]
            hidden = entering.astype(WIDE)
            normed, _, _ = layer_norm(hidden, norms[0:1], norms[2:3])
            held[own_block] = normed.astype(LOW)
            phase = Sends(refs.phase_sems)
            gather = Gather(plane, phase, held, sems)
            gather.open()
            fetch.require(3 * layer)
            kept = []

            def project(step, zz):
                group = span(zz, size)
                projected = dot(held[group], refs.w0[layer])
                refs.queries[layer, group] = (projected[:, :HD] + refs.b_qv[layer, 0:1]).astype(LOW)
                refs.keys[layer, group] = projected[:, HD : 2 * HD].astype(LOW)
                refs.values[layer, group] = (
                    projected[:, 2 * HD :] + refs.b_qv[layer, 1:2]
                ).astype(LOW)
                kept.append(copies.start(held.at[group], refs.rows_a.at[layer, group]))

            gather.run(project, fetch.tick)

            def attend(step, zz):
                group = span(zz, size)
                allowed = visible(refs, group, size, tokens)
                scores = dot_back(refs.queries[layer, group], refs.keys[layer]) * scaling
                scores = jnp.where(allowed, scores, NEG_FILL)
                top = jnp.max(scores, axis=-1, keepdims=True)
                raised = jnp.exp(scores - top)
                total = jnp.sum(raised, axis=-1, keepdims=True)
                refs.log_total[layer, group] = top + jnp.log(total)
                probs = (raised / total).astype(LOW)
                live = (refs.query_segment[group] >= 0).astype(WIDE)
                mixed = (dot(probs, refs.values[layer]) * live).astype(LOW)
                refs.mixed[layer, group] = mixed
                for cut in range(0, width, CUT):
                    refs.part[group, cut : cut + CUT] = dot(
                        mixed, refs.w1[layer, :, cut : cut + CUT]
                    ).astype(LOW)

            Scatter(plane, phase, refs, refs.sum).run(attend, fetch.tick)
            middle = hidden + refs.sum[...] + norms[3:4]
            refs.middle[layer] = middle
            copies.wait(*kept)
            phase.finish()

            number = number + 1
            held, sems = (refs.rows.at[number % 2], refs.gather_sems.at[number % 2])
            normed, _, _ = layer_norm(middle, norms[1:2], norms[4:5])
            held[own_block] = normed.astype(LOW)
            phase = Sends(refs.phase_sems)
            gather = Gather(plane, phase, held, sems)
            gather.open()
            fetch.require(3 * layer + 1)
            kept = []

            def expand(step, zz):
                group = span(zz, size)
                preact = dot(held[group], refs.w2[layer]) + refs.b_up[layer]
                refs.own_preact[layer, group] = preact
                refs.own_activated[layer, group] = (
                    0.5 * preact * (1.0 + lax.erf(preact * math.sqrt(0.5)))
                ).astype(LOW)
                for own, out in (
                    (held.at[group], refs.rows_b),
                    (refs.own_preact.at[layer, group], refs.preact),
                    (refs.own_activated.at[layer, group], refs.activated),
                ):
                    kept.append(copies.start(own, out.at[layer, group]))

            gather.run(expand, fetch.tick)
            fetch.require(3 * layer + 2)

            def shrink(step, zz):
                group = span(zz, size)
                for cut in range(0, width, CUT):
                    refs.part[group, cut : cut + CUT] = dot(
                        refs.own_activated[layer, group], refs.w3[layer, :, cut : cut + CUT]
                    ).astype(LOW)

            Scatter(plane, phase, refs, refs.sum).run(shrink, fetch.tick)
            refs.leaving[layer] = (refs.middle[layer] + refs.sum[...] + norms[5:6]).astype(LOW)
            copies.wait(*kept)
            phase.finish()

    head = ((2, tokens, HD), LOW, VMEM)
    gathers = Gather.count(levels, CHUNKS)
    lasting = Fetch.count(levels)
    return launch(
        "forward_planes",
        ident,
        kernel,
        (
            lasting[0],
            max(gathers + Scatter.count(levels, SUM_CHUNKS), 7 + Gather.count(levels, 1) + gathers),
            lasting[1] + 2 + levels + 2 * 4 * levels,
        ),
        dict(
            boundary=(boundary, HBM),
            packed=(packed, VMEM),
            query_segment=(segments[0], VMEM),
            key_segment=(segments[1], VMEM),
            shard0=(shards[0], HBM),
            shard1=(shards[1], HBM),
            shard2=(shards[2], HBM),
            shard3=(shards[3], HBM),
        ),
        dict(
            planes=((2, rows, width), LOW, VMEM),
            leaving=((2, rows, width), LOW, VMEM),
            middle=((2, rows, width), WIDE, VMEM),
            norms=((2, HEAD_LINES, width), WIDE, VMEM),
            queries=head,
            keys=head,
            values=head,
            mixed=head,
            log_total=((2, tokens, 1), WIDE, VMEM),
            gathered=((tokens, width), LOW, HBM),
            rows_a=((2, tokens, width), LOW, HBM),
            rows_b=((2, tokens, width), LOW, HBM),
            preact=((2, tokens, units), WIDE, HBM),
            activated=((2, tokens, units), LOW, HBM),
            out0=((2,) + slice_shapes[0], LOW, HBM),
            out1=((2,) + slice_shapes[1], LOW, HBM),
            out2=((2,) + slice_shapes[2], LOW, HBM),
            out3=((2,) + slice_shapes[3], LOW, HBM),
        ),
        dict(
            scatter_scratch(rows, width, levels, SUM_CHUNKS),
            rows=VMEM((2, tokens, width), LOW),
            gather_sems=DMAS((2, blocks, CHUNKS)),
            small=VMEM((2 * blocks * LINES, HD), LOW),
            small_sems=DMAS((blocks, 1)),
            pair_sem=DMAS((1,)),
            inward_sems=DMAS((2,)),
            landed_planes=VMEM((2, rows, width), LOW),
            b_qv=VMEM((2, 2, HD), WIDE),
            b_up=VMEM((2, 1, units), WIDE),
            w0=VMEM((2,) + slice_shapes[0], LOW),
            w1=VMEM((2,) + slice_shapes[1], LOW),
            w2=VMEM((2,) + slice_shapes[2], LOW),
            w3=VMEM((2,) + slice_shapes[3], LOW),
            own_preact=VMEM((2, tokens, units), WIDE),
            own_activated=VMEM((2, tokens, units), LOW),
            column_sems=DMAS((4, 2, levels)),
            cross_sems=DMAS((4, 2, levels)),
        ),
    )


def backward_planes(ident, kept, segments):
    levels = lax.axis_size("dp") // 2
    blocks, members = (4 * levels, 2 * levels)
    rows, width = kept.planes.shape[1:]
    tokens, size = (blocks * rows, 4 * rows)
    slice_shapes = [array.shape[1:] for array in (kept.out0, kept.out1, kept.out2, kept.out3)]
    shard_shapes = [shard_shape(which, shape, members) for which, shape in enumerate(slice_shapes)]
    units = slice_shapes[2][1]
    unit_lines = units // HD
    scaling = HD ** (-0.5)
    vector_lines = (2 + members) * HEAD_LINES

    def landing(which):
        shape = slice_shapes[which]
        if by_rows(which):
            return VMEM((2, levels, shape[0], shape[1] // members), LOW)
        return VMEM((2, levels, shape[0] // members, shape[1]), LOW)

    def kernel(refs, plane, greet, sends, copies):
        own_block = span(plane.block, rows)
        back = Return(
            plane,
            [refs.grad0, refs.grad1, refs.grad2, refs.grad3],
            [refs.landed0, refs.landed1, refs.landed2, refs.landed3],
            [refs.shard0, refs.shard1, refs.shard2, refs.shard3],
            refs,
            sends,
            copies,
        )
        acts = Outward(plane, refs.acts, refs.acts_sems)
        ends = Outward(plane, refs.input_grads, refs.ends_sems)

        def load(layer):
            return [
                copies.start(refs.out3.at[layer], refs.w3),
                copies.start(refs.preact.at[layer], refs.own_preact),
                copies.start(refs.out2.at[layer], refs.w2),
                copies.start(refs.activated.at[layer], refs.own_activated),
                copies.start(refs.rows_b.at[layer], refs.own_rows),
                copies.start(refs.out1.at[layer], refs.w1),
                copies.start(refs.out0.at[layer], refs.w0),
                copies.start(refs.all_queries.at[layer], refs.queries),
                copies.start(refs.all_keys.at[layer], refs.keys),
                copies.start(refs.all_values.at[layer], refs.values),
                copies.start(refs.all_mixed.at[layer], refs.mixed),
                copies.start(refs.all_totals.at[layer], refs.log_total),
            ]

        loads = load(1)
        first = copies.start(refs.gathered, refs.rows.at[0])
        greet()
        acts.give(0, refs.leaving.at[0], sends, copies)
        acts.give(1, refs.leaving.at[1], sends, copies)

        for layer in (1, 0):
            number = 2 * (1 - layer)
            norms = refs.norms.at[layer]
            vectors = refs.vectors.at[layer]
            held, sems = (refs.rows.at[number % 2], refs.gather_sems.at[number % 2])
            phase = Sends(refs.phase_sems)
            low = refs.planes[1] if layer == 1 else refs.leaving_grads[1].astype(LOW)
            vectors[5:6] = jnp.sum(low.astype(WIDE), axis=0, keepdims=True)
            refs.unit_sums[layer] = jnp.zeros((1, units), WIDE)
            if layer == 0:
                held[own_block] = low
                gather = Gather(plane, phase, held, sems)
                gather.open()
            else:
                copies.wait(first)
            copies.wait(loads[0], loads[1])

            def slope(step, zz):
                group = span(zz, size)
                grad_act = dot_back(held[group], refs.w3[...])
                value = refs.own_preact[group]
                rise = 0.5 * (1.0 + lax.erf(value * math.sqrt(0.5))) + value * jnp.exp(
                    -0.5 * value * value
                ) * (1.0 / math.sqrt(2.0 * math.pi))
                grad_pre = (grad_act * rise).astype(LOW)
                refs.grad_pre[group] = grad_pre
                refs.unit_sums[layer] += jnp.sum(grad_pre.astype(WIDE), axis=0, keepdims=True)

            if layer == 0:
                gather.run(slope, back.tick)
            copies.wait(loads[2])

            def widen_units(step, zz):
                group = span(zz, size)
                if layer == 1:
                    slope(step, zz)
                for cut in range(0, width, CUT):
                    refs.part[group, cut : cut + CUT] = dot_back(
                        refs.grad_pre[group], refs.w2[cut : cut + CUT]
                    ).astype(LOW)

            def down_product(at, carry):
                cut = span(at, 128)
                refs.grad3[cut] = dot_rows(refs.own_activated[:, cut], held[...]).astype(LOW)
                return carry

            def up_product(at, carry):
                cut = span(at, 256)
                refs.grad2[cut] = dot_rows(refs.own_rows[:, cut], refs.grad_pre[...]).astype(LOW)
                return carry

            def products(at):
                if at == 0:
                    copies.wait(loads[3], loads[4])
                    if layer == 0:
                        back.require(1, 3)
                        back.require(1, 2)
                    lax.fori_loop(0, units // 128, down_product, 0)
                    back.give(layer, 3)
                if at == 1:
                    lax.fori_loop(0, width // 512, up_product, 0)
                if at == 2:
                    lax.fori_loop(width // 512, width // 256, up_product, 0)
                    back.give(layer, 2)

            Scatter(plane, phase, refs, refs.sum).run(widen_units, back.tick, products)
            loads.append(copies.start(refs.rows_a.at[layer], refs.own_rows))
            _, unit, inverse = layer_norm(refs.middle[layer], norms[1:2], norms[1:2])
            vectors[1:2] = jnp.sum(refs.sum[...] * unit, axis=0, keepdims=True)
            vectors[4:5] = jnp.sum(refs.sum[...], axis=0, keepdims=True)
            grad_out = refs.planes[1].astype(WIDE) if layer == 1 else refs.leaving_grads[1].astype(LOW).astype(WIDE)
            grad_middle = grad_out + norm_back(refs.sum[...], unit, inverse, norms[1:2])
            phase.finish()

            number = number + 1
            held, sems = (refs.rows.at[number % 2], refs.gather_sems.at[number % 2])
            phase = Sends(refs.phase_sems)
            refs.grad_middle[...] = grad_middle
            low = grad_middle.astype(LOW)
            held[own_block] = low
            gather = Gather(plane, phase, held, sems)
            gather.open()
            vectors[3:4] = jnp.sum(low.astype(WIDE), axis=0, keepdims=True)
            refs.grad_keys[...] = jnp.zeros_like(refs.grad_keys)
            refs.grad_values[...] = jnp.zeros_like(refs.grad_values)
            copies.wait(loads[5], *loads[7:12])

            def attend(step, zz):
                group = span(zz, size)
                live = (refs.query_segment[group] >= 0).astype(WIDE)
                grad_mixed = (
                    dot_back(held[group], refs.w1[...]).astype(LOW) * live
                ).astype(LOW)
                allowed = visible(refs, group, size, tokens)
                queries = refs.queries[group]
                scores = dot_back(queries, refs.keys[...]) * scaling
                scores = jnp.where(allowed, scores, NEG_FILL)
                probs = jnp.exp(scores - refs.log_total[group])
                grad_probs = dot_back(grad_mixed, refs.values[...])
                delta = jnp.sum(probs * grad_probs, axis=-1, keepdims=True)
                grad_scores = jnp.where(allowed, probs * (grad_probs - delta), 0.0).astype(LOW)
                refs.grad_proj[group, :HD] = (dot(grad_scores, refs.keys[...]) * scaling).astype(LOW)
                refs.grad_keys[...] += dot_rows(grad_scores, queries)
                refs.grad_values[...] += dot_rows(probs.astype(LOW), grad_mixed)

            gather.run(attend, back.tick)
            refs.grad_proj[:, HD : 2 * HD] = (refs.grad_keys[...] * scaling).astype(LOW)
            refs.grad_proj[:, 2 * HD :] = refs.grad_values[...].astype(LOW)
            copies.wait(loads[6])

            def widen_heads(step, zz):
                group = span(zz, size)
                for cut in range(0, width, CUT):
                    refs.part[group, cut : cut + CUT] = dot_back(
                        refs.grad_proj[group], refs.w0[cut : cut + CUT]
                    ).astype(LOW)

            def qkv_product(at, carry):
                cut = span(at, 256)
                refs.grad0[cut] = dot_rows(refs.own_rows[:, cut], refs.grad_proj[...]).astype(LOW)
                return carry

            def more_products(at):
                if at == 0:
                    sums = jnp.sum(refs.grad_proj[...].astype(WIDE), axis=0, keepdims=True)
                    refs.head_sums[layer, 0:1] = sums[:, :HD]
                    refs.head_sums[layer, 1:2] = sums[:, 2 * HD :]
                    copies.wait(loads[12])
                    if layer == 0:
                        back.require(1, 1)
                        back.require(1, 0)
                if at == (1 if layer else 0):
                    refs.grad1[...] = dot_rows(refs.mixed[...], held[...]).astype(LOW)
                    back.give(layer, 1)
                if at == (2 if layer else 0):
                    lax.fori_loop(0, width // 512, qkv_product, 0)
                if at == (3 if layer else 0):
                    lax.fori_loop(width // 512, width // 256, qkv_product, 0)
                    back.give(layer, 0)

            Scatter(plane, phase, refs, refs.sum).run(widen_heads, back.tick, more_products)
            if layer == 1:
                loads = load(0)
            entering = refs.planes[0] if layer == 0 else refs.leaving[0]
            _, unit, inverse = layer_norm(entering.astype(WIDE), norms[0:1], norms[0:1])
            vectors[0:1] = jnp.sum(refs.sum[...] * unit, axis=0, keepdims=True)
            vectors[2:3] = jnp.sum(refs.sum[...], axis=0, keepdims=True)
            refs.leaving_grads[layer] = refs.grad_middle[...] + norm_back(
                refs.sum[...], unit, inverse, norms[0:1]
            )
            ends.give(layer, refs.leaving_grads.at[layer], sends, copies)
            phase.finish()

        tail = SimpleNamespace(
            part=refs.vector_part,
            from_sibling=refs.vector_from_sibling,
            from_across=refs.vector_from_across,
            from_behind=refs.vector_from_behind,
            total=refs.vector_total,
            sibling_sems=refs.vector_sibling_sems,
            across_sems=refs.vector_across_sems,
            behind_sems=refs.vector_behind_sems,
        )
        tail.part[...] = jnp.zeros_like(tail.part)
        for layer in (0, 1):
            own = [refs.head_sums[layer]]
            for at in range(unit_lines):
                own.append(refs.unit_sums[layer, :, at * HD : (at + 1) * HD])
            own.append(jnp.zeros((HEAD_LINES - 2 - unit_lines, HD), WIDE))
            own = jnp.concatenate(own, axis=0)
            for z in range(levels):
                for y in (0, 1):
                    base = (z * 4 + layer * 2 + y) * vector_lines
                    for x in (0, 1):
                        cut = (z * 4 + x * 2 + y) * HD
                        line = base + x * HEAD_LINES
                        tail.part[line : line + HEAD_LINES] = refs.vectors[layer, :, cut : cut + HD]
                start = (z * 4 + layer * 2 + plane.y) * vector_lines
                start = start + (2 + plane.member) * HEAD_LINES
                tail.part[pl.ds(pl.multiple_of(start, HEAD_LINES), HEAD_LINES)] = own
        phase = Sends(refs.phase_sems)
        Scatter(plane, phase, tail, refs.vector_sum).run(lambda step, zz: None, back.tick)
        phase.start(True, refs.vector_sum, refs.vector_other, refs.pair_sem.at[0], plane.over)
        await_block(refs.vector_other, refs.pair_sem.at[0], plane.over)
        refs.vector_out[...] = refs.vector_sum[...] + refs.vector_other[...]
        acts.finish()
        back.finish()
        ends.finish()
        phase.finish()

    lasting = Return.count(levels)
    outward = Outward.count()
    vector = scatter_scratch(vector_lines, HD, levels, 1, WIDE)
    return launch(
        "backward_planes",
        ident,
        kernel,
        (
            lasting[0] + 2 * outward[0],
            Gather.count(levels, CHUNKS) + Scatter.count(levels, SUM_CHUNKS),
            lasting[1] + 2 * outward[1] + 2 * 13 + 1,
        ),
        dict(
            planes=(kept.planes, VMEM),
            leaving=(kept.leaving, VMEM),
            middle=(kept.middle, VMEM),
            norms=(kept.norms, VMEM),
            query_segment=(segments[0], VMEM),
            key_segment=(segments[1], VMEM),
            all_queries=(kept.queries, HBM),
            all_keys=(kept.keys, HBM),
            all_values=(kept.values, HBM),
            all_mixed=(kept.mixed, HBM),
            all_totals=(kept.log_total, HBM),
            gathered=(kept.gathered, HBM),
            rows_a=(kept.rows_a, HBM),
            rows_b=(kept.rows_b, HBM),
            preact=(kept.preact, HBM),
            activated=(kept.activated, HBM),
            out0=(kept.out0, HBM),
            out1=(kept.out1, HBM),
            out2=(kept.out2, HBM),
            out3=(kept.out3, HBM),
        ),
        dict(
            acts=((2, rows, width), LOW, HBM),
            input_grads=((2, rows, width), WIDE, HBM),
            shard0=(shard_shapes[0], LOW, HBM),
            shard1=(shard_shapes[1], LOW, HBM),
            shard2=(shard_shapes[2], LOW, HBM),
            shard3=(shard_shapes[3], LOW, HBM),
            vector_out=((vector_lines, HD), WIDE, VMEM),
        ),
        dict(
            scatter_scratch(rows, width, levels, SUM_CHUNKS),
            rows=VMEM((2, tokens, width), LOW),
            gather_sems=DMAS((2, blocks, CHUNKS)),
            w0=VMEM(slice_shapes[0], LOW),
            w1=VMEM(slice_shapes[1], LOW),
            w2=VMEM(slice_shapes[2], LOW),
            w3=VMEM(slice_shapes[3], LOW),
            own_preact=VMEM((tokens, units), WIDE),
            own_activated=VMEM((tokens, units), LOW),
            own_rows=VMEM((tokens, width), LOW),
            grad_pre=VMEM((tokens, units), LOW),
            grad_proj=VMEM((tokens, 3 * HD), LOW),
            queries=VMEM((tokens, HD), LOW),
            keys=VMEM((tokens, HD), LOW),
            values=VMEM((tokens, HD), LOW),
            mixed=VMEM((tokens, HD), LOW),
            log_total=VMEM((tokens, 1), WIDE),
            grad_keys=VMEM((tokens, HD), WIDE),
            grad_values=VMEM((tokens, HD), WIDE),
            grad_middle=VMEM((rows, width), WIDE),
            leaving_grads=VMEM((2, rows, width), WIDE),
            grad0=VMEM(slice_shapes[0], LOW),
            grad1=VMEM(slice_shapes[1], LOW),
            grad2=VMEM(slice_shapes[2], LOW),
            grad3=VMEM(slice_shapes[3], LOW),
            landed0=landing(0),
            landed1=landing(1),
            landed2=landing(2),
            landed3=landing(3),
            column_sems=DMAS((4, 2, levels)),
            cross_sems=DMAS((4, 2, levels)),
            acts_sems=DMAS((2,)),
            ends_sems=DMAS((2,)),
            pair_sem=DMAS((1,)),
            vectors=VMEM((2, HEAD_LINES, width), WIDE),
            head_sums=VMEM((2, 2, HD), WIDE),
            unit_sums=VMEM((2, 1, units), WIDE),
            vector_part=vector["part"],
            vector_from_sibling=vector["from_sibling"],
            vector_from_across=vector["from_across"],
            vector_from_behind=vector["from_behind"],
            vector_total=vector["total"],
            vector_sum=vector["sum"],
            vector_other=VMEM((vector_lines, HD), WIDE),
            vector_sibling_sems=vector["sibling_sems"],
            vector_across_sems=vector["across_sems"],
            vector_behind_sems=vector["behind_sems"],
        ),
    )


def plane_body(
    boundary,
    doc_lengths,
    qkv_weight,
    qv_bias,
    out_weight,
    up_weight,
    up_bias,
    down_weight,
    norm_gains,
    norm_biases,
):
    plane = Plane()
    levels = plane.levels
    members = 2 * levels
    head_cut = qv_bias.shape[3]
    block_shard = up_bias.shape[1]
    own_blocks = block_shard // members

    def lines(piece):
        return piece.reshape(-1, HD)

    packed = jnp.concatenate(
        (
            lines(norm_gains[0]),
            lines(norm_biases[0]),
            jnp.zeros((HEAD_LINES - NORM_LINES, HD), LOW),
            lines(qv_bias[0]),
            lines(up_bias[0]),
            jnp.zeros((LINES - HEAD_LINES - 2 - up_bias[0].size // HD, HD), LOW),
        )
    )
    lengths = lax.dynamic_index_in_dim(doc_lengths, plane.x, 0, keepdims=False)
    tokens = boundary.shape[2] * 4 * levels
    _, segment, live, _, _, _ = visibility(lengths, 0, tokens, tokens)
    segments = (jnp.where(live, segment, -1)[:, None], segment[None, :])

    kept = forward_planes(
        0, boundary[0], packed, segments, (qkv_weight[0].transpose(1, 0, 2), out_weight[0], up_weight[0], down_weight[0])
    )
    end = backward_planes(1, kept, segments)

    summed = end.vector_out.reshape(2 + members, HEAD_LINES, HD)
    norms = lax.dynamic_index_in_dim(summed, plane.x, 0, keepdims=False)
    by_member = lax.dynamic_slice_in_dim(
        summed[2:], (plane.z * 2 + plane.x) * head_cut, head_cut, axis=2
    )
    return (
        end.acts[None],
        end.input_grads[None],
        end.shard0.transpose(1, 0, 2).astype(WIDE)[None],
        by_member[:, :2].transpose(1, 0, 2)[None],
        end.shard1.astype(WIDE)[None],
        end.shard2.astype(WIDE)[None],
        by_member[:, 2 : 2 + own_blocks].reshape(1, block_shard, head_cut),
        end.shard3.astype(WIDE)[None],
        norms[None, :2],
        norms[None, 2:NORM_LINES],
    )


def fits_plane(mesh):
    return mesh.shape["dp"] == 8 and mesh.shape["tensor"] == 2 and mesh.shape["section"] == 2


def solution(mesh):
    placed = (
        P("section", None, ("dp", "tensor"), None),
        P(),
        P("section", "dp", None, "tensor"),
        P("section", None, "tensor", "dp"),
        P("section", "tensor", "dp"),
        P("section", "dp", "tensor"),
        P("section", "tensor", "dp"),
        P("section", "tensor", "dp"),
        P("section", None, ("dp", "tensor")),
        P("section", None, ("dp", "tensor")),
    )
    return jax.shard_map(
        plane_body if fits_plane(mesh) else body,
        mesh=mesh,
        in_specs=placed,
        out_specs=(
            P("section", None, ("dp", "tensor"), None),
            P("section", None, ("dp", "tensor"), None),
            P("section", "dp", None, "tensor"),
            P("section", None, "tensor", "dp"),
            P("section", "tensor", "dp"),
            P("section", "dp", "tensor"),
            P("section", "tensor", "dp"),
            P("section", "tensor", "dp"),
            P("section", None, ("dp", "tensor")),
            P("section", None, ("dp", "tensor")),
        ),
        check_vma=False,
    )
```
